32 devices in a mesh: leaf: 8 (over y, x, core), path: 4 (over z).
Axes of the slice: x: 2, y: 2, z: 4, core: 2. Of those that a mesh axis runs over, the one named last changes fastest.
Arguments:
- tokens: bfloat16 [8, 2048, 768], P('leaf', 'path'), may hold values from -6 to 6
- encoded: bfloat16 [8, 1024, 768], P('leaf', 'path'), may hold values from -6 to 6
- cotangent: bfloat16 [8, 2048, 768], P('leaf', 'path'), may hold values from -6 to 6
- parent: int32 [8, 16], P('leaf'), may hold values from 0 to 14, as said below
- assignment: int32 [8, 16], P('leaf'), may hold values from 0 to 15, each once within a row
- attn_in: bfloat16 [6, 768, 768], P(None, ('leaf', 'path')), may hold values from -0.21875 to 0.21875
- attn_out: bfloat16 [2, 768, 768], P(None, ('leaf', 'path')), may hold values from -2.5 to 2.5
- ffn_in: bfloat16 [768, 3072], P(('leaf', 'path')), may hold values from -0.21875 to 0.21875
- ffn_out: bfloat16 [3072, 768], P(('leaf', 'path')), may hold values from -0.109375 to 0.109375
- shifts: bfloat16 [10, 768], P(None, ('leaf', 'path')), may hold values from -0.3984375 to 0.3984375
- gains: bfloat16 [3, 768], P(None, ('leaf', 'path')), may hold values from 0.5 to 1.5
- ffn_bias: bfloat16 [3072], P(('leaf', 'path')), may hold values from -0.5 to 0.5
Outputs:
- output: bfloat16 [8, 2048, 768], P('leaf', 'path')
- grad_tokens: float32 [8, 2048, 768], P('leaf', 'path')
- grad_encoded: float32 [8, 1024, 768], P('leaf', 'path')
- grad_attn_in: float32 [6, 768, 768], P(None, ('leaf', 'path'))
- grad_attn_out: float32 [2, 768, 768], P(None, ('leaf', 'path'))
- grad_ffn_in: float32 [768, 3072], P(('leaf', 'path'))
- grad_ffn_out: float32 [3072, 768], P(('leaf', 'path'))
- grad_shifts: float32 [10, 768], P(None, ('leaf', 'path'))
- grad_gains: float32 [3, 768], P(None, ('leaf', 'path'))
- gradient_feedforward_bias: float32 [3072], P(('leaf', 'path'))
The draws below stay inside these ranges and needn't reach their ends.
Inputs may be any that keep to these rules, and one draw needn't show every extreme that they name: Entry 0 of each tree is 0 (the root); every other block's parent is one of the three blocks before it, or block 0; block 15 continues block 14. `assignment`: each tree's entries are a permutation of 0 to 15.
All inputs are finite; a program needn't handle non-finite values.
Results may differ from the reference program's by a relative error of at most 0.02.
Values may be sent and summed in bfloat16 or wider, within the bound.
A program may use at most 192 MiB of HBM per device.

```python
import jax
import jax.numpy as jnp
from jax import lax

D = 768
HEADS = 12
FF = 3072
HEAD = 64
BLK = 128
NB = 16
ENC = 1024
TREES = 8
ROWS = 2048


def draw_parent(key, part):
    offsets = jax.random.randint(key, (TREES, NB), 1, 4)
    blocks = jnp.arange(NB, dtype=jnp.int32)[None, :]
    chosen = jnp.maximum(blocks - offsets, 0)
    chosen = jnp.where(blocks == NB - 1, NB - 2, chosen)
    return chosen.astype(jnp.int32)


def level_of(own_key, dims, cuts, low, high):
    def one(position, blocks):
        heights = jax.random.uniform(jax.random.fold_in(jax.random.fold_in(own_key, 6), position), (blocks,), jnp.float32, low / len(cuts), high / len(cuts))
        return jnp.repeat(jnp.exp(heights), dims[position] // blocks).reshape((-1,) + (1,) * (len(dims) - position - 1))

    factor_of = one(*cuts[0])
    for cut in cuts[1:]:
        factor_of = factor_of * one(*cut)
    return factor_of


def gaussian(key, extent, scale, most, split=(), held_as=jnp.bfloat16):
    values = scale * jax.random.normal(key, extent, jnp.float32)
    if split:
        values = values * level_of(key, extent, split, -0.22, 0.18)
    return jnp.clip(values, -most, most).astype(held_as)


def setup_inputs(seed: int = 0) -> dict:
    splits = jax.random.split(jax.random.key(seed), 13)
    tokens = gaussian(splits[0], (TREES, ROWS, D), 1.0, 6.0, ((0, 8), (1, 4)))
    encoded = gaussian(splits[1], (TREES, ENC, D), 1.0, 6.0, ((0, 8), (1, 4)))
    cotangent = gaussian(splits[2], (TREES, ROWS, D), 1.0, 6.0, ((0, 8), (1, 4)))
    parent = draw_parent(jax.random.fold_in(splits[12], 71), 0)
    assignment = jax.vmap(lambda own: jax.random.permutation(own, NB))(jax.random.split(splits[4], TREES)).reshape((TREES, NB)).astype(jnp.int32)
    attn_in = gaussian(splits[5], (6, D, D), D ** -0.5, 0.21875, ((1, 32),))
    attn_out = gaussian(splits[6], (2, D, D), (D // 128) ** -0.5, 2.5, ((1, 32),))
    ffn_in = gaussian(splits[7], (D, FF), D ** -0.5, 0.21875, ((0, 32),))
    ffn_out = gaussian(splits[8], (FF, D), FF ** -0.5, 0.109375, ((0, 32),))
    shifts = gaussian(splits[9], (10, D), 0.08, 0.3984375, ((1, 32),))
    gains = jnp.clip(1.0 + 0.1 * jax.random.normal(splits[10], (3, D), jnp.float32), 0.5, 1.5).astype(jnp.bfloat16)
    ffn_bias = gaussian(splits[11], (FF,), 0.1, 0.5, ((0, 32),))
    return dict(tokens=tokens, encoded=encoded, cotangent=cotangent, parent=parent, assignment=assignment, attn_in=attn_in, attn_out=attn_out, ffn_in=ffn_in, ffn_out=ffn_out, shifts=shifts, gains=gains, ffn_bias=ffn_bias)


@jax.custom_vjp
def low(v):
    return lax.optimization_barrier(v.astype(jnp.bfloat16)).astype(jnp.float32)

@jax.custom_vjp
def low_back(v):
    return v

def low_keep(v):
    return (low(v), None)

def low_pass(kept, grad):
    return (grad,)

def back_keep(v):
    return (v, None)

def back_low(kept, grad):
    return (low(grad),)
low.defvjp(low_keep, low_pass)
low_back.defvjp(back_keep, back_low)

def matmul(left, right):
    return jnp.dot(left, right, precision=lax.Precision.HIGHEST)

def layer_norm(values, norm_gain, norm_shift):
    centre = values - lax.optimization_barrier(jnp.mean(values, axis=-1, keepdims=True))
    spread = lax.optimization_barrier(jnp.mean(centre * centre, axis=-1, keepdims=True))
    return centre * lax.rsqrt(spread + 1e-05) * norm_gain + norm_shift

def gelu_exact(values):
    return 0.5 * values * (1.0 + jax.scipy.special.erf(values * 0.7071067811865476))

def slot_links(parent, assignment):
    block_count = parent.shape[1]
    blocks = jnp.arange(block_count, dtype=jnp.int32)
    upward = (parent[:, :, None] == blocks[None, None, :]) & (blocks[:, None] != blocks[None, :])[None]
    reached_ancestor = upward.astype(jnp.float32)
    for sweep_turn in range(block_count.bit_length()):
        reached_ancestor = jnp.minimum(reached_ancestor + jnp.einsum('fjd,fdz->fjz', reached_ancestor, reached_ancestor, precision=lax.Precision.HIGHEST), 1.0)
    placed = (assignment[:, :, None] == blocks[None, None, :]).astype(jnp.float32)
    linked = jnp.einsum('tsa,tab->tsb', placed, reached_ancestor, precision=lax.Precision.HIGHEST)
    return jnp.einsum('tsb,trb->tsr', linked, placed, precision=lax.Precision.HIGHEST)

def visible(linked, first_query, query_count, first_key, key_count):
    slot_ids = jnp.arange(linked.shape[1], dtype=jnp.int32)
    query_pos = first_query + jnp.arange(query_count, dtype=jnp.int32)
    key_pos = first_key + jnp.arange(key_count, dtype=jnp.int32)
    query_pick = (query_pos[:, None] // BLK == slot_ids[None, :]).astype(jnp.float32)
    key_pick = (key_pos[:, None] // BLK == slot_ids[None, :]).astype(jnp.float32)
    ancestral = jnp.einsum('qa,tab->tqb', query_pick, linked, precision=lax.Precision.HIGHEST)
    ancestral = jnp.einsum('tqb,kb->tqk', ancestral, key_pick, precision=lax.Precision.HIGHEST)
    inside = (query_pos[:, None] // BLK == key_pos[None, :] // BLK) & (key_pos[None, :] <= query_pos[:, None])
    return (ancestral > 0.5) | inside[None]

def attend(queries, key_rows, value_rows, allowed):
    row_count = queries.shape[0]

    def per_head(head_items):
        query_head, key_head, value_head = head_items
        scores = low_back(matmul(query_head, key_head.T))
        if allowed is not None:
            scores = jnp.where(allowed, scores, -1e+30)
        raised = jnp.exp(scores - lax.optimization_barrier(jnp.max(scores, axis=1, keepdims=True)))
        weights = raised / lax.optimization_barrier(jnp.sum(raised, axis=1, keepdims=True))
        return matmul(low(weights), value_head)

    def by_head(matrix):
        return matrix.reshape(matrix.shape[0], HEADS, HEAD).transpose(1, 0, 2)
    mixed = lax.map(jax.checkpoint(per_head), (by_head(queries), by_head(key_rows), by_head(value_rows)))
    return mixed.transpose(1, 0, 2).reshape(row_count, HEADS * HEAD)

def tree_forward(params, token_rows, encoder_rows, parent_row, assign_row):
    attn_in, attn_out, ffn_in, ffn_out, shifts, gains, ffn_bias = params
    score_scale = HEAD ** (-0.5)
    row_count = token_rows.shape[0]
    linked = slot_links(parent_row[None], assign_row[None])
    allowed = visible(linked, 0, row_count, 0, row_count)[0]
    queries = low(low_back((matmul(token_rows, attn_in[0]) + shifts[0]) * score_scale))
    key_rows = low(low_back(matmul(token_rows, attn_in[1])))
    value_rows = low(low_back(matmul(token_rows, attn_in[2]) + shifts[1]))
    attended = low(low_back(attend(queries, key_rows, value_rows, allowed)))
    branch = low_back(matmul(attended, attn_out[0]) + shifts[2])
    first_norm = layer_norm(token_rows + branch, gains[0], shifts[7])
    cross_queries = low(low_back((matmul(low(first_norm), attn_in[3]) + shifts[3]) * score_scale))
    cross_keys = low(low_back(matmul(encoder_rows, attn_in[4])))
    cross_values = low(low_back(matmul(encoder_rows, attn_in[5]) + shifts[4]))
    crossed = low(low_back(attend(cross_queries, cross_keys, cross_values, None)))
    cross_branch = low_back(matmul(crossed, attn_out[1]) + shifts[5])
    second_norm = layer_norm(first_norm + cross_branch, gains[1], shifts[8])
    hidden = low(gelu_exact(low_back(matmul(low(second_norm), ffn_in) + ffn_bias)))
    ffn_branch = low_back(matmul(hidden, ffn_out) + shifts[6])
    return layer_norm(second_norm + ffn_branch, gains[2], shifts[9])

def reference(tokens, encoded, cotangent, parent, assignment, attn_in, attn_out, ffn_in, ffn_out, shifts, gains, ffn_bias):
    params = tuple((argument.astype(jnp.float32) for argument in (attn_in, attn_out, ffn_in, ffn_out, shifts, gains, ffn_bias)))

    def forward(weight_set, token_all, encoder_all):

        def per_tree(tree_items):
            return tree_forward(weight_set, tree_items[0], tree_items[1], tree_items[2], tree_items[3])
        return lax.map(jax.checkpoint(per_tree), (token_all, encoder_all, parent, assignment))
    result, pullback = jax.vjp(forward, params, tokens.astype(jnp.float32), encoded.astype(jnp.float32))
    grad_params, grad_tokens, grad_encoded = pullback(cotangent.astype(jnp.float32))
    return (result.astype(jnp.bfloat16), grad_tokens, grad_encoded, grad_params[0], grad_params[1], grad_params[2], grad_params[3], grad_params[4], grad_params[5], grad_params[6])
```

```python
import functools

import jax
import jax.numpy as jnp
from jax import lax
from jax.experimental import pallas as pl
from jax.experimental.pallas import tpu as pltpu
from jax.sharding import PartitionSpec as P

HEAD = 64
BLK = 128
PAIR = 2 * HEAD
MESH = pl.DeviceIdType.MESH
F32 = jnp.float32
BF16 = jnp.bfloat16
VMEM_LIMIT = 62 * 1024 * 1024


class Place:
    def __init__(self, leaf_count, path_count):
        self.leafs, self.paths = leaf_count, path_count
        outer = leaf_count // 2
        self.A = 2 if outer % 2 == 0 else 1
        self.B = outer // self.A
        leaf = lax.axis_index("leaf")
        self.leaf, self.p = leaf, lax.axis_index("path")
        self.c = leaf % 2
        self.a = (leaf // 2) // self.B
        self.b = (leaf // 2) % self.B

    def leaf_at(self, a, b, c):
        return (a * self.B + b) * 2 + c

    def at_core(self):
        return (self.leaf_at(self.a, self.b, 1 - self.c), self.p)

    def at_a(self, a):
        return (self.leaf_at(a, self.b, self.c), self.p)

    def at_b(self, b):
        return (self.leaf_at(self.a, b, self.c), self.p)

    def at_p(self, p):
        return (self.leaf, p)

    def lines(self):
        return [
            (self.paths, self.p, self.at_p),
            (self.A, self.a, self.at_a),
            (self.B, self.b, self.at_b),
            (2, self.c, lambda c: (self.leaf_at(self.a, self.b, c), self.p)),
        ]


def greet(place):
    barrier = pltpu.get_barrier_semaphore()
    peers = 0
    for size, pos, to in place.lines():
        if size == 1:
            continue
        if size == 2:
            pl.semaphore_signal(barrier, inc=1, device_id=to(1 - pos), device_id_type=MESH)
            peers = peers + 1
            continue
        for step in (-1, 1):
            there = pos + step
            inside = (there >= 0) & (there < size)

            @pl.when(inside)
            def _():
                pl.semaphore_signal(barrier, inc=1, device_id=to(there), device_id_type=MESH)

            peers = peers + jnp.where(inside, 1, 0)
    pl.semaphore_wait(barrier, peers)


class Mail:
    def __init__(self, send_sems, recv_sems):
        self.send_sems, self.recv_sems = send_sems, recv_sems
        self.count = 0
        self.sent = []

    def post(self, when, src, dst, to, hear_when, landing):
        k = self.count
        self.count += 1
        send = pltpu.make_async_remote_copy(
            src_ref=src,
            dst_ref=dst,
            send_sem=self.send_sems.at[k],
            recv_sem=self.recv_sems.at[k],
            device_id=to,
            device_id_type=MESH,
        )
        hear = pltpu.make_async_remote_copy(
            src_ref=landing,
            dst_ref=landing,
            send_sem=self.send_sems.at[k],
            recv_sem=self.recv_sems.at[k],
            device_id=to,
            device_id_type=MESH,
        )
        self.sent.append((when, send))

        def start():
            guarded(when, send.start)

        def wait():
            guarded(hear_when, hear.wait_recv)

        return start, wait

    def finish(self):
        for when, send in self.sent:
            guarded(when, send.wait_send)


def guarded(when, action):
    if when is None:
        action()
    else:

        @pl.when(when)
        def _():
            action()


def clamp(index, size):
    return jnp.clip(index, 0, size - 1)


def flood(mail, line, views, src_views=None):
    size, pos, to = line
    steps = []
    if size == 1:
        return steps
    first = src_views if src_views is not None else views(pos)
    if size == 2:
        jobs = [
            mail.post(None, s, d, to(1 - pos), None, w)
            for s, d, w in zip(first, views(pos), views(1 - pos))
        ]
        return [([j[0] for j in jobs], [j[1] for j in jobs])]
    for step in range(1, size):
        starts, waits = [], []
        for sign in (1, -1):
            item = pos - sign * (step - 1)
            there = pos + sign
            when = (there >= 0) & (there < size) & (item >= 0) & (item < size)
            heard = pos - sign * step
            hear_when = (heard >= 0) & (heard < size)
            item_c = clamp(item, size)
            sources = first if step == 1 else views(item_c)
            for s, d, w in zip(sources, views(item_c), views(clamp(heard, size))):
                start, wait = mail.post(when, s, d, to(clamp(there, size)), hear_when, w)
                starts.append(start)
                waits.append(wait)
        steps.append((starts, waits))
    return steps


def run(actions):
    for action in actions:
        action()


def gather_stages(mail, place, shards, wholes):
    A, B, c = place.A, place.B, place.c

    def half(ref, leaf, h):
        width = ref.shape[-1] // 2
        return ref.at[:, leaf, :, :, pl.ds(h * width, width)]

    line_p, line_a, line_b, line_c = place.lines()
    along_p = flood(
        mail, line_p, lambda i: [w.at[:, place.leaf, i] for w in wholes], list(shards)
    )

    def of_b(h, across_a):
        ays = range(A) if across_a else [place.a]
        return lambda i: [half(w, place.leaf_at(a, i, c), h) for a in ays for w in wholes]

    def of_a(h, across_b):
        bees = range(B) if across_b else [place.b]
        return lambda i: [half(w, place.leaf_at(i, b, c), h) for b in bees for w in wholes]

    first = [flood(mail, line_b, of_b(0, False)), flood(mail, line_a, of_a(1, False))]
    second = [flood(mail, line_a, of_a(0, True)), flood(mail, line_b, of_b(1, True))]
    own_core = [
        mail.post(
            None,
            w.at[:, place.leaf],
            w.at[:, place.leaf],
            place.at_core(),
            None,
            w.at[:, place.leaf_at(place.a, place.b, 1 - c)],
        )
        for w in wholes
    ]
    rest_core = []
    for offset in range(1, A * B):
        spot = (place.a * B + place.b + offset) % (A * B)
        for w in wholes:
            rest_core.append(
                mail.post(
                    None,
                    w.at[:, spot * 2 + c],
                    w.at[:, spot * 2 + c],
                    place.at_core(),
                    None,
                    w.at[:, spot * 2 + 1 - c],
                )
            )
    stages = []
    pending = []

    def advance(waits, starts):
        def stage():
            run(waits)
            run(starts)

        stages.append(stage)

    for starts, waits in along_p:
        advance(pending, starts)
        pending = waits
    opening = [own_core[i][0] for i in range(len(wholes))]
    for phase in (first, second):
        for s in range(max(len(f) for f in phase)):
            starts, waits = [], []
            for f in phase:
                if s < len(f):
                    starts += f[s][0]
                    waits += f[s][1]
            advance(pending, starts + opening)
            opening = []
            pending = waits
    advance(pending, opening + [j[0] for j in rest_core])
    advance([j[1] for j in own_core + rest_core], [])
    return stages


def gather_kernel(sizes, n, n_rows, *refs):
    place = Place(*sizes)
    shards, rows = refs[:n], refs[n : n + n_rows]
    wholes, all_rows = refs[n + n_rows : 2 * n + n_rows], refs[2 * n + n_rows : 2 * (n + n_rows)]
    send_sems, recv_sems, own_sems = refs[2 * (n + n_rows) :]
    greet(place)
    mail = Mail(send_sems, recv_sems)
    own = []
    for k, (s, w) in enumerate(zip(shards, wholes)):
        own.append(pltpu.make_async_copy(s, w.at[:, place.leaf, place.p], own_sems.at[k]))
    for k, (s, w) in enumerate(zip(rows, all_rows)):
        own.append(pltpu.make_async_copy(s, w.at[place.p], own_sems.at[n + k]))
    for copy in own:
        copy.start()
    lists = [gather_stages(mail, place, [s], [w]) for s, w in zip(shards, wholes)]
    row_lists = []
    for s, w in zip(rows, all_rows):
        steps = flood(mail, place.lines()[0], lambda i, w=w: [w.at[i]], [s])
        stages = []
        pending = []
        for starts, waits in steps:
            stages.append(functools.partial(lambda p, q: (run(p), run(q)), pending, starts))
            pending = waits
        stages.append(functools.partial(run, pending))
        row_lists.append(stages)
    for copy in own:
        copy.wait()
    order = lists[:1] + row_lists + lists[1:]
    for t in range(max(len(l) + g for g, l in enumerate(order))):
        for g, l in enumerate(order):
            if 0 <= t - g < len(l):
                l[t - g]()
    mail.finish()


ANY = pl.BlockSpec(memory_space=pl.ANY)


def gather_all(sizes, shards, rows, collective_id):
    leafs, paths = sizes
    out_shape = [
        jax.ShapeDtypeStruct((s.shape[0], leafs, paths) + s.shape[1:], s.dtype) for s in shards
    ] + [jax.ShapeDtypeStruct((paths,) + r.shape, r.dtype) for r in rows]
    count = 100 * (len(shards) + len(rows))
    return pl.pallas_call(
        functools.partial(gather_kernel, sizes, len(shards), len(rows)),
        out_shape=out_shape,
        in_specs=[ANY] * (len(shards) + len(rows)),
        out_specs=[ANY] * len(out_shape),
        scratch_shapes=[
            pltpu.SemaphoreType.DMA((count,)),
            pltpu.SemaphoreType.DMA((count,)),
            pltpu.SemaphoreType.DMA((len(out_shape),)),
        ],
        compiler_params=pltpu.CompilerParams(
            collective_id=collective_id, has_side_effects=True, vmem_limit_bytes=VMEM_LIMIT
        ),
        name="gather_all",
    )(*shards, *rows)


def shift_sum(mail, line, mine, slots_up, slots_down, add):
    size, pos, to = line
    if size == 1:
        return []
    if size == 2:
        jobs = [
            mail.post(None, s, slot, to(1 - pos), None, slot)
            for s, slot in zip(mine(1 - pos), slots_up[0])
        ]

        def begin():
            run([j[0] for j in jobs])

        def end():
            for job, dst, slot in zip(jobs, mine(pos), slots_up[0]):
                job[1]()
                add(dst, slot)

        return [begin, end]
    stages = []
    for k in range(size - 1):
        actions = []
        for sign, slots in ((1, slots_up), (-1, slots_down)):
            dest = size - 1 - k if sign == 1 else k
            when = (pos < dest) if sign == 1 else (pos > dest)
            hear_when = (
                ((pos > 0) & (pos <= dest)) if sign == 1 else ((pos < size - 1) & (pos >= dest))
            )
            there = clamp(pos + sign, size)
            jobs = [
                mail.post(when, s, slot, to(there), None, slot)
                for s, slot in zip(mine(dest), slots[k])
            ]

            def take(jobs=jobs, dst_refs=mine(dest), slot_refs=slots[k]):
                for job, dst, slot in zip(jobs, dst_refs, slot_refs):
                    job[1]()
                    add(dst, slot)

            actions.append(functools.partial(guarded, hear_when, take))
            actions += [job[0] for job in jobs]
        stages.append(functools.partial(run, actions))
    return stages


def add_rows(dst, src):
    lead = dst.shape[:-2]
    total = 1
    for extent in lead:
        total *= extent

    def body(i, _):
        index = []
        rest = i
        for extent in reversed(lead):
            index.insert(0, rest % extent)
            rest = rest // extent
        index = tuple(index)
        dst[index] = dst[index] + src[index]
        return 0

    lax.fori_loop(0, total, body, 0)


def scatter_scratch(sizes, shapes, dtypes):
    leafs, paths = sizes
    outer = leafs // 2
    A = 2 if outer % 2 == 0 else 1
    B = outer // A
    out = []
    for (k, R, C), dtype in zip(shapes, dtypes):
        nb, na = max(B - 1, 1) * (2 if B > 2 else 1), max(A - 1, 1)
        out += [
            pltpu.VMEM((k, A, B, paths, R, C), dtype),
            pltpu.VMEM((k, A, B, paths, R, C), dtype),
            pltpu.VMEM((nb, k, A, paths, R, C // 2), dtype),
            pltpu.VMEM((na, k, paths, R, C // 2), dtype),
            pltpu.VMEM((na, k, B, paths, R, C // 2), dtype),
            pltpu.VMEM((nb, k, paths, R, C // 2), dtype),
            pltpu.VMEM((2 * max(paths - 1, 1), k, R, C), dtype),
        ]
    return out


def scatter_stages(mail, place, own_sem, partials, outs, scratch):
    A, B, c, p = place.A, place.B, place.c, place.p
    line_p, line_a, line_b, line_c = place.lines()
    groups = [scratch[7 * i : 7 * i + 7] for i in range(len(partials))]
    local = [
        pltpu.make_async_copy(x.at[:, :, :, c], g[0], own_sem.at[i])
        for i, (x, g) in enumerate(zip(partials, groups))
    ]
    cores = [
        mail.post(None, x.at[:, :, :, 1 - c], g[1], place.at_core(), None, g[1])
        for x, g in zip(partials, groups)
    ]

    def begin():
        for copy in local:
            copy.start()
        run([j[0] for j in cores])

    def join():
        for copy, job, g in zip(local, cores, groups):
            copy.wait()
            job[1]()
            add_rows(g[0], g[1])

    def cols(ref, h):
        width = ref.shape[-1] // 2
        return pl.ds(h * width, width)

    def up_down(ref, size, at):
        if size <= 2:
            return [[at(r, 0) for r in ref]], None
        return (
            [[at(r, k) for r in ref] for k in range(size - 1)],
            [[at(r, size - 1 + k) for r in ref] for k in range(size - 1)],
        )

    acc = [g[0] for g in groups]
    pick = lambda r, k: r.at[k]
    up, down = up_down([g[2] for g in groups], B, pick)
    h0_b = shift_sum(
        mail, line_b, lambda d: [x.at[:, :, d, :, :, cols(x, 0)] for x in acc], up, down, add_rows
    )
    up, down = up_down([g[3] for g in groups], A, pick)
    h0_a = shift_sum(
        mail, line_a, lambda d: [x.at[:, d, place.b, :, :, cols(x, 0)] for x in acc], up, down, add_rows
    )
    up, down = up_down([g[4] for g in groups], A, pick)
    h1_a = shift_sum(
        mail, line_a, lambda d: [x.at[:, d, :, :, :, cols(x, 1)] for x in acc], up, down, add_rows
    )
    up, down = up_down([g[5] for g in groups], B, pick)
    h1_b = shift_sum(
        mail, line_b, lambda d: [x.at[:, place.a, d, :, :, cols(x, 1)] for x in acc], up, down, add_rows
    )
    up, down = up_down([g[6] for g in groups], place.paths, pick)
    along_p = shift_sum(
        mail, line_p, lambda d: [x.at[:, place.a, place.b, d] for x in acc], up, down, add_rows
    )

    def finish():
        for x, out in zip(acc, outs):
            for j in range(out.shape[0]):
                out[j] = x[j, place.a, place.b, p].astype(out.dtype)

    def side_by_side(one, two):
        merged = []
        for k in range(max(len(one), len(two))):
            merged.append(functools.partial(run, [s[k] for s in (one, two) if k < len(s)]))
        return merged

    return [
        begin,
        join,
        *side_by_side(h0_b, h1_a),
        *side_by_side(h0_a, h1_b),
        *along_p,
        finish,
    ]


def scatter_kernel(sizes, n, n_rows, *refs):
    place = Place(*sizes)
    partials, rows = refs[:n], refs[n : n + n_rows]
    bases = refs[n + n_rows : n + 2 * n_rows]
    refs = refs[n + 2 * n_rows :]
    outs, row_outs = refs[:n], refs[n : n + n_rows]
    refs = refs[n + n_rows :]
    send_sems, recv_sems, own_sems = refs[:3]
    scratch = refs[3 : 3 + 7 * n]
    row_scratch = refs[3 + 7 * n :]
    greet(place)
    mail = Mail(send_sems, recv_sems)
    line_p = place.lines()[0]
    lists = []
    for i in range(n):
        lists.append(
            scatter_stages(
                mail,
                place,
                own_sems.at[pl.ds(i, 1)],
                [partials[i]],
                [outs[i]],
                scratch[7 * i : 7 * i + 7],
            )
        )
    row_lists = []
    for i in range(n_rows):
        held, slots = row_scratch[2 * i : 2 * i + 2]
        load = pltpu.make_async_copy(rows[i], held, own_sems.at[n + i])
        size = place.paths
        if size == 2:
            ups, downs = [[slots.at[0]]], None
        else:
            ups = [[slots.at[k]] for k in range(size - 1)]
            downs = [[slots.at[size - 1 + k]] for k in range(size - 1)]
        load.start()
        load.wait()
        stages = shift_sum(
            mail, line_p, lambda d, held=held: [held.at[d]], ups, downs, add_tall
        )

        def last(i=i, held=held):
            def body(r, _):
                at = pl.ds(pl.multiple_of(r * 16, 16), 16)
                row_outs[i][at] = bases[i][at] + held[place.p, at].astype(F32)
                return 0

            lax.fori_loop(0, row_outs[i].shape[0] // 16, body, 0)

        row_lists.append(stages + [last])
    order = row_lists + lists
    for t in range(max(len(l) + g for g, l in enumerate(order))):
        for g, l in enumerate(order):
            if 0 <= t - g < len(l):
                l[t - g]()
    mail.finish()


def add_tall(dst, src):
    def body(r, _):
        at = pl.ds(pl.multiple_of(r * 16, 16), 16)
        dst[at] = dst[at] + src[at]
        return 0

    lax.fori_loop(0, dst.shape[0] // 16, body, 0)


def scatter_all(sizes, partials, rows, bases, collective_id):
    leafs, paths = sizes
    outer = leafs // 2
    A = 2 if outer % 2 == 0 else 1
    B = outer // A
    shapes = [(x.shape[0],) + x.shape[3:] for x in partials]
    partials = [
        x.reshape((x.shape[0], A, B, 2, paths) + x.shape[3:]) for x in partials
    ]
    n, n_rows = len(partials), len(rows)
    out_shape = [jax.ShapeDtypeStruct(s, F32) for s in shapes] + [
        jax.ShapeDtypeStruct(b.shape, F32) for b in bases
    ]
    row_scratch = []
    for r in rows:
        row_scratch += [
            pltpu.VMEM(r.shape, r.dtype),
            pltpu.VMEM((2 * max(paths - 1, 1),) + r.shape[1:], r.dtype),
        ]
    count = 120 * (n + n_rows)
    VM = pl.BlockSpec(memory_space=pltpu.VMEM)
    return pl.pallas_call(
        functools.partial(scatter_kernel, sizes, n, n_rows),
        out_shape=out_shape,
        in_specs=[ANY] * (n + n_rows) + [VM] * n_rows,
        out_specs=[VM] * (n + n_rows),
        scratch_shapes=[
            pltpu.SemaphoreType.DMA((count,)),
            pltpu.SemaphoreType.DMA((count,)),
            pltpu.SemaphoreType.DMA((n + n_rows,)),
            *scatter_scratch(sizes, shapes, [x.dtype for x in partials]),
            *row_scratch,
        ],
        compiler_params=pltpu.CompilerParams(
            collective_id=collective_id, has_side_effects=True, vmem_limit_bytes=VMEM_LIMIT
        ),
        name="scatter_all",
    )(*partials, *rows, *bases)


def dot(x, y, contract):
    return lax.dot_general(x, y, (contract, ((), ())), preferred_element_type=F32)


def attend_kernel(masked, q_ref, k_ref, v_ref, *refs):
    if masked:
        bias_ref, o_ref, lse_ref = refs
    else:
        o_ref, lse_ref = refs
    rows = q_ref.shape[0]
    step = min(256, rows)
    lane = lax.broadcasted_iota(jnp.int32, (1, PAIR), 1)
    k = k_ref[...]
    v = v_ref[...]

    def block(i, _):
        at = pl.ds(pl.multiple_of(i * step, step), step)
        q = q_ref[at]
        out = jnp.zeros((step, PAIR), F32)
        lse = jnp.zeros((step, PAIR), F32)
        for h in range(2):
            own = (lane >= HEAD) if h else (lane < HEAD)
            s = dot(jnp.where(own, q, jnp.zeros_like(q)), k, ((1,), (1,)))
            if masked:
                s = s + bias_ref[at].astype(F32)
            peak = jnp.max(s, axis=1, keepdims=True)
            e = jnp.exp(s - peak)
            mass = jnp.sum(e, axis=1, keepdims=True)
            o = dot(e.astype(BF16), v, ((1,), (0,)))
            out = jnp.where(own, o / mass, out)
            lse = jnp.where(own, peak + jnp.log(mass), lse)
        o_ref[at] = out.astype(BF16)
        lse_ref[at] = lse
        return 0

    lax.fori_loop(0, rows // step, block, 0)


def attend(q, k, v, bias):
    rows, width = q.shape
    keys = k.shape[0]
    pairs = width // PAIR
    qs = pl.BlockSpec((rows, PAIR), lambda h: (0, h))
    ks = pl.BlockSpec((keys, PAIR), lambda h: (0, h))
    ins, specs = [q, k, v], [qs, ks, ks]
    if bias is not None:
        ins.append(bias)
        specs.append(pl.BlockSpec((rows, keys), lambda h: (0, 0)))
    return pl.pallas_call(
        functools.partial(attend_kernel, bias is not None),
        grid=(pairs,),
        in_specs=specs,
        out_specs=[qs, qs],
        out_shape=[
            jax.ShapeDtypeStruct((rows, width), BF16),
            jax.ShapeDtypeStruct((rows, width), F32),
        ],
        compiler_params=pltpu.CompilerParams(vmem_limit_bytes=VMEM_LIMIT),
        name="attend",
    )(*ins)


def attend_back_kernel(masked, q_ref, k_ref, v_ref, do_ref, o_ref, lse_ref, *refs):
    if masked:
        bias_ref, dq_ref, dk_ref, dv_ref, dk_acc, dv_acc = refs
    else:
        dq_ref, dk_ref, dv_ref, dk_acc, dv_acc = refs
    rows = q_ref.shape[0]
    step = min(256, rows)
    lane = lax.broadcasted_iota(jnp.int32, (1, PAIR), 1)
    k = k_ref[...]
    v = v_ref[...]
    dk_acc[...] = jnp.zeros_like(dk_acc)
    dv_acc[...] = jnp.zeros_like(dv_acc)

    def block(i, _):
        at = pl.ds(pl.multiple_of(i * step, step), step)
        q = q_ref[at]
        do = do_ref[at]
        both = do.astype(F32) * o_ref[at].astype(F32)
        lse_pair = lse_ref[at]
        dq = jnp.zeros((step, PAIR), F32)
        for h in range(2):
            own = (lane >= HEAD) if h else (lane < HEAD)
            q_h = jnp.where(own, q, jnp.zeros_like(q))
            do_h = jnp.where(own, do, jnp.zeros_like(do))
            delta = jnp.sum(jnp.where(own, both, 0.0), axis=1, keepdims=True)
            lse = lse_pair[:, h * HEAD : h * HEAD + 1]
            s = dot(q_h, k, ((1,), (1,)))
            if masked:
                s = s + bias_ref[at].astype(F32)
            e = jnp.exp(s - lse)
            dp = dot(do_h, v, ((1,), (1,)))
            ds = (e * (dp - delta)).astype(BF16)
            dq = jnp.where(own, dot(ds, k, ((1,), (0,))), dq)
            dk_acc[...] += dot(ds, q_h, ((0,), (0,)))
            dv_acc[...] += dot(e.astype(BF16), do_h, ((0,), (0,)))
        dq_ref[at] = (dq.astype(BF16) * BF16(HEAD**-0.5)).astype(BF16)
        return 0

    lax.fori_loop(0, rows // step, block, 0)
    dk_ref[...] = dk_acc[...].astype(BF16)
    dv_ref[...] = dv_acc[...].astype(BF16)


def attend_back(q, k, v, do, o, lse, bias):
    rows, width = q.shape
    keys = k.shape[0]
    pairs = width // PAIR
    qs = pl.BlockSpec((rows, PAIR), lambda h: (0, h))
    ks = pl.BlockSpec((keys, PAIR), lambda h: (0, h))
    ins, specs = [q, k, v, do, o, lse], [qs, ks, ks, qs, qs, qs]
    if bias is not None:
        ins.append(bias)
        specs.append(pl.BlockSpec((rows, keys), lambda h: (0, 0)))
    return pl.pallas_call(
        functools.partial(attend_back_kernel, bias is not None),
        grid=(pairs,),
        in_specs=specs,
        out_specs=[qs, ks, ks],
        out_shape=[
            jax.ShapeDtypeStruct((rows, width), BF16),
            jax.ShapeDtypeStruct((keys, width), BF16),
            jax.ShapeDtypeStruct((keys, width), BF16),
        ],
        scratch_shapes=[pltpu.VMEM((keys, PAIR), F32), pltpu.VMEM((keys, PAIR), F32)],
        compiler_params=pltpu.CompilerParams(vmem_limit_bytes=VMEM_LIMIT),
        name="attend_back",
    )(*ins)


def layer_norm(values, norm_gain, norm_shift):
    centre = values - jnp.mean(values, axis=-1, keepdims=True)
    spread = jnp.mean(centre * centre, axis=-1, keepdims=True)
    return centre * lax.rsqrt(spread + 1e-05) * norm_gain + norm_shift


def gelu_exact(values):
    return 0.5 * values * (1.0 + jax.scipy.special.erf(values * 0.7071067811865476))


def slot_links(parent, assignment):
    count = parent.shape[0]
    blocks = jnp.arange(count, dtype=jnp.int32)
    reached = (
        (parent[:, None] == blocks[None, :]) & (blocks[:, None] != blocks[None, :])
    ).astype(F32)
    turns = count.bit_length()
    for _ in range(turns):
        reached = jnp.minimum(
            reached + jnp.sum(reached[:, :, None] * reached[None, :, :], axis=1), 1.0
        )
    placed = (assignment[:, None] == blocks[None, :]).astype(F32)
    linked = jnp.sum(placed[:, :, None] * reached[None], axis=1)
    return jnp.sum(linked[:, None, :] * placed[None, :, :], axis=2)


def mask_bias(linked, first_query, query_count, key_count):
    query_pos = first_query + jnp.arange(query_count, dtype=jnp.int32)
    key_pos = jnp.arange(key_count, dtype=jnp.int32)
    slots = linked.shape[0]
    own = lax.dynamic_slice_in_dim(linked, first_query // BLK, query_count // BLK, 0)
    ancestral = jnp.broadcast_to(
        own[:, None, :, None], (query_count // BLK, BLK, slots, BLK)
    ).reshape(query_count, key_count)
    inside = (query_pos[:, None] // BLK == key_pos[None, :] // BLK) & (
        key_pos[None, :] <= query_pos[:, None]
    )
    return jnp.where((ancestral > 0.5) | inside, 0.0, -1e30).astype(BF16)


def mm(x, w):
    return jnp.dot(x, w, preferred_element_type=F32)


def mm_t(x, w):
    return lax.dot_general(x, w, (((1,), (1,)), ((), ())), preferred_element_type=F32)


def t_mm(x, y):
    return lax.dot_general(x, y, (((0,), (0,)), ((), ())), preferred_element_type=F32)


def col(x):
    return jnp.sum(x.astype(F32), axis=0)


def body(
    tokens, encoded, cotangent, parent, assignment, attn_in, attn_out, ffn_in, ffn_out, shifts, gains, ffn_bias
):
    sizes = (lax.axis_size("leaf"), lax.axis_size("path"))
    leafs, paths = sizes
    devices = leafs * paths
    scale = HEAD ** (-0.5)
    tokens, encoded, cotangent = tokens[0], encoded[0], cotangent[0]
    rows, width = tokens.shape
    hidden_width = ffn_in.shape[1]
    tree_rows = rows * paths
    n_shift, piece = shifts.shape
    n_gain = gains.shape[0]
    n_bias = ffn_bias.shape[0]

    small = jnp.concatenate([shifts.reshape(-1), gains.reshape(-1), ffn_bias])
    small_rows = -(-small.shape[0] // 4096) * 16
    small = jnp.pad(small, (0, small_rows * 256 - small.shape[0])).reshape(1, small_rows, 256)

    got = gather_all(
        sizes,
        [small, attn_in, attn_out, ffn_in[None], ffn_out[None]],
        [tokens, encoded],
        0,
    )
    small_all, w_in, w_out, w1, w2, all_tokens, all_encoded = got
    w_in = w_in.reshape(attn_in.shape[0], width, width)
    w_out = w_out.reshape(attn_out.shape[0], width, width)
    w1 = w1.reshape(width, hidden_width)
    w2 = w2.reshape(hidden_width, width)
    all_tokens = all_tokens.reshape(tree_rows, width)
    all_encoded = all_encoded.reshape(-1, width)
    small_all = small_all.reshape(devices, -1).astype(F32)
    shift = small_all[:, : n_shift * piece].reshape(devices, n_shift, piece)
    shift = shift.transpose(1, 0, 2).reshape(n_shift, width)
    gain = small_all[:, n_shift * piece : (n_shift + n_gain) * piece]
    gain = gain.reshape(devices, n_gain, piece).transpose(1, 0, 2).reshape(n_gain, width)
    start = (n_shift + n_gain) * piece
    b1 = small_all[:, start : start + n_bias].reshape(hidden_width)

    first_row = lax.axis_index("path") * rows
    linked = slot_links(parent[0], assignment[0])
    bias = mask_bias(linked, first_row, rows, tree_rows)

    q = ((mm(tokens, w_in[0]) + shift[0]) * scale).astype(BF16)
    k = mm(all_tokens, w_in[1]).astype(BF16)
    v = (mm(all_tokens, w_in[2]) + shift[1]).astype(BF16)
    ck = mm(all_encoded, w_in[4]).astype(BF16)
    cv = (mm(all_encoded, w_in[5]) + shift[4]).astype(BF16)
    attended, self_mass = attend(q, k, v, bias)
    branch = mm(attended, w_out[0]) + shift[2]
    first_norm, norm_back_one = jax.vjp(
        layer_norm, tokens.astype(F32) + branch, gain[0], shift[7]
    )
    first_low = first_norm.astype(BF16)
    cq = ((mm(first_low, w_in[3]) + shift[3]) * scale).astype(BF16)
    crossed, cross_mass = attend(cq, ck, cv, None)
    cross_branch = mm(crossed, w_out[1]) + shift[5]
    second_norm, norm_back_two = jax.vjp(layer_norm, first_norm + cross_branch, gain[1], shift[8])
    second_low = second_norm.astype(BF16)
    hidden_pre = mm(second_low, w1) + b1
    hidden, gelu_back = jax.vjp(gelu_exact, hidden_pre)
    hidden_low = hidden.astype(BF16)
    ffn_branch = mm(hidden_low, w2) + shift[6]
    result, norm_back_three = jax.vjp(layer_norm, second_norm + ffn_branch, gain[2], shift[9])
    output = result.astype(BF16)

    g_pre3, g_gain3, g_shift9 = norm_back_three(cotangent.astype(F32))
    g_ffn = g_pre3.astype(BF16)
    g_w2 = t_mm(hidden_low, g_ffn).astype(BF16)
    (g_hidden_pre,) = gelu_back(mm_t(g_ffn, w2))
    g_hidden = g_hidden_pre.astype(BF16)
    g_w1 = t_mm(second_low, g_hidden).astype(BF16)
    g_b1 = col(g_hidden)
    g_pre2, g_gain2, g_shift8 = norm_back_two(g_pre3 + mm_t(g_hidden, w1))
    g_cb = g_pre2.astype(BF16)
    g_wo1 = t_mm(crossed, g_cb).astype(BF16)
    g_crossed = mm_t(g_cb, w_out[1]).astype(BF16)
    g_cq, g_ck, g_cv = attend_back(cq, ck, cv, g_crossed, crossed, cross_mass, None)
    g_in3 = t_mm(first_low, g_cq).astype(BF16)
    g_in4 = t_mm(all_encoded, g_ck).astype(BF16)
    g_in5 = t_mm(all_encoded, g_cv).astype(BF16)
    g_enc = (mm_t(g_ck, w_in[4]) + mm_t(g_cv, w_in[5])).astype(BF16)
    g_pre1, g_gain1, g_shift7 = norm_back_one(g_pre2 + mm_t(g_cq, w_in[3]))
    g_br = g_pre1.astype(BF16)
    g_wo0 = t_mm(attended, g_br).astype(BF16)
    g_att = mm_t(g_br, w_out[0]).astype(BF16)
    g_q, g_k, g_v = attend_back(q, k, v, g_att, attended, self_mass, bias)
    g_in0 = t_mm(tokens, g_q).astype(BF16)
    g_in1 = t_mm(all_tokens, g_k).astype(BF16)
    g_in2 = t_mm(all_tokens, g_v).astype(BF16)
    g_tok = (mm_t(g_k, w_in[1]) + mm_t(g_v, w_in[2])).astype(BF16)
    g_tok_own = g_pre1 + mm_t(g_q, w_in[0])

    g_shifts = jnp.stack(
        [col(g_q), col(g_v), col(g_br), col(g_cq), col(g_cv), col(g_cb), col(g_ffn), g_shift7, g_shift8, g_shift9]
    )
    g_gains = jnp.stack([g_gain1, g_gain2, g_gain3])
    g_small = jnp.concatenate(
        [
            g_shifts.reshape(n_shift, devices, piece).transpose(1, 0, 2).reshape(devices, -1),
            g_gains.reshape(n_gain, devices, piece).transpose(1, 0, 2).reshape(devices, -1),
            g_b1.reshape(devices, n_bias),
        ],
        axis=1,
    )
    small_count = g_small.shape[1]
    g_small_rows = -(-small_count // 2048) * 8
    g_small = jnp.pad(g_small, ((0, 0), (0, g_small_rows * 256 - small_count)))
    g_small = g_small.reshape(1, leafs, paths, g_small_rows, 256)

    g_w_in = jnp.stack([g_in0, g_in1, g_in2, g_in3, g_in4, g_in5])
    g_w_out = jnp.stack([g_wo0, g_wo1])

    def spread(g):
        return g.reshape(g.shape[0], leafs, paths, g.shape[1] // devices, g.shape[2])

    o_w1, o_w2, o_out, o_in, o_small, o_tok, o_enc = scatter_all(
        sizes,
        [spread(g_w1[None]), spread(g_w2[None]), spread(g_w_out), spread(g_w_in), g_small],
        [g_tok.reshape(paths, rows, width), g_enc.reshape(paths, -1, width)],
        [g_tok_own, jnp.zeros(encoded.shape, F32)],
        1,
    )
    o_small = o_small.reshape(-1)
    o_shifts = o_small[: n_shift * piece].reshape(n_shift, piece)
    o_gains = o_small[n_shift * piece : (n_shift + n_gain) * piece].reshape(n_gain, piece)
    o_bias = o_small[start : start + n_bias]
    return (
        output[None],
        o_tok[None],
        o_enc[None],
        o_in,
        o_out,
        o_w1[0],
        o_w2[0],
        o_shifts,
        o_gains,
        o_bias,
    )


def solution(mesh):
    both = ("leaf", "path")
    rows = P("leaf", "path", None)
    return jax.shard_map(
        body,
        mesh=mesh,
        in_specs=(
            rows,
            rows,
            rows,
            P("leaf", None),
            P("leaf", None),
            P(None, both, None),
            P(None, both, None),
            P(both, None),
            P(both, None),
            P(None, both),
            P(None, both),
            P(both),
        ),
        out_specs=(
            rows,
            rows,
            rows,
            P(None, both, None),
            P(None, both, None),
            P(both, None),
            P(both, None),
            P(None, both),
            P(None, both),
            P(both),
        ),
        check_vma=False,
    )
```

```python
import functools

import jax
import jax.numpy as jnp
from jax import lax
from jax.experimental import pallas as pl
from jax.experimental.pallas import tpu as pltpu
from jax.sharding import PartitionSpec as P

HEAD = 64
BLK = 128
PAIR = 2 * HEAD
MESH = pl.DeviceIdType.MESH
F32 = jnp.float32
BF16 = jnp.bfloat16
VMEM_LIMIT = 62 * 1024 * 1024
ANY = pl.BlockSpec(memory_space=pl.ANY)
VMEM = pl.BlockSpec(memory_space=pltpu.VMEM)


class Shape:
    def __init__(self, leafs, paths):
        self.leafs, self.paths, self.half = leafs, paths, paths // 2
        outer = leafs // 2
        self.A = 2 if outer % 2 == 0 else 1
        self.B = outer // self.A


class Place:
    def __init__(self, shape):
        self.shape = shape
        self.leafs, self.paths, self.half = shape.leafs, shape.paths, shape.half
        self.A, self.B = shape.A, shape.B
        leaf = lax.axis_index("leaf")
        self.leaf, self.p = leaf, lax.axis_index("path")
        self.c = leaf % 2
        self.a = (leaf // 2) // self.B
        self.b = (leaf // 2) % self.B
        n = self.paths
        self.tree = jnp.where(self.p >= self.half, 1, 0)
        self.primary = self.c == self.tree
        self.pm = jnp.where(self.tree == 0, self.p, n - 1 - self.p)
        self.inward = jnp.where(self.tree == 0, 1, -1)
        self.own_rank = jnp.where(self.c == 0, self.p, n - 1 - self.p)
        self.block = jnp.where(self.primary, self.p, n - 1 - self.p)

    def leaf_at(self, a, b, c):
        return (a * self.B + b) * 2 + c

    def at_core(self):
        return (self.leaf_at(self.a, self.b, 1 - self.c), self.p)

    def at_a(self, a):
        return (self.leaf_at(a, self.b, self.c), self.p)

    def at_b(self, b):
        return (self.leaf_at(self.a, b, self.c), self.p)

    def at_p(self, p):
        return (self.leaf, clamp(p, self.paths))

    def at_mirror(self):
        return (self.leaf_at(self.a, self.b, 1 - self.c), self.paths - 1 - self.p)

    def shard_of_rank(self, rank):
        return jnp.where(self.tree == 0, rank, self.paths - 1 - rank)

    def line_p(self):
        return (self.paths, self.p, self.at_p)

    def line_a(self):
        return (self.A, self.a, self.at_a)

    def line_b(self):
        return (self.B, self.b, self.at_b)


def clamp(index, size):
    return jnp.clip(index, 0, size - 1)


def guarded(when, action):
    if when is None:
        action()
    else:

        @pl.when(when)
        def _():
            action()


def run(actions):
    for action in actions:
        action()


def greet(place, column, mirror):
    barrier = pltpu.get_barrier_semaphore()
    peers = 1

    def signal(to):
        pl.semaphore_signal(barrier, inc=1, device_id=to, device_id_type=MESH)

    signal(place.at_core())
    if column:
        for k in range(1, place.paths):
            for core in range(2):
                there = (place.p + k) % place.paths
                signal((place.leaf_at(place.a, place.b, core), there))
        peers = peers + 2 * (place.paths - 1)
    for size, pos, to in (place.line_a(), place.line_b()):
        if size == 1:
            continue
        if size == 2:
            signal(to(1 - pos))
            peers = peers + 1
            continue
        for step in (-1, 1):
            there = pos + step
            inside = (there >= 0) & (there < size)

            @pl.when(inside)
            def _():
                signal(to(clamp(there, size)))

            peers = peers + jnp.where(inside, 1, 0)
    if mirror and not column:

        @pl.when(jnp.logical_not(place.primary))
        def _():
            signal(place.at_mirror())

        peers = peers + jnp.where(place.primary, 0, 1)
    pl.semaphore_wait(barrier, peers)


class Mail:
    def __init__(self, send_sems, recv_sems, own_sems):
        self.send_sems, self.recv_sems, self.own_sems = send_sems, recv_sems, own_sems
        self.sends = self.recvs = self.owns = 0
        self.sent = []

    def new_recv(self, count=1):
        self.recvs += count
        return self.recvs - count

    def send(self, when, src, dst, to, recv):
        k = self.sends
        self.sends += 1
        copy = pltpu.make_async_remote_copy(
            src_ref=src,
            dst_ref=dst,
            send_sem=self.send_sems.at[k],
            recv_sem=self.recv_sems.at[recv],
            device_id=to,
            device_id_type=MESH,
        )
        self.sent.append((when, copy))
        return functools.partial(guarded, when, copy.start)

    def hear(self, when, landing, to, recv):
        copy = pltpu.make_async_remote_copy(
            src_ref=landing,
            dst_ref=landing,
            send_sem=self.send_sems.at[0],
            recv_sem=self.recv_sems.at[recv],
            device_id=to,
            device_id_type=MESH,
        )
        return functools.partial(guarded, when, copy.wait_recv)

    def post(self, when, src, dst, to, hear_when, landing):
        k = self.new_recv()
        return self.send(when, src, dst, to, k), self.hear(hear_when, landing, to, k)

    def local(self, when, src, dst):
        k = self.owns
        self.owns += 1
        copy = pltpu.make_async_copy(src, dst, self.own_sems.at[k])
        return functools.partial(guarded, when, copy.start), functools.partial(guarded, when, copy.wait)

    def finish(self):
        for when, copy in self.sent:
            guarded(when, copy.wait_send)


def mail_scratch(count=160, own=24):
    return [
        pltpu.SemaphoreType.DMA((count,)),
        pltpu.SemaphoreType.DMA((count,)),
        pltpu.SemaphoreType.DMA((own,)),
    ]


def flood(mail, line, views, first=None):
    size, pos, to = line
    steps = []
    if size == 1:
        return steps
    first = first if first is not None else views(pos)
    if size == 2:
        jobs = [
            mail.post(None, s, d, to(1 - pos), None, w)
            for s, d, w in zip(first, views(pos), views(1 - pos))
        ]
        return [([j[0] for j in jobs], [j[1] for j in jobs])]
    for step in range(1, size):
        starts, waits = [], []
        for sign in (1, -1):
            item = pos - sign * (step - 1)
            there = pos + sign
            when = (there >= 0) & (there < size) & (item >= 0) & (item < size)
            heard = pos - sign * step
            hear_when = (heard >= 0) & (heard < size)
            item_c = clamp(item, size)
            sources = first if step == 1 else views(item_c)
            for s, d, w in zip(sources, views(item_c), views(clamp(heard, size))):
                start, wait = mail.post(when, s, d, to(clamp(there, size)), hear_when, w)
                starts.append(start)
                waits.append(wait)
        steps.append((starts, waits))
    return steps


def chain(steps, first_starts=()):
    stages, pending = [], []
    for k, (starts, waits) in enumerate(steps):
        stages.append(functools.partial(run, pending + (list(first_starts) if k == 0 else []) + starts))
        pending = waits
    stages.append(functools.partial(run, pending))
    return stages


def half_columns(ref, leaf, h):
    width = ref.shape[-1] // 2
    return ref.at[:, leaf, :, :, pl.ds(h * width, width)]


def block_stages(mail, place, shards, block_views):
    n = place.paths
    own = [mail.local(None, s, d) for s, d in zip(shards, block_views(place.p))]
    starts, waits = [o[0] for o in own], [o[1] for o in own]
    lands = [mail.new_recv(n) for _ in shards]
    for k in range(1, n):
        there = (place.p + k) % n
        for s, d, w, land in zip(shards, block_views(place.p), block_views(there), lands):
            starts.append(mail.send(None, s, d, place.at_p(there), land + place.p))
            waits.append(mail.hear(None, w, place.at_p(there), land + there))
    return [functools.partial(run, starts), functools.partial(run, waits)]


def path_half(ref, h):
    n = ref.shape[1] // 2
    return ref.at[:, pl.ds(h * n, n)]


def spread_stages(mail, place, wholes, blocks=None):
    if (place.A, place.B) != (2, 2):
        return spread_lines(mail, place, wholes, blocks)
    a, b, c = place.a, place.b, place.c
    at = lambda w, a, b, c: w.at[:, place.leaf_at(a, b, c)]
    to_a, to_b, to_core = place.at_a(1 - a), place.at_b(1 - b), place.at_core()
    own = []
    sources = [at(w, a, b, c) for w in wholes]
    if blocks is not None:
        own = [mail.local(None, x, s) for x, s in zip(blocks, sources)]
        sources = list(blocks)
    urgent, calm, relay, near, far = [], [], [], [], []
    for w, s in zip(wholes, sources):
        mine, from_a, from_b = at(w, a, b, c), at(w, 1 - a, b, c), at(w, a, 1 - b, c)
        from_ab = at(w, 1 - a, 1 - b, c)

        def post(src, dst, to, landing, h):
            return mail.post(
                None, path_half(src, h), path_half(dst, h), to, None, path_half(landing, h)
            )

        urgent += [post(s, mine, to_b, from_b, 0), post(s, mine, to_a, from_a, 1)]
        calm += [post(s, mine, to_b, from_b, 1), post(s, mine, to_a, from_a, 0)]
        relay += [post(from_b, from_b, to_a, from_ab, 0), post(from_a, from_a, to_b, from_ab, 1)]
        near.append(mail.post(None, s, mine, to_core, None, at(w, a, b, 1 - c)))
        for x, y, l in ((1 - a, b, near), (a, 1 - b, near), (1 - a, 1 - b, far)):
            l.append(mail.post(None, at(w, x, y, c), at(w, x, y, c), to_core, None, at(w, x, y, 1 - c)))
    start = lambda jobs: run([j[0] for j in jobs])
    wait = lambda jobs: run([j[1] for j in jobs])
    first = near[::3]
    second = [j for k, j in enumerate(near) if k % 3]

    def opening():
        start(urgent)
        start(calm)
        start(first)
        run([o[0] for o in own])

    def passing():
        wait(urgent)
        start(relay)

    def sharing():
        wait(calm)
        run([o[1] for o in own])
        start(second)

    def ending():
        wait(relay)
        start(far)

    return [opening, passing, sharing, ending, lambda: wait(near + far)]


def spread_lines(mail, place, wholes, blocks=None):
    A, B, c = place.A, place.B, place.c

    def of_b(h, across_a):
        ays = range(A) if across_a else [place.a]
        return lambda i: [half_columns(w, place.leaf_at(a, i, c), h) for a in ays for w in wholes]

    def of_a(h, across_b):
        bees = range(B) if across_b else [place.b]
        return lambda i: [half_columns(w, place.leaf_at(i, b, c), h) for b in bees for w in wholes]

    own = []
    firsts = [None, None]
    sources = [w.at[:, place.leaf] for w in wholes]
    if blocks is not None:
        own = [mail.local(None, x, w.at[:, place.leaf]) for x, w in zip(blocks, wholes)]
        firsts = [
            [x.at[:, :, :, pl.ds(h * (x.shape[-1] // 2), x.shape[-1] // 2)] for x in blocks]
            for h in range(2)
        ]
        sources = list(blocks)
    line_a, line_b = place.line_a(), place.line_b()
    phases = [
        (flood(mail, line_b, of_b(0, False), firsts[0]), flood(mail, line_a, of_a(1, False), firsts[1])),
        (flood(mail, line_a, of_a(0, True)), flood(mail, line_b, of_b(1, True))),
    ]
    core = [
        mail.post(
            None,
            s,
            w.at[:, place.leaf],
            place.at_core(),
            None,
            w.at[:, place.leaf_at(place.a, place.b, 1 - c)],
        )
        for s, w in zip(sources, wholes)
    ]
    rest = []
    for offset in range(1, A * B):
        spot = (place.a * B + place.b + offset) % (A * B)
        for w in wholes:
            mine, other = w.at[:, spot * 2 + c], w.at[:, spot * 2 + 1 - c]
            rest.append(mail.post(None, mine, mine, place.at_core(), None, other))
    steps = []
    opening = [o[0] for o in own] + [j[0] for j in core]
    for n_phase, phase in enumerate(phases):
        before = [o[1] for o in own] if n_phase == 1 else []
        for s in range(max(len(f) for f in phase)):
            starts, waits = list(before), []
            before = []
            for f in phase:
                if s < len(f):
                    starts += f[s][0]
                    waits += f[s][1]
            steps.append((starts + opening, waits))
            opening = []
    steps.append((opening + [j[0] for j in rest], [j[1] for j in core + rest]))
    return chain(steps)


def pair_gather_stages(mail, place, shard, whole):
    n, h = place.paths, place.half
    rows = shard.shape[0] // 2
    half = lambda ref, u: ref.at[pl.ds(pl.multiple_of(u * rows, rows), rows)]
    lands, core_lands = mail.new_recv(n), mail.new_recv(n)
    own = mail.local(place.primary, shard, whole.at[place.p])
    starts = [own[0]]
    first = jnp.where(place.c == 0, 0, h)
    order = [(first + q) for q in range(h)]
    for u in range(2):
        for q in order:
            to = (place.leaf_at(place.a, place.b, u), q)
            away = jnp.logical_not((q == place.p) & (place.c == u))
            starts.append(
                mail.send(away, half(shard, u), half(whole.at[place.p], u), to, lands + place.p)
            )
    stages = [functools.partial(run, starts)]
    for r in range(n):
        j = place.shard_of_rank(r)
        item = whole.at[j]
        mine = place.primary & (place.p == j)
        got = jnp.logical_not(mine)
        actions = [
            mail.hear(got, half(item, place.c), place.at_core(), lands + j),
            mail.send(
                jnp.logical_not(place.p == j),
                half(item, place.c),
                half(item, place.c),
                place.at_core(),
                core_lands + j,
            ),
        ]
        stages.append(functools.partial(run, actions))
    rest = [own[1]]
    k = mail.new_recv()
    near = place.primary
    mate = whole.at[place.p]
    send_rest = mail.send(
        near, half(shard, place.c), half(mate, place.c), place.at_core(), k
    )
    stages[0] = functools.partial(run, starts + [send_rest])
    rest.append(mail.hear(jnp.logical_not(near), half(mate, 1 - place.c), place.at_core(), k))
    for r in range(n):
        j = place.shard_of_rank(r)
        rest.append(
            mail.hear(
                jnp.logical_not(place.p == j),
                half(whole.at[j], 1 - place.c),
                place.at_core(),
                core_lands + j,
            )
        )
    stages.append(functools.partial(run, rest))
    return stages


def mirror_stages(mail, place, own, mine):
    local = mail.local(place.primary, own, mine)
    other = jnp.logical_not(place.primary)
    start, wait = mail.post(other, own, mine, place.at_mirror(), other, mine)
    return [lambda: run([local[0], start]), lambda: run([local[1], wait])]


def add_rows(dst, src):
    lead = dst.shape[:-2]
    total = 1
    for extent in lead:
        total *= extent

    def body(i, _):
        index = []
        rest = i
        for extent in reversed(lead):
            index.insert(0, rest % extent)
            rest = rest // extent
        index = tuple(index)
        dst[index] = dst[index] + src[index]
        return 0

    if total == 1:
        body(0, 0)
    else:
        lax.fori_loop(0, total, body, 0)


def add_tall(dst, src):
    rows = dst.shape[0]
    step = 64 if rows % 64 == 0 else rows

    def body(r, _):
        at = pl.ds(pl.multiple_of(r * step, step), step)
        dst[at] = dst[at] + src[at]
        return 0

    lax.fori_loop(0, rows // step, body, 0)


def shift_sum(mail, line, mine, slots_up, slots_down, add):
    size, pos, to = line
    if size == 1:
        return []
    if size == 2:
        jobs = [
            mail.post(None, s, slot, to(1 - pos), None, slot)
            for s, slot in zip(mine(1 - pos), slots_up[0])
        ]

        def end():
            for job, dst, slot in zip(jobs, mine(pos), slots_up[0]):
                job[1]()
                add(dst, slot)

        return [lambda: run([j[0] for j in jobs]), end]
    stages = []
    for k in range(size - 1):
        early, actions = [], []
        for sign, slots in ((1, slots_up), (-1, slots_down)):
            dest = size - 1 - k if sign == 1 else k
            when = (pos < dest) if sign == 1 else (pos > dest)
            hear_when = (
                ((pos > 0) & (pos <= dest)) if sign == 1 else ((pos < size - 1) & (pos >= dest))
            )
            there = clamp(pos + sign, size)
            jobs = [
                mail.post(when, s, slot, to(there), None, slot)
                for s, slot in zip(mine(dest), slots[k])
            ]

            def take(jobs=jobs, dst_refs=mine(dest), slot_refs=slots[k]):
                for job, dst, slot in zip(jobs, dst_refs, slot_refs):
                    job[1]()
                    add(dst, slot)

            end = (pos == 0) if sign == 1 else (pos == size - 1)
            starts = functools.partial(run, [job[0] for job in jobs])
            early.append(functools.partial(guarded, end, starts))
            actions.append(functools.partial(guarded, hear_when, take))
            actions.append(functools.partial(guarded, jnp.logical_not(end), starts))
        stages.append(functools.partial(run, early + actions))
    return stages


def fold_scratch(shape, k, R, C, dtype):
    if (shape.A, shape.B) != (2, 2):
        return fold_lines_scratch(shape, k, R, C, dtype)
    block = (k, 2, 2, shape.paths, R, C)
    halves = (2, k, shape.paths // 2, R, C)
    return [pltpu.VMEM(block, dtype)] * 2 + [pltpu.VMEM(halves, dtype)] * 3 + [pltpu.VMEM((1, R, C), dtype)]


def fold_lines_scratch(shape, k, R, C, dtype):
    A, B, paths = shape.A, shape.B, shape.paths
    nb, na = max(B - 1, 1) * (2 if B > 2 else 1), max(A - 1, 1)
    return [
        pltpu.VMEM((k, A, B, paths, R, C), dtype),
        pltpu.VMEM((k, A, B, paths, R, C), dtype),
        pltpu.VMEM((nb, k, A, paths, R, C // 2), dtype),
        pltpu.VMEM((na, k, paths, R, C // 2), dtype),
        pltpu.VMEM((na, k, B, paths, R, C // 2), dtype),
        pltpu.VMEM((nb, k, paths, R, C // 2), dtype),
    ]


N_FOLD = 6


def up_down(ref, size):
    if size <= 2:
        return [[ref.at[0]]], None
    return (
        [[ref.at[k]] for k in range(size - 1)],
        [[ref.at[size - 1 + k]] for k in range(size - 1)],
    )


def fold_stages(mail, place, partial, scratch):
    if (place.A, place.B) != (2, 2):
        return fold_lines(mail, place, partial, scratch)
    a, b, c = place.a, place.b, place.c
    acc, got, far, direct, relayed = scratch[:5]
    own = mail.local(None, partial.at[:, :, :, c], acc)
    core = mail.post(None, partial.at[:, :, :, 1 - c], got, place.at_core(), None, got)
    to_a, to_b = place.at_a(1 - a), place.at_b(1 - b)
    of_a, of_b, of_ab = acc.at[:, 1 - a, b], acc.at[:, a, 1 - b], acc.at[:, 1 - a, 1 - b]
    mine = acc.at[:, a, b]

    def post(src, h, slot, to):
        return mail.post(None, path_half(src, h), slot, to, None, slot)

    urgent = [post(of_ab, 0, far.at[0], to_b), post(of_ab, 1, far.at[1], to_a)]
    calm = [post(of_b, 0, direct.at[0], to_b), post(of_a, 1, direct.at[1], to_a)]
    late = [post(of_a, 0, relayed.at[0], to_a), post(of_b, 1, relayed.at[1], to_b)]

    def join():
        own[1]()
        core[1]()
        add_rows(of_ab, got.at[:, 1 - a, 1 - b])
        run([j[0] for j in urgent])
        add_rows(of_b, got.at[:, a, 1 - b])
        calm[0][0]()
        add_rows(of_a, got.at[:, 1 - a, b])
        calm[1][0]()
        add_rows(mine, got.at[:, a, b])

    def passing():
        urgent[0][1]()
        add_rows(path_half(of_a, 0), far.at[0])
        late[0][0]()
        urgent[1][1]()
        add_rows(path_half(of_b, 1), far.at[1])
        late[1][0]()

    def taking():
        for h in range(2):
            calm[h][1]()
            add_rows(path_half(mine, h), direct.at[h])

    def ending():
        for h in range(2):
            late[h][1]()
            add_rows(path_half(mine, h), relayed.at[h])

    return [lambda: run([own[0], core[0]]), join, passing, taking, ending], mine


def fold_lines(mail, place, partial, scratch):
    c = place.c
    acc, got, sb0, sa0, sa1, sb1 = scratch
    own = mail.local(None, partial.at[:, :, :, c], acc)
    core = mail.post(None, partial.at[:, :, :, 1 - c], got, place.at_core(), None, got)
    width = acc.shape[-1] // 2
    left, right = pl.ds(0, width), pl.ds(width, width)

    def join():
        own[1]()
        core[1]()
        add_rows(acc, got)

    line_a, line_b = place.line_a(), place.line_b()
    h0_b = shift_sum(
        mail, line_b, lambda d: [acc.at[:, :, d, :, :, left]], *up_down(sb0, place.B), add_rows
    )
    h1_a = shift_sum(
        mail, line_a, lambda d: [acc.at[:, d, :, :, :, right]], *up_down(sa1, place.A), add_rows
    )
    h0_a = shift_sum(
        mail, line_a, lambda d: [acc.at[:, d, place.b, :, :, left]], *up_down(sa0, place.A), add_rows
    )
    h1_b = shift_sum(
        mail, line_b, lambda d: [acc.at[:, place.a, d, :, :, right]], *up_down(sb1, place.B), add_rows
    )

    def beside(one, two):
        return [
            functools.partial(run, [s[k] for s in (one, two) if k < len(s)])
            for k in range(max(len(one), len(two)))
        ]

    def joined(first, second):
        if not first or not second:
            return first + second
        return first[:-1] + [functools.partial(run, [first[-1], second[0]])] + second[1:]

    stages = joined(
        [lambda: run([own[0], core[0]]), join], beside(h0_b, h1_a)
    )
    stages = joined(stages, beside(h0_a, h1_b))
    return stages, acc.at[:, place.a, place.b]


def line_scratch(shape, k, R, C, dtype):
    return [pltpu.VMEM((max(shape.paths - 1, 1), k, R, C), dtype)]


def line_stages(mail, place, sums, slots, out):
    n = place.paths
    jobs = []
    for k in range(1, n):
        there = (place.p + k) % n
        slot = slots.at[k - 1]
        jobs.append(mail.post(None, sums.at[:, there], slot, place.at_p(there), None, slot))

    def end():
        run([j[1] for j in jobs])
        for j in range(out.shape[0]):
            total = sums[j, place.p].astype(F32)
            for k in range(n - 1):
                total = total + slots[k, j].astype(F32)
            out[j] = total.astype(out.dtype)

    return [lambda: run([j[0] for j in jobs]), end]


def pair_sum_scratch(shape, R, C):
    return [pltpu.VMEM((shape.paths, R // 2, C), BF16), pltpu.VMEM((shape.half, R, C), BF16)]


def pair_sum_stages(mail, place, part, scratch, out):
    n, h = place.paths, place.half
    core_slot, landing = scratch
    rows = part.shape[1] // 2
    half = lambda ref, u: ref.at[pl.ds(pl.multiple_of(u * rows, rows), rows)]
    lands = [mail.new_recv(2) for _ in range(h)]
    sends, sums = [], []
    for r in range(n - 1, -1, -1):
        j = place.shard_of_rank(r)
        item = part.at[j]
        send, hear = mail.post(
            None, half(item, 1 - place.c), core_slot.at[r], place.at_core(), None, core_slot.at[r]
        )
        owner = (place.leaf_at(place.a, place.b, place.tree), j)
        away = jnp.logical_not(place.primary & (place.p == j))
        out_copy = []
        for q in range(h):
            out_copy.append(
                mail.send(
                    away & (place.pm == q),
                    half(item, place.c),
                    half(landing.at[q], place.c),
                    owner,
                    lands[q] + place.c,
                )
            )

        def settle(hear=hear, item=item, slot=core_slot.at[r], out_copy=out_copy):
            hear()
            add_tall(half(item, place.c), slot)
            run(out_copy)

        sends.append(send)
        sums.append(settle)
    stages = [sends[0]]
    for k in range(1, n):
        stages.append(functools.partial(run, [sends[k], sums[k - 1]]))
    stages.append(sums[n - 1])

    def end():
        own_rank = jnp.where(place.c == 0, place.p, n - 1 - place.p)
        for q in range(h):
            for u in range(2):
                self_made = place.primary & (own_rank == q) & (place.c == u)
                mail.hear(
                    jnp.logical_not(self_made), half(landing.at[q], u), place.at_core(), lands[q] + u
                )()

        step = 64 if rows % 64 == 0 else rows
        for u in range(2):

            def body(i, _, u=u):
                at = pl.ds(pl.multiple_of(u * rows + i * step, step), step)
                for q in range(h):
                    self_made = place.primary & (own_rank == q) & (place.c == u)
                    term = jnp.where(self_made, part[place.p, at], landing[q, at]).astype(F32)
                    total = term if q == 0 else total + term
                out[at] = total
                return 0

            lax.fori_loop(0, rows // step, body, 0)

    return stages + [end]


def hooked(count, unit, hooks):
    def body(i, _):
        for at, stages in hooks.items():
            if stages:

                @pl.when(i == at)
                def _():
                    run(stages)

        unit(i)
        return 0

    lax.fori_loop(0, count, body, 0)


def kernel_call(kernel, name, collective_id, ins, in_specs, outs, out_specs, scratch):
    return pl.pallas_call(
        kernel,
        out_shape=outs,
        in_specs=in_specs,
        out_specs=out_specs,
        scratch_shapes=scratch,
        compiler_params=pltpu.CompilerParams(
            collective_id=collective_id,
            has_side_effects=True,
            vmem_limit_bytes=VMEM_LIMIT,
        )
        if collective_id is not None
        else pltpu.CompilerParams(vmem_limit_bytes=VMEM_LIMIT),
        name=name,
    )(*ins)


def dot(x, y, contract):
    return lax.dot_general(x, y, (contract, ((), ())), preferred_element_type=F32)


def mm(x, w):
    return dot(x, w, ((1,), (0,)))


def mm_t(x, w):
    return dot(x, w, ((1,), (1,)))


def t_mm(x, y):
    return dot(x, y, ((0,), (0,)))


def open_kernel(shape, column, mirror, sems):
    place = Place(shape)
    greet(place, column, mirror)
    return place, Mail(*sems)


def opening_kernel(shape, turns, tok, small, attn_in, links, all_tok, g_small, g_qkv, bias, *scratch):
    sems, (links_got, reach, spot) = scratch[:3], scratch[3:]
    place, mail = open_kernel(shape, True, False, sems)
    three = g_qkv.shape[0]
    to_core = mail.post(None, links, links_got, place.at_core(), None, links_got)
    to_core[0]()
    shards = [small, attn_in.at[pl.ds(0, three)]]
    wholes = [g_small, g_qkv]
    weights = block_stages(
        mail, place, shards, lambda i: [w.at[:, place.leaf, i] for w in wholes]
    )
    spread = spread_stages(mail, place, wholes)
    tokens = pair_gather_stages(mail, place, tok, all_tok)
    weights[0]()
    tokens[0]()
    to_core[1]()

    count = links.shape[0] // 2
    mine = jnp.where(place.primary, links[...], links_got[...])
    reach[...] = jnp.zeros_like(reach)
    spot[...] = jnp.zeros_like(spot)
    reach[pl.ds(0, count)] = mine[:count]
    spot[pl.ds(0, count)] = mine[count:]
    for _ in range(turns):
        r = reach[...]
        reach[...] = jnp.minimum(r + mm(r.astype(BF16), r.astype(BF16)), 1.0)
    placed = spot[...].astype(BF16)
    linked = mm_t(mm(placed, reach[...].astype(BF16)).astype(BF16), placed).astype(BF16)
    rows, keys = bias.shape
    step = min(128, rows)

    def fill(i, _):
        first = i * step
        at = pl.ds(pl.multiple_of(first, step), step)
        q_slot = (place.block * rows + first + lax.broadcasted_iota(jnp.int32, (step, 128), 0)) // BLK
        pick_q = (q_slot == lax.broadcasted_iota(jnp.int32, (step, 128), 1)).astype(F32)
        own = mm(pick_q.astype(BF16), linked).astype(BF16)
        k_slot = lax.broadcasted_iota(jnp.int32, (128, keys), 1) // BLK
        pick_k = (k_slot == lax.broadcasted_iota(jnp.int32, (128, keys), 0)).astype(F32)
        seen = mm(own, pick_k.astype(BF16))
        q_at = place.block * rows + first + lax.broadcasted_iota(jnp.int32, (step, keys), 0)
        k_at = lax.broadcasted_iota(jnp.int32, (step, keys), 1)
        inside = (q_at // BLK == k_at // BLK) & (k_at <= q_at)
        bias[at] = jnp.where((seen > 0.5) | inside, 0.0, -1e30).astype(bias.dtype)
        return 0

    run(weights[1:] + spread[:1])
    lax.fori_loop(0, rows // step, fill, 0)
    spread[1]()
    tokens[1]()
    spread[2]()
    tokens[2]()
    run(spread[3:])
    run(tokens[3:])
    mail.finish()


def attend_unit(q_ref, k_ref, v_ref, bias_ref, o_ref, lse_ref, row, step, pair):
    at = pl.ds(pl.multiple_of(row, step), step)
    cols = pl.ds(pl.multiple_of(pair * PAIR, PAIR), PAIR)
    lane = lax.broadcasted_iota(jnp.int32, (1, PAIR), 1)
    q = q_ref[at, cols]
    k = k_ref[:, cols]
    v = v_ref[:, cols]
    out = jnp.zeros((step, PAIR), F32)
    lse = jnp.zeros((step, PAIR), F32)
    for h in range(2):
        own = (lane >= HEAD) if h else (lane < HEAD)
        s = mm_t(jnp.where(own, q, jnp.zeros_like(q)), k)
        if bias_ref is not None:
            s = s + bias_ref[at].astype(F32)
        peak = jnp.max(s, axis=1, keepdims=True)
        e = jnp.exp(s - peak)
        mass = jnp.sum(e, axis=1, keepdims=True)
        o = mm(e.astype(BF16), v)
        out = jnp.where(own, o / mass, out)
        lse = jnp.where(own, peak + jnp.log(mass), lse)
    o_ref[at, cols] = out.astype(BF16)
    lse_ref[at, cols] = lse


def attend_back_unit(q_ref, k_ref, v_ref, bias_ref, do_ref, o_ref, lse_ref, dq_ref, dk_acc, dv_acc, row, step, pair):
    at = pl.ds(pl.multiple_of(row, step), step)
    cols = pl.ds(pl.multiple_of(pair * PAIR, PAIR), PAIR)
    lane = lax.broadcasted_iota(jnp.int32, (1, PAIR), 1)
    k = k_ref[:, cols]
    v = v_ref[:, cols]
    q = q_ref[at, cols]
    do = do_ref[at, cols]
    both = do.astype(F32) * o_ref[at, cols].astype(F32)
    lse_pair = lse_ref[at, cols]
    dq = jnp.zeros((step, PAIR), F32)
    for h in range(2):
        own = (lane >= HEAD) if h else (lane < HEAD)
        q_h = jnp.where(own, q, jnp.zeros_like(q))
        do_h = jnp.where(own, do, jnp.zeros_like(do))
        delta = jnp.sum(jnp.where(own, both, 0.0), axis=1, keepdims=True)
        lse = lse_pair[:, h * HEAD : h * HEAD + 1]
        s = mm_t(q_h, k)
        if bias_ref is not None:
            s = s + bias_ref[at].astype(F32)
        e = jnp.exp(s - lse)
        dp = mm_t(do_h, v)
        ds = (e * (dp - delta)).astype(BF16)
        dq = jnp.where(own, mm(ds, k), dq)
        dk_acc[...] += t_mm(ds, q_h)
        dv_acc[...] += t_mm(e.astype(BF16), do_h)
    dq_ref[at, cols] = dq.astype(BF16) * BF16(HEAD**-0.5)


def attend_units(rows, width):
    step = min(256, rows)
    return rows // step, step, width // PAIR


def self_kernel(
    shape, all_tok, w_qkv, vec, bias, enc, attn_in, attn_out, ffn_in, ffn_out,
    q, k, v, att, lse, all_enc, g_in, g_out, z_1, z_2, *sems,
):
    place, mail = open_kernel(shape, True, False, sems)
    n, rows, width = all_tok.shape
    three = g_in.shape[0]
    e = pair_gather_stages(mail, place, enc, all_enc)
    shards = [attn_in.at[pl.ds(attn_in.shape[0] - three, three)], attn_out]
    wholes = [g_in, g_out]
    w = block_stages(mail, place, shards, lambda i: [g.at[:, place.leaf, i] for g in wholes])
    w += spread_stages(mail, place, wholes)
    f = block_stages(mail, place, [ffn_in, ffn_out], lambda i: [z_1.at[:, i], z_2.at[:, i]])
    plan = []
    w[0]()
    e[0]()
    scale = HEAD**-0.5
    q[...] = ((mm(all_tok[place.block], w_qkv[0]) + vec[pl.ds(0, 1)]) * scale).astype(BF16)

    def project(i):
        x = all_tok[i]
        at = pl.ds(pl.multiple_of(i * rows, rows), rows)
        k[at] = mm(x, w_qkv[1]).astype(BF16)
        v[at] = (mm(x, w_qkv[2]) + vec[pl.ds(1, 1)]).astype(BF16)

    stages = w[1:3] + e[1:3] + w[3:4] + f[:1] + e[3:] + w[4:5] + f[1:2] + w[5:6] + f[2:3] + w[6:] + f[3:]
    blocks, step, pairs = attend_units(rows, width)
    total = n + blocks * pairs
    early, late = {}, {}
    for s, stage in enumerate(stages):
        at = min(1 + (s * (total - 2)) // len(stages), total - 1)
        if at < n:
            early.setdefault(at, []).append(stage)
        else:
            late.setdefault(at - n, []).append(stage)
    hooked(n, project, early)

    def unit(i):
        attend_unit(q, k, v, bias, att, lse, (i % blocks) * step, step, i // blocks)

    hooked(blocks * pairs, unit, late)
    mail.finish()


def cross_kernel(
    shape, cq, all_enc, w_k, w_v, vec, z_1, z_2, cot,
    ck, cv, crossed, lse, g_1, g_2, my_cot, *sems,
):
    place, mail = open_kernel(shape, False, True, sems)
    rows, width = cq.shape
    n, enc_rows, _ = all_enc.shape
    w = spread_stages(mail, place, [g_1, g_2], [z_1, z_2])
    c = mirror_stages(mail, place, cot, my_cot)
    w[0]()
    c[0]()

    def project(i):
        x = all_enc[i]
        at = pl.ds(pl.multiple_of(i * enc_rows, enc_rows), enc_rows)
        ck[at] = mm(x, w_k[...]).astype(BF16)
        cv[at] = (mm(x, w_v[...]) + vec[pl.ds(4, 1)]).astype(BF16)

    hooked(n, project, {})
    blocks, step, pairs = attend_units(rows, width)
    total = blocks * pairs
    late = {}
    stages = w[1:] + c[1:]
    for s, stage in enumerate(stages):
        late.setdefault(min((s + 1) * total // (len(stages)), total - 1), []).append(stage)

    def unit(i):
        attend_unit(cq, ck, cv, None, crossed, lse, (i % blocks) * step, step, i // blocks)

    hooked(total, unit, late)
    mail.finish()


def cross_back_kernel(
    shape, cq, ck, cv, do, o, lse, p_1, p_2, out_rows,
    dq, dk, dv, s_1, s_2, my_out, dk_acc, dv_acc, *scratch,
):
    sems, scratch = scratch[:3], scratch[3:]
    place, mail = open_kernel(shape, False, True, sems)
    rows, width = cq.shape
    f_1, sum_1 = fold_stages(mail, place, p_1, scratch[:N_FOLD])
    f_2, sum_2 = fold_stages(mail, place, p_2, scratch[N_FOLD:])
    c = mirror_stages(mail, place, out_rows, my_out)
    f_1[0]()
    blocks, step, pairs = attend_units(rows, width)
    total = blocks * pairs
    stages = f_2[:1] + c[:1]
    for k in range(max(len(f_1), len(f_2))):
        stages += f_1[k + 1 : k + 2] + f_2[k + 1 : k + 2]
    stages += c[1:]
    hooks = {}
    for s, stage in enumerate(stages):
        hooks.setdefault(min((s + 1) * total // len(stages), total - 1), []).append(stage)

    def unit(i):
        first = i % blocks == 0

        @pl.when(first)
        def _():
            dk_acc[...] = jnp.zeros_like(dk_acc)
            dv_acc[...] = jnp.zeros_like(dv_acc)

        pair = i // blocks
        attend_back_unit(cq, ck, cv, None, do, o, lse, dq, dk_acc, dv_acc, (i % blocks) * step, step, pair)

        @pl.when(i % blocks == blocks - 1)
        def _():
            cols = pl.ds(pl.multiple_of(pair * PAIR, PAIR), PAIR)
            dk[:, cols] = dk_acc[...].astype(BF16)
            dv[:, cols] = dv_acc[...].astype(BF16)

    hooked(total, unit, hooks)
    s_1[...] = sum_1[...]
    s_2[...] = sum_2[...]
    mail.finish()


def self_back_kernel(
    shape, q, k, v, bias, do, o, lse, z_1, z_2, p_in, p_out, p_enc,
    dq, dk, dv, o_1, o_2, o_in, o_out, o_enc, dk_acc, dv_acc, *scratch,
):
    sems, scratch = scratch[:3], scratch[3:]
    place, mail = open_kernel(shape, True, False, sems)
    rows, width = q.shape
    l_1 = line_stages(mail, place, z_1, scratch[0], o_1)
    l_2 = line_stages(mail, place, z_2, scratch[1], o_2)
    f_in, sum_in = fold_stages(mail, place, p_in, scratch[2 : 2 + N_FOLD])
    f_out, sum_out = fold_stages(mail, place, p_out, scratch[2 + N_FOLD : 2 + 2 * N_FOLD])
    rest = scratch[2 + 2 * N_FOLD :]
    l_in = line_stages(mail, place, sum_in, rest[0], o_in)
    l_out = line_stages(mail, place, sum_out, rest[1], o_out)
    e = pair_sum_stages(mail, place, p_enc, rest[2:], o_enc)
    f_in[0]()
    f_out[0]()
    l_1[0]()
    blocks, step, pairs = attend_units(rows, width)
    total = blocks * pairs
    stages = []
    tracks = [
        [f for two in zip(f_in[1:], f_out[1:]) for f in two] + l_in + l_out,
        l_1[1:] + l_2 + e,
    ]
    longest = max(len(t) for t in tracks)
    hooks = {}
    for t in tracks:
        for s, stage in enumerate(t):
            hooks.setdefault(min((s + 1) * total // len(t), total - 1), []).append(stage)

    def unit(i):
        @pl.when(i % blocks == 0)
        def _():
            dk_acc[...] = jnp.zeros_like(dk_acc)
            dv_acc[...] = jnp.zeros_like(dv_acc)

        pair = i // blocks
        attend_back_unit(q, k, v, bias, do, o, lse, dq, dk_acc, dv_acc, (i % blocks) * step, step, pair)

        @pl.when(i % blocks == blocks - 1)
        def _():
            cols = pl.ds(pl.multiple_of(pair * PAIR, PAIR), PAIR)
            dk[:, cols] = dk_acc[...].astype(BF16)
            dv[:, cols] = dv_acc[...].astype(BF16)

    hooked(total, unit, hooks)
    mail.finish()


def closing_kernel(shape, p_qkv, p_small, p_tok, o_qkv, o_small, o_tok, *scratch):
    sems, scratch = scratch[:3], scratch[3:]
    place, mail = open_kernel(shape, True, False, sems)
    f_q, sum_q = fold_stages(mail, place, p_qkv, scratch[:N_FOLD])
    f_s, sum_s = fold_stages(mail, place, p_small, scratch[N_FOLD : 2 * N_FOLD])
    rest = scratch[2 * N_FOLD :]
    l_q = line_stages(mail, place, sum_q, rest[0], o_qkv)
    l_s = line_stages(mail, place, sum_s, rest[1], o_small)
    t = pair_sum_stages(mail, place, p_tok, rest[2:], o_tok)
    a = [functools.partial(run, two) for two in zip(f_q, f_s)]
    b = [functools.partial(run, two) for two in zip(l_q, l_s)]
    a[0]()
    t[0]()
    tracks = [a[1:], t[1:]]
    for k in range(max(len(x) for x in tracks)):
        for x in tracks:
            if k < len(x) and x[k] is not t[-1]:
                x[k]()
    run(b)
    t[-1]()
    mail.finish()


def layer_norm(values, norm_gain, norm_shift):
    centre = values - jnp.mean(values, axis=-1, keepdims=True)
    spread = jnp.mean(centre * centre, axis=-1, keepdims=True)
    return centre * lax.rsqrt(spread + 1e-05) * norm_gain + norm_shift


def gelu_exact(values):
    return 0.5 * values * (1.0 + jax.scipy.special.erf(values * 0.7071067811865476))


def col(x):
    return jnp.sum(x.astype(F32), axis=0)


def body(
    tokens, encoded, cotangent, parent, assignment, attn_in, attn_out, ffn_in, ffn_out, shifts, gains, ffn_bias
):
    shape = Shape(lax.axis_size("leaf"), lax.axis_size("path"))
    leafs, paths = shape.leafs, shape.paths
    devices = leafs * paths
    scale = HEAD ** (-0.5)
    tokens, encoded, cotangent = tokens[0], encoded[0], cotangent[0]
    rows, width = tokens.shape
    enc_rows = encoded.shape[0]
    hidden_width = ffn_in.shape[1]
    tree_rows, tree_enc = rows * paths, enc_rows * paths
    piece = shifts.shape[1]
    n_shift, n_gain, n_bias = shifts.shape[0], gains.shape[0], ffn_bias.shape[0]
    n_vec = n_shift + n_gain
    ffn_in, ffn_out = ffn_in[None], ffn_out[None]

    def sds(shape_, dtype=BF16):
        return jax.ShapeDtypeStruct(shape_, dtype)

    small = jnp.concatenate([shifts.reshape(-1), gains.reshape(-1), ffn_bias])
    small_rows = -(-small.shape[0] // 4096) * 16
    small = jnp.pad(small, (0, small_rows * 256 - small.shape[0])).reshape(1, small_rows, 256)
    blocks = parent.shape[1]
    ids = jnp.arange(blocks, dtype=jnp.int32)
    lanes = jnp.arange(128, dtype=jnp.int32)
    links = jnp.concatenate(
        [
            (parent[0][:, None] == lanes[None, :]) & (ids[:, None] != lanes[None, :]),
            assignment[0][:, None] == lanes[None, :],
        ]
    ).astype(F32)

    three = 3
    all_tok, g_small, w_qkv, bias = kernel_call(
        functools.partial(opening_kernel, shape, blocks.bit_length()),
        "opening",
        0,
        [tokens, small, attn_in, links],
        [ANY, ANY, ANY, VMEM],
        [
            sds((paths, rows, width)),
            sds((1, leafs, paths) + small.shape[1:]),
            sds((three, leafs, paths) + attn_in.shape[1:]),
            sds((rows, tree_rows)),
        ],
        [ANY, ANY, ANY, VMEM],
        mail_scratch()
        + [pltpu.VMEM(links.shape, F32), pltpu.VMEM((128, 128), F32), pltpu.VMEM((128, 128), F32)],
    )
    flat = g_small.reshape(devices, -1)
    vec = flat[:, : n_vec * piece].reshape(devices, n_vec, piece).transpose(1, 0, 2)
    vec = vec.reshape(n_vec, width).astype(F32)
    shift, gain = vec[:n_shift], vec[n_shift:]
    b1 = flat[:, n_vec * piece : n_vec * piece + n_bias].reshape(hidden_width).astype(F32)
    w_qkv = w_qkv.reshape(three, width, width)

    rest_in = attn_in.shape[0] - three
    q, k, v, attended, self_mass, all_enc, w_in, w_out, z_1, z_2 = kernel_call(
        functools.partial(self_kernel, shape),
        "self_attention",
        1,
        [all_tok, w_qkv, vec, bias, encoded, attn_in, attn_out, ffn_in, ffn_out],
        [VMEM] * 4 + [ANY] * 5,
        [
            sds((rows, width)),
            sds((tree_rows, width)),
            sds((tree_rows, width)),
            sds((rows, width)),
            sds((rows, width), F32),
            sds((paths, enc_rows, width)),
            sds((rest_in, leafs, paths) + attn_in.shape[1:]),
            sds((attn_out.shape[0], leafs, paths) + attn_out.shape[1:]),
            sds((1, paths) + ffn_in.shape[1:]),
            sds((1, paths) + ffn_out.shape[1:]),
        ],
        [VMEM] * 5 + [ANY] * 5,
        mail_scratch(),
    )
    w_in = w_in.reshape(rest_in, width, width)
    w_out = w_out.reshape(attn_out.shape[0], width, width)

    p = lax.axis_index("path")
    upper = p >= shape.half
    primary = (lax.axis_index("leaf") % 2 == 1) == upper
    block = jnp.where(primary, p, paths - 1 - p)
    my_tokens = lax.dynamic_index_in_dim(all_tok, block, 0, False)
    branch = mm(attended, w_out[0]) + shift[2]
    first_norm, norm_back_one = jax.vjp(
        layer_norm, my_tokens.astype(F32) + branch, gain[0], shift[7]
    )
    first_low = first_norm.astype(BF16)
    cq = ((mm(first_low, w_in[0]) + shift[3]) * scale).astype(BF16)
    ck, cv, crossed, cross_mass, w1, w2, my_cot = kernel_call(
        functools.partial(cross_kernel, shape),
        "cross_attention",
        2,
        [cq, all_enc, w_in[1], w_in[2], vec, z_1, z_2, cotangent],
        [VMEM] * 5 + [ANY] * 3,
        [
            sds((tree_enc, width)),
            sds((tree_enc, width)),
            sds((rows, width)),
            sds((rows, width), F32),
            sds((1, leafs, paths) + ffn_in.shape[1:]),
            sds((1, leafs, paths) + ffn_out.shape[1:]),
            sds((rows, width)),
        ],
        [VMEM] * 4 + [ANY] * 3,
        mail_scratch(),
    )
    w1 = w1.reshape(width, hidden_width)
    w2 = w2.reshape(hidden_width, width)
    cross_branch = mm(crossed, w_out[1]) + shift[5]
    second_norm, norm_back_two = jax.vjp(layer_norm, first_norm + cross_branch, gain[1], shift[8])
    second_low = second_norm.astype(BF16)
    hidden_pre = mm(second_low, w1) + b1
    hidden, gelu_back = jax.vjp(gelu_exact, hidden_pre)
    hidden_low = hidden.astype(BF16)
    ffn_branch = mm(hidden_low, w2) + shift[6]
    result, norm_back_three = jax.vjp(layer_norm, second_norm + ffn_branch, gain[2], shift[9])
    output = result.astype(BF16)

    g_pre3, g_gain3, g_shift9 = norm_back_three(my_cot.astype(F32))
    g_ffn = g_pre3.astype(BF16)
    g_w2 = t_mm(hidden_low, g_ffn).astype(BF16)
    (g_hidden_pre,) = gelu_back(mm_t(g_ffn, w2))
    g_hidden = g_hidden_pre.astype(BF16)
    g_w1 = t_mm(second_low, g_hidden).astype(BF16)
    g_b1 = col(g_hidden)
    g_pre2, g_gain2, g_shift8 = norm_back_two(g_pre3 + mm_t(g_hidden, w1))
    g_cb = g_pre2.astype(BF16)
    g_crossed = mm_t(g_cb, w_out[1]).astype(BF16)

    def spread(g):
        return g.reshape(
            g.shape[0], shape.A, shape.B, 2, paths, g.shape[1] // devices, g.shape[2]
        )

    r1, r2 = ffn_in.shape[1:], ffn_out.shape[1:]
    g_cq, g_ck, g_cv, s_1, s_2, output = kernel_call(
        functools.partial(cross_back_kernel, shape),
        "cross_back",
        3,
        [cq, ck, cv, g_crossed, crossed, cross_mass, spread(g_w1[None]), spread(g_w2[None]), output],
        [VMEM] * 6 + [ANY] * 3,
        [
            sds((rows, width)),
            sds((tree_enc, width)),
            sds((tree_enc, width)),
            sds((1, paths) + r1),
            sds((1, paths) + r2),
            sds((rows, width)),
        ],
        [VMEM] * 5 + [ANY],
        [pltpu.VMEM((tree_enc, PAIR), F32)] * 2
        + mail_scratch()
        + fold_scratch(shape, 1, *r1, BF16)
        + fold_scratch(shape, 1, *r2, BF16),
    )
    flat_enc = all_enc.reshape(tree_enc, width)
    g_wo1 = t_mm(crossed, g_cb).astype(BF16)
    g_in3 = t_mm(first_low, g_cq).astype(BF16)
    g_in4 = t_mm(flat_enc, g_ck).astype(BF16)
    g_in5 = t_mm(flat_enc, g_cv).astype(BF16)
    g_enc = (mm_t(g_ck, w_in[1]) + mm_t(g_cv, w_in[2])).astype(BF16)
    g_pre1, g_gain1, g_shift7 = norm_back_one(g_pre2 + mm_t(g_cq, w_in[0]))
    g_br = g_pre1.astype(BF16)
    g_wo0 = t_mm(attended, g_br).astype(BF16)
    g_att = mm_t(g_br, w_out[0]).astype(BF16)
    p_in = spread(jnp.stack([g_in3, g_in4, g_in5]))
    p_out = spread(jnp.stack([g_wo0, g_wo1]))
    ri = attn_in.shape[1:]
    g_q, g_k, g_v, o_w1, o_w2, o_in, o_out, o_enc = kernel_call(
        functools.partial(self_back_kernel, shape),
        "self_back",
        4,
        [q, k, v, bias, g_att, attended, self_mass, s_1, s_2, p_in, p_out, g_enc.reshape(paths, enc_rows, width)],
        [VMEM] * 9 + [ANY] * 2 + [VMEM],
        [
            sds((rows, width)),
            sds((tree_rows, width)),
            sds((tree_rows, width)),
            sds((1,) + r1, F32),
            sds((1,) + r2, F32),
            sds((rest_in,) + ri, F32),
            sds((2,) + ri, F32),
            sds((enc_rows, width), F32),
        ],
        [VMEM] * 8,
        [pltpu.VMEM((tree_rows, PAIR), F32)] * 2
        + mail_scratch()
        + line_scratch(shape, 1, *r1, BF16)
        + line_scratch(shape, 1, *r2, BF16)
        + fold_scratch(shape, rest_in, *ri, BF16)
        + fold_scratch(shape, 2, *ri, BF16)
        + line_scratch(shape, rest_in, *ri, BF16)
        + line_scratch(shape, 2, *ri, BF16)
        + pair_sum_scratch(shape, enc_rows, width),
    )
    flat_tok = all_tok.reshape(tree_rows, width)
    g_in0 = t_mm(my_tokens, g_q).astype(BF16)
    g_in1 = t_mm(flat_tok, g_k).astype(BF16)
    g_in2 = t_mm(flat_tok, g_v).astype(BF16)
    g_tok = (mm_t(g_k, w_qkv[1]) + mm_t(g_v, w_qkv[2])).reshape(paths, rows, width)
    g_own = g_pre1 + mm_t(g_q, w_qkv[0])
    mine = (jnp.arange(paths) == block)[:, None, None]
    g_tok = jnp.where(mine, g_tok + g_own[None], g_tok).astype(BF16)

    g_vec = jnp.stack(
        [
            col(g_q), col(g_v), col(g_br), col(g_cq), col(g_cv), col(g_cb), col(g_ffn),
            g_shift7, g_shift8, g_shift9, g_gain1, g_gain2, g_gain3,
        ]
    )
    g_small = jnp.concatenate(
        [
            g_vec.reshape(n_vec, devices, piece).transpose(1, 0, 2).reshape(devices, -1),
            g_b1.reshape(devices, n_bias),
        ],
        axis=1,
    )
    small_count = g_small.shape[1]
    g_small_rows = -(-small_count // 2048) * 8
    g_small = jnp.pad(g_small, ((0, 0), (0, g_small_rows * 256 - small_count)))
    p_small = g_small.reshape(1, shape.A, shape.B, 2, paths, g_small_rows, 256)
    p_qkv = spread(jnp.stack([g_in0, g_in1, g_in2]))
    o_qkv, o_small, o_tok = kernel_call(
        functools.partial(closing_kernel, shape),
        "closing",
        5,
        [p_qkv, p_small, g_tok],
        [ANY, ANY, VMEM],
        [
            sds((three,) + ri, F32),
            sds((1, g_small_rows, 256), F32),
            sds((rows, width), F32),
        ],
        [VMEM] * 3,
        mail_scratch()
        + fold_scratch(shape, three, *ri, BF16)
        + fold_scratch(shape, 1, g_small_rows, 256, F32)
        + line_scratch(shape, three, *ri, BF16)
        + line_scratch(shape, 1, g_small_rows, 256, F32)
        + pair_sum_scratch(shape, rows, width),
    )
    o_small = o_small.reshape(-1)
    o_vec = o_small[: n_vec * piece].reshape(n_vec, piece)
    return (
        output[None],
        o_tok[None],
        o_enc[None],
        jnp.concatenate([o_qkv, o_in]),
        o_out,
        o_w1[0],
        o_w2[0],
        o_vec[:n_shift],
        o_vec[n_shift:],
        o_small[n_vec * piece : n_vec * piece + n_bias],
    )


def solution(mesh):
    both = ("leaf", "path")
    rows = P("leaf", "path", None)
    weights = (P(None, both, None), P(None, both, None), P(both, None), P(both, None), P(None, both), P(None, both), P(both))
    return jax.shard_map(
        body,
        mesh=mesh,
        in_specs=(rows, rows, rows, P("leaf", None), P("leaf", None)) + weights,
        out_specs=(rows, rows, rows) + weights,
        check_vma=False,
    )
```

```python
import functools

import jax
import jax.numpy as jnp
from jax import lax
from jax.experimental import pallas as pl
from jax.experimental.pallas import tpu as pltpu
from jax.sharding import PartitionSpec as P

HEAD = 64
BLK = 128
PAIR = 2 * HEAD
MESH = pl.DeviceIdType.MESH
F32 = jnp.float32
BF16 = jnp.bfloat16
VMEM_LIMIT = 62 * 1024 * 1024
ANY = pl.BlockSpec(memory_space=pl.ANY)
VMEM = pl.BlockSpec(memory_space=pltpu.VMEM)


class Shape:
    def __init__(self, leafs, paths):
        self.leafs, self.paths, self.half = leafs, paths, paths // 2
        outer = leafs // 2
        self.A = 2 if outer % 2 == 0 else 1
        self.B = outer // self.A


class Place:
    def __init__(self, shape):
        self.shape = shape
        self.leafs, self.paths, self.half = shape.leafs, shape.paths, shape.half
        self.A, self.B = shape.A, shape.B
        leaf = lax.axis_index("leaf")
        self.leaf, self.p = leaf, lax.axis_index("path")
        self.c = leaf % 2
        self.a = (leaf // 2) // self.B
        self.b = (leaf // 2) % self.B
        n = self.paths
        self.tree = jnp.where(self.p >= self.half, 1, 0)
        self.primary = self.c == self.tree
        self.pm = jnp.where(self.tree == 0, self.p, n - 1 - self.p)
        self.inward = jnp.where(self.tree == 0, 1, -1)
        self.own_rank = jnp.where(self.c == 0, self.p, n - 1 - self.p)
        self.block = jnp.where(self.primary, self.p, n - 1 - self.p)

    def leaf_at(self, a, b, c):
        return (a * self.B + b) * 2 + c

    def at_core(self):
        return (self.leaf_at(self.a, self.b, 1 - self.c), self.p)

    def at_a(self, a):
        return (self.leaf_at(a, self.b, self.c), self.p)

    def at_b(self, b):
        return (self.leaf_at(self.a, b, self.c), self.p)

    def at_p(self, p):
        return (self.leaf, clamp(p, self.paths))

    def at_mirror(self):
        return (self.leaf_at(self.a, self.b, 1 - self.c), self.paths - 1 - self.p)

    def shard_of_rank(self, rank):
        return jnp.where(self.tree == 0, rank, self.paths - 1 - rank)

    def line_p(self):
        return (self.paths, self.p, self.at_p)

    def line_a(self):
        return (self.A, self.a, self.at_a)

    def line_b(self):
        return (self.B, self.b, self.at_b)


def clamp(index, size):
    return jnp.clip(index, 0, size - 1)


def guarded(when, action):
    if when is None:
        action()
    else:

        @pl.when(when)
        def _():
            action()


def run(actions):
    for action in actions:
        action()


def greet(place, column, mirror):
    barrier = pltpu.get_barrier_semaphore()
    peers = 1

    def signal(to):
        pl.semaphore_signal(barrier, inc=1, device_id=to, device_id_type=MESH)

    signal(place.at_core())
    if column:
        for k in range(1, place.paths):
            for core in range(2):
                there = (place.p + k) % place.paths
                signal((place.leaf_at(place.a, place.b, core), there))
        peers = peers + 2 * (place.paths - 1)
    for size, pos, to in (place.line_a(), place.line_b()):
        if size == 1:
            continue
        if size == 2:
            signal(to(1 - pos))
            peers = peers + 1
            continue
        for step in (-1, 1):
            there = pos + step
            inside = (there >= 0) & (there < size)

            @pl.when(inside)
            def _():
                signal(to(clamp(there, size)))

            peers = peers + jnp.where(inside, 1, 0)
    if mirror and not column:

        @pl.when(jnp.logical_not(place.primary))
        def _():
            signal(place.at_mirror())

        peers = peers + jnp.where(place.primary, 0, 1)
    pl.semaphore_wait(barrier, peers)


class Mail:
    def __init__(self, send_sems, recv_sems, own_sems):
        self.send_sems, self.recv_sems, self.own_sems = send_sems, recv_sems, own_sems
        self.sends = self.recvs = self.owns = 0
        self.sent = []

    def new_recv(self, count=1):
        self.recvs += count
        return self.recvs - count

    def send(self, when, src, dst, to, recv):
        k = self.sends
        self.sends += 1
        copy = pltpu.make_async_remote_copy(
            src_ref=src,
            dst_ref=dst,
            send_sem=self.send_sems.at[k],
            recv_sem=self.recv_sems.at[recv],
            device_id=to,
            device_id_type=MESH,
        )
        self.sent.append((when, copy))
        return functools.partial(guarded, when, copy.start)

    def hear(self, when, landing, to, recv):
        copy = pltpu.make_async_remote_copy(
            src_ref=landing,
            dst_ref=landing,
            send_sem=self.send_sems.at[0],
            recv_sem=self.recv_sems.at[recv],
            device_id=to,
            device_id_type=MESH,
        )
        return functools.partial(guarded, when, copy.wait_recv)

    def post(self, when, src, dst, to, hear_when, landing):
        k = self.new_recv()
        return self.send(when, src, dst, to, k), self.hear(hear_when, landing, to, k)

    def local(self, when, src, dst):
        k = self.owns
        self.owns += 1
        copy = pltpu.make_async_copy(src, dst, self.own_sems.at[k])
        return functools.partial(guarded, when, copy.start), functools.partial(guarded, when, copy.wait)

    def finish(self):
        for when, copy in self.sent:
            guarded(when, copy.wait_send)


def mail_scratch(count=160, own=24):
    return [
        pltpu.SemaphoreType.DMA((count,)),
        pltpu.SemaphoreType.DMA((count,)),
        pltpu.SemaphoreType.DMA((own,)),
    ]


def flood(mail, line, views, first=None):
    size, pos, to = line
    steps = []
    if size == 1:
        return steps
    first = first if first is not None else views(pos)
    if size == 2:
        jobs = [
            mail.post(None, s, d, to(1 - pos), None, w)
            for s, d, w in zip(first, views(pos), views(1 - pos))
        ]
        return [([j[0] for j in jobs], [j[1] for j in jobs])]
    for step in range(1, size):
        starts, waits = [], []
        for sign in (1, -1):
            item = pos - sign * (step - 1)
            there = pos + sign
            when = (there >= 0) & (there < size) & (item >= 0) & (item < size)
            heard = pos - sign * step
            hear_when = (heard >= 0) & (heard < size)
            item_c = clamp(item, size)
            sources = first if step == 1 else views(item_c)
            for s, d, w in zip(sources, views(item_c), views(clamp(heard, size))):
                start, wait = mail.post(when, s, d, to(clamp(there, size)), hear_when, w)
                starts.append(start)
                waits.append(wait)
        steps.append((starts, waits))
    return steps


def chain(steps, first_starts=()):
    stages, pending = [], []
    for k, (starts, waits) in enumerate(steps):
        stages.append(functools.partial(run, pending + (list(first_starts) if k == 0 else []) + starts))
        pending = waits
    stages.append(functools.partial(run, pending))
    return stages


def half_columns(ref, leaf, h):
    width = ref.shape[-1] // 2
    return ref.at[:, leaf, :, :, pl.ds(h * width, width)]


def block_stages(mail, place, shards, block_views):
    n = place.paths
    own = [mail.local(None, s, d) for s, d in zip(shards, block_views(place.p))]
    starts, waits = [o[0] for o in own], [o[1] for o in own]
    lands = [mail.new_recv(n) for _ in shards]
    for k in range(1, n):
        there = (place.p + k) % n
        for s, d, w, land in zip(shards, block_views(place.p), block_views(there), lands):
            starts.append(mail.send(None, s, d, place.at_p(there), land + place.p))
            waits.append(mail.hear(None, w, place.at_p(there), land + there))
    return [functools.partial(run, starts), functools.partial(run, waits)]


def path_half(ref, h):
    n = ref.shape[1] // 2
    return ref.at[:, pl.ds(h * n, n)]


def spread_stages(mail, place, wholes, blocks=None):
    if (place.A, place.B) != (2, 2):
        return spread_lines(mail, place, wholes, blocks)
    a, b, c = place.a, place.b, place.c
    at = lambda w, a, b, c: w.at[:, place.leaf_at(a, b, c)]
    to_a, to_b, to_core = place.at_a(1 - a), place.at_b(1 - b), place.at_core()
    own = []
    sources = [at(w, a, b, c) for w in wholes]
    if blocks is not None:
        own = [mail.local(None, x, s) for x, s in zip(blocks, sources)]
        sources = list(blocks)
    urgent, calm, relay, near, far = [], [], [], [], []
    for w, s in zip(wholes, sources):
        mine, from_a, from_b = at(w, a, b, c), at(w, 1 - a, b, c), at(w, a, 1 - b, c)
        from_ab = at(w, 1 - a, 1 - b, c)

        def post(src, dst, to, landing, h):
            return mail.post(
                None, path_half(src, h), path_half(dst, h), to, None, path_half(landing, h)
            )

        urgent += [post(s, mine, to_b, from_b, 0), post(s, mine, to_a, from_a, 1)]
        calm += [post(s, mine, to_b, from_b, 1), post(s, mine, to_a, from_a, 0)]
        relay += [post(from_b, from_b, to_a, from_ab, 0), post(from_a, from_a, to_b, from_ab, 1)]
        near.append(mail.post(None, s, mine, to_core, None, at(w, a, b, 1 - c)))
        for x, y, l in ((1 - a, b, near), (a, 1 - b, near), (1 - a, 1 - b, far)):
            l.append(mail.post(None, at(w, x, y, c), at(w, x, y, c), to_core, None, at(w, x, y, 1 - c)))
    start = lambda jobs: run([j[0] for j in jobs])
    wait = lambda jobs: run([j[1] for j in jobs])
    first = near[::3]
    second = [j for k, j in enumerate(near) if k % 3]

    def opening():
        start(urgent)
        start(calm)
        start(first)
        run([o[0] for o in own])

    def passing():
        wait(urgent)
        start(relay)

    def sharing():
        wait(calm)
        run([o[1] for o in own])
        start(second)

    def ending():
        wait(relay)
        start(far)

    return [opening, passing, sharing, ending, lambda: wait(near + far)]


def spread_lines(mail, place, wholes, blocks=None):
    A, B, c = place.A, place.B, place.c

    def of_b(h, across_a):
        ays = range(A) if across_a else [place.a]
        return lambda i: [half_columns(w, place.leaf_at(a, i, c), h) for a in ays for w in wholes]

    def of_a(h, across_b):
        bees = range(B) if across_b else [place.b]
        return lambda i: [half_columns(w, place.leaf_at(i, b, c), h) for b in bees for w in wholes]

    own = []
    firsts = [None, None]
    sources = [w.at[:, place.leaf] for w in wholes]
    if blocks is not None:
        own = [mail.local(None, x, w.at[:, place.leaf]) for x, w in zip(blocks, wholes)]
        firsts = [
            [x.at[:, :, :, pl.ds(h * (x.shape[-1] // 2), x.shape[-1] // 2)] for x in blocks]
            for h in range(2)
        ]
        sources = list(blocks)
    line_a, line_b = place.line_a(), place.line_b()
    phases = [
        (flood(mail, line_b, of_b(0, False), firsts[0]), flood(mail, line_a, of_a(1, False), firsts[1])),
        (flood(mail, line_a, of_a(0, True)), flood(mail, line_b, of_b(1, True))),
    ]
    core = [
        mail.post(
            None,
            s,
            w.at[:, place.leaf],
            place.at_core(),
            None,
            w.at[:, place.leaf_at(place.a, place.b, 1 - c)],
        )
        for s, w in zip(sources, wholes)
    ]
    rest = []
    for offset in range(1, A * B):
        spot = (place.a * B + place.b + offset) % (A * B)
        for w in wholes:
            mine, other = w.at[:, spot * 2 + c], w.at[:, spot * 2 + 1 - c]
            rest.append(mail.post(None, mine, mine, place.at_core(), None, other))
    steps = []
    opening = [o[0] for o in own] + [j[0] for j in core]
    for n_phase, phase in enumerate(phases):
        before = [o[1] for o in own] if n_phase == 1 else []
        for s in range(max(len(f) for f in phase)):
            starts, waits = list(before), []
            before = []
            for f in phase:
                if s < len(f):
                    starts += f[s][0]
                    waits += f[s][1]
            steps.append((starts + opening, waits))
            opening = []
    steps.append((opening + [j[0] for j in rest], [j[1] for j in core + rest]))
    return chain(steps)


def pair_gather_stages(mail, place, shard, whole):
    n, h = place.paths, place.half
    rows = shard.shape[0] // 2
    half = lambda ref, u: ref.at[pl.ds(pl.multiple_of(u * rows, rows), rows)]
    lands, core_lands = mail.new_recv(n), mail.new_recv(n)
    own = mail.local(place.primary, shard, whole.at[place.p])
    first = jnp.where(place.c == 0, 0, h)
    edge = jnp.where(place.c == 0, h - 1, h)
    starts = []
    for u in range(2):
        for q in range(h):
            q = first + q
            to = (place.leaf_at(place.a, place.b, u), q)
            near = place.primary & jnp.logical_not((q == place.p) & (place.c == u))
            away = near | (jnp.logical_not(place.primary) & (q == edge))
            starts.append(
                mail.send(away, half(shard, u), half(whole.at[place.p], u), to, lands + place.p)
            )
    k = mail.new_recv()
    mate = whole.at[place.p]
    starts.append(
        mail.send(place.primary, half(shard, place.c), half(mate, place.c), place.at_core(), k)
    )
    starts.append(own[0])
    stages = [functools.partial(run, starts)]
    outward = place.at_p(place.p - place.inward)
    for r in range(n):
        j = place.shard_of_rank(r)
        item = half(whole.at[j], place.c)
        got = jnp.logical_not(place.primary & (place.p == j))
        actions = [mail.hear(got, item, place.at_core(), lands + j)]
        if r >= h and h > 1:
            actions.append(mail.send(place.pm > 0, item, item, outward, lands + j))
        actions.append(
            mail.send(jnp.logical_not(place.p == j), item, item, place.at_core(), core_lands + j)
        )
        stages.append(functools.partial(run, actions))
    rest = [own[1]]
    rest.append(
        mail.hear(jnp.logical_not(place.primary), half(mate, 1 - place.c), place.at_core(), k)
    )
    for r in range(n):
        j = place.shard_of_rank(r)
        rest.append(
            mail.hear(
                jnp.logical_not(place.p == j),
                half(whole.at[j], 1 - place.c),
                place.at_core(),
                core_lands + j,
            )
        )
    stages.append(functools.partial(run, rest))
    return stages


def mirror_stages(mail, place, own, mine):
    local = mail.local(place.primary, own, mine)
    other = jnp.logical_not(place.primary)
    start, wait = mail.post(other, own, mine, place.at_mirror(), other, mine)
    return [lambda: run([local[0], start]), lambda: run([local[1], wait])]


def add_rows(dst, src):
    lead = dst.shape[:-2]
    total = 1
    for extent in lead:
        total *= extent

    def body(i, _):
        index = []
        rest = i
        for extent in reversed(lead):
            index.insert(0, rest % extent)
            rest = rest // extent
        index = tuple(index)
        dst[index] = dst[index] + src[index]
        return 0

    if total == 1:
        body(0, 0)
    else:
        lax.fori_loop(0, total, body, 0)


def add_tall(dst, src):
    rows = dst.shape[0]
    step = 64 if rows % 64 == 0 else rows

    def body(r, _):
        at = pl.ds(pl.multiple_of(r * step, step), step)
        dst[at] = dst[at] + src[at]
        return 0

    lax.fori_loop(0, rows // step, body, 0)


def shift_sum(mail, line, mine, slots_up, slots_down, add):
    size, pos, to = line
    if size == 1:
        return []
    if size == 2:
        jobs = [
            mail.post(None, s, slot, to(1 - pos), None, slot)
            for s, slot in zip(mine(1 - pos), slots_up[0])
        ]

        def end():
            for job, dst, slot in zip(jobs, mine(pos), slots_up[0]):
                job[1]()
                add(dst, slot)

        return [lambda: run([j[0] for j in jobs]), end]
    stages = []
    for k in range(size - 1):
        early, actions = [], []
        for sign, slots in ((1, slots_up), (-1, slots_down)):
            dest = size - 1 - k if sign == 1 else k
            when = (pos < dest) if sign == 1 else (pos > dest)
            hear_when = (
                ((pos > 0) & (pos <= dest)) if sign == 1 else ((pos < size - 1) & (pos >= dest))
            )
            there = clamp(pos + sign, size)
            jobs = [
                mail.post(when, s, slot, to(there), None, slot)
                for s, slot in zip(mine(dest), slots[k])
            ]

            def take(jobs=jobs, dst_refs=mine(dest), slot_refs=slots[k]):
                for job, dst, slot in zip(jobs, dst_refs, slot_refs):
                    job[1]()
                    add(dst, slot)

            end = (pos == 0) if sign == 1 else (pos == size - 1)
            starts = functools.partial(run, [job[0] for job in jobs])
            early.append(functools.partial(guarded, end, starts))
            actions.append(functools.partial(guarded, hear_when, take))
            actions.append(functools.partial(guarded, jnp.logical_not(end), starts))
        stages.append(functools.partial(run, early + actions))
    return stages


def fold_scratch(shape, k, R, C, dtype):
    if (shape.A, shape.B) != (2, 2):
        return fold_lines_scratch(shape, k, R, C, dtype)
    block = (k, 2, 2, shape.paths, R, C)
    halves = (2, k, shape.paths // 2, R, C)
    return [pltpu.VMEM(block, dtype)] * 2 + [pltpu.VMEM(halves, dtype)] * 3 + [pltpu.VMEM((1, R, C), dtype)]


def fold_lines_scratch(shape, k, R, C, dtype):
    A, B, paths = shape.A, shape.B, shape.paths
    nb, na = max(B - 1, 1) * (2 if B > 2 else 1), max(A - 1, 1)
    return [
        pltpu.VMEM((k, A, B, paths, R, C), dtype),
        pltpu.VMEM((k, A, B, paths, R, C), dtype),
        pltpu.VMEM((nb, k, A, paths, R, C // 2), dtype),
        pltpu.VMEM((na, k, paths, R, C // 2), dtype),
        pltpu.VMEM((na, k, B, paths, R, C // 2), dtype),
        pltpu.VMEM((nb, k, paths, R, C // 2), dtype),
    ]


N_FOLD = 6


def up_down(ref, size):
    if size <= 2:
        return [[ref.at[0]]], None
    return (
        [[ref.at[k]] for k in range(size - 1)],
        [[ref.at[size - 1 + k]] for k in range(size - 1)],
    )


def fold_stages(mail, place, partial, scratch):
    if (place.A, place.B) != (2, 2):
        return fold_lines(mail, place, partial, scratch)
    a, b, c = place.a, place.b, place.c
    acc, got, far, direct, relayed = scratch[:5]
    own = mail.local(None, partial.at[:, :, :, c], acc)
    core = mail.post(None, partial.at[:, :, :, 1 - c], got, place.at_core(), None, got)
    to_a, to_b = place.at_a(1 - a), place.at_b(1 - b)
    of_a, of_b, of_ab = acc.at[:, 1 - a, b], acc.at[:, a, 1 - b], acc.at[:, 1 - a, 1 - b]
    mine = acc.at[:, a, b]

    def post(src, h, slot, to):
        return mail.post(None, path_half(src, h), slot, to, None, slot)

    urgent = [post(of_ab, 0, far.at[0], to_b), post(of_ab, 1, far.at[1], to_a)]
    calm = [post(of_b, 0, direct.at[0], to_b), post(of_a, 1, direct.at[1], to_a)]
    late = [post(of_a, 0, relayed.at[0], to_a), post(of_b, 1, relayed.at[1], to_b)]

    def join():
        own[1]()
        core[1]()
        add_rows(of_ab, got.at[:, 1 - a, 1 - b])
        run([j[0] for j in urgent])
        add_rows(of_b, got.at[:, a, 1 - b])
        calm[0][0]()
        add_rows(of_a, got.at[:, 1 - a, b])
        calm[1][0]()
        add_rows(mine, got.at[:, a, b])

    def passing():
        urgent[0][1]()
        add_rows(path_half(of_a, 0), far.at[0])
        late[0][0]()
        urgent[1][1]()
        add_rows(path_half(of_b, 1), far.at[1])
        late[1][0]()

    def taking():
        for h in range(2):
            calm[h][1]()
            add_rows(path_half(mine, h), direct.at[h])

    def ending():
        for h in range(2):
            late[h][1]()
            add_rows(path_half(mine, h), relayed.at[h])

    return [lambda: run([own[0], core[0]]), join, passing, taking, ending], mine


def fold_lines(mail, place, partial, scratch):
    c = place.c
    acc, got, sb0, sa0, sa1, sb1 = scratch
    own = mail.local(None, partial.at[:, :, :, c], acc)
    core = mail.post(None, partial.at[:, :, :, 1 - c], got, place.at_core(), None, got)
    width = acc.shape[-1] // 2
    left, right = pl.ds(0, width), pl.ds(width, width)

    def join():
        own[1]()
        core[1]()
        add_rows(acc, got)

    line_a, line_b = place.line_a(), place.line_b()
    h0_b = shift_sum(
        mail, line_b, lambda d: [acc.at[:, :, d, :, :, left]], *up_down(sb0, place.B), add_rows
    )
    h1_a = shift_sum(
        mail, line_a, lambda d: [acc.at[:, d, :, :, :, right]], *up_down(sa1, place.A), add_rows
    )
    h0_a = shift_sum(
        mail, line_a, lambda d: [acc.at[:, d, place.b, :, :, left]], *up_down(sa0, place.A), add_rows
    )
    h1_b = shift_sum(
        mail, line_b, lambda d: [acc.at[:, place.a, d, :, :, right]], *up_down(sb1, place.B), add_rows
    )

    def beside(one, two):
        return [
            functools.partial(run, [s[k] for s in (one, two) if k < len(s)])
            for k in range(max(len(one), len(two)))
        ]

    def joined(first, second):
        if not first or not second:
            return first + second
        return first[:-1] + [functools.partial(run, [first[-1], second[0]])] + second[1:]

    stages = joined(
        [lambda: run([own[0], core[0]]), join], beside(h0_b, h1_a)
    )
    stages = joined(stages, beside(h0_a, h1_b))
    return stages, acc.at[:, place.a, place.b]


def line_scratch(shape, k, R, C, dtype):
    return [pltpu.VMEM((max(shape.paths - 1, 1), k, R, C), dtype)]


def line_stages(mail, place, sums, slots, out):
    n = place.paths
    jobs = []
    for k in range(1, n):
        there = (place.p + k) % n
        slot = slots.at[k - 1]
        jobs.append(mail.post(None, sums.at[:, there], slot, place.at_p(there), None, slot))

    def end():
        run([j[1] for j in jobs])
        for j in range(out.shape[0]):
            total = sums[j, place.p].astype(F32)
            for k in range(n - 1):
                total = total + slots[k, j].astype(F32)
            out[j] = total.astype(out.dtype)

    return [lambda: run([j[0] for j in jobs]), end]


def pair_sum_scratch(shape, R, C):
    return [
        pltpu.VMEM((shape.paths, R // 2, C), BF16),
        pltpu.VMEM((shape.paths, R // 2, C), BF16),
        pltpu.VMEM((shape.half, R, C), BF16),
    ]


def pair_sum_stages(mail, place, part, scratch, out):
    n, h = place.paths, place.half
    core_slot, in_slot, landing = scratch
    rows = part.shape[1] // 2
    half = lambda ref, u: ref.at[pl.ds(pl.multiple_of(u * rows, rows), rows)]
    lands = [mail.new_recv(2) for _ in range(h)]
    inner = place.at_p(place.p + place.inward)
    sends, sums, passes = [], [], []
    for r in range(n - 1, -1, -1):
        j = place.shard_of_rank(r)
        item = part.at[j]
        mine = half(item, place.c)
        send, hear = mail.post(
            None, half(item, 1 - place.c), core_slot.at[r], place.at_core(), None, core_slot.at[r]
        )
        owner = (place.leaf_at(place.a, place.b, place.tree), j)
        leave = []
        if r >= h:
            k = mail.new_recv()
            slot = in_slot.at[r]
            in_send = mail.send(place.pm < h - 1, mine, slot, inner, k)
            in_hear = mail.hear(None, slot, place.at_core(), k)
            go = mail.send(
                place.pm == h - 1, mine, half(landing.at[h - 1], place.c), owner, lands[h - 1] + place.c
            )

            def inward(in_send=in_send, in_hear=in_hear, mine=mine, slot=slot, go=go):
                if h > 1:

                    @pl.when(place.pm > 0)
                    def _():
                        in_hear()
                        add_tall(mine, slot)

                    in_send()
                go()

            passes.append(inward)
        else:
            away = jnp.logical_not(place.primary & (place.p == j))
            for q in range(h):
                leave.append(
                    mail.send(
                        away & (place.pm == q),
                        mine,
                        half(landing.at[q], place.c),
                        owner,
                        lands[q] + place.c,
                    )
                )

        def settle(hear=hear, mine=mine, slot=core_slot.at[r], leave=leave):
            hear()
            add_tall(mine, slot)
            run(leave)

        sends.append(send)
        sums.append(settle)
    stages = [[sends[0]]]
    for k in range(1, n):
        stages.append([sends[k], sums[k - 1]])
    stages.append([sums[n - 1]])
    for k, step in enumerate(passes):
        stages[k + 1].append(step)

    def end():
        for q in range(h):
            for u in range(2):
                self_made = place.primary & (place.own_rank == q) & (place.c == u)
                comes = jnp.logical_not(self_made) & (place.primary | (q == h - 1))
                mail.hear(comes, half(landing.at[q], u), place.at_core(), lands[q] + u)()

        step = 64 if rows % 64 == 0 else rows
        for u in range(2):

            def body(i, _, u=u):
                at = pl.ds(pl.multiple_of(u * rows + i * step, step), step)

                @pl.when(place.primary)
                def _():
                    for q in range(h):
                        self_made = (place.own_rank == q) & (place.c == u)
                        term = jnp.where(self_made, part[place.p, at], landing[q, at]).astype(F32)
                        total = term if q == 0 else total + term
                    out[at] = total

                @pl.when(jnp.logical_not(place.primary))
                def _():
                    out[at] = landing[h - 1, at].astype(F32)

                return 0

            lax.fori_loop(0, rows // step, body, 0)

    return [functools.partial(run, x) for x in stages] + [end]


def at_units(hooks, stages, units):
    for stage, unit in zip(stages, units, strict=True):
        hooks.setdefault(unit, []).append(stage)


def hooked(count, unit, hooks):
    def body(i, _):
        for at, stages in hooks.items():
            if at < count:

                @pl.when(i == at)
                def _():
                    run(stages)

        unit(i)
        return 0

    lax.fori_loop(0, count, body, 0)
    for at in sorted(hooks):
        if at >= count:
            run(hooks[at])


def kernel_call(kernel, name, collective_id, ins, in_specs, outs, out_specs, scratch):
    return pl.pallas_call(
        kernel,
        out_shape=outs,
        in_specs=in_specs,
        out_specs=out_specs,
        scratch_shapes=scratch,
        compiler_params=pltpu.CompilerParams(
            collective_id=collective_id,
            has_side_effects=True,
            vmem_limit_bytes=VMEM_LIMIT,
        )
        if collective_id is not None
        else pltpu.CompilerParams(vmem_limit_bytes=VMEM_LIMIT),
        name=name,
    )(*ins)


def dot(x, y, contract):
    return lax.dot_general(x, y, (contract, ((), ())), preferred_element_type=F32)


def mm(x, w):
    return dot(x, w, ((1,), (0,)))


def mm_t(x, w):
    return dot(x, w, ((1,), (1,)))


def t_mm(x, y):
    return dot(x, y, ((0,), (0,)))


def open_kernel(shape, column, mirror, sems):
    place = Place(shape)
    greet(place, column, mirror)
    return place, Mail(*sems)


def opening_kernel(shape, turns, tok, small, attn_in, links, all_tok, g_small, g_qkv, bias, *scratch):
    sems, (links_got, reach, spot) = scratch[:3], scratch[3:]
    place, mail = open_kernel(shape, True, False, sems)
    three = g_qkv.shape[0]
    to_core = mail.post(None, links, links_got, place.at_core(), None, links_got)
    to_core[0]()
    shards = [small, attn_in.at[pl.ds(0, three)]]
    wholes = [g_small, g_qkv]
    weights = block_stages(
        mail, place, shards, lambda i: [w.at[:, place.leaf, i] for w in wholes]
    )
    spread = spread_stages(mail, place, wholes)
    tokens = pair_gather_stages(mail, place, tok, all_tok)
    weights[0]()
    tokens[0]()
    to_core[1]()

    count = links.shape[0] // 2
    mine = jnp.where(place.primary, links[...], links_got[...])
    reach[...] = jnp.zeros_like(reach)
    spot[...] = jnp.zeros_like(spot)
    reach[pl.ds(0, count)] = mine[:count]
    spot[pl.ds(0, count)] = mine[count:]
    for _ in range(turns):
        r = reach[...]
        reach[...] = jnp.minimum(r + mm(r.astype(BF16), r.astype(BF16)), 1.0)
    placed = spot[...].astype(BF16)
    linked = mm_t(mm(placed, reach[...].astype(BF16)).astype(BF16), placed).astype(BF16)
    rows, keys = bias.shape
    step = min(128, rows)

    def fill(i, _):
        first = i * step
        at = pl.ds(pl.multiple_of(first, step), step)
        q_slot = (place.block * rows + first + lax.broadcasted_iota(jnp.int32, (step, 128), 0)) // BLK
        pick_q = (q_slot == lax.broadcasted_iota(jnp.int32, (step, 128), 1)).astype(F32)
        own = mm(pick_q.astype(BF16), linked).astype(BF16)
        k_slot = lax.broadcasted_iota(jnp.int32, (128, keys), 1) // BLK
        pick_k = (k_slot == lax.broadcasted_iota(jnp.int32, (128, keys), 0)).astype(F32)
        seen = mm(own, pick_k.astype(BF16))
        q_at = place.block * rows + first + lax.broadcasted_iota(jnp.int32, (step, keys), 0)
        k_at = lax.broadcasted_iota(jnp.int32, (step, keys), 1)
        inside = (q_at // BLK == k_at // BLK) & (k_at <= q_at)
        bias[at] = jnp.where((seen > 0.5) | inside, 0.0, -1e30).astype(bias.dtype)
        return 0

    run(weights[1:] + spread[:1])
    run(tokens[1:-3])
    spread[1]()
    lax.fori_loop(0, rows // step, fill, 0)
    run(tokens[-3:-1])
    run(spread[2:])
    tokens[-1]()
    mail.finish()


def attend_unit(q_ref, k_ref, v_ref, bias_ref, o_ref, lse_ref, row, step, pair):
    at = pl.ds(pl.multiple_of(row, step), step)
    cols = pl.ds(pl.multiple_of(pair * PAIR, PAIR), PAIR)
    lane = lax.broadcasted_iota(jnp.int32, (1, PAIR), 1)
    q = q_ref[at, cols]
    k = k_ref[:, cols]
    v = v_ref[:, cols]
    out = jnp.zeros((step, PAIR), F32)
    lse = jnp.zeros((step, PAIR), F32)
    for h in range(2):
        own = (lane >= HEAD) if h else (lane < HEAD)
        s = mm_t(jnp.where(own, q, jnp.zeros_like(q)), k)
        if bias_ref is not None:
            s = s + bias_ref[at].astype(F32)
        peak = jnp.max(s, axis=1, keepdims=True)
        e = jnp.exp(s - peak)
        mass = jnp.sum(e, axis=1, keepdims=True)
        o = mm(e.astype(BF16), v)
        out = jnp.where(own, o / mass, out)
        lse = jnp.where(own, peak + jnp.log(mass), lse)
    o_ref[at, cols] = out.astype(BF16)
    lse_ref[at, cols] = lse


def attend_back_unit(q_ref, k_ref, v_ref, bias_ref, do_ref, o_ref, lse_ref, dq_ref, dk_acc, dv_acc, row, step, pair):
    at = pl.ds(pl.multiple_of(row, step), step)
    cols = pl.ds(pl.multiple_of(pair * PAIR, PAIR), PAIR)
    lane = lax.broadcasted_iota(jnp.int32, (1, PAIR), 1)
    k = k_ref[:, cols]
    v = v_ref[:, cols]
    q = q_ref[at, cols]
    do = do_ref[at, cols]
    both = do.astype(F32) * o_ref[at, cols].astype(F32)
    lse_pair = lse_ref[at, cols]
    dq = jnp.zeros((step, PAIR), F32)
    for h in range(2):
        own = (lane >= HEAD) if h else (lane < HEAD)
        q_h = jnp.where(own, q, jnp.zeros_like(q))
        do_h = jnp.where(own, do, jnp.zeros_like(do))
        delta = jnp.sum(jnp.where(own, both, 0.0), axis=1, keepdims=True)
        lse = lse_pair[:, h * HEAD : h * HEAD + 1]
        s = mm_t(q_h, k)
        if bias_ref is not None:
            s = s + bias_ref[at].astype(F32)
        e = jnp.exp(s - lse)
        dp = mm_t(do_h, v)
        ds = (e * (dp - delta)).astype(BF16)
        dq = jnp.where(own, mm(ds, k), dq)
        dk_acc[...] += t_mm(ds, q_h)
        dv_acc[...] += t_mm(e.astype(BF16), do_h)
    dq_ref[at, cols] = dq.astype(BF16) * BF16(HEAD**-0.5)


def attend_units(rows, width):
    step = min(256, rows)
    return rows // step, step, width // PAIR


def self_kernel(
    shape, all_tok, w_qkv, vec, bias, enc, attn_in, attn_out, ffn_in, ffn_out,
    q, k, v, att, lse, all_enc, g_in, g_out, g_1, z_2, *sems,
):
    place, mail = open_kernel(shape, True, False, sems)
    n, rows, width = all_tok.shape
    three = g_in.shape[0]
    e = pair_gather_stages(mail, place, enc, all_enc)
    shards = [attn_in.at[pl.ds(attn_in.shape[0] - three, three)], attn_out]
    wholes = [g_in, g_out]
    w = block_stages(mail, place, shards, lambda i: [g.at[:, place.leaf, i] for g in wholes])
    w += spread_stages(mail, place, wholes)
    f = block_stages(mail, place, [ffn_in], lambda i: [g_1.at[:, place.leaf, i]])
    f += spread_stages(mail, place, [g_1])
    z = block_stages(mail, place, [ffn_out], lambda i: [z_2.at[:, i]])
    w[0]()
    scale = HEAD**-0.5
    q[...] = ((mm(all_tok[place.block], w_qkv[0]) + vec[pl.ds(0, 1)]) * scale).astype(BF16)

    def project(i):
        x = all_tok[i]
        at = pl.ds(pl.multiple_of(i * rows, rows), rows)
        k[at] = mm(x, w_qkv[1]).astype(BF16)
        v[at] = (mm(x, w_qkv[2]) + vec[pl.ds(1, 1)]).astype(BF16)

    blocks, step, pairs = attend_units(rows, width)
    units = blocks * pairs
    t = lambda x: n + (x * units) // 12
    hooks, last = {}, n + units
    at_units(hooks, w[1:3], [t(1)] * 2)
    at_units(hooks, e[:1], [1])
    at_units(hooks, f[:1], [2])
    at_units(hooks, z[:1], [t(1)])
    at_units(hooks, w[3:5] + w[5:-1], [t(4), t(6)] + [t(7)] * len(w[5:-1]))
    at_units(hooks, e[1:-1], [t(3)] * len(e[1:3]) + [t(8)] * len(e[3:-1]))
    at_units(hooks, f[1:5] + f[5:-1], [t(6), t(6), t(10), t(11)] + [last] * len(f[5:-1]))
    at_units(hooks, e[-1:] + w[-1:] + f[-1:] + z[1:], [last] * 4)
    early = {at: stages for at, stages in hooks.items() if at < n}
    late = {at - n: stages for at, stages in hooks.items() if at >= n}
    hooked(n, project, early)

    def unit(i):
        attend_unit(q, k, v, bias, att, lse, (i % blocks) * step, step, i // blocks)

    hooked(blocks * pairs, unit, late)
    mail.finish()


ROOT_HALF = 0.7071067811865476
NORM = 0.3989422804014327


def normed(v):
    centre = v - jnp.mean(v, axis=1, keepdims=True)
    inverse = lax.rsqrt(jnp.mean(centre * centre, axis=1, keepdims=True) + 1e-05)
    return centre * inverse, inverse


def normed_back(g, gain, hat, inverse):
    gx = g * gain
    mean_g = jnp.mean(gx, axis=1, keepdims=True)
    mean_gh = jnp.mean(gx * hat, axis=1, keepdims=True)
    return inverse * (gx - mean_g - hat * mean_gh)


def by_rows(rows, action):
    step = min(128, rows)

    def one(i, _):
        action(pl.ds(pl.multiple_of(i * step, step), step))
        return 0

    lax.fori_loop(0, rows // step, one, 0)


def row_sum(x):
    return jnp.sum(x, axis=0, keepdims=True)


def cross_kernel(
    shape, shifts, att, all_tok, all_enc, w_in, w_out, vec, z_2, cot,
    hat1, inv1, first_low, cq, ck, cv, crossed, lse, g_2, my_cot, toks, *sems,
):
    place, mail = open_kernel(shape, False, True, sems)
    rows, width = cq.shape
    n, enc_rows, _ = all_enc.shape
    w = spread_stages(mail, place, [g_2], [z_2])
    c = mirror_stages(mail, place, cot, my_cot)
    mine = mail.local(None, all_tok.at[place.block], toks)
    mine[0]()
    w[0]()
    c[0]()

    def project(i):
        x = all_enc[i]
        at = pl.ds(pl.multiple_of(i * enc_rows, enc_rows), enc_rows)
        ck[at] = mm(x, w_in[1]).astype(BF16)
        cv[at] = (mm(x, w_in[2]) + vec[pl.ds(4, 1)]).astype(BF16)

    hooked(n, project, {})
    mine[1]()
    scale = HEAD**-0.5

    def first(at):
        v = toks[at].astype(F32) + mm(att[at], w_out[0]) + vec[pl.ds(2, 1)]
        hat, inverse = normed(v)
        hat1[at] = hat
        inv1[at] = jnp.broadcast_to(inverse, (hat.shape[0], 128))
        low = (hat * vec[pl.ds(shifts, 1)] + vec[pl.ds(7, 1)]).astype(BF16)
        first_low[at] = low
        cq[at] = ((mm(low, w_in[0]) + vec[pl.ds(3, 1)]) * scale).astype(BF16)

    by_rows(rows, first)
    blocks, step, pairs = attend_units(rows, width)
    total = blocks * pairs
    t = lambda x: (x * total) // 12
    late = {}
    at_units(late, w[1:], [t(1), t(4), t(5)] + [total] * (len(w) - 4))
    at_units(late, c[1:], [total])

    def unit(i):
        attend_unit(cq, ck, cv, None, crossed, lse, (i % blocks) * step, step, i // blocks)

    hooked(total, unit, late)
    mail.finish()


def ffn_kernel(
    shifts, hat1, crossed, w_out, w1, w2, vec, b1, cot,
    out, gw1, gw2, gwo, g_crossed, g_pre2, sums, gb1,
    hat2, inv2, low2, acc, slope, hidden, g_pre3, g_ffn, acc2, g_cb,
):
    rows, width = crossed.shape
    wide = hidden.shape[1]
    piece = 512
    gain = lambda i: vec[pl.ds(shifts + i, 1)]
    shift = lambda i: vec[pl.ds(i, 1)]
    sums[...] = jnp.zeros_like(sums)

    def second(at):
        v = hat1[at] * gain(0) + shift(7) + mm(crossed[at], w_out[1]) + shift(5)
        hat, inverse = normed(v)
        hat2[at] = hat
        inv2[at] = jnp.broadcast_to(inverse, (hat.shape[0], 128))
        low2[at] = (hat * gain(1) + shift(8)).astype(BF16)

    by_rows(rows, second)
    acc[...] = jnp.zeros_like(acc)

    def up(j, _):
        cols = pl.ds(pl.multiple_of(j * piece, piece), piece)
        u = mm(low2[...], w1[:, cols]) + b1[:, cols]
        phi = 0.5 * (1.0 + lax.erf(u * ROOT_HALF))
        slope[:, cols] = phi + u * jnp.exp(-0.5 * u * u) * NORM
        h = (u * phi).astype(BF16)
        hidden[:, cols] = h
        acc[...] += mm(h, w2[cols])
        return 0

    lax.fori_loop(0, wide // piece, up, 0)

    def third(at):
        v = hat2[at] * gain(1) + shift(8) + acc[at] + shift(6)
        hat, inverse = normed(v)
        out[at] = (hat * gain(2) + shift(9)).astype(BF16)
        g = cot[at].astype(F32)
        sums[pl.ds(shifts + 2, 1)] += row_sum(g * hat)
        sums[pl.ds(9, 1)] += row_sum(g)
        back = normed_back(g, gain(2), hat, inverse)
        g_pre3[at] = back
        low = back.astype(BF16)
        g_ffn[at] = low
        sums[pl.ds(6, 1)] += row_sum(low.astype(F32))

    by_rows(rows, third)
    acc2[...] = jnp.zeros_like(acc2)

    def down(j, _):
        cols = pl.ds(pl.multiple_of(j * piece, piece), piece)
        g = (mm_t(g_ffn[...], w2[cols]) * slope[:, cols]).astype(BF16)
        gb1[:, cols] = row_sum(g.astype(F32))
        gw2[cols] = t_mm(hidden[:, cols], g_ffn[...]).astype(BF16)
        gw1[:, cols] = t_mm(low2[...], g).astype(BF16)
        acc2[...] += mm_t(g, w1[:, cols])
        return 0

    lax.fori_loop(0, wide // piece, down, 0)

    def back_two(at):
        g = g_pre3[at] + acc2[at]
        hat = hat2[at]
        sums[pl.ds(shifts + 1, 1)] += row_sum(g * hat)
        sums[pl.ds(8, 1)] += row_sum(g)
        back = normed_back(g, gain(1), hat, inv2[at, :1])
        g_pre2[at] = back
        low = back.astype(BF16)
        g_cb[at] = low
        sums[pl.ds(5, 1)] += row_sum(low.astype(F32))
        g_crossed[at] = mm_t(low, w_out[1]).astype(BF16)

    by_rows(rows, back_two)
    gwo[...] = t_mm(crossed[...], g_cb[...]).astype(BF16)


def cross_back_kernel(
    shape, shifts, cq, ck, cv, do, o, lse, first_low, hat1, inv1, all_enc, w_in, w_out, att, g_pre2, vec, sums_in, p_2, out_rows,
    g_in, g_wo, g_enc, g_att, g_pre1, sums, s_2, my_out, dq, dk, dv, g_br, dk_acc, dv_acc, *scratch,
):
    sems, scratch = scratch[:3], scratch[3:]
    place, mail = open_kernel(shape, False, True, sems)
    rows, width = cq.shape
    f, sum_2 = fold_stages(mail, place, p_2, scratch[:N_FOLD])
    c = mirror_stages(mail, place, out_rows, my_out)
    f[0]()
    blocks, step, pairs = attend_units(rows, width)
    total = blocks * pairs
    t = lambda x: (x * total) // 12
    hooks = {}
    at_units(hooks, f[1:5] + f[5:], [t(1), t(5), t(7), t(10)] + [total] * len(f[5:]))
    at_units(hooks, c, [0, total])

    def unit(i):
        first = i % blocks == 0

        @pl.when(first)
        def _():
            dk_acc[...] = jnp.zeros_like(dk_acc)
            dv_acc[...] = jnp.zeros_like(dv_acc)

        pair = i // blocks
        attend_back_unit(cq, ck, cv, None, do, o, lse, dq, dk_acc, dv_acc, (i % blocks) * step, step, pair)

        @pl.when(i % blocks == blocks - 1)
        def _():
            cols = pl.ds(pl.multiple_of(pair * PAIR, PAIR), PAIR)
            dk[:, cols] = dk_acc[...].astype(BF16)
            dv[:, cols] = dv_acc[...].astype(BF16)

    last = hooks.pop(total)
    hooked(total, unit, hooks)
    sums[...] = sums_in[...]
    n, enc_rows, _ = all_enc.shape
    g_in[0] = t_mm(first_low[...], dq[...]).astype(BF16)
    flat = all_enc.reshape(n * enc_rows, width)
    g_in[1] = t_mm(flat[...], dk[...]).astype(BF16)
    g_in[2] = t_mm(flat[...], dv[...]).astype(BF16)
    sums[pl.ds(3, 1)] = row_sum(dq[...].astype(F32))
    sums[pl.ds(4, 1)] = row_sum(dv[...].astype(F32))

    def encoder(i, _):
        at = pl.ds(pl.multiple_of(i * enc_rows, enc_rows), enc_rows)
        g_enc[i] = (mm_t(dk[at], w_in[1]) + mm_t(dv[at], w_in[2])).astype(BF16)
        return 0

    lax.fori_loop(0, n, encoder, 0)

    def back_one(at):
        g = g_pre2[at] + mm_t(dq[at], w_in[0])
        hat = hat1[at]
        sums[pl.ds(shifts, 1)] += row_sum(g * hat)
        sums[pl.ds(7, 1)] += row_sum(g)
        back = normed_back(g, vec[pl.ds(shifts, 1)], hat, inv1[at, :1])
        g_pre1[at] = back
        low = back.astype(BF16)
        g_br[at] = low
        sums[pl.ds(2, 1)] += row_sum(low.astype(F32))
        g_att[at] = mm_t(low, w_out[0]).astype(BF16)

    by_rows(rows, back_one)
    g_wo[...] = t_mm(att[...], g_br[...]).astype(BF16)
    run(last)
    s_2[...] = sum_2[...]
    mail.finish()


def self_back_kernel(
    shape, q, k, v, bias, do, o, lse, z_2, sums_in, p_1, p_in, p_o0, p_o1, p_enc,
    dq, dk, dv, o_1, o_2, o_in, o_o0, o_o1, o_enc, sums, dk_acc, dv_acc, *scratch,
):
    sems, scratch = scratch[:3], scratch[3:]
    place, mail = open_kernel(shape, True, False, sems)
    rows, width = q.shape
    l_2 = line_stages(mail, place, z_2, scratch[0], o_2)
    f_1, sum_1 = fold_stages(mail, place, p_1, scratch[1 : 1 + N_FOLD])
    rest = scratch[1 + N_FOLD :]
    f_in, sum_in = fold_stages(mail, place, p_in, rest[:N_FOLD])
    f_o0, sum_o0 = fold_stages(mail, place, p_o0, rest[N_FOLD : 2 * N_FOLD])
    f_o1, sum_o1 = fold_stages(mail, place, p_o1, rest[2 * N_FOLD : 3 * N_FOLD])
    rest = rest[3 * N_FOLD :]
    l_1 = line_stages(mail, place, sum_1, rest[0], o_1)
    l_in = line_stages(mail, place, sum_in, rest[1], o_in)
    l_o0 = line_stages(mail, place, sum_o0, rest[2], o_o0)
    l_o1 = line_stages(mail, place, sum_o1, rest[3], o_o1)
    e = pair_sum_stages(mail, place, p_enc, rest[4:], o_enc)
    f_w = [functools.partial(run, three) for three in zip(f_in, f_o0, f_o1)]
    l_w = [functools.partial(run, three) for three in zip(l_in, l_o0, l_o1)]
    f_1[0]()
    l_2[0]()
    e[0]()
    blocks, step, pairs = attend_units(rows, width)
    total = blocks * pairs
    t = lambda x: (x * total) // 12
    hooks = {}
    more = len(f_1) - 5
    at_units(hooks, f_1[1:], [t(1), t(4), t(5), t(6)] + [t(6)] * more)
    at_units(hooks, f_w, [t(1), t(3), t(8), t(9), t(11)] + [t(11)] * more)
    at_units(hooks, e[1:-1], [t(2)] * 2 + [t(4)] * (len(e) - 4))
    at_units(hooks, l_2[1:] + l_1[:1] + l_w[:1], [t(4), t(6), t(11)])
    at_units(hooks, l_1[1:] + e[-1:] + l_w[1:], [total] * 3)

    def unit(i):
        @pl.when(i % blocks == 0)
        def _():
            dk_acc[...] = jnp.zeros_like(dk_acc)
            dv_acc[...] = jnp.zeros_like(dv_acc)

        pair = i // blocks
        attend_back_unit(q, k, v, bias, do, o, lse, dq, dk_acc, dv_acc, (i % blocks) * step, step, pair)

        @pl.when(i % blocks == blocks - 1)
        def _():
            cols = pl.ds(pl.multiple_of(pair * PAIR, PAIR), PAIR)
            dk[:, cols] = dk_acc[...].astype(BF16)
            dv[:, cols] = dv_acc[...].astype(BF16)

    last = hooks.pop(total)
    hooked(total, unit, hooks)
    sums[...] = sums_in[...]
    sums[pl.ds(0, 1)] = row_sum(dq[...].astype(F32))
    sums[pl.ds(1, 1)] = row_sum(dv[...].astype(F32))
    run(last)
    mail.finish()


def closing_kernel(shape, p_qkv, p_small, p_tok, o_qkv, o_small, o_tok, *scratch):
    sems, scratch = scratch[:3], scratch[3:]
    place, mail = open_kernel(shape, True, False, sems)
    f_q, sum_q = fold_stages(mail, place, p_qkv, scratch[:N_FOLD])
    f_s, sum_s = fold_stages(mail, place, p_small, scratch[N_FOLD : 2 * N_FOLD])
    rest = scratch[2 * N_FOLD :]
    l_q = line_stages(mail, place, sum_q, rest[0], o_qkv)
    l_s = line_stages(mail, place, sum_s, rest[1], o_small)
    t = pair_sum_stages(mail, place, p_tok, rest[2:], o_tok)
    a = [functools.partial(run, two) for two in zip(f_q, f_s)]
    b = [functools.partial(run, two) for two in zip(l_q, l_s)]
    a[0]()
    t[0]()
    tracks = [a[1:], t[1:]]
    for k in range(max(len(x) for x in tracks)):
        for x in tracks:
            if k < len(x) and x[k] is not t[-1]:
                x[k]()
    run(b)
    t[-1]()
    mail.finish()


def body(
    tokens, encoded, cotangent, parent, assignment, attn_in, attn_out, ffn_in, ffn_out, shifts, gains, ffn_bias
):
    shape = Shape(lax.axis_size("leaf"), lax.axis_size("path"))
    leafs, paths = shape.leafs, shape.paths
    devices = leafs * paths
    scale = HEAD ** (-0.5)
    tokens, encoded, cotangent = tokens[0], encoded[0], cotangent[0]
    rows, width = tokens.shape
    enc_rows = encoded.shape[0]
    hidden_width = ffn_in.shape[1]
    tree_rows, tree_enc = rows * paths, enc_rows * paths
    piece = shifts.shape[1]
    n_shift, n_gain, n_bias = shifts.shape[0], gains.shape[0], ffn_bias.shape[0]
    n_vec = n_shift + n_gain
    ffn_in, ffn_out = ffn_in[None], ffn_out[None]

    def sds(shape_, dtype=BF16):
        return jax.ShapeDtypeStruct(shape_, dtype)

    small = jnp.concatenate([shifts.reshape(-1), gains.reshape(-1), ffn_bias])
    small_rows = -(-small.shape[0] // 4096) * 16
    small = jnp.pad(small, (0, small_rows * 256 - small.shape[0])).reshape(1, small_rows, 256)
    blocks = parent.shape[1]
    ids = jnp.arange(blocks, dtype=jnp.int32)
    lanes = jnp.arange(128, dtype=jnp.int32)
    links = jnp.concatenate(
        [
            (parent[0][:, None] == lanes[None, :]) & (ids[:, None] != lanes[None, :]),
            assignment[0][:, None] == lanes[None, :],
        ]
    ).astype(F32)

    three = 3
    all_tok, g_small, w_qkv, bias = kernel_call(
        functools.partial(opening_kernel, shape, blocks.bit_length()),
        "opening",
        0,
        [tokens, small, attn_in, links],
        [ANY, ANY, ANY, VMEM],
        [
            sds((paths, rows, width)),
            sds((1, leafs, paths) + small.shape[1:]),
            sds((three, leafs, paths) + attn_in.shape[1:]),
            sds((rows, tree_rows)),
        ],
        [ANY, ANY, ANY, VMEM],
        mail_scratch()
        + [pltpu.VMEM(links.shape, F32), pltpu.VMEM((128, 128), F32), pltpu.VMEM((128, 128), F32)],
    )
    flat = g_small.reshape(devices, -1)
    vec = flat[:, : n_vec * piece].reshape(devices, n_vec, piece).transpose(1, 0, 2)
    vec = jnp.pad(vec.reshape(n_vec, width).astype(F32), ((0, -n_vec % 8), (0, 0)))
    b1 = flat[:, n_vec * piece : n_vec * piece + n_bias].reshape(1, hidden_width).astype(F32)
    w_qkv = w_qkv.reshape(three, width, width)

    rest_in = attn_in.shape[0] - three
    q, k, v, attended, self_mass, all_enc, w_in, w_out, w1, z_2 = kernel_call(
        functools.partial(self_kernel, shape),
        "self_attention",
        1,
        [all_tok, w_qkv, vec, bias, encoded, attn_in, attn_out, ffn_in, ffn_out],
        [VMEM] * 4 + [ANY] * 5,
        [
            sds((rows, width)),
            sds((tree_rows, width)),
            sds((tree_rows, width)),
            sds((rows, width)),
            sds((rows, width), F32),
            sds((paths, enc_rows, width)),
            sds((rest_in, leafs, paths) + attn_in.shape[1:]),
            sds((attn_out.shape[0], leafs, paths) + attn_out.shape[1:]),
            sds((1, leafs, paths) + ffn_in.shape[1:]),
            sds((1, paths) + ffn_out.shape[1:]),
        ],
        [VMEM] * 5 + [ANY] * 5,
        mail_scratch(),
    )
    w_in = w_in.reshape(rest_in, width, width)
    w_out = w_out.reshape(attn_out.shape[0], width, width)

    p = lax.axis_index("path")
    upper = p >= shape.half
    primary = (lax.axis_index("leaf") % 2 == 1) == upper
    block = jnp.where(primary, p, paths - 1 - p)
    my_tokens = lax.dynamic_index_in_dim(all_tok, block, 0, False)
    hat1, inv1, first_low, cq, ck, cv, crossed, cross_mass, w2, my_cot = kernel_call(
        functools.partial(cross_kernel, shape, n_shift),
        "cross_attention",
        2,
        [attended, all_tok, all_enc, w_in, w_out, vec, z_2, cotangent],
        [VMEM, ANY] + [VMEM] * 4 + [ANY] * 2,
        [
            sds((rows, width), F32),
            sds((rows, 128), F32),
            sds((rows, width)),
            sds((rows, width)),
            sds((tree_enc, width)),
            sds((tree_enc, width)),
            sds((rows, width)),
            sds((rows, width), F32),
            sds((1, leafs, paths) + ffn_out.shape[1:]),
            sds((rows, width)),
        ],
        [VMEM] * 8 + [ANY] * 2,
        [pltpu.VMEM((rows, width), BF16)] + mail_scratch(),
    )
    w1 = w1.reshape(width, hidden_width)
    w2 = w2.reshape(hidden_width, width)
    vm = lambda s, dtype=BF16: pltpu.VMEM(s, dtype)
    output, g_w1, g_w2, g_wo1, g_crossed, g_pre2, sums, g_b1 = kernel_call(
        functools.partial(ffn_kernel, n_shift),
        "feed_forward",
        None,
        [hat1, crossed, w_out, w1, w2, vec, b1, my_cot],
        [VMEM] * 8,
        [
            sds((rows, width)),
            sds((width, hidden_width)),
            sds((hidden_width, width)),
            sds((width, width)),
            sds((rows, width)),
            sds((rows, width), F32),
            sds(vec.shape, F32),
            sds((1, hidden_width), F32),
        ],
        [VMEM] * 8,
        [
            vm((rows, width), F32),
            vm((rows, 128), F32),
            vm((rows, width)),
            vm((rows, width), F32),
            vm((rows, hidden_width), F32),
            vm((rows, hidden_width)),
            vm((rows, width), F32),
            vm((rows, width)),
            vm((rows, width), F32),
            vm((rows, width)),
        ],
    )

    def spread(g):
        return g.reshape(
            g.shape[0], shape.A, shape.B, 2, paths, g.shape[1] // devices, g.shape[2]
        )

    r1, r2 = ffn_in.shape[1:], ffn_out.shape[1:]
    g_rest, g_wo0, g_enc, g_att, g_pre1, sums, s_2, output = kernel_call(
        functools.partial(cross_back_kernel, shape, n_shift),
        "cross_back",
        3,
        [
            cq, ck, cv, g_crossed, crossed, cross_mass, first_low, hat1, inv1, all_enc, w_in, w_out, attended,
            g_pre2, vec, sums, spread(g_w2[None]), output,
        ],
        [VMEM] * 16 + [ANY] * 2,
        [
            sds((rest_in, width, width)),
            sds((width, width)),
            sds((paths, enc_rows, width)),
            sds((rows, width)),
            sds((rows, width), F32),
            sds(vec.shape, F32),
            sds((1, paths) + r2),
            sds((rows, width)),
        ],
        [VMEM] * 7 + [ANY],
        [vm((rows, width)), vm((tree_enc, width)), vm((tree_enc, width)), vm((rows, width))]
        + [pltpu.VMEM((tree_enc, PAIR), F32)] * 2
        + mail_scratch()
        + fold_scratch(shape, 1, *r2, BF16),
    )
    ri = attn_in.shape[1:]
    g_q, g_k, g_v, o_w1, o_w2, o_in, o_o0, o_o1, o_enc, sums = kernel_call(
        functools.partial(self_back_kernel, shape),
        "self_back",
        4,
        [
            q, k, v, bias, g_att, attended, self_mass, s_2, sums, spread(g_w1[None]), spread(g_rest),
            spread(g_wo0[None]), spread(g_wo1[None]), g_enc,
        ],
        [VMEM] * 9 + [ANY] * 4 + [VMEM],
        [
            sds((rows, width)),
            sds((tree_rows, width)),
            sds((tree_rows, width)),
            sds((1,) + r1, F32),
            sds((1,) + r2, F32),
            sds((rest_in,) + ri, F32),
            sds((1,) + ri, F32),
            sds((1,) + ri, F32),
            sds((enc_rows, width), F32),
            sds(vec.shape, F32),
        ],
        [VMEM] * 10,
        [pltpu.VMEM((tree_rows, PAIR), F32)] * 2
        + mail_scratch()
        + line_scratch(shape, 1, *r2, BF16)
        + fold_scratch(shape, 1, *r1, BF16)
        + fold_scratch(shape, rest_in, *ri, BF16)
        + fold_scratch(shape, 1, *ri, BF16)
        + fold_scratch(shape, 1, *ri, BF16)
        + line_scratch(shape, 1, *r1, BF16)
        + line_scratch(shape, rest_in, *ri, BF16)
        + line_scratch(shape, 1, *ri, BF16)
        + line_scratch(shape, 1, *ri, BF16)
        + pair_sum_scratch(shape, enc_rows, width),
    )
    flat_tok = all_tok.reshape(tree_rows, width)
    g_in0 = t_mm(my_tokens, g_q).astype(BF16)
    g_in1 = t_mm(flat_tok, g_k).astype(BF16)
    g_in2 = t_mm(flat_tok, g_v).astype(BF16)
    g_tok = (mm_t(g_k, w_qkv[1]) + mm_t(g_v, w_qkv[2])).reshape(paths, rows, width)
    g_own = g_pre1 + mm_t(g_q, w_qkv[0])
    mine = (jnp.arange(paths) == block)[:, None, None]
    g_tok = jnp.where(mine, g_tok + g_own[None], g_tok).astype(BF16)

    g_vec = sums[:n_vec]
    g_small = jnp.concatenate(
        [
            g_vec.reshape(n_vec, devices, piece).transpose(1, 0, 2).reshape(devices, -1),
            g_b1.reshape(devices, n_bias),
        ],
        axis=1,
    )
    small_count = g_small.shape[1]
    g_small_rows = -(-small_count // 2048) * 8
    g_small = jnp.pad(g_small, ((0, 0), (0, g_small_rows * 256 - small_count)))
    p_small = g_small.reshape(1, shape.A, shape.B, 2, paths, g_small_rows, 256)
    p_qkv = spread(jnp.stack([g_in0, g_in1, g_in2]))
    o_qkv, o_small, o_tok = kernel_call(
        functools.partial(closing_kernel, shape),
        "closing",
        5,
        [p_qkv, p_small, g_tok],
        [ANY, ANY, VMEM],
        [
            sds((three,) + ri, F32),
            sds((1, g_small_rows, 256), F32),
            sds((rows, width), F32),
        ],
        [VMEM] * 3,
        mail_scratch()
        + fold_scratch(shape, three, *ri, BF16)
        + fold_scratch(shape, 1, g_small_rows, 256, F32)
        + line_scratch(shape, three, *ri, BF16)
        + line_scratch(shape, 1, g_small_rows, 256, F32)
        + pair_sum_scratch(shape, rows, width),
    )
    o_small = o_small.reshape(-1)
    o_vec = o_small[: n_vec * piece].reshape(n_vec, piece)
    return (
        output[None],
        o_tok[None],
        o_enc[None],
        jnp.concatenate([o_qkv, o_in]),
        jnp.concatenate([o_o0, o_o1]),
        o_w1[0],
        o_w2[0],
        o_vec[:n_shift],
        o_vec[n_shift:],
        o_small[n_vec * piece : n_vec * piece + n_bias],
    )


def solution(mesh):
    both = ("leaf", "path")
    rows = P("leaf", "path", None)
    weights = (P(None, both, None), P(None, both, None), P(both, None), P(both, None), P(None, both), P(None, both), P(both))
    return jax.shard_map(
        body,
        mesh=mesh,
        in_specs=(rows, rows, rows, P("leaf", None), P("leaf", None)) + weights,
        out_specs=(rows, rows, rows) + weights,
        check_vma=False,
    )
```

```python
import functools

import jax
import jax.numpy as jnp
from jax import lax
from jax.experimental import pallas as pl
from jax.experimental.pallas import tpu as pltpu
from jax.sharding import PartitionSpec as P

HEAD = 64
BLK = 128
PAIR = 2 * HEAD
MESH = pl.DeviceIdType.MESH
F32 = jnp.float32
BF16 = jnp.bfloat16
VMEM_OF = {"opening": 8}
ANY = pl.BlockSpec(memory_space=pl.ANY)
VMEM = pl.BlockSpec(memory_space=pltpu.VMEM)


class Shape:
    def __init__(self, leafs, paths):
        self.leafs, self.paths, self.half = leafs, paths, paths // 2
        outer = leafs // 2
        self.A = 2 if outer % 2 == 0 else 1
        self.B = outer // self.A


class Place:
    def __init__(self, shape):
        self.shape = shape
        self.leafs, self.paths, self.half = shape.leafs, shape.paths, shape.half
        self.A, self.B = shape.A, shape.B
        leaf = lax.axis_index("leaf")
        self.leaf, self.p = leaf, lax.axis_index("path")
        self.c = leaf % 2
        self.a = (leaf // 2) // self.B
        self.b = (leaf // 2) % self.B
        n = self.paths
        self.tree = jnp.where(self.p >= self.half, 1, 0)
        self.primary = self.c == self.tree
        self.pm = jnp.where(self.tree == 0, self.p, n - 1 - self.p)
        self.inward = jnp.where(self.tree == 0, 1, -1)
        self.own_rank = jnp.where(self.c == 0, self.p, n - 1 - self.p)
        self.block = jnp.where(self.primary, self.p, n - 1 - self.p)

    def leaf_at(self, a, b, c):
        return (a * self.B + b) * 2 + c

    def at_core(self):
        return (self.leaf_at(self.a, self.b, 1 - self.c), self.p)

    def at_a(self, a):
        return (self.leaf_at(a, self.b, self.c), self.p)

    def at_b(self, b):
        return (self.leaf_at(self.a, b, self.c), self.p)

    def at_p(self, p):
        return (self.leaf, clamp(p, self.paths))

    def at_mirror(self):
        return (self.leaf_at(self.a, self.b, 1 - self.c), self.paths - 1 - self.p)

    def shard_of_rank(self, rank):
        return jnp.where(self.tree == 0, rank, self.paths - 1 - rank)

    def line_p(self):
        return (self.paths, self.p, self.at_p)

    def line_a(self):
        return (self.A, self.a, self.at_a)

    def line_b(self):
        return (self.B, self.b, self.at_b)


def clamp(index, size):
    return jnp.clip(index, 0, size - 1)


def guarded(when, action):
    if when is None:
        action()
    else:

        @pl.when(when)
        def _():
            action()


def run(actions):
    for action in actions:
        action()


def greet(place, column, mirror):
    barrier = pltpu.get_barrier_semaphore()
    peers = 1

    def signal(to):
        pl.semaphore_signal(barrier, inc=1, device_id=to, device_id_type=MESH)

    signal(place.at_core())
    if column:
        for k in range(1, place.paths):
            for core in range(2):
                there = (place.p + k) % place.paths
                signal((place.leaf_at(place.a, place.b, core), there))
        peers = peers + 2 * (place.paths - 1)
    for size, pos, to in (place.line_a(), place.line_b()):
        if size == 1:
            continue
        if size == 2:
            signal(to(1 - pos))
            peers = peers + 1
            continue
        for step in (-1, 1):
            there = pos + step
            inside = (there >= 0) & (there < size)

            @pl.when(inside)
            def _():
                signal(to(clamp(there, size)))

            peers = peers + jnp.where(inside, 1, 0)
    if mirror and not column:

        @pl.when(jnp.logical_not(place.primary))
        def _():
            signal(place.at_mirror())

        peers = peers + jnp.where(place.primary, 0, 1)
    pl.semaphore_wait(barrier, peers)


class Mail:
    def __init__(self, send_sems, recv_sems, own_sems):
        self.send_sems, self.recv_sems, self.own_sems = send_sems, recv_sems, own_sems
        self.sends = self.recvs = self.owns = 0
        self.sent = []

    def new_recv(self, count=1):
        self.recvs += count
        return self.recvs - count

    def send(self, when, src, dst, to, recv):
        k = self.sends
        self.sends += 1
        copy = pltpu.make_async_remote_copy(
            src_ref=src,
            dst_ref=dst,
            send_sem=self.send_sems.at[k],
            recv_sem=self.recv_sems.at[recv],
            device_id=to,
            device_id_type=MESH,
        )
        self.sent.append((when, copy))
        return functools.partial(guarded, when, copy.start)

    def hear(self, when, landing, to, recv):
        copy = pltpu.make_async_remote_copy(
            src_ref=landing,
            dst_ref=landing,
            send_sem=self.send_sems.at[0],
            recv_sem=self.recv_sems.at[recv],
            device_id=to,
            device_id_type=MESH,
        )
        return functools.partial(guarded, when, copy.wait_recv)

    def post(self, when, src, dst, to, hear_when, landing):
        k = self.new_recv()
        return self.send(when, src, dst, to, k), self.hear(hear_when, landing, to, k)

    def local(self, when, src, dst):
        k = self.owns
        self.owns += 1
        copy = pltpu.make_async_copy(src, dst, self.own_sems.at[k])
        return functools.partial(guarded, when, copy.start), functools.partial(guarded, when, copy.wait)

    def finish(self):
        for when, copy in self.sent:
            guarded(when, copy.wait_send)


def mail_scratch(count=160, own=24):
    return [
        pltpu.SemaphoreType.DMA((count,)),
        pltpu.SemaphoreType.DMA((count,)),
        pltpu.SemaphoreType.DMA((own,)),
    ]


def flood(mail, line, views, first=None):
    size, pos, to = line
    steps = []
    if size == 1:
        return steps
    first = first if first is not None else views(pos)
    if size == 2:
        jobs = [
            mail.post(None, s, d, to(1 - pos), None, w)
            for s, d, w in zip(first, views(pos), views(1 - pos))
        ]
        return [([j[0] for j in jobs], [j[1] for j in jobs])]
    for step in range(1, size):
        starts, waits = [], []
        for sign in (1, -1):
            item = pos - sign * (step - 1)
            there = pos + sign
            when = (there >= 0) & (there < size) & (item >= 0) & (item < size)
            heard = pos - sign * step
            hear_when = (heard >= 0) & (heard < size)
            item_c = clamp(item, size)
            sources = first if step == 1 else views(item_c)
            for s, d, w in zip(sources, views(item_c), views(clamp(heard, size))):
                start, wait = mail.post(when, s, d, to(clamp(there, size)), hear_when, w)
                starts.append(start)
                waits.append(wait)
        steps.append((starts, waits))
    return steps


def chain(steps, first_starts=()):
    stages, pending = [], []
    for k, (starts, waits) in enumerate(steps):
        stages.append(functools.partial(run, pending + (list(first_starts) if k == 0 else []) + starts))
        pending = waits
    stages.append(functools.partial(run, pending))
    return stages


def half_columns(ref, leaf, h):
    width = ref.shape[-1] // 2
    return ref.at[:, leaf, :, :, pl.ds(h * width, width)]


def block_stages(mail, place, shards, block_views):
    n = place.paths
    own = [mail.local(None, s, d) for s, d in zip(shards, block_views(place.p))]
    starts, waits = [o[0] for o in own], [o[1] for o in own]
    lands = [mail.new_recv(n) for _ in shards]
    for k in range(1, n):
        there = (place.p + k) % n
        for s, d, w, land in zip(shards, block_views(place.p), block_views(there), lands):
            starts.append(mail.send(None, s, d, place.at_p(there), land + place.p))
            waits.append(mail.hear(None, w, place.at_p(there), land + there))
    return [functools.partial(run, starts), functools.partial(run, waits)]


def path_half(ref, h):
    n = ref.shape[1] // 2
    return ref.at[:, pl.ds(h * n, n)]


def spread_stages(mail, place, wholes, blocks=None):
    if (place.A, place.B) != (2, 2):
        return spread_lines(mail, place, wholes, blocks)
    a, b, c = place.a, place.b, place.c
    at = lambda w, a, b, c: w.at[:, place.leaf_at(a, b, c)]
    to_a, to_b, to_core = place.at_a(1 - a), place.at_b(1 - b), place.at_core()
    own = []
    sources = [at(w, a, b, c) for w in wholes]
    if blocks is not None:
        own = [mail.local(None, x, s) for x, s in zip(blocks, sources)]
        sources = list(blocks)
    urgent, calm, relay, near, far = [], [], [], [], []
    for w, s in zip(wholes, sources):
        mine, from_a, from_b = at(w, a, b, c), at(w, 1 - a, b, c), at(w, a, 1 - b, c)
        from_ab = at(w, 1 - a, 1 - b, c)

        def post(src, dst, to, landing, h):
            return mail.post(
                None, path_half(src, h), path_half(dst, h), to, None, path_half(landing, h)
            )

        urgent += [post(s, mine, to_b, from_b, 0), post(s, mine, to_a, from_a, 1)]
        calm += [post(s, mine, to_b, from_b, 1), post(s, mine, to_a, from_a, 0)]
        relay += [post(from_b, from_b, to_a, from_ab, 0), post(from_a, from_a, to_b, from_ab, 1)]
        near.append(mail.post(None, s, mine, to_core, None, at(w, a, b, 1 - c)))
        for x, y, l in ((1 - a, b, near), (a, 1 - b, near), (1 - a, 1 - b, far)):
            l.append(mail.post(None, at(w, x, y, c), at(w, x, y, c), to_core, None, at(w, x, y, 1 - c)))
    start = lambda jobs: run([j[0] for j in jobs])
    wait = lambda jobs: run([j[1] for j in jobs])
    first = near[::3]
    second = [j for k, j in enumerate(near) if k % 3]

    def opening():
        start(urgent)
        start(calm)
        start(first)
        run([o[0] for o in own])

    def passing():
        wait(urgent)
        start(relay)

    def sharing():
        wait(calm)
        run([o[1] for o in own])
        start(second)

    def ending():
        wait(relay)
        start(far)

    return [opening, passing, sharing, ending, lambda: wait(near + far)]


def spread_lines(mail, place, wholes, blocks=None):
    A, B, c = place.A, place.B, place.c

    def of_b(h, across_a):
        ays = range(A) if across_a else [place.a]
        return lambda i: [half_columns(w, place.leaf_at(a, i, c), h) for a in ays for w in wholes]

    def of_a(h, across_b):
        bees = range(B) if across_b else [place.b]
        return lambda i: [half_columns(w, place.leaf_at(i, b, c), h) for b in bees for w in wholes]

    own = []
    firsts = [None, None]
    sources = [w.at[:, place.leaf] for w in wholes]
    if blocks is not None:
        own = [mail.local(None, x, w.at[:, place.leaf]) for x, w in zip(blocks, wholes)]
        firsts = [
            [x.at[:, :, :, pl.ds(h * (x.shape[-1] // 2), x.shape[-1] // 2)] for x in blocks]
            for h in range(2)
        ]
        sources = list(blocks)
    line_a, line_b = place.line_a(), place.line_b()
    phases = [
        (flood(mail, line_b, of_b(0, False), firsts[0]), flood(mail, line_a, of_a(1, False), firsts[1])),
        (flood(mail, line_a, of_a(0, True)), flood(mail, line_b, of_b(1, True))),
    ]
    core = [
        mail.post(
            None,
            s,
            w.at[:, place.leaf],
            place.at_core(),
            None,
            w.at[:, place.leaf_at(place.a, place.b, 1 - c)],
        )
        for s, w in zip(sources, wholes)
    ]
    rest = []
    for offset in range(1, A * B):
        spot = (place.a * B + place.b + offset) % (A * B)
        for w in wholes:
            mine, other = w.at[:, spot * 2 + c], w.at[:, spot * 2 + 1 - c]
            rest.append(mail.post(None, mine, mine, place.at_core(), None, other))
    steps = []
    opening = [o[0] for o in own] + [j[0] for j in core]
    for n_phase, phase in enumerate(phases):
        before = [o[1] for o in own] if n_phase == 1 else []
        for s in range(max(len(f) for f in phase)):
            starts, waits = list(before), []
            before = []
            for f in phase:
                if s < len(f):
                    starts += f[s][0]
                    waits += f[s][1]
            steps.append((starts + opening, waits))
            opening = []
    steps.append((opening + [j[0] for j in rest], [j[1] for j in core + rest]))
    return chain(steps)


def pair_gather_stages(mail, place, shard, whole, pieces=1):
    n, h = place.paths, place.half
    rows = shard.shape[0] // (2 * pieces)
    part = lambda ref, u, s: ref.at[pl.ds(pl.multiple_of((u * pieces + s) * rows, rows), rows)]
    half = lambda ref, u: ref.at[pl.ds(pl.multiple_of(u * pieces * rows, rows), pieces * rows)]
    lands = [mail.new_recv(n) for _ in range(pieces)]
    core_lands = mail.new_recv(n)
    own = mail.local(place.primary, shard, whole.at[place.p])
    first = jnp.where(place.c == 0, 0, h)
    edge = jnp.where(place.c == 0, h - 1, h)
    starts = []
    for s in range(pieces):
        for u in range(2):
            for q in range(h):
                q = first + q
                to = (place.leaf_at(place.a, place.b, u), q)
                near = place.primary & jnp.logical_not((q == place.p) & (place.c == u))
                away = near | (jnp.logical_not(place.primary) & (q == edge))
                starts.append(
                    mail.send(
                        away, part(shard, u, s), part(whole.at[place.p], u, s), to, lands[s] + place.p
                    )
                )
    k = mail.new_recv()
    mate = whole.at[place.p]
    starts.append(
        mail.send(place.primary, half(shard, place.c), half(mate, place.c), place.at_core(), k)
    )
    starts.append(own[0])
    stages = [functools.partial(run, starts)]
    outward = place.at_p(place.p - place.inward)
    for s in range(pieces):
        for r in list(range(h, n)) + list(range(h)):
            j = place.shard_of_rank(r)
            item = part(whole.at[j], place.c, s)
            got = jnp.logical_not(place.primary & (place.p == j))
            actions = [mail.hear(got, item, place.at_core(), lands[s] + j)]
            if r >= h and h > 1:
                actions.append(mail.send(place.pm > 0, item, item, outward, lands[s] + j))
            if s == pieces - 1:
                whole_half = half(whole.at[j], place.c)
                actions.append(
                    mail.send(
                        jnp.logical_not(place.p == j),
                        whole_half,
                        whole_half,
                        place.at_core(),
                        core_lands + j,
                    )
                )
            stages.append(functools.partial(run, actions))
    rest = [own[1]]
    rest.append(
        mail.hear(jnp.logical_not(place.primary), half(mate, 1 - place.c), place.at_core(), k)
    )
    for r in range(n):
        j = place.shard_of_rank(r)
        rest.append(
            mail.hear(
                jnp.logical_not(place.p == j),
                half(whole.at[j], 1 - place.c),
                place.at_core(),
                core_lands + j,
            )
        )
    stages.append(functools.partial(run, rest))
    return stages


def mirror_stages(mail, place, own, mine):
    local = mail.local(place.primary, own, mine)
    other = jnp.logical_not(place.primary)
    start, wait = mail.post(other, own, mine, place.at_mirror(), other, mine)
    return [lambda: run([local[0], start]), lambda: run([local[1], wait])]


def add_rows(dst, src):
    lead = dst.shape[:-2]
    total = 1
    for extent in lead:
        total *= extent

    def body(i, _):
        index = []
        rest = i
        for extent in reversed(lead):
            index.insert(0, rest % extent)
            rest = rest // extent
        index = tuple(index)
        dst[index] = dst[index] + src[index]
        return 0

    if total == 1:
        body(0, 0)
    else:
        lax.fori_loop(0, total, body, 0)


def add_tall(dst, src):
    rows = dst.shape[0]
    step = 64 if rows % 64 == 0 else rows

    def body(r, _):
        at = pl.ds(pl.multiple_of(r * step, step), step)
        dst[at] = dst[at] + src[at]
        return 0

    lax.fori_loop(0, rows // step, body, 0)


def shift_sum(mail, line, mine, slots_up, slots_down, add):
    size, pos, to = line
    if size == 1:
        return []
    if size == 2:
        jobs = [
            mail.post(None, s, slot, to(1 - pos), None, slot)
            for s, slot in zip(mine(1 - pos), slots_up[0])
        ]

        def end():
            for job, dst, slot in zip(jobs, mine(pos), slots_up[0]):
                job[1]()
                add(dst, slot)

        return [lambda: run([j[0] for j in jobs]), end]
    stages = []
    for k in range(size - 1):
        early, actions = [], []
        for sign, slots in ((1, slots_up), (-1, slots_down)):
            dest = size - 1 - k if sign == 1 else k
            when = (pos < dest) if sign == 1 else (pos > dest)
            hear_when = (
                ((pos > 0) & (pos <= dest)) if sign == 1 else ((pos < size - 1) & (pos >= dest))
            )
            there = clamp(pos + sign, size)
            jobs = [
                mail.post(when, s, slot, to(there), None, slot)
                for s, slot in zip(mine(dest), slots[k])
            ]

            def take(jobs=jobs, dst_refs=mine(dest), slot_refs=slots[k]):
                for job, dst, slot in zip(jobs, dst_refs, slot_refs):
                    job[1]()
                    add(dst, slot)

            end = (pos == 0) if sign == 1 else (pos == size - 1)
            starts = functools.partial(run, [job[0] for job in jobs])
            early.append(functools.partial(guarded, end, starts))
            actions.append(functools.partial(guarded, hear_when, take))
            actions.append(functools.partial(guarded, jnp.logical_not(end), starts))
        stages.append(functools.partial(run, early + actions))
    return stages


def fold_scratch(shape, k, R, C, dtype):
    if (shape.A, shape.B) != (2, 2):
        return fold_lines_scratch(shape, k, R, C, dtype)
    block = (k, 2, 2, shape.paths, R, C)
    halves = (2, k, shape.paths // 2, R, C)
    return [pltpu.VMEM(block, dtype)] * 2 + [pltpu.VMEM(halves, dtype)] * 3 + [pltpu.VMEM((1, R, C), dtype)]


def fold_lines_scratch(shape, k, R, C, dtype):
    A, B, paths = shape.A, shape.B, shape.paths
    nb, na = max(B - 1, 1) * (2 if B > 2 else 1), max(A - 1, 1)
    return [
        pltpu.VMEM((k, A, B, paths, R, C), dtype),
        pltpu.VMEM((k, A, B, paths, R, C), dtype),
        pltpu.VMEM((nb, k, A, paths, R, C // 2), dtype),
        pltpu.VMEM((na, k, paths, R, C // 2), dtype),
        pltpu.VMEM((na, k, B, paths, R, C // 2), dtype),
        pltpu.VMEM((nb, k, paths, R, C // 2), dtype),
    ]


N_FOLD = 6


def up_down(ref, size):
    if size <= 2:
        return [[ref.at[0]]], None
    return (
        [[ref.at[k]] for k in range(size - 1)],
        [[ref.at[size - 1 + k]] for k in range(size - 1)],
    )


def fold_stages(mail, place, partial, scratch):
    if (place.A, place.B) != (2, 2):
        return fold_lines(mail, place, partial, scratch)
    a, b, c = place.a, place.b, place.c
    acc, got, far, direct, relayed = scratch[:5]
    own = mail.local(None, partial.at[:, :, :, c], acc)
    core = mail.post(None, partial.at[:, :, :, 1 - c], got, place.at_core(), None, got)
    to_a, to_b = place.at_a(1 - a), place.at_b(1 - b)
    of_a, of_b, of_ab = acc.at[:, 1 - a, b], acc.at[:, a, 1 - b], acc.at[:, 1 - a, 1 - b]
    mine = acc.at[:, a, b]

    def post(src, h, slot, to):
        return mail.post(None, path_half(src, h), slot, to, None, slot)

    urgent = [post(of_ab, 0, far.at[0], to_b), post(of_ab, 1, far.at[1], to_a)]
    calm = [post(of_b, 0, direct.at[0], to_b), post(of_a, 1, direct.at[1], to_a)]
    late = [post(of_a, 0, relayed.at[0], to_a), post(of_b, 1, relayed.at[1], to_b)]

    def join():
        own[1]()
        core[1]()
        add_rows(of_ab, got.at[:, 1 - a, 1 - b])
        run([j[0] for j in urgent])
        add_rows(of_b, got.at[:, a, 1 - b])
        calm[0][0]()
        add_rows(of_a, got.at[:, 1 - a, b])
        calm[1][0]()
        add_rows(mine, got.at[:, a, b])

    def passing():
        urgent[0][1]()
        add_rows(path_half(of_a, 0), far.at[0])
        late[0][0]()
        urgent[1][1]()
        add_rows(path_half(of_b, 1), far.at[1])
        late[1][0]()

    def taking():
        for h in range(2):
            calm[h][1]()
            add_rows(path_half(mine, h), direct.at[h])

    def ending():
        for h in range(2):
            late[h][1]()
            add_rows(path_half(mine, h), relayed.at[h])

    return [lambda: run([own[0], core[0]]), join, passing, taking, ending], mine


def fold_lines(mail, place, partial, scratch):
    c = place.c
    acc, got, sb0, sa0, sa1, sb1 = scratch
    own = mail.local(None, partial.at[:, :, :, c], acc)
    core = mail.post(None, partial.at[:, :, :, 1 - c], got, place.at_core(), None, got)
    width = acc.shape[-1] // 2
    left, right = pl.ds(0, width), pl.ds(width, width)

    def join():
        own[1]()
        core[1]()
        add_rows(acc, got)

    line_a, line_b = place.line_a(), place.line_b()
    h0_b = shift_sum(
        mail, line_b, lambda d: [acc.at[:, :, d, :, :, left]], *up_down(sb0, place.B), add_rows
    )
    h1_a = shift_sum(
        mail, line_a, lambda d: [acc.at[:, d, :, :, :, right]], *up_down(sa1, place.A), add_rows
    )
    h0_a = shift_sum(
        mail, line_a, lambda d: [acc.at[:, d, place.b, :, :, left]], *up_down(sa0, place.A), add_rows
    )
    h1_b = shift_sum(
        mail, line_b, lambda d: [acc.at[:, place.a, d, :, :, right]], *up_down(sb1, place.B), add_rows
    )

    def beside(one, two):
        return [
            functools.partial(run, [s[k] for s in (one, two) if k < len(s)])
            for k in range(max(len(one), len(two)))
        ]

    def joined(first, second):
        if not first or not second:
            return first + second
        return first[:-1] + [functools.partial(run, [first[-1], second[0]])] + second[1:]

    stages = joined(
        [lambda: run([own[0], core[0]]), join], beside(h0_b, h1_a)
    )
    stages = joined(stages, beside(h0_a, h1_b))
    return stages, acc.at[:, place.a, place.b]


def line_scratch(shape, k, R, C, dtype):
    return [pltpu.VMEM((max(shape.paths - 1, 1), k, R, C), dtype)]


def line_stages(mail, place, sums, slots, out):
    n = place.paths
    jobs = []
    for k in range(1, n):
        there = (place.p + k) % n
        slot = slots.at[k - 1]
        jobs.append(mail.post(None, sums.at[:, there], slot, place.at_p(there), None, slot))

    def end():
        run([j[1] for j in jobs])
        for j in range(out.shape[0]):
            total = sums[j, place.p].astype(F32)
            for k in range(n - 1):
                total = total + slots[k, j].astype(F32)
            out[j] = total.astype(out.dtype)

    return [lambda: run([j[0] for j in jobs]), end]


def pair_sum_scratch(shape, R, C):
    return [
        pltpu.VMEM((shape.paths, R // 2, C), BF16),
        pltpu.VMEM((shape.paths, R // 2, C), BF16),
        pltpu.VMEM((shape.half, R, C), BF16),
    ]


def pair_sum_stages(mail, place, part, scratch, out):
    n, h = place.paths, place.half
    core_slot, in_slot, landing = scratch
    rows = part.shape[1] // 2
    half = lambda ref, u: ref.at[pl.ds(pl.multiple_of(u * rows, rows), rows)]
    lands = [mail.new_recv(2) for _ in range(h)]
    inner = place.at_p(place.p + place.inward)
    sends, sums, passes = [], [], []
    for r in range(n - 1, -1, -1):
        j = place.shard_of_rank(r)
        item = part.at[j]
        mine = half(item, place.c)
        send, hear = mail.post(
            None, half(item, 1 - place.c), core_slot.at[r], place.at_core(), None, core_slot.at[r]
        )
        owner = (place.leaf_at(place.a, place.b, place.tree), j)
        leave = []
        if r >= h:
            k = mail.new_recv()
            slot = in_slot.at[r]
            in_send = mail.send(place.pm < h - 1, mine, slot, inner, k)
            in_hear = mail.hear(None, slot, place.at_core(), k)
            go = mail.send(
                place.pm == h - 1, mine, half(landing.at[h - 1], place.c), owner, lands[h - 1] + place.c
            )

            def inward(in_send=in_send, in_hear=in_hear, mine=mine, slot=slot, go=go):
                if h > 1:

                    @pl.when(place.pm > 0)
                    def _():
                        in_hear()
                        add_tall(mine, slot)

                    in_send()
                go()

            passes.append(inward)
        else:
            away = jnp.logical_not(place.primary & (place.p == j))
            for q in range(h):
                leave.append(
                    mail.send(
                        away & (place.pm == q),
                        mine,
                        half(landing.at[q], place.c),
                        owner,
                        lands[q] + place.c,
                    )
                )

        def settle(hear=hear, mine=mine, slot=core_slot.at[r], leave=leave):
            hear()
            add_tall(mine, slot)
            run(leave)

        sends.append(send)
        sums.append(settle)
    stages = [[sends[0]]]
    for k in range(1, n):
        stages.append([sends[k], sums[k - 1]])
    stages.append([sums[n - 1]])
    for k, step in enumerate(passes):
        stages[k + 1].append(step)

    def end():
        for q in range(h):
            for u in range(2):
                self_made = place.primary & (place.own_rank == q) & (place.c == u)
                comes = jnp.logical_not(self_made) & (place.primary | (q == h - 1))
                mail.hear(comes, half(landing.at[q], u), place.at_core(), lands[q] + u)()

        step = 64 if rows % 64 == 0 else rows
        for u in range(2):

            def body(i, _, u=u):
                at = pl.ds(pl.multiple_of(u * rows + i * step, step), step)

                @pl.when(place.primary)
                def _():
                    for q in range(h):
                        self_made = (place.own_rank == q) & (place.c == u)
                        term = jnp.where(self_made, part[place.p, at], landing[q, at]).astype(F32)
                        total = term if q == 0 else total + term
                    out[at] = total

                @pl.when(jnp.logical_not(place.primary))
                def _():
                    out[at] = landing[h - 1, at].astype(F32)

                return 0

            lax.fori_loop(0, rows // step, body, 0)

    return [functools.partial(run, x) for x in stages] + [end]


def at_units(hooks, stages, units):
    for stage, unit in zip(stages, units, strict=True):
        hooks.setdefault(unit, []).append(stage)


def hooked(count, unit, hooks):
    def body(i, _):
        for at, stages in hooks.items():
            if at < count:

                @pl.when(i == at)
                def _():
                    run(stages)

        unit(i)
        return 0

    lax.fori_loop(0, count, body, 0)
    for at in sorted(hooks):
        if at >= count:
            run(hooks[at])


def kernel_call(kernel, name, collective_id, ins, in_specs, outs, out_specs, scratch):
    return pl.pallas_call(
        kernel,
        out_shape=outs,
        in_specs=in_specs,
        out_specs=out_specs,
        scratch_shapes=scratch,
        compiler_params=pltpu.CompilerParams(
            collective_id=collective_id,
            has_side_effects=True,
            vmem_limit_bytes=VMEM_OF.get(name, 62) * 1024 * 1024,
        )
        if collective_id is not None
        else pltpu.CompilerParams(vmem_limit_bytes=62 * 1024 * 1024),
        name=name,
    )(*ins)


def dot(x, y, contract):
    return lax.dot_general(x, y, (contract, ((), ())), preferred_element_type=F32)


def mm(x, w):
    return dot(x, w, ((1,), (0,)))


def mm_t(x, w):
    return dot(x, w, ((1,), (1,)))


def t_mm(x, y):
    return dot(x, y, ((0,), (0,)))


def open_kernel(shape, column, mirror, sems):
    place = Place(shape)
    greet(place, column, mirror)
    return place, Mail(*sems)


def opening_kernel(shape, turns, tok, small, attn_in, links, all_tok, g_small, g_qkv, bias, *scratch):
    sems, (links_got, reach, spot) = scratch[:3], scratch[3:]
    place, mail = open_kernel(shape, True, False, sems)
    three = g_qkv.shape[0]
    to_core = mail.post(None, links, links_got, place.at_core(), None, links_got)
    to_core[0]()
    shards = [small, attn_in.at[pl.ds(0, three)]]
    wholes = [g_small, g_qkv]
    weights = block_stages(
        mail, place, shards, lambda i: [w.at[:, place.leaf, i] for w in wholes]
    )
    spread = spread_stages(mail, place, wholes)
    tokens = pair_gather_stages(mail, place, tok, all_tok)
    weights[0]()
    tokens[0]()
    to_core[1]()

    count = links.shape[0] // 2
    mine = jnp.where(place.primary, links[...], links_got[...])
    reach[...] = jnp.zeros_like(reach)
    spot[...] = jnp.zeros_like(spot)
    reach[pl.ds(0, count)] = mine[:count]
    spot[pl.ds(0, count)] = mine[count:]
    for _ in range(turns):
        r = reach[...]
        reach[...] = jnp.minimum(r + mm(r.astype(BF16), r.astype(BF16)), 1.0)
    placed = spot[...].astype(BF16)
    linked = mm_t(mm(placed, reach[...].astype(BF16)).astype(BF16), placed).astype(BF16)
    rows, keys = bias.shape
    step = min(128, rows)

    def fill(i, _):
        first = i * step
        at = pl.ds(pl.multiple_of(first, step), step)
        q_slot = (place.block * rows + first + lax.broadcasted_iota(jnp.int32, (step, 128), 0)) // BLK
        pick_q = (q_slot == lax.broadcasted_iota(jnp.int32, (step, 128), 1)).astype(F32)
        own = mm(pick_q.astype(BF16), linked).astype(BF16)
        k_slot = lax.broadcasted_iota(jnp.int32, (128, keys), 1) // BLK
        pick_k = (k_slot == lax.broadcasted_iota(jnp.int32, (128, keys), 0)).astype(F32)
        seen = mm(own, pick_k.astype(BF16))
        q_at = place.block * rows + first + lax.broadcasted_iota(jnp.int32, (step, keys), 0)
        k_at = lax.broadcasted_iota(jnp.int32, (step, keys), 1)
        inside = (q_at // BLK == k_at // BLK) & (k_at <= q_at)
        bias[at] = jnp.where((seen > 0.5) | inside, 0.0, -1e30).astype(bias.dtype)
        return 0

    run(weights[1:] + spread[:1])
    run(tokens[1:-3])
    spread[1]()
    lax.fori_loop(0, rows // step, fill, 0)
    run(tokens[-3:-1])
    run(spread[2:])
    tokens[-1]()
    mail.finish()


def attend_unit(q_ref, k_ref, v_ref, bias_ref, o_ref, lse_ref, row, step, pair):
    at = pl.ds(pl.multiple_of(row, step), step)
    cols = pl.ds(pl.multiple_of(pair * PAIR, PAIR), PAIR)
    lane = lax.broadcasted_iota(jnp.int32, (1, PAIR), 1)
    q = q_ref[at, cols]
    k = k_ref[:, cols]
    v = v_ref[:, cols]
    out = jnp.zeros((step, PAIR), F32)
    lse = jnp.zeros((step, PAIR), F32)
    for h in range(2):
        own = (lane >= HEAD) if h else (lane < HEAD)
        s = mm_t(jnp.where(own, q, jnp.zeros_like(q)), k)
        if bias_ref is not None:
            s = s + bias_ref[at].astype(F32)
        peak = jnp.max(s, axis=1, keepdims=True)
        e = jnp.exp(s - peak)
        mass = jnp.sum(e, axis=1, keepdims=True)
        o = mm(e.astype(BF16), v)
        out = jnp.where(own, o / mass, out)
        lse = jnp.where(own, peak + jnp.log(mass), lse)
    o_ref[at, cols] = out.astype(BF16)
    lse_ref[at, cols] = lse


def attend_back_unit(q_ref, k_ref, v_ref, bias_ref, do_ref, o_ref, lse_ref, dq_ref, dk_acc, dv_acc, row, step, pair):
    at = pl.ds(pl.multiple_of(row, step), step)
    cols = pl.ds(pl.multiple_of(pair * PAIR, PAIR), PAIR)
    lane = lax.broadcasted_iota(jnp.int32, (1, PAIR), 1)
    k = k_ref[:, cols]
    v = v_ref[:, cols]
    q = q_ref[at, cols]
    do = do_ref[at, cols]
    both = do.astype(F32) * o_ref[at, cols].astype(F32)
    lse_pair = lse_ref[at, cols]
    dq = jnp.zeros((step, PAIR), F32)
    for h in range(2):
        own = (lane >= HEAD) if h else (lane < HEAD)
        q_h = jnp.where(own, q, jnp.zeros_like(q))
        do_h = jnp.where(own, do, jnp.zeros_like(do))
        delta = jnp.sum(jnp.where(own, both, 0.0), axis=1, keepdims=True)
        lse = lse_pair[:, h * HEAD : h * HEAD + 1]
        s = mm_t(q_h, k)
        if bias_ref is not None:
            s = s + bias_ref[at].astype(F32)
        e = jnp.exp(s - lse)
        dp = mm_t(do_h, v)
        ds = (e * (dp - delta)).astype(BF16)
        dq = jnp.where(own, mm(ds, k), dq)
        dk_acc[...] += t_mm(ds, q_h)
        dv_acc[...] += t_mm(e.astype(BF16), do_h)
    dq_ref[at, cols] = dq.astype(BF16) * BF16(HEAD**-0.5)


def attend_units(rows, width):
    step = min(256, rows)
    return rows // step, step, width // PAIR


def self_kernel(
    shape, all_tok, w_qkv, vec, bias, enc, attn_in, attn_out, ffn_in,
    q, k, v, att, lse, all_enc, g_in, g_out, z_1, *sems,
):
    place, mail = open_kernel(shape, True, False, sems)
    n, rows, width = all_tok.shape
    three = g_in.shape[0]
    e = pair_gather_stages(mail, place, enc, all_enc)
    shards = [attn_in.at[pl.ds(attn_in.shape[0] - three, three)], attn_out]
    wholes = [g_in, g_out]
    w = block_stages(mail, place, shards, lambda i: [g.at[:, place.leaf, i] for g in wholes])
    w += spread_stages(mail, place, wholes)
    f = block_stages(mail, place, [ffn_in], lambda i: [z_1.at[:, i]])
    w[0]()
    scale = HEAD**-0.5
    q[...] = ((mm(all_tok[place.block], w_qkv[0]) + vec[pl.ds(0, 1)]) * scale).astype(BF16)

    def project(i):
        x = all_tok[i]
        at = pl.ds(pl.multiple_of(i * rows, rows), rows)
        k[at] = mm(x, w_qkv[1]).astype(BF16)
        v[at] = (mm(x, w_qkv[2]) + vec[pl.ds(1, 1)]).astype(BF16)

    blocks, step, pairs = attend_units(rows, width)
    units = blocks * pairs
    t = lambda x: n + (x * units) // 12
    hooks, last = {}, n + units
    at_units(hooks, f[:1], [t(2)])
    at_units(hooks, w[1:5] + w[5:-1], [t(3), t(3), t(6), t(8)] + [t(11)] * len(w[5:-1]))
    at_units(hooks, e[:1] + f[1:], [t(7), t(9)])
    at_units(hooks, w[-1:] + e[1:], [last] * len(e))
    early = {at: stages for at, stages in hooks.items() if at < n}
    late = {at - n: stages for at, stages in hooks.items() if at >= n}
    hooked(n, project, early)

    def unit(i):
        attend_unit(q, k, v, bias, att, lse, (i % blocks) * step, step, i // blocks)

    hooked(blocks * pairs, unit, late)
    mail.finish()


ROOT_HALF = 0.7071067811865476
NORM = 0.3989422804014327


def normed(v):
    centre = v - jnp.mean(v, axis=1, keepdims=True)
    inverse = lax.rsqrt(jnp.mean(centre * centre, axis=1, keepdims=True) + 1e-05)
    return centre * inverse, inverse


def normed_back(g, gain, hat, inverse):
    gx = g * gain
    mean_g = jnp.mean(gx, axis=1, keepdims=True)
    mean_gh = jnp.mean(gx * hat, axis=1, keepdims=True)
    return inverse * (gx - mean_g - hat * mean_gh)


def by_rows(rows, action):
    step = min(128, rows)

    def one(i, _):
        action(pl.ds(pl.multiple_of(i * step, step), step))
        return 0

    lax.fori_loop(0, rows // step, one, 0)


def row_sum(x):
    return jnp.sum(x, axis=0, keepdims=True)


def cross_kernel(
    shape, shifts, att, all_tok, all_enc, w_in, w_out, vec, z_1, ffn_out, cot,
    hat1, inv1, first_low, cq, ck, cv, crossed, lse, g_1, g_2, my_cot, toks, *sems,
):
    place, mail = open_kernel(shape, True, True, sems)
    rows, width = cq.shape
    n, enc_rows, _ = all_enc.shape
    f = spread_stages(mail, place, [g_1], [z_1])
    w = block_stages(mail, place, [ffn_out], lambda i: [g_2.at[:, place.leaf, i]])
    w += spread_stages(mail, place, [g_2])
    c = mirror_stages(mail, place, cot, my_cot)
    mine = mail.local(None, all_tok.at[place.block], toks)
    mine[0]()
    w[0]()
    f[0]()

    def project(i):
        x = all_enc[i]
        at = pl.ds(pl.multiple_of(i * enc_rows, enc_rows), enc_rows)
        ck[at] = mm(x, w_in[1]).astype(BF16)
        cv[at] = (mm(x, w_in[2]) + vec[pl.ds(4, 1)]).astype(BF16)

    hooked(n, project, {})
    f[1]()
    c[0]()
    mine[1]()
    scale = HEAD**-0.5

    def first(at):
        v = toks[at].astype(F32) + mm(att[at], w_out[0]) + vec[pl.ds(2, 1)]
        hat, inverse = normed(v)
        hat1[at] = hat
        inv1[at] = jnp.broadcast_to(inverse, (hat.shape[0], 128))
        low = (hat * vec[pl.ds(shifts, 1)] + vec[pl.ds(7, 1)]).astype(BF16)
        first_low[at] = low
        cq[at] = ((mm(low, w_in[0]) + vec[pl.ds(3, 1)]) * scale).astype(BF16)

    by_rows(rows, first)
    blocks, step, pairs = attend_units(rows, width)
    total = blocks * pairs
    t = lambda x: (x * total) // 12
    late = {}
    at_units(late, f[2:], [t(4)] + [t(6)] * (len(f) - 4) + [total])
    at_units(late, w[1:], [t(4), t(4), t(10)] + [total] * (len(w) - 4))
    at_units(late, c[1:], [total])

    def unit(i):
        attend_unit(cq, ck, cv, None, crossed, lse, (i % blocks) * step, step, i // blocks)

    hooked(total, unit, late)
    mail.finish()


def ffn_kernel(
    shifts, hat1, crossed, w_out, w1, w2, vec, b1, cot,
    out, gw1, gw2, gwo, g_crossed, g_pre2, sums, gb1,
    hat2, inv2, low2, acc, slope, hidden, g_pre3, g_ffn, acc2, g_cb,
):
    rows, width = crossed.shape
    wide = hidden.shape[1]
    piece = 512
    gain = lambda i: vec[pl.ds(shifts + i, 1)]
    shift = lambda i: vec[pl.ds(i, 1)]
    sums[...] = jnp.zeros_like(sums)

    def second(at):
        v = hat1[at] * gain(0) + shift(7) + mm(crossed[at], w_out[1]) + shift(5)
        hat, inverse = normed(v)
        hat2[at] = hat
        inv2[at] = jnp.broadcast_to(inverse, (hat.shape[0], 128))
        low2[at] = (hat * gain(1) + shift(8)).astype(BF16)

    by_rows(rows, second)
    acc[...] = jnp.zeros_like(acc)

    def up(j, _):
        cols = pl.ds(pl.multiple_of(j * piece, piece), piece)
        u = mm(low2[...], w1[:, cols]) + b1[:, cols]
        phi = 0.5 * (1.0 + lax.erf(u * ROOT_HALF))
        slope[:, cols] = phi + u * jnp.exp(-0.5 * u * u) * NORM
        h = (u * phi).astype(BF16)
        hidden[:, cols] = h
        acc[...] += mm(h, w2[cols])
        return 0

    lax.fori_loop(0, wide // piece, up, 0)

    def third(at):
        v = hat2[at] * gain(1) + shift(8) + acc[at] + shift(6)
        hat, inverse = normed(v)
        out[at] = (hat * gain(2) + shift(9)).astype(BF16)
        g = cot[at].astype(F32)
        sums[pl.ds(shifts + 2, 1)] += row_sum(g * hat)
        sums[pl.ds(9, 1)] += row_sum(g)
        back = normed_back(g, gain(2), hat, inverse)
        g_pre3[at] = back
        low = back.astype(BF16)
        g_ffn[at] = low
        sums[pl.ds(6, 1)] += row_sum(low.astype(F32))

    by_rows(rows, third)
    acc2[...] = jnp.zeros_like(acc2)

    def down(j, _):
        cols = pl.ds(pl.multiple_of(j * piece, piece), piece)
        g = (mm_t(g_ffn[...], w2[cols]) * slope[:, cols]).astype(BF16)
        gb1[:, cols] = row_sum(g.astype(F32))
        gw2[cols] = t_mm(hidden[:, cols], g_ffn[...]).astype(BF16)
        gw1[:, cols] = t_mm(low2[...], g).astype(BF16)
        acc2[...] += mm_t(g, w1[:, cols])
        return 0

    lax.fori_loop(0, wide // piece, down, 0)

    def back_two(at):
        g = g_pre3[at] + acc2[at]
        hat = hat2[at]
        sums[pl.ds(shifts + 1, 1)] += row_sum(g * hat)
        sums[pl.ds(8, 1)] += row_sum(g)
        back = normed_back(g, gain(1), hat, inv2[at, :1])
        g_pre2[at] = back
        low = back.astype(BF16)
        g_cb[at] = low
        sums[pl.ds(5, 1)] += row_sum(low.astype(F32))
        g_crossed[at] = mm_t(low, w_out[1]).astype(BF16)

    by_rows(rows, back_two)
    gwo[...] = t_mm(crossed[...], g_cb[...]).astype(BF16)


def cross_back_kernel(
    shape, shifts, cq, ck, cv, do, o, lse, first_low, hat1, inv1, all_enc, w_in, w_out, att, g_pre2, vec, sums_in, p_1, p_2, out_rows,
    g_in, g_wo, g_enc, g_att, g_pre1, sums, s_1, o_2, my_out, dq, dk, dv, g_br, dk_acc, dv_acc, *scratch,
):
    sems, scratch = scratch[:3], scratch[3:]
    place, mail = open_kernel(shape, True, True, sems)
    rows, width = cq.shape
    f_2, sum_2 = fold_stages(mail, place, p_2, scratch[:N_FOLD])
    f_1, sum_1 = fold_stages(mail, place, p_1, scratch[N_FOLD : 2 * N_FOLD])
    l_2 = line_stages(mail, place, sum_2, scratch[2 * N_FOLD], o_2)
    c = mirror_stages(mail, place, out_rows, my_out)
    f_2[0]()
    c[0]()
    blocks, step, pairs = attend_units(rows, width)
    total = blocks * pairs
    t = lambda x: (x * total) // 12
    hooks = {}
    more = len(f_1) - 5
    at_units(hooks, f_2[1:], [t(2), t(6), t(7), t(11)] + [t(11)] * more)
    at_units(hooks, l_2, [t(11), total + 6])
    at_units(hooks, f_1, [t(3), t(7), total, total + 2, total + 6] + [total + 6] * more)
    at_units(hooks, c[1:], [total + 6])

    def unit(i):
        first = i % blocks == 0

        @pl.when(first)
        def _():
            dk_acc[...] = jnp.zeros_like(dk_acc)
            dv_acc[...] = jnp.zeros_like(dv_acc)

        pair = i // blocks
        attend_back_unit(cq, ck, cv, None, do, o, lse, dq, dk_acc, dv_acc, (i % blocks) * step, step, pair)

        @pl.when(i % blocks == blocks - 1)
        def _():
            cols = pl.ds(pl.multiple_of(pair * PAIR, PAIR), PAIR)
            dk[:, cols] = dk_acc[...].astype(BF16)
            dv[:, cols] = dv_acc[...].astype(BF16)

    late = {at: hooks.pop(at) for at in list(hooks) if at >= total}
    hooked(total, unit, hooks)
    n, enc_rows, _ = all_enc.shape
    flat = all_enc.reshape(n * enc_rows, width)

    def query_grads():
        sums[...] = sums_in[...]
        sums[pl.ds(3, 1)] = row_sum(dq[...].astype(F32))
        sums[pl.ds(4, 1)] = row_sum(dv[...].astype(F32))
        g_in[0] = t_mm(first_low[...], dq[...]).astype(BF16)

    def key_grads():
        g_in[1] = t_mm(flat[...], dk[...]).astype(BF16)

    def value_grads():
        g_in[2] = t_mm(flat[...], dv[...]).astype(BF16)

    def encoder(i, _):
        at = pl.ds(pl.multiple_of(i * enc_rows, enc_rows), enc_rows)
        g_enc[i] = (mm_t(dk[at], w_in[1]) + mm_t(dv[at], w_in[2])).astype(BF16)
        return 0

    def back_one(at):
        g = g_pre2[at] + mm_t(dq[at], w_in[0])
        hat = hat1[at]
        sums[pl.ds(shifts, 1)] += row_sum(g * hat)
        sums[pl.ds(7, 1)] += row_sum(g)
        back = normed_back(g, vec[pl.ds(shifts, 1)], hat, inv1[at, :1])
        g_pre1[at] = back
        low = back.astype(BF16)
        g_br[at] = low
        sums[pl.ds(2, 1)] += row_sum(low.astype(F32))
        g_att[at] = mm_t(low, w_out[0]).astype(BF16)

    def out_grads():
        g_wo[...] = t_mm(att[...], g_br[...]).astype(BF16)

    steps = [
        query_grads,
        key_grads,
        value_grads,
        lambda: lax.fori_loop(0, n, encoder, 0),
        lambda: by_rows(rows, back_one),
        out_grads,
    ]
    for at, step_of in enumerate(steps):
        run(late.get(total + at, []))
        step_of()
    run(late[total + len(steps)])
    s_1[...] = sum_1[...]
    mail.finish()


def self_back_kernel(
    shape, q, k, v, bias, do, o, lse, z_1, sums_in, all_tok, p_in, p_o0, p_o1, p_enc,
    dq, dk, dv, g_qkv, o_1, o_in, o_o0, o_o1, o_enc, sums, dk_acc, dv_acc, *scratch,
):
    sems, scratch = scratch[:3], scratch[3:]
    place, mail = open_kernel(shape, True, False, sems)
    rows, width = q.shape
    l_1 = line_stages(mail, place, z_1, scratch[0], o_1)
    rest = scratch[1:]
    f_in, sum_in = fold_stages(mail, place, p_in, rest[:N_FOLD])
    f_o0, sum_o0 = fold_stages(mail, place, p_o0, rest[N_FOLD : 2 * N_FOLD])
    f_o1, sum_o1 = fold_stages(mail, place, p_o1, rest[2 * N_FOLD : 3 * N_FOLD])
    rest = rest[3 * N_FOLD :]
    l_in = line_stages(mail, place, sum_in, rest[0], o_in)
    l_o0 = line_stages(mail, place, sum_o0, rest[1], o_o0)
    l_o1 = line_stages(mail, place, sum_o1, rest[2], o_o1)
    e = pair_sum_stages(mail, place, p_enc, rest[3:], o_enc)
    f_w = [functools.partial(run, three) for three in zip(f_in, f_o0, f_o1)]
    l_w = [functools.partial(run, three) for three in zip(l_in, l_o0, l_o1)]
    f_w[0]()
    l_1[0]()
    blocks, step, pairs = attend_units(rows, width)
    total = blocks * pairs
    t = lambda x: (x * total) // 12
    hooks = {}
    more = len(f_w) - 5
    at_units(hooks, f_w[1:], [t(1), t(4), t(5), t(7)] + [t(7)] * more)
    at_units(hooks, e[:-1], [t(2)] + [t(3)] * 2 + [t(4)] * (len(e) - 4))
    at_units(hooks, l_1[1:] + l_w[:1], [t(5), t(7)])
    at_units(hooks, e[-1:] + l_w[1:], [total] * 2)

    def unit(i):
        @pl.when(i % blocks == 0)
        def _():
            dk_acc[...] = jnp.zeros_like(dk_acc)
            dv_acc[...] = jnp.zeros_like(dv_acc)

        pair = i // blocks
        attend_back_unit(q, k, v, bias, do, o, lse, dq, dk_acc, dv_acc, (i % blocks) * step, step, pair)

        @pl.when(i % blocks == blocks - 1)
        def _():
            cols = pl.ds(pl.multiple_of(pair * PAIR, PAIR), PAIR)
            dk[:, cols] = dk_acc[...].astype(BF16)
            dv[:, cols] = dv_acc[...].astype(BF16)

    last = hooks.pop(total)
    hooked(total, unit, hooks)
    sums[...] = sums_in[...]
    sums[pl.ds(0, 1)] = row_sum(dq[...].astype(F32))
    sums[pl.ds(1, 1)] = row_sum(dv[...].astype(F32))
    flat = all_tok.reshape(k.shape[0], width)
    g_qkv[0] = t_mm(all_tok[place.block], dq[...]).astype(BF16)
    g_qkv[1] = t_mm(flat[...], dk[...]).astype(BF16)
    g_qkv[2] = t_mm(flat[...], dv[...]).astype(BF16)
    run(last)
    mail.finish()


def closing_kernel(shape, p_qkv, p_small, dq, dk, dv, w_qkv, g_pre1, o_qkv, o_small, o_tok, p_tok, *scratch):
    sems, scratch = scratch[:3], scratch[3:]
    place, mail = open_kernel(shape, True, False, sems)
    f_q, sum_q = fold_stages(mail, place, p_qkv, scratch[:N_FOLD])
    f_s, sum_s = fold_stages(mail, place, p_small, scratch[N_FOLD : 2 * N_FOLD])
    rest = scratch[2 * N_FOLD :]
    l_q = line_stages(mail, place, sum_q, rest[0], o_qkv)
    l_s = line_stages(mail, place, sum_s, rest[1], o_small)
    t = pair_sum_stages(mail, place, p_tok, rest[2:], o_tok)
    a = [functools.partial(run, two) for two in zip(f_q, f_s)]
    b = [functools.partial(run, two) for two in zip(l_q, l_s)]
    n, rows, width = p_tok.shape
    step = min(128, rows)

    def terms(r):
        j = place.shard_of_rank(r)

        def some(i, _):
            at = pl.ds(pl.multiple_of(i * step, step), step)
            far = pl.ds(pl.multiple_of(j * rows + i * step, step), step)
            total = mm_t(dk[far], w_qkv[1]) + mm_t(dv[far], w_qkv[2])
            p_tok[j, at] = total.astype(BF16)

            @pl.when(j == place.block)
            def _():
                own = g_pre1[at] + mm_t(dq[at], w_qkv[0])
                p_tok[j, at] = (total + own).astype(BF16)

            return 0

        lax.fori_loop(0, rows // step, some, 0)

    a[0]()
    terms(n - 1)
    t[0]()
    for k in range(1, n):
        terms(n - 1 - k)
        t[k]()
        if k < len(a):
            a[k]()
    run(a[n:])
    run(b[:1])
    run(t[n:-1])
    t[-1]()
    run(b[1:])
    mail.finish()


def body(
    tokens, encoded, cotangent, parent, assignment, attn_in, attn_out, ffn_in, ffn_out, shifts, gains, ffn_bias
):
    shape = Shape(lax.axis_size("leaf"), lax.axis_size("path"))
    leafs, paths = shape.leafs, shape.paths
    devices = leafs * paths
    scale = HEAD ** (-0.5)
    tokens, encoded, cotangent = tokens[0], encoded[0], cotangent[0]
    rows, width = tokens.shape
    enc_rows = encoded.shape[0]
    hidden_width = ffn_in.shape[1]
    tree_rows, tree_enc = rows * paths, enc_rows * paths
    piece = shifts.shape[1]
    n_shift, n_gain, n_bias = shifts.shape[0], gains.shape[0], ffn_bias.shape[0]
    n_vec = n_shift + n_gain
    ffn_in, ffn_out = ffn_in[None], ffn_out[None]

    def sds(shape_, dtype=BF16):
        return jax.ShapeDtypeStruct(shape_, dtype)

    small = jnp.concatenate([shifts.reshape(-1), gains.reshape(-1), ffn_bias])
    small_rows = -(-small.shape[0] // 4096) * 16
    small = jnp.pad(small, (0, small_rows * 256 - small.shape[0])).reshape(1, small_rows, 256)
    blocks = parent.shape[1]
    ids = jnp.arange(blocks, dtype=jnp.int32)
    lanes = jnp.arange(128, dtype=jnp.int32)
    links = jnp.concatenate(
        [
            (parent[0][:, None] == lanes[None, :]) & (ids[:, None] != lanes[None, :]),
            assignment[0][:, None] == lanes[None, :],
        ]
    ).astype(F32)

    three = 3
    all_tok, g_small, w_qkv, bias = kernel_call(
        functools.partial(opening_kernel, shape, blocks.bit_length()),
        "opening",
        0,
        [tokens, small, attn_in, links],
        [ANY, ANY, ANY, VMEM],
        [
            sds((paths, rows, width)),
            sds((1, leafs, paths) + small.shape[1:]),
            sds((three, leafs, paths) + attn_in.shape[1:]),
            sds((rows, tree_rows)),
        ],
        [ANY, ANY, ANY, VMEM],
        mail_scratch()
        + [pltpu.VMEM(links.shape, F32), pltpu.VMEM((128, 128), F32), pltpu.VMEM((128, 128), F32)],
    )
    flat = g_small.reshape(devices, -1)
    vec = flat[:, : n_vec * piece].reshape(devices, n_vec, piece).transpose(1, 0, 2)
    vec = jnp.pad(vec.reshape(n_vec, width).astype(F32), ((0, -n_vec % 8), (0, 0)))
    b1 = flat[:, n_vec * piece : n_vec * piece + n_bias].reshape(1, hidden_width).astype(F32)
    w_qkv = w_qkv.reshape(three, width, width)

    rest_in = attn_in.shape[0] - three
    q, k, v, attended, self_mass, all_enc, w_in, w_out, z_1 = kernel_call(
        functools.partial(self_kernel, shape),
        "self_attention",
        1,
        [all_tok, w_qkv, vec, bias, encoded, attn_in, attn_out, ffn_in],
        [VMEM] * 4 + [ANY] * 4,
        [
            sds((rows, width)),
            sds((tree_rows, width)),
            sds((tree_rows, width)),
            sds((rows, width)),
            sds((rows, width), F32),
            sds((paths, enc_rows, width)),
            sds((rest_in, leafs, paths) + attn_in.shape[1:]),
            sds((attn_out.shape[0], leafs, paths) + attn_out.shape[1:]),
            sds((1, paths) + ffn_in.shape[1:]),
        ],
        [VMEM] * 5 + [ANY] * 4,
        mail_scratch(),
    )
    w_in = w_in.reshape(rest_in, width, width)
    w_out = w_out.reshape(attn_out.shape[0], width, width)

    hat1, inv1, first_low, cq, ck, cv, crossed, cross_mass, w1, w2, my_cot = kernel_call(
        functools.partial(cross_kernel, shape, n_shift),
        "cross_attention",
        2,
        [attended, all_tok, all_enc, w_in, w_out, vec, z_1, ffn_out, cotangent],
        [VMEM, ANY] + [VMEM] * 4 + [ANY] * 3,
        [
            sds((rows, width), F32),
            sds((rows, 128), F32),
            sds((rows, width)),
            sds((rows, width)),
            sds((tree_enc, width)),
            sds((tree_enc, width)),
            sds((rows, width)),
            sds((rows, width), F32),
            sds((1, leafs, paths) + ffn_in.shape[1:]),
            sds((1, leafs, paths) + ffn_out.shape[1:]),
            sds((rows, width)),
        ],
        [VMEM] * 8 + [ANY] * 3,
        [pltpu.VMEM((rows, width), BF16)] + mail_scratch(),
    )
    w1 = w1.reshape(width, hidden_width)
    w2 = w2.reshape(hidden_width, width)
    vm = lambda s, dtype=BF16: pltpu.VMEM(s, dtype)
    output, g_w1, g_w2, g_wo1, g_crossed, g_pre2, sums, g_b1 = kernel_call(
        functools.partial(ffn_kernel, n_shift),
        "feed_forward",
        None,
        [hat1, crossed, w_out, w1, w2, vec, b1, my_cot],
        [VMEM] * 8,
        [
            sds((rows, width)),
            sds((width, hidden_width)),
            sds((hidden_width, width)),
            sds((width, width)),
            sds((rows, width)),
            sds((rows, width), F32),
            sds(vec.shape, F32),
            sds((1, hidden_width), F32),
        ],
        [VMEM] * 8,
        [
            vm((rows, width), F32),
            vm((rows, 128), F32),
            vm((rows, width)),
            vm((rows, width), F32),
            vm((rows, hidden_width), F32),
            vm((rows, hidden_width)),
            vm((rows, width), F32),
            vm((rows, width)),
            vm((rows, width), F32),
            vm((rows, width)),
        ],
    )

    def spread(g):
        return g.reshape(
            g.shape[0], shape.A, shape.B, 2, paths, g.shape[1] // devices, g.shape[2]
        )

    r1, r2 = ffn_in.shape[1:], ffn_out.shape[1:]
    g_rest, g_wo0, g_enc, g_att, g_pre1, sums, s_1, o_w2, output = kernel_call(
        functools.partial(cross_back_kernel, shape, n_shift),
        "cross_back",
        3,
        [
            cq, ck, cv, g_crossed, crossed, cross_mass, first_low, hat1, inv1, all_enc, w_in, w_out, attended,
            g_pre2, vec, sums, spread(g_w1[None]), spread(g_w2[None]), output,
        ],
        [VMEM] * 16 + [ANY] * 3,
        [
            sds((rest_in, width, width)),
            sds((width, width)),
            sds((paths, enc_rows, width)),
            sds((rows, width)),
            sds((rows, width), F32),
            sds(vec.shape, F32),
            sds((1, paths) + r1),
            sds((1,) + r2, F32),
            sds((rows, width)),
        ],
        [VMEM] * 8 + [ANY],
        [vm((rows, width)), vm((tree_enc, width)), vm((tree_enc, width)), vm((rows, width))]
        + [pltpu.VMEM((tree_enc, PAIR), F32)] * 2
        + mail_scratch()
        + fold_scratch(shape, 1, *r2, BF16)
        + fold_scratch(shape, 1, *r1, BF16)
        + line_scratch(shape, 1, *r2, BF16),
    )
    ri = attn_in.shape[1:]
    g_q, g_k, g_v, g_qkv, o_w1, o_in, o_o0, o_o1, o_enc, sums = kernel_call(
        functools.partial(self_back_kernel, shape),
        "self_back",
        4,
        [
            q, k, v, bias, g_att, attended, self_mass, s_1, sums, all_tok, spread(g_rest),
            spread(g_wo0[None]), spread(g_wo1[None]), g_enc,
        ],
        [VMEM] * 10 + [ANY] * 3 + [VMEM],
        [
            sds((rows, width)),
            sds((tree_rows, width)),
            sds((tree_rows, width)),
            sds((three, width, width)),
            sds((1,) + r1, F32),
            sds((rest_in,) + ri, F32),
            sds((1,) + ri, F32),
            sds((1,) + ri, F32),
            sds((enc_rows, width), F32),
            sds(vec.shape, F32),
        ],
        [VMEM] * 10,
        [pltpu.VMEM((tree_rows, PAIR), F32)] * 2
        + mail_scratch()
        + line_scratch(shape, 1, *r1, BF16)
        + fold_scratch(shape, rest_in, *ri, BF16)
        + fold_scratch(shape, 1, *ri, BF16)
        + fold_scratch(shape, 1, *ri, BF16)
        + line_scratch(shape, rest_in, *ri, BF16)
        + line_scratch(shape, 1, *ri, BF16)
        + line_scratch(shape, 1, *ri, BF16)
        + pair_sum_scratch(shape, enc_rows, width),
    )
    g_vec = sums[:n_vec]
    g_small = jnp.concatenate(
        [
            g_vec.reshape(n_vec, devices, piece).transpose(1, 0, 2).reshape(devices, -1),
            g_b1.reshape(devices, n_bias),
        ],
        axis=1,
    )
    small_count = g_small.shape[1]
    g_small_rows = -(-small_count // 2048) * 8
    g_small = jnp.pad(g_small, ((0, 0), (0, g_small_rows * 256 - small_count)))
    p_small = g_small.reshape(1, shape.A, shape.B, 2, paths, g_small_rows, 256)
    o_qkv, o_small, o_tok = kernel_call(
        functools.partial(closing_kernel, shape),
        "closing",
        5,
        [spread(g_qkv), p_small, g_q, g_k, g_v, w_qkv, g_pre1],
        [ANY, ANY] + [VMEM] * 5,
        [
            sds((three,) + ri, F32),
            sds((1, g_small_rows, 256), F32),
            sds((rows, width), F32),
        ],
        [VMEM] * 3,
        [vm((paths, rows, width))]
        + mail_scratch()
        + fold_scratch(shape, three, *ri, BF16)
        + fold_scratch(shape, 1, g_small_rows, 256, F32)
        + line_scratch(shape, three, *ri, BF16)
        + line_scratch(shape, 1, g_small_rows, 256, F32)
        + pair_sum_scratch(shape, rows, width),
    )
    o_small = o_small.reshape(-1)
    o_vec = o_small[: n_vec * piece].reshape(n_vec, piece)
    return (
        output[None],
        o_tok[None],
        o_enc[None],
        jnp.concatenate([o_qkv, o_in]),
        jnp.concatenate([o_o0, o_o1]),
        o_w1[0],
        o_w2[0],
        o_vec[:n_shift],
        o_vec[n_shift:],
        o_small[n_vec * piece : n_vec * piece + n_bias],
    )


def solution(mesh):
    both = ("leaf", "path")
    rows = P("leaf", "path", None)
    weights = (P(None, both, None), P(None, both, None), P(both, None), P(both, None), P(None, both), P(None, both), P(both))
    return jax.shard_map(
        body,
        mesh=mesh,
        in_specs=(rows, rows, rows, P("leaf", None), P("leaf", None)) + weights,
        out_specs=(rows, rows, rows) + weights,
        check_vma=False,
    )
```

```python
import functools

import jax
import jax.numpy as jnp
from jax import lax
from jax.experimental import pallas as pl
from jax.experimental.pallas import tpu as pltpu
from jax.sharding import PartitionSpec as P

HEAD = 64
BLK = 128
PAIR = 2 * HEAD
MESH = pl.DeviceIdType.MESH
F32 = jnp.float32
BF16 = jnp.bfloat16
VMEM_OF = {"opening": 8}
ANY = pl.BlockSpec(memory_space=pl.ANY)
VMEM = pl.BlockSpec(memory_space=pltpu.VMEM)


class Shape:
    def __init__(self, leafs, paths):
        self.leafs, self.paths, self.half = leafs, paths, paths // 2
        outer = leafs // 2
        self.A = 2 if outer % 2 == 0 else 1
        self.B = outer // self.A


class Place:
    def __init__(self, shape):
        self.shape = shape
        self.leafs, self.paths, self.half = shape.leafs, shape.paths, shape.half
        self.A, self.B = shape.A, shape.B
        leaf = lax.axis_index("leaf")
        self.leaf, self.p = leaf, lax.axis_index("path")
        self.c = leaf % 2
        self.a = (leaf // 2) // self.B
        self.b = (leaf // 2) % self.B
        n = self.paths
        self.tree = jnp.where(self.p >= self.half, 1, 0)
        self.primary = self.c == self.tree
        self.pm = jnp.where(self.tree == 0, self.p, n - 1 - self.p)
        self.inward = jnp.where(self.tree == 0, 1, -1)
        self.own_rank = jnp.where(self.c == 0, self.p, n - 1 - self.p)
        self.block = jnp.where(self.primary, self.p, n - 1 - self.p)

    def leaf_at(self, a, b, c):
        return (a * self.B + b) * 2 + c

    def at_core(self):
        return (self.leaf_at(self.a, self.b, 1 - self.c), self.p)

    def at_a(self, a):
        return (self.leaf_at(a, self.b, self.c), self.p)

    def at_b(self, b):
        return (self.leaf_at(self.a, b, self.c), self.p)

    def at_p(self, p):
        return (self.leaf, clamp(p, self.paths))

    def at_mirror(self):
        return (self.leaf_at(self.a, self.b, 1 - self.c), self.paths - 1 - self.p)

    def shard_of_rank(self, rank):
        return jnp.where(self.tree == 0, rank, self.paths - 1 - rank)

    def line_p(self):
        return (self.paths, self.p, self.at_p)

    def line_a(self):
        return (self.A, self.a, self.at_a)

    def line_b(self):
        return (self.B, self.b, self.at_b)


def clamp(index, size):
    return jnp.clip(index, 0, size - 1)


def guarded(when, action):
    if when is None:
        action()
    else:

        @pl.when(when)
        def _():
            action()


def run(actions):
    for action in actions:
        action()


def greet(place, column, mirror):
    barrier = pltpu.get_barrier_semaphore()
    peers = 1

    def signal(to):
        pl.semaphore_signal(barrier, inc=1, device_id=to, device_id_type=MESH)

    signal(place.at_core())
    if column:
        for k in range(1, place.paths):
            for core in range(2):
                there = (place.p + k) % place.paths
                signal((place.leaf_at(place.a, place.b, core), there))
        peers = peers + 2 * (place.paths - 1)
    for size, pos, to in (place.line_a(), place.line_b()):
        if size == 1:
            continue
        if size == 2:
            signal(to(1 - pos))
            peers = peers + 1
            continue
        for step in (-1, 1):
            there = pos + step
            inside = (there >= 0) & (there < size)

            @pl.when(inside)
            def _():
                signal(to(clamp(there, size)))

            peers = peers + jnp.where(inside, 1, 0)
    if mirror and not column:

        @pl.when(jnp.logical_not(place.primary))
        def _():
            signal(place.at_mirror())

        peers = peers + jnp.where(place.primary, 0, 1)
    pl.semaphore_wait(barrier, peers)


class Mail:
    def __init__(self, send_sems, recv_sems, own_sems):
        self.send_sems, self.recv_sems, self.own_sems = send_sems, recv_sems, own_sems
        self.sends = self.recvs = self.owns = 0
        self.sent = []

    def new_recv(self, count=1):
        self.recvs += count
        return self.recvs - count

    def send(self, when, src, dst, to, recv):
        k = self.sends
        self.sends += 1
        copy = pltpu.make_async_remote_copy(
            src_ref=src,
            dst_ref=dst,
            send_sem=self.send_sems.at[k],
            recv_sem=self.recv_sems.at[recv],
            device_id=to,
            device_id_type=MESH,
        )
        self.sent.append((when, copy))
        return functools.partial(guarded, when, copy.start)

    def hear(self, when, landing, to, recv):
        copy = pltpu.make_async_remote_copy(
            src_ref=landing,
            dst_ref=landing,
            send_sem=self.send_sems.at[0],
            recv_sem=self.recv_sems.at[recv],
            device_id=to,
            device_id_type=MESH,
        )
        return functools.partial(guarded, when, copy.wait_recv)

    def post(self, when, src, dst, to, hear_when, landing):
        k = self.new_recv()
        return self.send(when, src, dst, to, k), self.hear(hear_when, landing, to, k)

    def local(self, when, src, dst):
        k = self.owns
        self.owns += 1
        copy = pltpu.make_async_copy(src, dst, self.own_sems.at[k])
        return functools.partial(guarded, when, copy.start), functools.partial(guarded, when, copy.wait)

    def finish(self):
        for when, copy in self.sent:
            guarded(when, copy.wait_send)


def mail_scratch(count=160, own=24):
    return [
        pltpu.SemaphoreType.DMA((count,)),
        pltpu.SemaphoreType.DMA((count,)),
        pltpu.SemaphoreType.DMA((own,)),
    ]


def flood(mail, line, views, first=None):
    size, pos, to = line
    steps = []
    if size == 1:
        return steps
    first = first if first is not None else views(pos)
    if size == 2:
        jobs = [
            mail.post(None, s, d, to(1 - pos), None, w)
            for s, d, w in zip(first, views(pos), views(1 - pos))
        ]
        return [([j[0] for j in jobs], [j[1] for j in jobs])]
    for step in range(1, size):
        starts, waits = [], []
        for sign in (1, -1):
            item = pos - sign * (step - 1)
            there = pos + sign
            when = (there >= 0) & (there < size) & (item >= 0) & (item < size)
            heard = pos - sign * step
            hear_when = (heard >= 0) & (heard < size)
            item_c = clamp(item, size)
            sources = first if step == 1 else views(item_c)
            for s, d, w in zip(sources, views(item_c), views(clamp(heard, size))):
                start, wait = mail.post(when, s, d, to(clamp(there, size)), hear_when, w)
                starts.append(start)
                waits.append(wait)
        steps.append((starts, waits))
    return steps


def chain(steps, first_starts=()):
    stages, pending = [], []
    for k, (starts, waits) in enumerate(steps):
        stages.append(functools.partial(run, pending + (list(first_starts) if k == 0 else []) + starts))
        pending = waits
    stages.append(functools.partial(run, pending))
    return stages


def half_columns(ref, leaf, h):
    width = ref.shape[-1] // 2
    return ref.at[:, leaf, :, :, pl.ds(h * width, width)]


def block_stages(mail, place, shards, block_views):
    n = place.paths
    own = [mail.local(None, s, d) for s, d in zip(shards, block_views(place.p))]
    starts, waits = [], []
    lands = [mail.new_recv(n) for _ in shards]
    relay = n == 4
    for k in (1, 3, 2) if relay else range(1, n):
        there = (place.p + k) % n
        near = None
        if relay and k != 2:
            near = (there - place.p != 3) & (place.p - there != 3)
        for s, d, w, land in zip(shards, block_views(place.p), block_views(there), lands):
            starts.append(mail.send(near, s, d, place.at_p(there), land + place.p))
            waits.append((there, mail.hear(None, w, place.at_p(there), land + there)))
    starts += [o[0] for o in own]
    ends = [o[1] for o in own]
    if not relay:
        return [functools.partial(run, starts), functools.partial(run, [w[1] for w in waits] + ends)]
    middle = (place.p == 1) | (place.p == 2)
    passed = jnp.where(place.p == 1, 3, 0)
    to = place.at_p(jnp.where(place.p == 1, 0, 3))
    passes = []
    for item, land in zip(block_views(passed), lands):
        passes.append(mail.hear(middle, item, to, land + passed))
        passes.append(mail.send(middle, item, item, to, land + passed))
    for there, wait in waits:
        ends.append(functools.partial(guarded, jnp.logical_not(middle & (there == passed)), wait))
    return [functools.partial(run, starts), functools.partial(run, passes), functools.partial(run, ends)]


def path_half(ref, h):
    n = ref.shape[1] // 2
    return ref.at[:, pl.ds(h * n, n)]


def spread_stages(mail, place, wholes, blocks=None):
    if (place.A, place.B) != (2, 2):
        return spread_lines(mail, place, wholes, blocks)
    a, b, c = place.a, place.b, place.c
    at = lambda w, a, b, c: w.at[:, place.leaf_at(a, b, c)]
    to_a, to_b, to_core = place.at_a(1 - a), place.at_b(1 - b), place.at_core()
    own = []
    sources = [at(w, a, b, c) for w in wholes]
    if blocks is not None:
        own = [mail.local(None, x, s) for x, s in zip(blocks, sources)]
        sources = list(blocks)
    urgent, calm, relay, near, far = [], [], [], [], []
    for w, s in zip(wholes, sources):
        mine, from_a, from_b = at(w, a, b, c), at(w, 1 - a, b, c), at(w, a, 1 - b, c)
        from_ab = at(w, 1 - a, 1 - b, c)

        def post(src, dst, to, landing, h):
            return mail.post(
                None, path_half(src, h), path_half(dst, h), to, None, path_half(landing, h)
            )

        urgent += [post(s, mine, to_b, from_b, 0), post(s, mine, to_a, from_a, 1)]
        calm += [post(s, mine, to_b, from_b, 1), post(s, mine, to_a, from_a, 0)]
        relay += [post(from_b, from_b, to_a, from_ab, 0), post(from_a, from_a, to_b, from_ab, 1)]
        near.append(mail.post(None, s, mine, to_core, None, at(w, a, b, 1 - c)))
        for x, y, l in ((1 - a, b, near), (a, 1 - b, near), (1 - a, 1 - b, far)):
            l.append(mail.post(None, at(w, x, y, c), at(w, x, y, c), to_core, None, at(w, x, y, 1 - c)))
    start = lambda jobs: run([j[0] for j in jobs])
    wait = lambda jobs: run([j[1] for j in jobs])
    first = near[::3]
    second = [j for k, j in enumerate(near) if k % 3]

    def opening():
        start(urgent)
        start(calm)
        start(first)
        run([o[0] for o in own])

    def passing():
        wait(urgent)
        start(relay)

    def sharing():
        wait(calm)
        run([o[1] for o in own])
        start(second)

    def ending():
        wait(relay)
        start(far)

    return [opening, passing, sharing, ending, lambda: wait(near + far)]


def spread_lines(mail, place, wholes, blocks=None):
    A, B, c = place.A, place.B, place.c

    def of_b(h, across_a):
        ays = range(A) if across_a else [place.a]
        return lambda i: [half_columns(w, place.leaf_at(a, i, c), h) for a in ays for w in wholes]

    def of_a(h, across_b):
        bees = range(B) if across_b else [place.b]
        return lambda i: [half_columns(w, place.leaf_at(i, b, c), h) for b in bees for w in wholes]

    own = []
    firsts = [None, None]
    sources = [w.at[:, place.leaf] for w in wholes]
    if blocks is not None:
        own = [mail.local(None, x, w.at[:, place.leaf]) for x, w in zip(blocks, wholes)]
        firsts = [
            [x.at[:, :, :, pl.ds(h * (x.shape[-1] // 2), x.shape[-1] // 2)] for x in blocks]
            for h in range(2)
        ]
        sources = list(blocks)
    line_a, line_b = place.line_a(), place.line_b()
    phases = [
        (flood(mail, line_b, of_b(0, False), firsts[0]), flood(mail, line_a, of_a(1, False), firsts[1])),
        (flood(mail, line_a, of_a(0, True)), flood(mail, line_b, of_b(1, True))),
    ]
    core = [
        mail.post(
            None,
            s,
            w.at[:, place.leaf],
            place.at_core(),
            None,
            w.at[:, place.leaf_at(place.a, place.b, 1 - c)],
        )
        for s, w in zip(sources, wholes)
    ]
    rest = []
    for offset in range(1, A * B):
        spot = (place.a * B + place.b + offset) % (A * B)
        for w in wholes:
            mine, other = w.at[:, spot * 2 + c], w.at[:, spot * 2 + 1 - c]
            rest.append(mail.post(None, mine, mine, place.at_core(), None, other))
    steps = []
    opening = [o[0] for o in own] + [j[0] for j in core]
    for n_phase, phase in enumerate(phases):
        before = [o[1] for o in own] if n_phase == 1 else []
        for s in range(max(len(f) for f in phase)):
            starts, waits = list(before), []
            before = []
            for f in phase:
                if s < len(f):
                    starts += f[s][0]
                    waits += f[s][1]
            steps.append((starts + opening, waits))
            opening = []
    steps.append((opening + [j[0] for j in rest], [j[1] for j in core + rest]))
    return chain(steps)


def pair_gather_stages(mail, place, shard, whole, pieces=1):
    n, h = place.paths, place.half
    rows = shard.shape[0] // (2 * pieces)
    part = lambda ref, u, s: ref.at[pl.ds(pl.multiple_of((u * pieces + s) * rows, rows), rows)]
    half = lambda ref, u: ref.at[pl.ds(pl.multiple_of(u * pieces * rows, rows), pieces * rows)]
    lands = [mail.new_recv(n) for _ in range(pieces)]
    core_lands = mail.new_recv(n)
    own = mail.local(place.primary, shard, whole.at[place.p])
    first = jnp.where(place.c == 0, 0, h)
    edge = jnp.where(place.c == 0, h - 1, h)
    starts = []
    for s in range(pieces):
        for u in range(2):
            for q in range(h):
                q = first + q
                to = (place.leaf_at(place.a, place.b, u), q)
                near = place.primary & jnp.logical_not((q == place.p) & (place.c == u))
                away = near | (jnp.logical_not(place.primary) & (q == edge))
                starts.append(
                    mail.send(
                        away, part(shard, u, s), part(whole.at[place.p], u, s), to, lands[s] + place.p
                    )
                )
    k = mail.new_recv()
    mate = whole.at[place.p]
    starts.append(
        mail.send(place.primary, half(shard, place.c), half(mate, place.c), place.at_core(), k)
    )
    starts.append(own[0])
    stages = [functools.partial(run, starts)]
    outward = place.at_p(place.p - place.inward)
    for s in range(pieces):
        for r in list(range(h, n)) + list(range(h)):
            j = place.shard_of_rank(r)
            item = part(whole.at[j], place.c, s)
            got = jnp.logical_not(place.primary & (place.p == j))
            actions = [mail.hear(got, item, place.at_core(), lands[s] + j)]
            if r >= h and h > 1:
                actions.append(mail.send(place.pm > 0, item, item, outward, lands[s] + j))
            if s == pieces - 1:
                whole_half = half(whole.at[j], place.c)
                actions.append(
                    mail.send(
                        jnp.logical_not(place.p == j),
                        whole_half,
                        whole_half,
                        place.at_core(),
                        core_lands + j,
                    )
                )
            stages.append(functools.partial(run, actions))
    rest = [own[1]]
    rest.append(
        mail.hear(jnp.logical_not(place.primary), half(mate, 1 - place.c), place.at_core(), k)
    )
    for r in range(n):
        j = place.shard_of_rank(r)
        rest.append(
            mail.hear(
                jnp.logical_not(place.p == j),
                half(whole.at[j], 1 - place.c),
                place.at_core(),
                core_lands + j,
            )
        )
    stages.append(functools.partial(run, rest))
    return stages


def mirror_stages(mail, place, own, mine):
    local = mail.local(place.primary, own, mine)
    other = jnp.logical_not(place.primary)
    start, wait = mail.post(other, own, mine, place.at_mirror(), other, mine)
    return [lambda: run([local[0], start]), lambda: run([local[1], wait])]


def add_rows(dst, src):
    lead = dst.shape[:-2]
    total = 1
    for extent in lead:
        total *= extent

    def body(i, _):
        index = []
        rest = i
        for extent in reversed(lead):
            index.insert(0, rest % extent)
            rest = rest // extent
        index = tuple(index)
        dst[index] = dst[index] + src[index]
        return 0

    if total == 1:
        body(0, 0)
    else:
        lax.fori_loop(0, total, body, 0)


def add_tall(dst, src):
    rows = dst.shape[0]
    step = 64 if rows % 64 == 0 else rows

    def body(r, _):
        at = pl.ds(pl.multiple_of(r * step, step), step)
        dst[at] = dst[at] + src[at]
        return 0

    lax.fori_loop(0, rows // step, body, 0)


def shift_sum(mail, line, mine, slots_up, slots_down, add):
    size, pos, to = line
    if size == 1:
        return []
    if size == 2:
        jobs = [
            mail.post(None, s, slot, to(1 - pos), None, slot)
            for s, slot in zip(mine(1 - pos), slots_up[0])
        ]

        def end():
            for job, dst, slot in zip(jobs, mine(pos), slots_up[0]):
                job[1]()
                add(dst, slot)

        return [lambda: run([j[0] for j in jobs]), end]
    stages = []
    for k in range(size - 1):
        early, actions = [], []
        for sign, slots in ((1, slots_up), (-1, slots_down)):
            dest = size - 1 - k if sign == 1 else k
            when = (pos < dest) if sign == 1 else (pos > dest)
            hear_when = (
                ((pos > 0) & (pos <= dest)) if sign == 1 else ((pos < size - 1) & (pos >= dest))
            )
            there = clamp(pos + sign, size)
            jobs = [
                mail.post(when, s, slot, to(there), None, slot)
                for s, slot in zip(mine(dest), slots[k])
            ]

            def take(jobs=jobs, dst_refs=mine(dest), slot_refs=slots[k]):
                for job, dst, slot in zip(jobs, dst_refs, slot_refs):
                    job[1]()
                    add(dst, slot)

            end = (pos == 0) if sign == 1 else (pos == size - 1)
            starts = functools.partial(run, [job[0] for job in jobs])
            early.append(functools.partial(guarded, end, starts))
            actions.append(functools.partial(guarded, hear_when, take))
            actions.append(functools.partial(guarded, jnp.logical_not(end), starts))
        stages.append(functools.partial(run, early + actions))
    return stages


def fold_scratch(shape, k, R, C, dtype):
    if (shape.A, shape.B) != (2, 2):
        return fold_lines_scratch(shape, k, R, C, dtype)
    block = (k, 2, 2, shape.paths, R, C)
    halves = (2, k, shape.paths // 2, R, C)
    return [pltpu.VMEM(block, dtype)] * 2 + [pltpu.VMEM(halves, dtype)] * 3 + [pltpu.VMEM((1, R, C), dtype)]


def fold_lines_scratch(shape, k, R, C, dtype):
    A, B, paths = shape.A, shape.B, shape.paths
    nb, na = max(B - 1, 1) * (2 if B > 2 else 1), max(A - 1, 1)
    return [
        pltpu.VMEM((k, A, B, paths, R, C), dtype),
        pltpu.VMEM((k, A, B, paths, R, C), dtype),
        pltpu.VMEM((nb, k, A, paths, R, C // 2), dtype),
        pltpu.VMEM((na, k, paths, R, C // 2), dtype),
        pltpu.VMEM((na, k, B, paths, R, C // 2), dtype),
        pltpu.VMEM((nb, k, paths, R, C // 2), dtype),
    ]


N_FOLD = 6


def up_down(ref, size):
    if size <= 2:
        return [[ref.at[0]]], None
    return (
        [[ref.at[k]] for k in range(size - 1)],
        [[ref.at[size - 1 + k]] for k in range(size - 1)],
    )


def fold_stages(mail, place, partial, scratch):
    if (place.A, place.B) != (2, 2):
        return fold_lines(mail, place, partial, scratch)
    a, b, c = place.a, place.b, place.c
    acc, got, far, direct, relayed = scratch[:5]
    own = mail.local(None, partial.at[:, :, :, c], acc)
    core = mail.post(None, partial.at[:, :, :, 1 - c], got, place.at_core(), None, got)
    to_a, to_b = place.at_a(1 - a), place.at_b(1 - b)
    of_a, of_b, of_ab = acc.at[:, 1 - a, b], acc.at[:, a, 1 - b], acc.at[:, 1 - a, 1 - b]
    mine = acc.at[:, a, b]

    def post(src, h, slot, to):
        return mail.post(None, path_half(src, h), slot, to, None, slot)

    urgent = [post(of_ab, 0, far.at[0], to_b), post(of_ab, 1, far.at[1], to_a)]
    calm = [post(of_b, 0, direct.at[0], to_b), post(of_a, 1, direct.at[1], to_a)]
    late = [post(of_a, 0, relayed.at[0], to_a), post(of_b, 1, relayed.at[1], to_b)]

    def join():
        own[1]()
        core[1]()
        add_rows(of_ab, got.at[:, 1 - a, 1 - b])
        run([j[0] for j in urgent])
        add_rows(of_b, got.at[:, a, 1 - b])
        calm[0][0]()
        add_rows(of_a, got.at[:, 1 - a, b])
        calm[1][0]()
        add_rows(mine, got.at[:, a, b])

    def passing():
        urgent[0][1]()
        add_rows(path_half(of_a, 0), far.at[0])
        late[0][0]()
        urgent[1][1]()
        add_rows(path_half(of_b, 1), far.at[1])
        late[1][0]()

    def taking():
        for h in range(2):
            calm[h][1]()
            add_rows(path_half(mine, h), direct.at[h])

    def ending():
        for h in range(2):
            late[h][1]()
            add_rows(path_half(mine, h), relayed.at[h])

    return [lambda: run([own[0], core[0]]), join, passing, taking, ending], mine


def fold_lines(mail, place, partial, scratch):
    c = place.c
    acc, got, sb0, sa0, sa1, sb1 = scratch
    own = mail.local(None, partial.at[:, :, :, c], acc)
    core = mail.post(None, partial.at[:, :, :, 1 - c], got, place.at_core(), None, got)
    width = acc.shape[-1] // 2
    left, right = pl.ds(0, width), pl.ds(width, width)

    def join():
        own[1]()
        core[1]()
        add_rows(acc, got)

    line_a, line_b = place.line_a(), place.line_b()
    h0_b = shift_sum(
        mail, line_b, lambda d: [acc.at[:, :, d, :, :, left]], *up_down(sb0, place.B), add_rows
    )
    h1_a = shift_sum(
        mail, line_a, lambda d: [acc.at[:, d, :, :, :, right]], *up_down(sa1, place.A), add_rows
    )
    h0_a = shift_sum(
        mail, line_a, lambda d: [acc.at[:, d, place.b, :, :, left]], *up_down(sa0, place.A), add_rows
    )
    h1_b = shift_sum(
        mail, line_b, lambda d: [acc.at[:, place.a, d, :, :, right]], *up_down(sb1, place.B), add_rows
    )

    def beside(one, two):
        return [
            functools.partial(run, [s[k] for s in (one, two) if k < len(s)])
            for k in range(max(len(one), len(two)))
        ]

    def joined(first, second):
        if not first or not second:
            return first + second
        return first[:-1] + [functools.partial(run, [first[-1], second[0]])] + second[1:]

    stages = joined(
        [lambda: run([own[0], core[0]]), join], beside(h0_b, h1_a)
    )
    stages = joined(stages, beside(h0_a, h1_b))
    return stages, acc.at[:, place.a, place.b]


def line_scratch(shape, k, R, C, dtype):
    return [pltpu.VMEM((max(shape.paths - 1, 1), k, R, C), dtype)]


def line_stages(mail, place, sums, slots, out):
    n = place.paths
    jobs = []
    for k in range(1, n):
        there = (place.p + k) % n
        slot = slots.at[k - 1]
        jobs.append(mail.post(None, sums.at[:, there], slot, place.at_p(there), None, slot))

    def end():
        run([j[1] for j in jobs])
        for j in range(out.shape[0]):
            total = sums[j, place.p].astype(F32)
            for k in range(n - 1):
                total = total + slots[k, j].astype(F32)
            out[j] = total.astype(out.dtype)

    return [lambda: run([j[0] for j in jobs]), end]


def pair_sum_scratch(shape, R, C):
    return [
        pltpu.VMEM((shape.paths, R // 2, C), BF16),
        pltpu.VMEM((shape.paths, R // 2, C), BF16),
        pltpu.VMEM((shape.half, R, C), BF16),
    ]


def pair_sum_stages(mail, place, part, scratch, out):
    n, h = place.paths, place.half
    core_slot, in_slot, landing = scratch
    rows = part.shape[1] // 2
    half = lambda ref, u: ref.at[pl.ds(pl.multiple_of(u * rows, rows), rows)]
    lands = [mail.new_recv(2) for _ in range(h)]
    inner = place.at_p(place.p + place.inward)
    sends, sums, passes = [], [], []
    for r in range(n - 1, -1, -1):
        j = place.shard_of_rank(r)
        item = part.at[j]
        mine = half(item, place.c)
        send, hear = mail.post(
            None, half(item, 1 - place.c), core_slot.at[r], place.at_core(), None, core_slot.at[r]
        )
        owner = (place.leaf_at(place.a, place.b, place.tree), j)
        leave = []
        if r >= h:
            k = mail.new_recv()
            slot = in_slot.at[r]
            in_send = mail.send(place.pm < h - 1, mine, slot, inner, k)
            in_hear = mail.hear(None, slot, place.at_core(), k)
            go = mail.send(
                place.pm == h - 1, mine, half(landing.at[h - 1], place.c), owner, lands[h - 1] + place.c
            )

            def inward(in_send=in_send, in_hear=in_hear, mine=mine, slot=slot, go=go):
                if h > 1:

                    @pl.when(place.pm > 0)
                    def _():
                        in_hear()
                        add_tall(mine, slot)

                    in_send()
                go()

            passes.append(inward)
        else:
            away = jnp.logical_not(place.primary & (place.p == j))
            for q in range(h):
                leave.append(
                    mail.send(
                        away & (place.pm == q),
                        mine,
                        half(landing.at[q], place.c),
                        owner,
                        lands[q] + place.c,
                    )
                )

        def settle(hear=hear, mine=mine, slot=core_slot.at[r], leave=leave):
            hear()
            add_tall(mine, slot)
            run(leave)

        sends.append(send)
        sums.append(settle)
    stages = [[sends[0]]]
    for k in range(1, n):
        stages.append([sends[k], sums[k - 1]])
    stages.append([sums[n - 1]])
    for k, step in enumerate(passes):
        stages[k + 1].append(step)

    def end():
        for q in range(h):
            for u in range(2):
                self_made = place.primary & (place.own_rank == q) & (place.c == u)
                comes = jnp.logical_not(self_made) & (place.primary | (q == h - 1))
                mail.hear(comes, half(landing.at[q], u), place.at_core(), lands[q] + u)()

        step = 64 if rows % 64 == 0 else rows
        for u in range(2):

            def body(i, _, u=u):
                at = pl.ds(pl.multiple_of(u * rows + i * step, step), step)

                @pl.when(place.primary)
                def _():
                    for q in range(h):
                        self_made = (place.own_rank == q) & (place.c == u)
                        term = jnp.where(self_made, part[place.p, at], landing[q, at]).astype(F32)
                        total = term if q == 0 else total + term
                    out[at] = total

                @pl.when(jnp.logical_not(place.primary))
                def _():
                    out[at] = landing[h - 1, at].astype(F32)

                return 0

            lax.fori_loop(0, rows // step, body, 0)

    return [functools.partial(run, x) for x in stages] + [end]


def at_units(hooks, stages, units):
    for stage, unit in zip(stages, units, strict=True):
        hooks.setdefault(unit, []).append(stage)


def hooked(count, unit, hooks):
    def body(i, _):
        for at, stages in hooks.items():
            if at < count:

                @pl.when(i == at)
                def _():
                    run(stages)

        unit(i)
        return 0

    lax.fori_loop(0, count, body, 0)
    for at in sorted(hooks):
        if at >= count:
            run(hooks[at])


def kernel_call(kernel, name, collective_id, ins, in_specs, outs, out_specs, scratch, late=(), early=()):
    n_in, n_out = len(ins), len(outs)
    in_specs, out_specs = list(in_specs), list(out_specs)
    for i in late:
        in_specs[i] = ANY
    for i in early:
        out_specs[i] = ANY
    held = [pltpu.VMEM(ins[i].shape, ins[i].dtype) for i in late]
    held += [pltpu.VMEM(outs[i].shape, outs[i].dtype) for i in early]
    moving = [pltpu.SemaphoreType.DMA((len(held),))] if held else []

    def whole(*refs):
        refs, extra = list(refs[: len(refs) - len(held) - 1]), refs[len(refs) - len(held) - 1 :]
        buffers, sems = extra[:-1], extra[-1]
        loads, stores = [], {}
        for k, i in enumerate(late):
            loads.append(pltpu.make_async_copy(refs[i], buffers[k], sems.at[k]))
            refs[i] = buffers[k]
        for k, i in enumerate(early):
            k = len(late) + k
            stores[i] = pltpu.make_async_copy(buffers[k], refs[n_in + i], sems.at[k])
            refs[n_in + i] = buffers[k]
        for load in loads:
            load.start()

        def arrive():
            for load in loads:
                load.wait()

        def leave(*which):
            for i in which:
                stores[i].start()

        kernel(arrive, leave, *refs)
        for store in stores.values():
            store.wait()

    limit = VMEM_OF.get(name, 62) * 1024 * 1024
    if collective_id is None:
        params = pltpu.CompilerParams(vmem_limit_bytes=limit)
    else:
        params = pltpu.CompilerParams(
            collective_id=collective_id, has_side_effects=True, vmem_limit_bytes=limit
        )
    return pl.pallas_call(
        whole if held else kernel,
        out_shape=outs,
        in_specs=in_specs,
        out_specs=out_specs,
        scratch_shapes=list(scratch) + held + moving,
        compiler_params=params,
        name=name,
    )(*ins)


def dot(x, y, contract):
    return lax.dot_general(x, y, (contract, ((), ())), preferred_element_type=F32)


def mm(x, w):
    return dot(x, w, ((1,), (0,)))


def mm_t(x, w):
    return dot(x, w, ((1,), (1,)))


def t_mm(x, y):
    return dot(x, y, ((0,), (0,)))


def open_kernel(shape, column, mirror, sems):
    place = Place(shape)
    greet(place, column, mirror)
    return place, Mail(*sems)


def opening_kernel(shape, turns, tok, small, attn_in, links, all_tok, g_small, g_qkv, bias, *scratch):
    sems, (links_got, reach, spot) = scratch[:3], scratch[3:]
    place, mail = open_kernel(shape, True, False, sems)
    three = g_qkv.shape[0]
    to_core = mail.post(None, links, links_got, place.at_core(), None, links_got)
    to_core[0]()
    shards = [small, attn_in.at[pl.ds(0, three)]]
    wholes = [g_small, g_qkv]
    weights = block_stages(
        mail, place, shards, lambda i: [w.at[:, place.leaf, i] for w in wholes]
    )
    spread = spread_stages(mail, place, wholes)
    tokens = pair_gather_stages(mail, place, tok, all_tok)
    weights[0]()
    tokens[0]()
    to_core[1]()

    count = links.shape[0] // 2
    mine = jnp.where(place.primary, links[...], links_got[...])
    reach[...] = jnp.zeros_like(reach)
    spot[...] = jnp.zeros_like(spot)
    reach[pl.ds(0, count)] = mine[:count]
    spot[pl.ds(0, count)] = mine[count:]
    for _ in range(turns):
        r = reach[...]
        reach[...] = jnp.minimum(r + mm(r.astype(BF16), r.astype(BF16)), 1.0)
    placed = spot[...].astype(BF16)
    linked = mm_t(mm(placed, reach[...].astype(BF16)).astype(BF16), placed).astype(BF16)
    rows, keys = bias.shape
    step = min(128, rows)

    def fill(i, _):
        first = i * step
        at = pl.ds(pl.multiple_of(first, step), step)
        q_slot = (place.block * rows + first + lax.broadcasted_iota(jnp.int32, (step, 128), 0)) // BLK
        pick_q = (q_slot == lax.broadcasted_iota(jnp.int32, (step, 128), 1)).astype(F32)
        own = mm(pick_q.astype(BF16), linked).astype(BF16)
        k_slot = lax.broadcasted_iota(jnp.int32, (128, keys), 1) // BLK
        pick_k = (k_slot == lax.broadcasted_iota(jnp.int32, (128, keys), 0)).astype(F32)
        seen = mm(own, pick_k.astype(BF16))
        q_at = place.block * rows + first + lax.broadcasted_iota(jnp.int32, (step, keys), 0)
        k_at = lax.broadcasted_iota(jnp.int32, (step, keys), 1)
        inside = (q_at // BLK == k_at // BLK) & (k_at <= q_at)
        bias[at] = jnp.where((seen > 0.5) | inside, 0.0, -1e30).astype(bias.dtype)
        return 0

    run(weights[1:] + spread[:1])
    run(tokens[1:-3])
    spread[1]()
    lax.fori_loop(0, rows // step, fill, 0)
    run(tokens[-3:-1])
    run(spread[2:])
    tokens[-1]()
    mail.finish()


def attend_unit(q_ref, k_ref, v_ref, bias_ref, o_ref, lse_ref, row, step, pair):
    at = pl.ds(pl.multiple_of(row, step), step)
    cols = pl.ds(pl.multiple_of(pair * PAIR, PAIR), PAIR)
    lane = lax.broadcasted_iota(jnp.int32, (1, PAIR), 1)
    q = q_ref[at, cols]
    k = k_ref[:, cols]
    v = v_ref[:, cols]
    out = jnp.zeros((step, PAIR), F32)
    lse = jnp.zeros((step, PAIR), F32)
    for h in range(2):
        own = (lane >= HEAD) if h else (lane < HEAD)
        s = mm_t(jnp.where(own, q, jnp.zeros_like(q)), k)
        if bias_ref is not None:
            s = s + bias_ref[at].astype(F32)
        peak = jnp.max(s, axis=1, keepdims=True)
        e = jnp.exp(s - peak)
        mass = jnp.sum(e, axis=1, keepdims=True)
        o = mm(e.astype(BF16), v)
        out = jnp.where(own, o / mass, out)
        lse = jnp.where(own, peak + jnp.log(mass), lse)
    o_ref[at, cols] = out.astype(BF16)
    lse_ref[at, cols] = lse


def attend_back_unit(q_ref, k_ref, v_ref, bias_ref, do_ref, o_ref, lse_ref, dq_ref, dk_acc, dv_acc, row, step, pair):
    at = pl.ds(pl.multiple_of(row, step), step)
    cols = pl.ds(pl.multiple_of(pair * PAIR, PAIR), PAIR)
    lane = lax.broadcasted_iota(jnp.int32, (1, PAIR), 1)
    k = k_ref[:, cols]
    v = v_ref[:, cols]
    q = q_ref[at, cols]
    do = do_ref[at, cols]
    both = do.astype(F32) * o_ref[at, cols].astype(F32)
    lse_pair = lse_ref[at, cols]
    dq = jnp.zeros((step, PAIR), F32)
    for h in range(2):
        own = (lane >= HEAD) if h else (lane < HEAD)
        q_h = jnp.where(own, q, jnp.zeros_like(q))
        do_h = jnp.where(own, do, jnp.zeros_like(do))
        delta = jnp.sum(jnp.where(own, both, 0.0), axis=1, keepdims=True)
        lse = lse_pair[:, h * HEAD : h * HEAD + 1]
        s = mm_t(q_h, k)
        if bias_ref is not None:
            s = s + bias_ref[at].astype(F32)
        e = jnp.exp(s - lse)
        dp = mm_t(do_h, v)
        ds = (e * (dp - delta)).astype(BF16)
        dq = jnp.where(own, mm(ds, k), dq)
        dk_acc[...] += t_mm(ds, q_h)
        dv_acc[...] += t_mm(e.astype(BF16), do_h)
    dq_ref[at, cols] = dq.astype(BF16) * BF16(HEAD**-0.5)


def attend_units(rows, width):
    step = min(256, rows)
    return rows // step, step, width // PAIR


def self_kernel(
    shape, arrive, leave, all_tok, w_qkv, vec, bias, enc, attn_in, attn_out, ffn_in,
    q, k, v, att, lse, all_enc, g_in, g_out, z_1, *sems,
):
    place, mail = open_kernel(shape, True, False, sems)
    n, rows, width = all_tok.shape
    three = g_in.shape[0]
    e = pair_gather_stages(mail, place, enc, all_enc)
    shards = [attn_in.at[pl.ds(attn_in.shape[0] - three, three)], attn_out]
    wholes = [g_in, g_out]
    w = block_stages(mail, place, shards, lambda i: [g.at[:, place.leaf, i] for g in wholes])
    zw = len(w)
    w += spread_stages(mail, place, wholes)
    f = block_stages(mail, place, [ffn_in], lambda i: [z_1.at[:, i]])
    w[0]()
    scale = HEAD**-0.5
    q[...] = ((mm(all_tok[place.block], w_qkv[0]) + vec[pl.ds(0, 1)]) * scale).astype(BF16)

    def project(i):
        x = all_tok[i]
        at = pl.ds(pl.multiple_of(i * rows, rows), rows)
        k[at] = mm(x, w_qkv[1]).astype(BF16)
        v[at] = (mm(x, w_qkv[2]) + vec[pl.ds(1, 1)]).astype(BF16)

    blocks, step, pairs = attend_units(rows, width)
    units = blocks * pairs
    t = lambda x: n + (x * units) // 12
    hooks, last = {}, n + units
    at_units(hooks, w[1 : zw - 1], [t(2)] * (zw - 2))
    at_units(hooks, f[:1] + w[zw - 1 : zw + 1], [t(2), t(3), t(3)])
    at_units(hooks, f[1:-1] + e[:1] + f[-1:], [t(7)] * (len(f) - 2) + [t(7), t(10)])
    tail = w[zw + 1 : -1] + e[1:-1] + w[-1:] + e[-1:]
    at_units(hooks, tail, [last] * len(tail))
    early = {at: stages for at, stages in hooks.items() if at < n}
    late = {at - n: stages for at, stages in hooks.items() if at >= n}
    hooked(n, project, early)
    leave(0, 1, 2)
    arrive()

    def unit(i):
        attend_unit(q, k, v, bias, att, lse, (i % blocks) * step, step, i // blocks)

    hooked(blocks * pairs, unit, late)
    mail.finish()


ROOT_HALF = 0.7071067811865476
NORM = 0.3989422804014327


def normed(v):
    centre = v - jnp.mean(v, axis=1, keepdims=True)
    inverse = lax.rsqrt(jnp.mean(centre * centre, axis=1, keepdims=True) + 1e-05)
    return centre * inverse, inverse


def normed_back(g, gain, hat, inverse):
    gx = g * gain
    mean_g = jnp.mean(gx, axis=1, keepdims=True)
    mean_gh = jnp.mean(gx * hat, axis=1, keepdims=True)
    return inverse * (gx - mean_g - hat * mean_gh)


def by_rows(rows, action):
    step = min(128, rows)

    def one(i, _):
        action(pl.ds(pl.multiple_of(i * step, step), step))
        return 0

    lax.fori_loop(0, rows // step, one, 0)


def row_sum(x):
    return jnp.sum(x, axis=0, keepdims=True)


def cross_kernel(
    shape, shifts, arrive, leave, att, all_tok, all_enc, w_in, w_out, vec, z_1, ffn_out, cot,
    hat1, inv1, first_low, cq, ck, cv, crossed, lse, g_1, g_2, my_cot, toks, *sems,
):
    place, mail = open_kernel(shape, True, True, sems)
    rows, width = cq.shape
    n, enc_rows, _ = all_enc.shape
    f = spread_stages(mail, place, [g_1], [z_1])
    w = block_stages(mail, place, [ffn_out], lambda i: [g_2.at[:, place.leaf, i]])
    zw = len(w)
    w += spread_stages(mail, place, [g_2])
    c = mirror_stages(mail, place, cot, my_cot)
    mine = mail.local(None, all_tok.at[place.block], toks)
    mine[0]()
    w[0]()
    f[0]()

    def project(i):
        x = all_enc[i]
        at = pl.ds(pl.multiple_of(i * enc_rows, enc_rows), enc_rows)
        ck[at] = mm(x, w_in[1]).astype(BF16)
        cv[at] = (mm(x, w_in[2]) + vec[pl.ds(4, 1)]).astype(BF16)

    hooked(n, project, {})
    leave(4, 5)
    arrive()
    mine[1]()
    scale = HEAD**-0.5

    def first(at):
        v = toks[at].astype(F32) + mm(att[at], w_out[0]) + vec[pl.ds(2, 1)]
        hat, inverse = normed(v)
        hat1[at] = hat
        inv1[at] = jnp.broadcast_to(inverse, (hat.shape[0], 128))
        low = (hat * vec[pl.ds(shifts, 1)] + vec[pl.ds(7, 1)]).astype(BF16)
        first_low[at] = low
        cq[at] = ((mm(low, w_in[0]) + vec[pl.ds(3, 1)]) * scale).astype(BF16)

    by_rows(rows, first)
    leave(0, 1, 2, 3)
    blocks, step, pairs = attend_units(rows, width)
    total = blocks * pairs
    t = lambda x: (x * total) // 12
    late = {}
    at_units(late, f[1:], [t(4), t(6)] + [t(10)] * (len(f) - 4) + [total])
    at_units(late, w[1 : zw - 1] + c[:1], [t(1)] * (zw - 2) + [t(3)])
    at_units(late, w[zw - 1 : zw + 1], [t(7)] * 2)
    at_units(late, w[zw + 1 :] + c[1:], [total] * (len(w) - zw))

    def unit(i):
        attend_unit(cq, ck, cv, None, crossed, lse, (i % blocks) * step, step, i // blocks)

    hooked(total, unit, late)
    mail.finish()


def ffn_kernel(
    shifts, arrive, leave, hat1, crossed, w_out, w1, w2, vec, b1, cot,
    out, gw1, gw2, gwo, g_crossed, g_pre2, sums, gb1,
    hat2, inv2, low2, acc, slope, hidden, g_pre3, g_ffn, acc2, g_cb,
):
    rows, width = crossed.shape
    wide = hidden.shape[1]
    piece = 512
    gain = lambda i: vec[pl.ds(shifts + i, 1)]
    shift = lambda i: vec[pl.ds(i, 1)]
    sums[...] = jnp.zeros_like(sums)

    def second(at):
        v = hat1[at] * gain(0) + shift(7) + mm(crossed[at], w_out[1]) + shift(5)
        hat, inverse = normed(v)
        hat2[at] = hat
        inv2[at] = jnp.broadcast_to(inverse, (hat.shape[0], 128))
        low2[at] = (hat * gain(1) + shift(8)).astype(BF16)

    by_rows(rows, second)
    arrive()
    acc[...] = jnp.zeros_like(acc)

    def up(j, _):
        cols = pl.ds(pl.multiple_of(j * piece, piece), piece)
        u = mm(low2[...], w1[:, cols]) + b1[:, cols]
        phi = 0.5 * (1.0 + lax.erf(u * ROOT_HALF))
        slope[:, cols] = phi + u * jnp.exp(-0.5 * u * u) * NORM
        h = (u * phi).astype(BF16)
        hidden[:, cols] = h
        acc[...] += mm(h, w2[cols])
        return 0

    lax.fori_loop(0, wide // piece, up, 0)

    def third(at):
        v = hat2[at] * gain(1) + shift(8) + acc[at] + shift(6)
        hat, inverse = normed(v)
        out[at] = (hat * gain(2) + shift(9)).astype(BF16)
        g = cot[at].astype(F32)
        sums[pl.ds(shifts + 2, 1)] += row_sum(g * hat)
        sums[pl.ds(9, 1)] += row_sum(g)
        back = normed_back(g, gain(2), hat, inverse)
        g_pre3[at] = back
        low = back.astype(BF16)
        g_ffn[at] = low
        sums[pl.ds(6, 1)] += row_sum(low.astype(F32))

    by_rows(rows, third)
    leave(0)
    acc2[...] = jnp.zeros_like(acc2)

    def down(j, _):
        cols = pl.ds(pl.multiple_of(j * piece, piece), piece)
        g = (mm_t(g_ffn[...], w2[cols]) * slope[:, cols]).astype(BF16)
        gb1[:, cols] = row_sum(g.astype(F32))
        gw2[cols] = t_mm(hidden[:, cols], g_ffn[...]).astype(BF16)
        gw1[:, cols] = t_mm(low2[...], g).astype(BF16)
        acc2[...] += mm_t(g, w1[:, cols])
        return 0

    lax.fori_loop(0, wide // piece, down, 0)
    leave(1, 2)

    def back_two(at):
        g = g_pre3[at] + acc2[at]
        hat = hat2[at]
        sums[pl.ds(shifts + 1, 1)] += row_sum(g * hat)
        sums[pl.ds(8, 1)] += row_sum(g)
        back = normed_back(g, gain(1), hat, inv2[at, :1])
        g_pre2[at] = back
        low = back.astype(BF16)
        g_cb[at] = low
        sums[pl.ds(5, 1)] += row_sum(low.astype(F32))
        g_crossed[at] = mm_t(low, w_out[1]).astype(BF16)

    by_rows(rows, back_two)
    gwo[...] = t_mm(crossed[...], g_cb[...]).astype(BF16)


def cross_back_kernel(
    shape, shifts, arrive, leave, cq, ck, cv, do, o, lse, first_low, hat1, inv1, all_enc, w_in, w_out, att, g_pre2, vec, sums_in, p_1, p_2, out_rows,
    g_in, g_wo, g_enc, g_att, g_pre1, sums, s_1, o_2, my_out, dq, dk, dv, g_br, dk_acc, dv_acc, *scratch,
):
    sems, scratch = scratch[:3], scratch[3:]
    place, mail = open_kernel(shape, True, True, sems)
    rows, width = cq.shape
    f_2, sum_2 = fold_stages(mail, place, p_2, scratch[:N_FOLD])
    f_1, sum_1 = fold_stages(mail, place, p_1, scratch[N_FOLD : 2 * N_FOLD])
    l_2 = line_stages(mail, place, sum_2, scratch[2 * N_FOLD], o_2)
    c = mirror_stages(mail, place, out_rows, my_out)
    f_2[0]()
    c[0]()
    blocks, step, pairs = attend_units(rows, width)
    total = blocks * pairs
    t = lambda x: (x * total) // 12
    hooks = {}
    more = len(f_1) - 5
    at_units(hooks, f_2[1:], [t(2), t(6), t(7), t(11)] + [t(11)] * more)
    at_units(hooks, l_2, [t(11), total + 6])
    at_units(hooks, f_1, [t(3), t(7), total, total + 2, total + 6] + [total + 6] * more)
    at_units(hooks, c[1:], [total + 6])

    def unit(i):
        first = i % blocks == 0

        @pl.when(first)
        def _():
            dk_acc[...] = jnp.zeros_like(dk_acc)
            dv_acc[...] = jnp.zeros_like(dv_acc)

        pair = i // blocks
        attend_back_unit(cq, ck, cv, None, do, o, lse, dq, dk_acc, dv_acc, (i % blocks) * step, step, pair)

        @pl.when(i % blocks == blocks - 1)
        def _():
            cols = pl.ds(pl.multiple_of(pair * PAIR, PAIR), PAIR)
            dk[:, cols] = dk_acc[...].astype(BF16)
            dv[:, cols] = dv_acc[...].astype(BF16)

    late = {at: hooks.pop(at) for at in list(hooks) if at >= total}
    hooked(total, unit, hooks)
    n, enc_rows, _ = all_enc.shape
    arrive()
    flat = all_enc.reshape(n * enc_rows, width)

    def query_grads():
        sums[...] = sums_in[...]
        sums[pl.ds(3, 1)] = row_sum(dq[...].astype(F32))
        sums[pl.ds(4, 1)] = row_sum(dv[...].astype(F32))
        g_in[0] = t_mm(first_low[...], dq[...]).astype(BF16)

    def key_grads():
        g_in[1] = t_mm(flat[...], dk[...]).astype(BF16)

    def value_grads():
        g_in[2] = t_mm(flat[...], dv[...]).astype(BF16)

    def encoder(i, _):
        at = pl.ds(pl.multiple_of(i * enc_rows, enc_rows), enc_rows)
        g_enc[i] = (mm_t(dk[at], w_in[1]) + mm_t(dv[at], w_in[2])).astype(BF16)
        return 0

    def back_one(at):
        g = g_pre2[at] + mm_t(dq[at], w_in[0])
        hat = hat1[at]
        sums[pl.ds(shifts, 1)] += row_sum(g * hat)
        sums[pl.ds(7, 1)] += row_sum(g)
        back = normed_back(g, vec[pl.ds(shifts, 1)], hat, inv1[at, :1])
        g_pre1[at] = back
        low = back.astype(BF16)
        g_br[at] = low
        sums[pl.ds(2, 1)] += row_sum(low.astype(F32))
        g_att[at] = mm_t(low, w_out[0]).astype(BF16)

    def out_grads():
        leave(0, 2, 3, 4)
        g_wo[...] = t_mm(att[...], g_br[...]).astype(BF16)

    steps = [
        query_grads,
        key_grads,
        value_grads,
        lambda: lax.fori_loop(0, n, encoder, 0),
        lambda: by_rows(rows, back_one),
        out_grads,
    ]
    for at, step_of in enumerate(steps):
        run(late.get(total + at, []))
        step_of()
    run(late[total + len(steps)])
    s_1[...] = sum_1[...]
    mail.finish()


def self_back_kernel(
    shape, arrive, leave, q, k, v, bias, do, o, lse, z_1, sums_in, all_tok, p_in, p_o0, p_o1, p_enc,
    dq, dk, dv, g_qkv, o_1, o_in, o_o0, o_o1, o_enc, sums, dk_acc, dv_acc, *scratch,
):
    sems, scratch = scratch[:3], scratch[3:]
    place, mail = open_kernel(shape, True, False, sems)
    rows, width = q.shape
    l_1 = line_stages(mail, place, z_1, scratch[0], o_1)
    rest = scratch[1:]
    f_in, sum_in = fold_stages(mail, place, p_in, rest[:N_FOLD])
    f_o0, sum_o0 = fold_stages(mail, place, p_o0, rest[N_FOLD : 2 * N_FOLD])
    f_o1, sum_o1 = fold_stages(mail, place, p_o1, rest[2 * N_FOLD : 3 * N_FOLD])
    rest = rest[3 * N_FOLD :]
    l_in = line_stages(mail, place, sum_in, rest[0], o_in)
    l_o0 = line_stages(mail, place, sum_o0, rest[1], o_o0)
    l_o1 = line_stages(mail, place, sum_o1, rest[2], o_o1)
    e = pair_sum_stages(mail, place, p_enc, rest[3:], o_enc)
    f_w = [functools.partial(run, three) for three in zip(f_in, f_o0, f_o1)]
    l_w = [functools.partial(run, three) for three in zip(l_in, l_o0, l_o1)]
    f_w[0]()
    l_1[0]()
    blocks, step, pairs = attend_units(rows, width)
    total = blocks * pairs
    t = lambda x: (x * total) // 12
    hooks = {}
    more = len(f_w) - 5
    at_units(hooks, f_w[1:], [t(1), t(4), t(5), t(7)] + [t(7)] * more)
    at_units(hooks, e[:-1], [t(2)] + [t(3)] * 2 + [t(4)] * (len(e) - 4))
    at_units(hooks, l_1[1:] + l_w[:1], [t(5), t(7)])
    at_units(hooks, e[-1:] + l_w[1:], [total] * 2)

    def unit(i):
        @pl.when(i % blocks == 0)
        def _():
            dk_acc[...] = jnp.zeros_like(dk_acc)
            dv_acc[...] = jnp.zeros_like(dv_acc)

        pair = i // blocks
        attend_back_unit(q, k, v, bias, do, o, lse, dq, dk_acc, dv_acc, (i % blocks) * step, step, pair)

        @pl.when(i % blocks == blocks - 1)
        def _():
            cols = pl.ds(pl.multiple_of(pair * PAIR, PAIR), PAIR)
            dk[:, cols] = dk_acc[...].astype(BF16)
            dv[:, cols] = dv_acc[...].astype(BF16)

    last = hooks.pop(total)
    hooked(total, unit, hooks)
    sums[...] = sums_in[...]
    sums[pl.ds(0, 1)] = row_sum(dq[...].astype(F32))
    sums[pl.ds(1, 1)] = row_sum(dv[...].astype(F32))
    leave(0, 1, 2)
    arrive()
    flat = all_tok.reshape(k.shape[0], width)
    g_qkv[0] = t_mm(all_tok[place.block], dq[...]).astype(BF16)
    g_qkv[1] = t_mm(flat[...], dk[...]).astype(BF16)
    g_qkv[2] = t_mm(flat[...], dv[...]).astype(BF16)
    run(last)
    mail.finish()


def closing_kernel(shape, p_qkv, p_small, dq, dk, dv, w_qkv, g_pre1, o_qkv, o_small, o_tok, p_tok, *scratch):
    sems, scratch = scratch[:3], scratch[3:]
    place, mail = open_kernel(shape, True, False, sems)
    f_q, sum_q = fold_stages(mail, place, p_qkv, scratch[:N_FOLD])
    f_s, sum_s = fold_stages(mail, place, p_small, scratch[N_FOLD : 2 * N_FOLD])
    rest = scratch[2 * N_FOLD :]
    l_q = line_stages(mail, place, sum_q, rest[0], o_qkv)
    l_s = line_stages(mail, place, sum_s, rest[1], o_small)
    t = pair_sum_stages(mail, place, p_tok, rest[2:], o_tok)
    a = [functools.partial(run, two) for two in zip(f_q, f_s)]
    b = [functools.partial(run, two) for two in zip(l_q, l_s)]
    n, rows, width = p_tok.shape
    step = min(128, rows)

    def terms(r):
        j = place.shard_of_rank(r)

        def some(i, _):
            at = pl.ds(pl.multiple_of(i * step, step), step)
            far = pl.ds(pl.multiple_of(j * rows + i * step, step), step)
            total = mm_t(dk[far], w_qkv[1]) + mm_t(dv[far], w_qkv[2])
            p_tok[j, at] = total.astype(BF16)

            @pl.when(j == place.block)
            def _():
                own = g_pre1[at] + mm_t(dq[at], w_qkv[0])
                p_tok[j, at] = (total + own).astype(BF16)

            return 0

        lax.fori_loop(0, rows // step, some, 0)

    a[0]()
    terms(n - 1)
    t[0]()
    for k in range(1, n):
        terms(n - 1 - k)
        t[k]()
        if k < len(a):
            a[k]()
    run(a[n:])
    run(b[:1])
    run(t[n:-1])
    t[-1]()
    run(b[1:])
    mail.finish()


def body(
    tokens, encoded, cotangent, parent, assignment, attn_in, attn_out, ffn_in, ffn_out, shifts, gains, ffn_bias
):
    shape = Shape(lax.axis_size("leaf"), lax.axis_size("path"))
    leafs, paths = shape.leafs, shape.paths
    devices = leafs * paths
    scale = HEAD ** (-0.5)
    tokens, encoded, cotangent = tokens[0], encoded[0], cotangent[0]
    rows, width = tokens.shape
    enc_rows = encoded.shape[0]
    hidden_width = ffn_in.shape[1]
    tree_rows, tree_enc = rows * paths, enc_rows * paths
    piece = shifts.shape[1]
    n_shift, n_gain, n_bias = shifts.shape[0], gains.shape[0], ffn_bias.shape[0]
    n_vec = n_shift + n_gain
    ffn_in, ffn_out = ffn_in[None], ffn_out[None]

    def sds(shape_, dtype=BF16):
        return jax.ShapeDtypeStruct(shape_, dtype)

    small = jnp.concatenate([shifts.reshape(-1), gains.reshape(-1), ffn_bias])
    small_rows = -(-small.shape[0] // 4096) * 16
    small = jnp.pad(small, (0, small_rows * 256 - small.shape[0])).reshape(1, small_rows, 256)
    blocks = parent.shape[1]
    ids = jnp.arange(blocks, dtype=jnp.int32)
    lanes = jnp.arange(128, dtype=jnp.int32)
    links = jnp.concatenate(
        [
            (parent[0][:, None] == lanes[None, :]) & (ids[:, None] != lanes[None, :]),
            assignment[0][:, None] == lanes[None, :],
        ]
    ).astype(F32)

    three = 3
    all_tok, g_small, w_qkv, bias = kernel_call(
        functools.partial(opening_kernel, shape, blocks.bit_length()),
        "opening",
        0,
        [tokens, small, attn_in, links],
        [ANY, ANY, ANY, VMEM],
        [
            sds((paths, rows, width)),
            sds((1, leafs, paths) + small.shape[1:]),
            sds((three, leafs, paths) + attn_in.shape[1:]),
            sds((rows, tree_rows)),
        ],
        [ANY, ANY, ANY, VMEM],
        mail_scratch()
        + [pltpu.VMEM(links.shape, F32), pltpu.VMEM((128, 128), F32), pltpu.VMEM((128, 128), F32)],
    )
    flat = g_small.reshape(devices, -1)
    vec = flat[:, : n_vec * piece].reshape(devices, n_vec, piece).transpose(1, 0, 2)
    vec = jnp.pad(vec.reshape(n_vec, width).astype(F32), ((0, -n_vec % 8), (0, 0)))
    b1 = flat[:, n_vec * piece : n_vec * piece + n_bias].reshape(1, hidden_width).astype(F32)
    w_qkv = w_qkv.reshape(three, width, width)

    rest_in = attn_in.shape[0] - three
    q, k, v, attended, self_mass, all_enc, w_in, w_out, z_1 = kernel_call(
        functools.partial(self_kernel, shape),
        "self_attention",
        1,
        [all_tok, w_qkv, vec, bias, encoded, attn_in, attn_out, ffn_in],
        [VMEM] * 4 + [ANY] * 4,
        [
            sds((rows, width)),
            sds((tree_rows, width)),
            sds((tree_rows, width)),
            sds((rows, width)),
            sds((rows, width), F32),
            sds((paths, enc_rows, width)),
            sds((rest_in, leafs, paths) + attn_in.shape[1:]),
            sds((attn_out.shape[0], leafs, paths) + attn_out.shape[1:]),
            sds((1, paths) + ffn_in.shape[1:]),
        ],
        [VMEM] * 5 + [ANY] * 4,
        mail_scratch(),
        late=(3,),
        early=(0, 1, 2),
    )
    w_in = w_in.reshape(rest_in, width, width)
    w_out = w_out.reshape(attn_out.shape[0], width, width)

    hat1, inv1, first_low, cq, ck, cv, crossed, cross_mass, w1, w2, my_cot = kernel_call(
        functools.partial(cross_kernel, shape, n_shift),
        "cross_attention",
        2,
        [attended, all_tok, all_enc, w_in, w_out, vec, z_1, ffn_out, cotangent],
        [VMEM, ANY] + [VMEM] * 4 + [ANY] * 3,
        [
            sds((rows, width), F32),
            sds((rows, 128), F32),
            sds((rows, width)),
            sds((rows, width)),
            sds((tree_enc, width)),
            sds((tree_enc, width)),
            sds((rows, width)),
            sds((rows, width), F32),
            sds((1, leafs, paths) + ffn_in.shape[1:]),
            sds((1, leafs, paths) + ffn_out.shape[1:]),
            sds((rows, width)),
        ],
        [VMEM] * 8 + [ANY] * 3,
        [pltpu.VMEM((rows, width), BF16)] + mail_scratch(),
        late=(0, 4),
        early=(0, 1, 2, 3, 4, 5),
    )
    w1 = w1.reshape(width, hidden_width)
    w2 = w2.reshape(hidden_width, width)
    vm = lambda s, dtype=BF16: pltpu.VMEM(s, dtype)
    output, g_w1, g_w2, g_wo1, g_crossed, g_pre2, sums, g_b1 = kernel_call(
        functools.partial(ffn_kernel, n_shift),
        "feed_forward",
        None,
        [hat1, crossed, w_out, w1, w2, vec, b1, my_cot],
        [VMEM] * 8,
        [
            sds((rows, width)),
            sds((width, hidden_width)),
            sds((hidden_width, width)),
            sds((width, width)),
            sds((rows, width)),
            sds((rows, width), F32),
            sds(vec.shape, F32),
            sds((1, hidden_width), F32),
        ],
        [VMEM] * 8,
        [
            vm((rows, width), F32),
            vm((rows, 128), F32),
            vm((rows, width)),
            vm((rows, width), F32),
            vm((rows, hidden_width), F32),
            vm((rows, hidden_width)),
            vm((rows, width), F32),
            vm((rows, width)),
            vm((rows, width), F32),
            vm((rows, width)),
        ],
        late=(3, 4, 7),
        early=(0, 1, 2),
    )

    def spread(g):
        return g.reshape(
            g.shape[0], shape.A, shape.B, 2, paths, g.shape[1] // devices, g.shape[2]
        )

    r1, r2 = ffn_in.shape[1:], ffn_out.shape[1:]
    g_rest, g_wo0, g_enc, g_att, g_pre1, sums, s_1, o_w2, output = kernel_call(
        functools.partial(cross_back_kernel, shape, n_shift),
        "cross_back",
        3,
        [
            cq, ck, cv, g_crossed, crossed, cross_mass, first_low, hat1, inv1, all_enc, w_in, w_out, attended,
            g_pre2, vec, sums, spread(g_w1[None]), spread(g_w2[None]), output,
        ],
        [VMEM] * 16 + [ANY] * 3,
        [
            sds((rest_in, width, width)),
            sds((width, width)),
            sds((paths, enc_rows, width)),
            sds((rows, width)),
            sds((rows, width), F32),
            sds(vec.shape, F32),
            sds((1, paths) + r1),
            sds((1,) + r2, F32),
            sds((rows, width)),
        ],
        [VMEM] * 8 + [ANY],
        [vm((rows, width)), vm((tree_enc, width)), vm((tree_enc, width)), vm((rows, width))]
        + [pltpu.VMEM((tree_enc, PAIR), F32)] * 2
        + mail_scratch()
        + fold_scratch(shape, 1, *r2, BF16)
        + fold_scratch(shape, 1, *r1, BF16)
        + line_scratch(shape, 1, *r2, BF16),
        late=(6, 7, 8, 9, 10, 11, 12, 13),
        early=(0, 2, 3, 4),
    )
    ri = attn_in.shape[1:]
    g_q, g_k, g_v, g_qkv, o_w1, o_in, o_o0, o_o1, o_enc, sums = kernel_call(
        functools.partial(self_back_kernel, shape),
        "self_back",
        4,
        [
            q, k, v, bias, g_att, attended, self_mass, s_1, sums, all_tok, spread(g_rest),
            spread(g_wo0[None]), spread(g_wo1[None]), g_enc,
        ],
        [VMEM] * 10 + [ANY] * 3 + [VMEM],
        [
            sds((rows, width)),
            sds((tree_rows, width)),
            sds((tree_rows, width)),
            sds((three, width, width)),
            sds((1,) + r1, F32),
            sds((rest_in,) + ri, F32),
            sds((1,) + ri, F32),
            sds((1,) + ri, F32),
            sds((enc_rows, width), F32),
            sds(vec.shape, F32),
        ],
        [VMEM] * 10,
        [pltpu.VMEM((tree_rows, PAIR), F32)] * 2
        + mail_scratch()
        + line_scratch(shape, 1, *r1, BF16)
        + fold_scratch(shape, rest_in, *ri, BF16)
        + fold_scratch(shape, 1, *ri, BF16)
        + fold_scratch(shape, 1, *ri, BF16)
        + line_scratch(shape, rest_in, *ri, BF16)
        + line_scratch(shape, 1, *ri, BF16)
        + line_scratch(shape, 1, *ri, BF16)
        + pair_sum_scratch(shape, enc_rows, width),
        late=(9,),
        early=(0, 1, 2),
    )
    g_vec = sums[:n_vec]
    g_small = jnp.concatenate(
        [
            g_vec.reshape(n_vec, devices, piece).transpose(1, 0, 2).reshape(devices, -1),
            g_b1.reshape(devices, n_bias),
        ],
        axis=1,
    )
    small_count = g_small.shape[1]
    g_small_rows = -(-small_count // 2048) * 8
    g_small = jnp.pad(g_small, ((0, 0), (0, g_small_rows * 256 - small_count)))
    p_small = g_small.reshape(1, shape.A, shape.B, 2, paths, g_small_rows, 256)
    o_qkv, o_small, o_tok = kernel_call(
        functools.partial(closing_kernel, shape),
        "closing",
        5,
        [spread(g_qkv), p_small, g_q, g_k, g_v, w_qkv, g_pre1],
        [ANY, ANY] + [VMEM] * 5,
        [
            sds((three,) + ri, F32),
            sds((1, g_small_rows, 256), F32),
            sds((rows, width), F32),
        ],
        [VMEM] * 3,
        [vm((paths, rows, width))]
        + mail_scratch()
        + fold_scratch(shape, three, *ri, BF16)
        + fold_scratch(shape, 1, g_small_rows, 256, F32)
        + line_scratch(shape, three, *ri, BF16)
        + line_scratch(shape, 1, g_small_rows, 256, F32)
        + pair_sum_scratch(shape, rows, width),
    )
    o_small = o_small.reshape(-1)
    o_vec = o_small[: n_vec * piece].reshape(n_vec, piece)
    return (
        output[None],
        o_tok[None],
        o_enc[None],
        jnp.concatenate([o_qkv, o_in]),
        jnp.concatenate([o_o0, o_o1]),
        o_w1[0],
        o_w2[0],
        o_vec[:n_shift],
        o_vec[n_shift:],
        o_small[n_vec * piece : n_vec * piece + n_bias],
    )


def solution(mesh):
    both = ("leaf", "path")
    rows = P("leaf", "path", None)
    weights = (P(None, both, None), P(None, both, None), P(both, None), P(both, None), P(None, both), P(None, both), P(both))
    return jax.shard_map(
        body,
        mesh=mesh,
        in_specs=(rows, rows, rows, P("leaf", None), P("leaf", None)) + weights,
        out_specs=(rows, rows, rows) + weights,
        check_vma=False,
    )
```

```python
import functools

import jax
import jax.numpy as jnp
from jax import lax
from jax.experimental import pallas as pl
from jax.experimental.pallas import tpu as pltpu
from jax.sharding import PartitionSpec as P

HEAD = 64
BLK = 128
PAIR = 2 * HEAD
MESH = pl.DeviceIdType.MESH
F32 = jnp.float32
BF16 = jnp.bfloat16
VMEM_OF = {"opening": 8}
ANY = pl.BlockSpec(memory_space=pl.ANY)
VMEM = pl.BlockSpec(memory_space=pltpu.VMEM)


class Shape:
    def __init__(self, leafs, paths):
        self.leafs, self.paths, self.half = leafs, paths, paths // 2
        outer = leafs // 2
        self.A = 2 if outer % 2 == 0 else 1
        self.B = outer // self.A


class Place:
    def __init__(self, shape):
        self.shape = shape
        self.leafs, self.paths, self.half = shape.leafs, shape.paths, shape.half
        self.A, self.B = shape.A, shape.B
        leaf = lax.axis_index("leaf")
        self.leaf, self.p = leaf, lax.axis_index("path")
        self.c = leaf % 2
        self.a = (leaf // 2) // self.B
        self.b = (leaf // 2) % self.B
        n = self.paths
        self.tree = jnp.where(self.p >= self.half, 1, 0)
        self.primary = self.c == self.tree
        self.pm = jnp.where(self.tree == 0, self.p, n - 1 - self.p)
        self.inward = jnp.where(self.tree == 0, 1, -1)
        self.own_rank = jnp.where(self.c == 0, self.p, n - 1 - self.p)
        self.block = jnp.where(self.primary, self.p, n - 1 - self.p)

    def leaf_at(self, a, b, c):
        return (a * self.B + b) * 2 + c

    def at_core(self):
        return (self.leaf_at(self.a, self.b, 1 - self.c), self.p)

    def at_a(self, a):
        return (self.leaf_at(a, self.b, self.c), self.p)

    def at_b(self, b):
        return (self.leaf_at(self.a, b, self.c), self.p)

    def at_p(self, p):
        return (self.leaf, clamp(p, self.paths))

    def at_mirror(self):
        return (self.leaf_at(self.a, self.b, 1 - self.c), self.paths - 1 - self.p)

    def shard_of_rank(self, rank):
        return jnp.where(self.tree == 0, rank, self.paths - 1 - rank)

    def line_p(self):
        return (self.paths, self.p, self.at_p)

    def line_a(self):
        return (self.A, self.a, self.at_a)

    def line_b(self):
        return (self.B, self.b, self.at_b)


def clamp(index, size):
    return jnp.clip(index, 0, size - 1)


def guarded(when, action):
    if when is None:
        action()
    else:

        @pl.when(when)
        def _():
            action()


def run(actions):
    for action in actions:
        action()


def greet(place, column, mirror):
    barrier = pltpu.get_barrier_semaphore()
    peers = 1

    def signal(to):
        pl.semaphore_signal(barrier, inc=1, device_id=to, device_id_type=MESH)

    signal(place.at_core())
    if column:
        for k in range(1, place.paths):
            for core in range(2):
                there = (place.p + k) % place.paths
                signal((place.leaf_at(place.a, place.b, core), there))
        peers = peers + 2 * (place.paths - 1)
    for size, pos, to in (place.line_a(), place.line_b()):
        if size == 1:
            continue
        if size == 2:
            signal(to(1 - pos))
            peers = peers + 1
            continue
        for step in (-1, 1):
            there = pos + step
            inside = (there >= 0) & (there < size)

            @pl.when(inside)
            def _():
                signal(to(clamp(there, size)))

            peers = peers + jnp.where(inside, 1, 0)
    if mirror and not column:

        @pl.when(jnp.logical_not(place.primary))
        def _():
            signal(place.at_mirror())

        peers = peers + jnp.where(place.primary, 0, 1)
    pl.semaphore_wait(barrier, peers)


class Mail:
    def __init__(self, send_sems, recv_sems, own_sems):
        self.send_sems, self.recv_sems, self.own_sems = send_sems, recv_sems, own_sems
        self.sends = self.recvs = self.owns = 0
        self.sent = []

    def new_recv(self, count=1):
        self.recvs += count
        return self.recvs - count

    def send(self, when, src, dst, to, recv):
        k = self.sends
        self.sends += 1
        copy = pltpu.make_async_remote_copy(
            src_ref=src,
            dst_ref=dst,
            send_sem=self.send_sems.at[k],
            recv_sem=self.recv_sems.at[recv],
            device_id=to,
            device_id_type=MESH,
        )
        self.sent.append((when, copy))
        return functools.partial(guarded, when, copy.start)

    def hear(self, when, landing, to, recv):
        copy = pltpu.make_async_remote_copy(
            src_ref=landing,
            dst_ref=landing,
            send_sem=self.send_sems.at[0],
            recv_sem=self.recv_sems.at[recv],
            device_id=to,
            device_id_type=MESH,
        )
        return functools.partial(guarded, when, copy.wait_recv)

    def post(self, when, src, dst, to, hear_when, landing):
        k = self.new_recv()
        return self.send(when, src, dst, to, k), self.hear(hear_when, landing, to, k)

    def local(self, when, src, dst):
        k = self.owns
        self.owns += 1
        copy = pltpu.make_async_copy(src, dst, self.own_sems.at[k])
        return functools.partial(guarded, when, copy.start), functools.partial(guarded, when, copy.wait)

    def finish(self):
        for when, copy in self.sent:
            guarded(when, copy.wait_send)


def mail_scratch(count=160, own=24):
    return [
        pltpu.SemaphoreType.DMA((count,)),
        pltpu.SemaphoreType.DMA((count,)),
        pltpu.SemaphoreType.DMA((own,)),
    ]


def flood(mail, line, views, first=None):
    size, pos, to = line
    steps = []
    if size == 1:
        return steps
    first = first if first is not None else views(pos)
    if size == 2:
        jobs = [
            mail.post(None, s, d, to(1 - pos), None, w)
            for s, d, w in zip(first, views(pos), views(1 - pos))
        ]
        return [([j[0] for j in jobs], [j[1] for j in jobs])]
    for step in range(1, size):
        starts, waits = [], []
        for sign in (1, -1):
            item = pos - sign * (step - 1)
            there = pos + sign
            when = (there >= 0) & (there < size) & (item >= 0) & (item < size)
            heard = pos - sign * step
            hear_when = (heard >= 0) & (heard < size)
            item_c = clamp(item, size)
            sources = first if step == 1 else views(item_c)
            for s, d, w in zip(sources, views(item_c), views(clamp(heard, size))):
                start, wait = mail.post(when, s, d, to(clamp(there, size)), hear_when, w)
                starts.append(start)
                waits.append(wait)
        steps.append((starts, waits))
    return steps


def chain(steps, first_starts=()):
    stages, pending = [], []
    for k, (starts, waits) in enumerate(steps):
        stages.append(functools.partial(run, pending + (list(first_starts) if k == 0 else []) + starts))
        pending = waits
    stages.append(functools.partial(run, pending))
    return stages


def half_columns(ref, leaf, h):
    width = ref.shape[-1] // 2
    return ref.at[:, leaf, :, :, pl.ds(h * width, width)]


def block_stages(mail, place, shards, block_views):
    n = place.paths
    own = [mail.local(None, s, d) for s, d in zip(shards, block_views(place.p))]
    starts, waits = [], []
    lands = [mail.new_recv(n) for _ in shards]
    relay = n == 4
    for k in (1, 3, 2) if relay else range(1, n):
        there = (place.p + k) % n
        near = None
        if relay and k != 2:
            near = (there - place.p != 3) & (place.p - there != 3)
        for s, d, w, land in zip(shards, block_views(place.p), block_views(there), lands):
            starts.append(mail.send(near, s, d, place.at_p(there), land + place.p))
            waits.append((there, mail.hear(None, w, place.at_p(there), land + there)))
    starts += [o[0] for o in own]
    ends = [o[1] for o in own]
    if not relay:
        return [functools.partial(run, starts), functools.partial(run, [w[1] for w in waits] + ends)]
    middle = (place.p == 1) | (place.p == 2)
    passed = jnp.where(place.p == 1, 3, 0)
    to = place.at_p(jnp.where(place.p == 1, 0, 3))
    passes = []
    for item, land in zip(block_views(passed), lands):
        passes.append(mail.hear(middle, item, to, land + passed))
        passes.append(mail.send(middle, item, item, to, land + passed))
    for there, wait in waits:
        ends.append(functools.partial(guarded, jnp.logical_not(middle & (there == passed)), wait))
    return [functools.partial(run, starts), functools.partial(run, passes), functools.partial(run, ends)]


def path_half(ref, h):
    n = ref.shape[1] // 2
    return ref.at[:, pl.ds(h * n, n)]


def spread_stages(mail, place, wholes, blocks=None):
    if (place.A, place.B) != (2, 2):
        return spread_lines(mail, place, wholes, blocks)
    a, b, c = place.a, place.b, place.c
    at = lambda w, a, b, c: w.at[:, place.leaf_at(a, b, c)]
    to_a, to_b, to_core = place.at_a(1 - a), place.at_b(1 - b), place.at_core()
    own = []
    sources = [at(w, a, b, c) for w in wholes]
    if blocks is not None:
        own = [mail.local(None, x, s) for x, s in zip(blocks, sources)]
        sources = list(blocks)
    urgent, calm, relay, near, far = [], [], [], [], []
    for w, s in zip(wholes, sources):
        mine, from_a, from_b = at(w, a, b, c), at(w, 1 - a, b, c), at(w, a, 1 - b, c)
        from_ab = at(w, 1 - a, 1 - b, c)

        def post(src, dst, to, landing, h):
            return mail.post(
                None, path_half(src, h), path_half(dst, h), to, None, path_half(landing, h)
            )

        urgent += [post(s, mine, to_b, from_b, 0), post(s, mine, to_a, from_a, 1)]
        calm += [post(s, mine, to_b, from_b, 1), post(s, mine, to_a, from_a, 0)]
        relay += [post(from_b, from_b, to_a, from_ab, 0), post(from_a, from_a, to_b, from_ab, 1)]
        near.append(mail.post(None, s, mine, to_core, None, at(w, a, b, 1 - c)))
        for x, y, l in ((1 - a, b, near), (a, 1 - b, near), (1 - a, 1 - b, far)):
            l.append(mail.post(None, at(w, x, y, c), at(w, x, y, c), to_core, None, at(w, x, y, 1 - c)))
    start = lambda jobs: run([j[0] for j in jobs])
    wait = lambda jobs: run([j[1] for j in jobs])
    first = near[::3]
    second = [j for k, j in enumerate(near) if k % 3]

    def opening():
        start(urgent)
        start(calm)
        start(first)
        run([o[0] for o in own])

    def passing():
        wait(urgent)
        start(relay)

    def sharing():
        wait(calm)
        run([o[1] for o in own])
        start(second)

    def ending():
        wait(relay)
        start(far)

    return [opening, passing, sharing, ending, lambda: wait(near + far)]


def spread_lines(mail, place, wholes, blocks=None):
    A, B, c = place.A, place.B, place.c

    def of_b(h, across_a):
        ays = range(A) if across_a else [place.a]
        return lambda i: [half_columns(w, place.leaf_at(a, i, c), h) for a in ays for w in wholes]

    def of_a(h, across_b):
        bees = range(B) if across_b else [place.b]
        return lambda i: [half_columns(w, place.leaf_at(i, b, c), h) for b in bees for w in wholes]

    own = []
    firsts = [None, None]
    sources = [w.at[:, place.leaf] for w in wholes]
    if blocks is not None:
        own = [mail.local(None, x, w.at[:, place.leaf]) for x, w in zip(blocks, wholes)]
        firsts = [
            [x.at[:, :, :, pl.ds(h * (x.shape[-1] // 2), x.shape[-1] // 2)] for x in blocks]
            for h in range(2)
        ]
        sources = list(blocks)
    line_a, line_b = place.line_a(), place.line_b()
    phases = [
        (flood(mail, line_b, of_b(0, False), firsts[0]), flood(mail, line_a, of_a(1, False), firsts[1])),
        (flood(mail, line_a, of_a(0, True)), flood(mail, line_b, of_b(1, True))),
    ]
    core = [
        mail.post(
            None,
            s,
            w.at[:, place.leaf],
            place.at_core(),
            None,
            w.at[:, place.leaf_at(place.a, place.b, 1 - c)],
        )
        for s, w in zip(sources, wholes)
    ]
    rest = []
    for offset in range(1, A * B):
        spot = (place.a * B + place.b + offset) % (A * B)
        for w in wholes:
            mine, other = w.at[:, spot * 2 + c], w.at[:, spot * 2 + 1 - c]
            rest.append(mail.post(None, mine, mine, place.at_core(), None, other))
    steps = []
    opening = [o[0] for o in own] + [j[0] for j in core]
    for n_phase, phase in enumerate(phases):
        before = [o[1] for o in own] if n_phase == 1 else []
        for s in range(max(len(f) for f in phase)):
            starts, waits = list(before), []
            before = []
            for f in phase:
                if s < len(f):
                    starts += f[s][0]
                    waits += f[s][1]
            steps.append((starts + opening, waits))
            opening = []
    steps.append((opening + [j[0] for j in rest], [j[1] for j in core + rest]))
    return chain(steps)


def pair_gather_stages(mail, place, shard, whole, pieces=1):
    n, h = place.paths, place.half
    rows = shard.shape[0] // (2 * pieces)
    part = lambda ref, u, s: ref.at[pl.ds(pl.multiple_of((u * pieces + s) * rows, rows), rows)]
    half = lambda ref, u: ref.at[pl.ds(pl.multiple_of(u * pieces * rows, rows), pieces * rows)]
    lands = [mail.new_recv(n) for _ in range(pieces)]
    core_lands = mail.new_recv(n)
    own = mail.local(place.primary, shard, whole.at[place.p])
    first = jnp.where(place.c == 0, 0, h)
    edge = jnp.where(place.c == 0, h - 1, h)
    starts = []
    for s in range(pieces):
        for u in range(2):
            for q in range(h):
                q = first + q
                to = (place.leaf_at(place.a, place.b, u), q)
                near = place.primary & jnp.logical_not((q == place.p) & (place.c == u))
                away = near | (jnp.logical_not(place.primary) & (q == edge))
                starts.append(
                    mail.send(
                        away, part(shard, u, s), part(whole.at[place.p], u, s), to, lands[s] + place.p
                    )
                )
    k = mail.new_recv()
    mate = whole.at[place.p]
    starts.append(
        mail.send(place.primary, half(shard, place.c), half(mate, place.c), place.at_core(), k)
    )
    starts.append(own[0])
    stages = [functools.partial(run, starts)]
    outward = place.at_p(place.p - place.inward)
    for s in range(pieces):
        for r in list(range(h, n)) + list(range(h)):
            j = place.shard_of_rank(r)
            item = part(whole.at[j], place.c, s)
            got = jnp.logical_not(place.primary & (place.p == j))
            actions = [mail.hear(got, item, place.at_core(), lands[s] + j)]
            if r >= h and h > 1:
                actions.append(mail.send(place.pm > 0, item, item, outward, lands[s] + j))
            if s == pieces - 1:
                whole_half = half(whole.at[j], place.c)
                actions.append(
                    mail.send(
                        jnp.logical_not(place.p == j),
                        whole_half,
                        whole_half,
                        place.at_core(),
                        core_lands + j,
                    )
                )
            stages.append(functools.partial(run, actions))
    rest = [own[1]]
    rest.append(
        mail.hear(jnp.logical_not(place.primary), half(mate, 1 - place.c), place.at_core(), k)
    )
    for r in range(n):
        j = place.shard_of_rank(r)
        rest.append(
            mail.hear(
                jnp.logical_not(place.p == j),
                half(whole.at[j], 1 - place.c),
                place.at_core(),
                core_lands + j,
            )
        )
    stages.append(functools.partial(run, rest))
    return stages


def mirror_stages(mail, place, own, mine):
    local = mail.local(place.primary, own, mine)
    other = jnp.logical_not(place.primary)
    start, wait = mail.post(other, own, mine, place.at_mirror(), other, mine)
    return [lambda: run([local[0], start]), lambda: run([local[1], wait])]


def add_rows(dst, src):
    lead = dst.shape[:-2]
    total = 1
    for extent in lead:
        total *= extent

    def body(i, _):
        index = []
        rest = i
        for extent in reversed(lead):
            index.insert(0, rest % extent)
            rest = rest // extent
        index = tuple(index)
        dst[index] = dst[index] + src[index]
        return 0

    if total == 1:
        body(0, 0)
    else:
        lax.fori_loop(0, total, body, 0)


def add_tall(dst, src):
    rows = dst.shape[0]
    step = 64 if rows % 64 == 0 else rows

    def body(r, _):
        at = pl.ds(pl.multiple_of(r * step, step), step)
        dst[at] = dst[at] + src[at]
        return 0

    lax.fori_loop(0, rows // step, body, 0)


def shift_sum(mail, line, mine, slots_up, slots_down, add):
    size, pos, to = line
    if size == 1:
        return []
    if size == 2:
        jobs = [
            mail.post(None, s, slot, to(1 - pos), None, slot)
            for s, slot in zip(mine(1 - pos), slots_up[0])
        ]

        def end():
            for job, dst, slot in zip(jobs, mine(pos), slots_up[0]):
                job[1]()
                add(dst, slot)

        return [lambda: run([j[0] for j in jobs]), end]
    stages = []
    for k in range(size - 1):
        early, actions = [], []
        for sign, slots in ((1, slots_up), (-1, slots_down)):
            dest = size - 1 - k if sign == 1 else k
            when = (pos < dest) if sign == 1 else (pos > dest)
            hear_when = (
                ((pos > 0) & (pos <= dest)) if sign == 1 else ((pos < size - 1) & (pos >= dest))
            )
            there = clamp(pos + sign, size)
            jobs = [
                mail.post(when, s, slot, to(there), None, slot)
                for s, slot in zip(mine(dest), slots[k])
            ]

            def take(jobs=jobs, dst_refs=mine(dest), slot_refs=slots[k]):
                for job, dst, slot in zip(jobs, dst_refs, slot_refs):
                    job[1]()
                    add(dst, slot)

            end = (pos == 0) if sign == 1 else (pos == size - 1)
            starts = functools.partial(run, [job[0] for job in jobs])
            early.append(functools.partial(guarded, end, starts))
            actions.append(functools.partial(guarded, hear_when, take))
            actions.append(functools.partial(guarded, jnp.logical_not(end), starts))
        stages.append(functools.partial(run, early + actions))
    return stages


def fold_scratch(shape, k, R, C, dtype):
    if (shape.A, shape.B) != (2, 2):
        return fold_lines_scratch(shape, k, R, C, dtype)
    block = (k, 2, 2, shape.paths, R, C)
    halves = (2, k, shape.paths // 2, R, C)
    return [pltpu.VMEM(block, dtype)] * 2 + [pltpu.VMEM(halves, dtype)] * 3 + [pltpu.VMEM((1, R, C), dtype)]


def fold_lines_scratch(shape, k, R, C, dtype):
    A, B, paths = shape.A, shape.B, shape.paths
    nb, na = max(B - 1, 1) * (2 if B > 2 else 1), max(A - 1, 1)
    return [
        pltpu.VMEM((k, A, B, paths, R, C), dtype),
        pltpu.VMEM((k, A, B, paths, R, C), dtype),
        pltpu.VMEM((nb, k, A, paths, R, C // 2), dtype),
        pltpu.VMEM((na, k, paths, R, C // 2), dtype),
        pltpu.VMEM((na, k, B, paths, R, C // 2), dtype),
        pltpu.VMEM((nb, k, paths, R, C // 2), dtype),
    ]


N_FOLD = 6


def up_down(ref, size):
    if size <= 2:
        return [[ref.at[0]]], None
    return (
        [[ref.at[k]] for k in range(size - 1)],
        [[ref.at[size - 1 + k]] for k in range(size - 1)],
    )


def fold_stages(mail, place, partial, scratch):
    if (place.A, place.B) != (2, 2):
        return fold_lines(mail, place, partial, scratch)
    a, b, c = place.a, place.b, place.c
    acc, got, far, direct, relayed = scratch[:5]
    own = mail.local(None, partial.at[:, :, :, c], acc)
    core = mail.post(None, partial.at[:, :, :, 1 - c], got, place.at_core(), None, got)
    to_a, to_b = place.at_a(1 - a), place.at_b(1 - b)
    of_a, of_b, of_ab = acc.at[:, 1 - a, b], acc.at[:, a, 1 - b], acc.at[:, 1 - a, 1 - b]
    mine = acc.at[:, a, b]

    def post(src, h, slot, to):
        return mail.post(None, path_half(src, h), slot, to, None, slot)

    urgent = [post(of_ab, 0, far.at[0], to_b), post(of_ab, 1, far.at[1], to_a)]
    calm = [post(of_b, 0, direct.at[0], to_b), post(of_a, 1, direct.at[1], to_a)]
    late = [post(of_a, 0, relayed.at[0], to_a), post(of_b, 1, relayed.at[1], to_b)]

    def join():
        own[1]()
        core[1]()
        add_rows(of_ab, got.at[:, 1 - a, 1 - b])
        run([j[0] for j in urgent])
        add_rows(of_b, got.at[:, a, 1 - b])
        calm[0][0]()
        add_rows(of_a, got.at[:, 1 - a, b])
        calm[1][0]()
        add_rows(mine, got.at[:, a, b])

    def passing():
        urgent[0][1]()
        add_rows(path_half(of_a, 0), far.at[0])
        late[0][0]()
        urgent[1][1]()
        add_rows(path_half(of_b, 1), far.at[1])
        late[1][0]()

    def taking():
        for h in range(2):
            calm[h][1]()
            add_rows(path_half(mine, h), direct.at[h])

    def ending():
        for h in range(2):
            late[h][1]()
            add_rows(path_half(mine, h), relayed.at[h])

    return [lambda: run([own[0], core[0]]), join, passing, taking, ending], mine


def fold_lines(mail, place, partial, scratch):
    c = place.c
    acc, got, sb0, sa0, sa1, sb1 = scratch
    own = mail.local(None, partial.at[:, :, :, c], acc)
    core = mail.post(None, partial.at[:, :, :, 1 - c], got, place.at_core(), None, got)
    width = acc.shape[-1] // 2
    left, right = pl.ds(0, width), pl.ds(width, width)

    def join():
        own[1]()
        core[1]()
        add_rows(acc, got)

    line_a, line_b = place.line_a(), place.line_b()
    h0_b = shift_sum(
        mail, line_b, lambda d: [acc.at[:, :, d, :, :, left]], *up_down(sb0, place.B), add_rows
    )
    h1_a = shift_sum(
        mail, line_a, lambda d: [acc.at[:, d, :, :, :, right]], *up_down(sa1, place.A), add_rows
    )
    h0_a = shift_sum(
        mail, line_a, lambda d: [acc.at[:, d, place.b, :, :, left]], *up_down(sa0, place.A), add_rows
    )
    h1_b = shift_sum(
        mail, line_b, lambda d: [acc.at[:, place.a, d, :, :, right]], *up_down(sb1, place.B), add_rows
    )

    def beside(one, two):
        return [
            functools.partial(run, [s[k] for s in (one, two) if k < len(s)])
            for k in range(max(len(one), len(two)))
        ]

    def joined(first, second):
        if not first or not second:
            return first + second
        return first[:-1] + [functools.partial(run, [first[-1], second[0]])] + second[1:]

    stages = joined(
        [lambda: run([own[0], core[0]]), join], beside(h0_b, h1_a)
    )
    stages = joined(stages, beside(h0_a, h1_b))
    return stages, acc.at[:, place.a, place.b]


def line_scratch(shape, k, R, C, dtype):
    return [pltpu.VMEM((max(shape.paths - 1, 1), k, R, C), dtype)]


def line_stages(mail, place, sums, slots, out):
    n = place.paths
    jobs = []
    for k in range(1, n):
        there = (place.p + k) % n
        slot = slots.at[k - 1]
        jobs.append(mail.post(None, sums.at[:, there], slot, place.at_p(there), None, slot))

    def end():
        run([j[1] for j in jobs])
        for j in range(out.shape[0]):
            total = sums[j, place.p].astype(F32)
            for k in range(n - 1):
                total = total + slots[k, j].astype(F32)
            out[j] = total.astype(out.dtype)

    return [lambda: run([j[0] for j in jobs]), end]


def pair_sum_scratch(shape, R, C):
    return [
        pltpu.VMEM((shape.paths, R // 2, C), BF16),
        pltpu.VMEM((shape.paths, R // 2, C), BF16),
        pltpu.VMEM((shape.half, R, C), BF16),
    ]


def pair_sum_stages(mail, place, part, scratch, out):
    n, h = place.paths, place.half
    core_slot, in_slot, landing = scratch
    rows = part.shape[1] // 2
    half = lambda ref, u: ref.at[pl.ds(pl.multiple_of(u * rows, rows), rows)]
    lands = [mail.new_recv(2) for _ in range(h)]
    inner = place.at_p(place.p + place.inward)
    sends, sums, passes = [], [], []
    for r in range(n - 1, -1, -1):
        j = place.shard_of_rank(r)
        item = part.at[j]
        mine = half(item, place.c)
        send, hear = mail.post(
            None, half(item, 1 - place.c), core_slot.at[r], place.at_core(), None, core_slot.at[r]
        )
        owner = (place.leaf_at(place.a, place.b, place.tree), j)
        leave = []
        if r >= h:
            k = mail.new_recv()
            slot = in_slot.at[r]
            in_send = mail.send(place.pm < h - 1, mine, slot, inner, k)
            in_hear = mail.hear(None, slot, place.at_core(), k)
            go = mail.send(
                place.pm == h - 1, mine, half(landing.at[h - 1], place.c), owner, lands[h - 1] + place.c
            )

            def inward(in_send=in_send, in_hear=in_hear, mine=mine, slot=slot, go=go):
                if h > 1:

                    @pl.when(place.pm > 0)
                    def _():
                        in_hear()
                        add_tall(mine, slot)

                    in_send()
                go()

            passes.append(inward)
        else:
            away = jnp.logical_not(place.primary & (place.p == j))
            for q in range(h):
                leave.append(
                    mail.send(
                        away & (place.pm == q),
                        mine,
                        half(landing.at[q], place.c),
                        owner,
                        lands[q] + place.c,
                    )
                )

        def settle(hear=hear, mine=mine, slot=core_slot.at[r], leave=leave):
            hear()
            add_tall(mine, slot)
            run(leave)

        sends.append(send)
        sums.append(settle)
    stages = [[sends[0]]]
    for k in range(1, n):
        stages.append([sends[k], sums[k - 1]])
    stages.append([sums[n - 1]])
    for k, step in enumerate(passes):
        stages[k + 1].append(step)

    def end():
        for q in range(h):
            for u in range(2):
                self_made = place.primary & (place.own_rank == q) & (place.c == u)
                comes = jnp.logical_not(self_made) & (place.primary | (q == h - 1))
                mail.hear(comes, half(landing.at[q], u), place.at_core(), lands[q] + u)()

        step = 64 if rows % 64 == 0 else rows
        for u in range(2):

            def body(i, _, u=u):
                at = pl.ds(pl.multiple_of(u * rows + i * step, step), step)

                @pl.when(place.primary)
                def _():
                    for q in range(h):
                        self_made = (place.own_rank == q) & (place.c == u)
                        term = jnp.where(self_made, part[place.p, at], landing[q, at]).astype(F32)
                        total = term if q == 0 else total + term
                    out[at] = total

                @pl.when(jnp.logical_not(place.primary))
                def _():
                    out[at] = landing[h - 1, at].astype(F32)

                return 0

            lax.fori_loop(0, rows // step, body, 0)

    return [functools.partial(run, x) for x in stages] + [end]


def at_units(hooks, stages, units):
    for stage, unit in zip(stages, units, strict=True):
        hooks.setdefault(unit, []).append(stage)


def hooked(count, unit, hooks):
    def body(i, _):
        for at, stages in hooks.items():
            if at < count:

                @pl.when(i == at)
                def _():
                    run(stages)

        unit(i)
        return 0

    lax.fori_loop(0, count, body, 0)
    for at in sorted(hooks):
        if at >= count:
            run(hooks[at])


def kernel_call(kernel, name, collective_id, ins, in_specs, outs, out_specs, scratch, late=(), early=()):
    n_in, n_out = len(ins), len(outs)
    in_specs, out_specs = list(in_specs), list(out_specs)
    for i in late:
        in_specs[i] = ANY
    for i in early:
        out_specs[i] = ANY
    held = [pltpu.VMEM(ins[i].shape, ins[i].dtype) for i in late]
    held += [pltpu.VMEM(outs[i].shape, outs[i].dtype) for i in early]
    moving = [pltpu.SemaphoreType.DMA((len(held),))] if held else []

    def whole(*refs):
        refs, extra = list(refs[: len(refs) - len(held) - 1]), refs[len(refs) - len(held) - 1 :]
        buffers, sems = extra[:-1], extra[-1]
        loads, stores = [], {}
        for k, i in enumerate(late):
            loads.append(pltpu.make_async_copy(refs[i], buffers[k], sems.at[k]))
            refs[i] = buffers[k]
        for k, i in enumerate(early):
            k = len(late) + k
            stores[i] = pltpu.make_async_copy(buffers[k], refs[n_in + i], sems.at[k])
            refs[n_in + i] = buffers[k]
        for load in loads:
            load.start()

        def arrive():
            for load in loads:
                load.wait()

        def leave(*which):
            for i in which:
                stores[i].start()

        kernel(arrive, leave, *refs)
        for store in stores.values():
            store.wait()

    limit = VMEM_OF.get(name, 62) * 1024 * 1024
    if collective_id is None:
        params = pltpu.CompilerParams(vmem_limit_bytes=limit)
    else:
        params = pltpu.CompilerParams(
            collective_id=collective_id, has_side_effects=True, vmem_limit_bytes=limit
        )
    return pl.pallas_call(
        whole if held else kernel,
        out_shape=outs,
        in_specs=in_specs,
        out_specs=out_specs,
        scratch_shapes=list(scratch) + held + moving,
        compiler_params=params,
        name=name,
    )(*ins)


def dot(x, y, contract):
    return lax.dot_general(x, y, (contract, ((), ())), preferred_element_type=F32)


def mm(x, w):
    return dot(x, w, ((1,), (0,)))


def mm_t(x, w):
    return dot(x, w, ((1,), (1,)))


def t_mm(x, y):
    return dot(x, y, ((0,), (0,)))


def open_kernel(shape, column, mirror, sems):
    place = Place(shape)
    greet(place, column, mirror)
    return place, Mail(*sems)


def opening_kernel(shape, turns, tok, small, attn_in, links, all_tok, g_small, g_qkv, bias, *scratch):
    sems, (links_got, reach, spot) = scratch[:3], scratch[3:]
    place, mail = open_kernel(shape, True, False, sems)
    three = g_qkv.shape[0]
    to_core = mail.post(None, links, links_got, place.at_core(), None, links_got)
    to_core[0]()
    shards = [small, attn_in.at[pl.ds(0, three)]]
    wholes = [g_small, g_qkv]
    weights = block_stages(
        mail, place, shards, lambda i: [w.at[:, place.leaf, i] for w in wholes]
    )
    spread = spread_stages(mail, place, wholes)
    tokens = pair_gather_stages(mail, place, tok, all_tok)
    weights[0]()
    tokens[0]()
    to_core[1]()

    count = links.shape[0] // 2
    mine = jnp.where(place.primary, links[...], links_got[...])
    reach[...] = jnp.zeros_like(reach)
    spot[...] = jnp.zeros_like(spot)
    reach[pl.ds(0, count)] = mine[:count]
    spot[pl.ds(0, count)] = mine[count:]
    for _ in range(turns):
        r = reach[...]
        reach[...] = jnp.minimum(r + mm(r.astype(BF16), r.astype(BF16)), 1.0)
    placed = spot[...].astype(BF16)
    linked = mm_t(mm(placed, reach[...].astype(BF16)).astype(BF16), placed).astype(BF16)
    rows, keys = bias.shape
    step = min(128, rows)

    def fill(i, _):
        first = i * step
        at = pl.ds(pl.multiple_of(first, step), step)
        q_slot = (place.block * rows + first + lax.broadcasted_iota(jnp.int32, (step, 128), 0)) // BLK
        pick_q = (q_slot == lax.broadcasted_iota(jnp.int32, (step, 128), 1)).astype(F32)
        own = mm(pick_q.astype(BF16), linked).astype(BF16)
        k_slot = lax.broadcasted_iota(jnp.int32, (128, keys), 1) // BLK
        pick_k = (k_slot == lax.broadcasted_iota(jnp.int32, (128, keys), 0)).astype(F32)
        seen = mm(own, pick_k.astype(BF16))
        q_at = place.block * rows + first + lax.broadcasted_iota(jnp.int32, (step, keys), 0)
        k_at = lax.broadcasted_iota(jnp.int32, (step, keys), 1)
        inside = (q_at // BLK == k_at // BLK) & (k_at <= q_at)
        bias[at] = jnp.where((seen > 0.5) | inside, 0.0, -1e30).astype(bias.dtype)
        return 0

    run(weights[1:] + spread[:1])
    run(tokens[1:-3])
    spread[1]()
    lax.fori_loop(0, rows // step, fill, 0)
    run(tokens[-3:-1])
    run(spread[2:])
    tokens[-1]()
    mail.finish()


def attend_unit(q_ref, k_ref, v_ref, bias_ref, o_ref, lse_ref, row, step, pair):
    at = pl.ds(pl.multiple_of(row, step), step)
    cols = pl.ds(pl.multiple_of(pair * PAIR, PAIR), PAIR)
    lane = lax.broadcasted_iota(jnp.int32, (1, PAIR), 1)
    q = q_ref[at, cols]
    k = k_ref[:, cols]
    v = v_ref[:, cols]
    out = jnp.zeros((step, PAIR), F32)
    lse = jnp.zeros((step, PAIR), F32)
    for h in range(2):
        own = (lane >= HEAD) if h else (lane < HEAD)
        s = mm_t(jnp.where(own, q, jnp.zeros_like(q)), k)
        if bias_ref is not None:
            s = s + bias_ref[at].astype(F32)
        peak = jnp.max(s, axis=1, keepdims=True)
        e = jnp.exp(s - peak)
        mass = jnp.sum(e, axis=1, keepdims=True)
        o = mm(e.astype(BF16), v)
        out = jnp.where(own, o / mass, out)
        lse = jnp.where(own, peak + jnp.log(mass), lse)
    o_ref[at, cols] = out.astype(BF16)
    lse_ref[at, cols] = lse


def attend_back_unit(q_ref, k_ref, v_ref, bias_ref, do_ref, o_ref, lse_ref, dq_ref, dk_acc, dv_acc, row, step, pair):
    at = pl.ds(pl.multiple_of(row, step), step)
    cols = pl.ds(pl.multiple_of(pair * PAIR, PAIR), PAIR)
    lane = lax.broadcasted_iota(jnp.int32, (1, PAIR), 1)
    k = k_ref[:, cols]
    v = v_ref[:, cols]
    q = q_ref[at, cols]
    do = do_ref[at, cols]
    both = do.astype(F32) * o_ref[at, cols].astype(F32)
    lse_pair = lse_ref[at, cols]
    dq = jnp.zeros((step, PAIR), F32)
    for h in range(2):
        own = (lane >= HEAD) if h else (lane < HEAD)
        q_h = jnp.where(own, q, jnp.zeros_like(q))
        do_h = jnp.where(own, do, jnp.zeros_like(do))
        delta = jnp.sum(jnp.where(own, both, 0.0), axis=1, keepdims=True)
        lse = lse_pair[:, h * HEAD : h * HEAD + 1]
        s = mm_t(q_h, k)
        if bias_ref is not None:
            s = s + bias_ref[at].astype(F32)
        e = jnp.exp(s - lse)
        dp = mm_t(do_h, v)
        ds = (e * (dp - delta)).astype(BF16)
        dq = jnp.where(own, mm(ds, k), dq)
        dk_acc[...] += t_mm(ds, q_h)
        dv_acc[...] += t_mm(e.astype(BF16), do_h)
    dq_ref[at, cols] = dq.astype(BF16) * BF16(HEAD**-0.5)


def attend_units(rows, width):
    step = min(256, rows)
    return rows // step, step, width // PAIR


def self_kernel(
    shape, arrive, leave, all_tok, w_qkv, vec, bias, enc, attn_in, attn_out, ffn_in,
    q, k, v, att, lse, all_enc, g_in, g_out, z_1, *sems,
):
    place, mail = open_kernel(shape, True, False, sems)
    n, rows, width = all_tok.shape
    three = g_in.shape[0]
    e = pair_gather_stages(mail, place, enc, all_enc)
    shards = [attn_in.at[pl.ds(attn_in.shape[0] - three, three)], attn_out]
    wholes = [g_in, g_out]
    w = block_stages(mail, place, shards, lambda i: [g.at[:, place.leaf, i] for g in wholes])
    zw = len(w)
    w += spread_stages(mail, place, wholes)
    f = block_stages(mail, place, [ffn_in], lambda i: [z_1.at[:, i]])
    w[0]()
    scale = HEAD**-0.5
    q[...] = ((mm(all_tok[place.block], w_qkv[0]) + vec[pl.ds(0, 1)]) * scale).astype(BF16)

    def project(i):
        x = all_tok[i]
        at = pl.ds(pl.multiple_of(i * rows, rows), rows)
        k[at] = mm(x, w_qkv[1]).astype(BF16)
        v[at] = (mm(x, w_qkv[2]) + vec[pl.ds(1, 1)]).astype(BF16)

    blocks, step, pairs = attend_units(rows, width)
    units = blocks * pairs
    t = lambda x: n + (x * units) // 12
    hooks, last = {}, n + units
    at_units(hooks, w[1 : zw - 1], [t(2)] * (zw - 2))
    at_units(hooks, f[:1] + w[zw - 1 : zw + 1], [t(2), t(3), t(3)])
    at_units(hooks, f[1:-1] + e[:1] + f[-1:], [t(7)] * (len(f) - 2) + [t(7), t(10)])
    tail = w[zw + 1 : -1] + e[1:-1] + w[-1:] + e[-1:]
    at_units(hooks, tail, [last] * len(tail))
    early = {at: stages for at, stages in hooks.items() if at < n}
    late = {at - n: stages for at, stages in hooks.items() if at >= n}
    hooked(n, project, early)
    leave(0, 1, 2)
    arrive()

    def unit(i):
        attend_unit(q, k, v, bias, att, lse, (i % blocks) * step, step, i // blocks)

    hooked(blocks * pairs, unit, late)
    mail.finish()


ROOT_HALF = 0.7071067811865476
NORM = 0.3989422804014327


def normed(v):
    centre = v - jnp.mean(v, axis=1, keepdims=True)
    inverse = lax.rsqrt(jnp.mean(centre * centre, axis=1, keepdims=True) + 1e-05)
    return centre * inverse, inverse


def normed_back(g, gain, hat, inverse):
    gx = g * gain
    mean_g = jnp.mean(gx, axis=1, keepdims=True)
    mean_gh = jnp.mean(gx * hat, axis=1, keepdims=True)
    return inverse * (gx - mean_g - hat * mean_gh)


def by_rows(rows, action):
    step = min(128, rows)

    def one(i, _):
        action(pl.ds(pl.multiple_of(i * step, step), step))
        return 0

    lax.fori_loop(0, rows // step, one, 0)


def row_sum(x):
    return jnp.sum(x, axis=0, keepdims=True)


def cross_kernel(
    shape, shifts, arrive, leave, att, all_tok, all_enc, w_in, w_out, vec, z_1, ffn_out, cot,
    hat1, inv1, first_low, cq, ck, cv, crossed, lse, g_1, g_2, my_cot, toks, *sems,
):
    place, mail = open_kernel(shape, True, True, sems)
    rows, width = cq.shape
    n, enc_rows, _ = all_enc.shape
    f = spread_stages(mail, place, [g_1], [z_1])
    w = block_stages(mail, place, [ffn_out], lambda i: [g_2.at[:, place.leaf, i]])
    zw = len(w)
    w += spread_stages(mail, place, [g_2])
    c = mirror_stages(mail, place, cot, my_cot)
    mine = mail.local(None, all_tok.at[place.block], toks)
    mine[0]()
    w[0]()
    f[0]()

    def project(i):
        x = all_enc[i]
        at = pl.ds(pl.multiple_of(i * enc_rows, enc_rows), enc_rows)
        ck[at] = mm(x, w_in[1]).astype(BF16)
        cv[at] = (mm(x, w_in[2]) + vec[pl.ds(4, 1)]).astype(BF16)

    hooked(n, project, {})
    leave(4, 5)
    arrive()
    mine[1]()
    scale = HEAD**-0.5

    def first(at):
        v = toks[at].astype(F32) + mm(att[at], w_out[0]) + vec[pl.ds(2, 1)]
        hat, inverse = normed(v)
        hat1[at] = hat
        inv1[at] = jnp.broadcast_to(inverse, (hat.shape[0], 128))
        low = (hat * vec[pl.ds(shifts, 1)] + vec[pl.ds(7, 1)]).astype(BF16)
        first_low[at] = low
        cq[at] = ((mm(low, w_in[0]) + vec[pl.ds(3, 1)]) * scale).astype(BF16)

    by_rows(rows, first)
    leave(0, 1, 2, 3)
    blocks, step, pairs = attend_units(rows, width)
    total = blocks * pairs
    t = lambda x: (x * total) // 12
    late = {}
    at_units(late, f[1:], [t(4), t(6)] + [t(10)] * (len(f) - 4) + [total])
    at_units(late, w[1 : zw - 1] + c[:1], [t(1)] * (zw - 2) + [t(3)])
    at_units(late, w[zw - 1 : zw + 1], [t(7)] * 2)
    at_units(late, w[zw + 1 :] + c[1:], [total] * (len(w) - zw))

    def unit(i):
        attend_unit(cq, ck, cv, None, crossed, lse, (i % blocks) * step, step, i // blocks)

    hooked(total, unit, late)
    mail.finish()


def ffn_kernel(
    shifts, arrive, leave, hat1, crossed, w_out, w1, w2, vec, b1, cot,
    out, gw1, gw2, gwo, g_crossed, g_pre2, sums, gb1,
    hat2, inv2, low2, acc, slope, hidden, g_pre3, g_ffn, acc2, g_cb,
):
    rows, width = crossed.shape
    wide = hidden.shape[1]
    piece = 512
    gain = lambda i: vec[pl.ds(shifts + i, 1)]
    shift = lambda i: vec[pl.ds(i, 1)]
    sums[...] = jnp.zeros_like(sums)

    def second(at):
        v = hat1[at] * gain(0) + shift(7) + mm(crossed[at], w_out[1]) + shift(5)
        hat, inverse = normed(v)
        hat2[at] = hat
        inv2[at] = jnp.broadcast_to(inverse, (hat.shape[0], 128))
        low2[at] = (hat * gain(1) + shift(8)).astype(BF16)

    by_rows(rows, second)
    arrive()
    acc[...] = jnp.zeros_like(acc)

    def up(j, _):
        cols = pl.ds(pl.multiple_of(j * piece, piece), piece)
        u = mm(low2[...], w1[:, cols]) + b1[:, cols]
        phi = 0.5 * (1.0 + lax.erf(u * ROOT_HALF))
        slope[:, cols] = phi + u * jnp.exp(-0.5 * u * u) * NORM
        h = (u * phi).astype(BF16)
        hidden[:, cols] = h
        acc[...] += mm(h, w2[cols])
        return 0

    lax.fori_loop(0, wide // piece, up, 0)

    def third(at):
        v = hat2[at] * gain(1) + shift(8) + acc[at] + shift(6)
        hat, inverse = normed(v)
        out[at] = (hat * gain(2) + shift(9)).astype(BF16)
        g = cot[at].astype(F32)
        sums[pl.ds(shifts + 2, 1)] += row_sum(g * hat)
        sums[pl.ds(9, 1)] += row_sum(g)
        back = normed_back(g, gain(2), hat, inverse)
        g_pre3[at] = back
        low = back.astype(BF16)
        g_ffn[at] = low
        sums[pl.ds(6, 1)] += row_sum(low.astype(F32))

    by_rows(rows, third)
    leave(0)
    acc2[...] = jnp.zeros_like(acc2)

    def down(j, _):
        cols = pl.ds(pl.multiple_of(j * piece, piece), piece)
        g = (mm_t(g_ffn[...], w2[cols]) * slope[:, cols]).astype(BF16)
        gb1[:, cols] = row_sum(g.astype(F32))
        gw2[cols] = t_mm(hidden[:, cols], g_ffn[...]).astype(BF16)
        gw1[:, cols] = t_mm(low2[...], g).astype(BF16)
        acc2[...] += mm_t(g, w1[:, cols])
        return 0

    lax.fori_loop(0, wide // piece, down, 0)
    leave(1, 2)

    def back_two(at):
        g = g_pre3[at] + acc2[at]
        hat = hat2[at]
        sums[pl.ds(shifts + 1, 1)] += row_sum(g * hat)
        sums[pl.ds(8, 1)] += row_sum(g)
        back = normed_back(g, gain(1), hat, inv2[at, :1])
        g_pre2[at] = back
        low = back.astype(BF16)
        g_cb[at] = low
        sums[pl.ds(5, 1)] += row_sum(low.astype(F32))
        g_crossed[at] = mm_t(low, w_out[1]).astype(BF16)

    by_rows(rows, back_two)
    gwo[...] = t_mm(crossed[...], g_cb[...]).astype(BF16)


def cross_back_kernel(
    shape, shifts, arrive, leave, cq, ck, cv, do, o, lse, first_low, hat1, inv1, all_enc, w_in, w_out, att, g_pre2, vec, sums_in, p_1, p_2, out_rows,
    g_in, g_wo, g_enc, g_att, g_pre1, sums, s_1, o_2, my_out, dq, dk, dv, g_br, dk_acc, dv_acc, *scratch,
):
    sems, scratch = scratch[:3], scratch[3:]
    place, mail = open_kernel(shape, True, True, sems)
    rows, width = cq.shape
    f_2, sum_2 = fold_stages(mail, place, p_2, scratch[:N_FOLD])
    f_1, sum_1 = fold_stages(mail, place, p_1, scratch[N_FOLD : 2 * N_FOLD])
    l_2 = line_stages(mail, place, sum_2, scratch[2 * N_FOLD], o_2)
    c = mirror_stages(mail, place, out_rows, my_out)
    f_2[0]()
    c[0]()
    blocks, step, pairs = attend_units(rows, width)
    total = blocks * pairs
    t = lambda x: (x * total) // 12
    hooks = {}
    more = len(f_1) - 5
    at_units(hooks, f_2[1:], [t(2), t(8), t(9), total] + [total] * more)
    at_units(hooks, l_2, [total, total + 6])
    at_units(hooks, f_1, [t(3), t(9), total + 3, total + 4, total + 6] + [total + 6] * more)
    at_units(hooks, c[1:], [total + 6])

    def unit(i):
        first = i % blocks == 0

        @pl.when(first)
        def _():
            dk_acc[...] = jnp.zeros_like(dk_acc)
            dv_acc[...] = jnp.zeros_like(dv_acc)

        pair = i // blocks
        attend_back_unit(cq, ck, cv, None, do, o, lse, dq, dk_acc, dv_acc, (i % blocks) * step, step, pair)

        @pl.when(i % blocks == blocks - 1)
        def _():
            cols = pl.ds(pl.multiple_of(pair * PAIR, PAIR), PAIR)
            dk[:, cols] = dk_acc[...].astype(BF16)
            dv[:, cols] = dv_acc[...].astype(BF16)

    late = {at: hooks.pop(at) for at in list(hooks) if at >= total}
    hooked(total, unit, hooks)
    n, enc_rows, _ = all_enc.shape
    arrive()
    flat = all_enc.reshape(n * enc_rows, width)

    def query_grads():
        sums[...] = sums_in[...]
        sums[pl.ds(3, 1)] = row_sum(dq[...].astype(F32))
        sums[pl.ds(4, 1)] = row_sum(dv[...].astype(F32))
        g_in[0] = t_mm(first_low[...], dq[...]).astype(BF16)

    def key_grads():
        g_in[1] = t_mm(flat[...], dk[...]).astype(BF16)

    def value_grads():
        g_in[2] = t_mm(flat[...], dv[...]).astype(BF16)

    def encoder(i, _):
        at = pl.ds(pl.multiple_of(i * enc_rows, enc_rows), enc_rows)
        g_enc[i] = (mm_t(dk[at], w_in[1]) + mm_t(dv[at], w_in[2])).astype(BF16)
        return 0

    def back_one(at):
        g = g_pre2[at] + mm_t(dq[at], w_in[0])
        hat = hat1[at]
        sums[pl.ds(shifts, 1)] += row_sum(g * hat)
        sums[pl.ds(7, 1)] += row_sum(g)
        back = normed_back(g, vec[pl.ds(shifts, 1)], hat, inv1[at, :1])
        g_pre1[at] = back
        low = back.astype(BF16)
        g_br[at] = low
        sums[pl.ds(2, 1)] += row_sum(low.astype(F32))
        g_att[at] = mm_t(low, w_out[0]).astype(BF16)

    def out_grads():
        leave(0, 2, 3, 4)
        g_wo[...] = t_mm(att[...], g_br[...]).astype(BF16)

    steps = [
        query_grads,
        key_grads,
        value_grads,
        lambda: lax.fori_loop(0, n, encoder, 0),
        lambda: by_rows(rows, back_one),
        out_grads,
    ]
    for at, step_of in enumerate(steps):
        run(late.get(total + at, []))
        step_of()
    run(late[total + len(steps)])
    s_1[...] = sum_1[...]
    mail.finish()


def self_back_kernel(
    shape, arrive, leave, q, k, v, bias, do, o, lse, z_1, sums_in, all_tok, p_in, p_o0, p_o1, p_enc,
    dq, dk, dv, g_qkv, o_1, o_in, o_o0, o_o1, o_enc, sums, dk_acc, dv_acc, *scratch,
):
    sems, scratch = scratch[:3], scratch[3:]
    place, mail = open_kernel(shape, True, False, sems)
    rows, width = q.shape
    l_1 = line_stages(mail, place, z_1, scratch[0], o_1)
    rest = scratch[1:]
    f_in, sum_in = fold_stages(mail, place, p_in, rest[:N_FOLD])
    f_o0, sum_o0 = fold_stages(mail, place, p_o0, rest[N_FOLD : 2 * N_FOLD])
    f_o1, sum_o1 = fold_stages(mail, place, p_o1, rest[2 * N_FOLD : 3 * N_FOLD])
    rest = rest[3 * N_FOLD :]
    l_in = line_stages(mail, place, sum_in, rest[0], o_in)
    l_o0 = line_stages(mail, place, sum_o0, rest[1], o_o0)
    l_o1 = line_stages(mail, place, sum_o1, rest[2], o_o1)
    e = pair_sum_stages(mail, place, p_enc, rest[3:], o_enc)
    f_w = [functools.partial(run, three) for three in zip(f_in, f_o0, f_o1)]
    l_w = [functools.partial(run, three) for three in zip(l_in, l_o0, l_o1)]
    f_w[0]()
    l_1[0]()
    blocks, step, pairs = attend_units(rows, width)
    total = blocks * pairs
    t = lambda x: (x * total) // 12
    hooks = {}
    more = len(f_w) - 5
    at_units(hooks, f_w[1:], [t(2), t(6), t(7), t(10)] + [t(10)] * more)
    at_units(hooks, e[:-1], [t(2), t(3), t(4)] + [t(5)] * (len(e) - 4))
    at_units(hooks, l_1[1:] + l_w[:1], [t(6), t(10)])
    at_units(hooks, e[-1:] + l_w[1:], [total] * 2)

    def unit(i):
        @pl.when(i % blocks == 0)
        def _():
            dk_acc[...] = jnp.zeros_like(dk_acc)
            dv_acc[...] = jnp.zeros_like(dv_acc)

        pair = i // blocks
        attend_back_unit(q, k, v, bias, do, o, lse, dq, dk_acc, dv_acc, (i % blocks) * step, step, pair)

        @pl.when(i % blocks == blocks - 1)
        def _():
            cols = pl.ds(pl.multiple_of(pair * PAIR, PAIR), PAIR)
            dk[:, cols] = dk_acc[...].astype(BF16)
            dv[:, cols] = dv_acc[...].astype(BF16)

    last = hooks.pop(total)
    hooked(total, unit, hooks)
    sums[...] = sums_in[...]
    sums[pl.ds(0, 1)] = row_sum(dq[...].astype(F32))
    sums[pl.ds(1, 1)] = row_sum(dv[...].astype(F32))
    leave(0, 1, 2)
    arrive()
    flat = all_tok.reshape(k.shape[0], width)
    g_qkv[0] = t_mm(all_tok[place.block], dq[...]).astype(BF16)
    g_qkv[1] = t_mm(flat[...], dk[...]).astype(BF16)
    g_qkv[2] = t_mm(flat[...], dv[...]).astype(BF16)
    run(last)
    mail.finish()


def closing_kernel(shape, p_qkv, p_small, dq, dk, dv, w_qkv, g_pre1, o_qkv, o_small, o_tok, p_tok, *scratch):
    sems, scratch = scratch[:3], scratch[3:]
    place, mail = open_kernel(shape, True, False, sems)
    f_q, sum_q = fold_stages(mail, place, p_qkv, scratch[:N_FOLD])
    f_s, sum_s = fold_stages(mail, place, p_small, scratch[N_FOLD : 2 * N_FOLD])
    rest = scratch[2 * N_FOLD :]
    l_q = line_stages(mail, place, sum_q, rest[0], o_qkv)
    l_s = line_stages(mail, place, sum_s, rest[1], o_small)
    t = pair_sum_stages(mail, place, p_tok, rest[2:], o_tok)
    a = [functools.partial(run, two) for two in zip(f_q, f_s)]
    b = [functools.partial(run, two) for two in zip(l_q, l_s)]
    n, rows, width = p_tok.shape
    step = min(128, rows)

    def terms(r):
        j = place.shard_of_rank(r)

        def some(i, _):
            at = pl.ds(pl.multiple_of(i * step, step), step)
            far = pl.ds(pl.multiple_of(j * rows + i * step, step), step)
            total = mm_t(dk[far], w_qkv[1]) + mm_t(dv[far], w_qkv[2])
            p_tok[j, at] = total.astype(BF16)

            @pl.when(j == place.block)
            def _():
                own = g_pre1[at] + mm_t(dq[at], w_qkv[0])
                p_tok[j, at] = (total + own).astype(BF16)

            return 0

        lax.fori_loop(0, rows // step, some, 0)

    a[0]()
    terms(n - 1)
    t[0]()
    for k in range(1, n):
        terms(n - 1 - k)
        t[k]()
        if k < len(a):
            a[k]()
    run(a[n:])
    run(b[:1])
    run(t[n:-1])
    t[-1]()
    run(b[1:])
    mail.finish()


def body(
    tokens, encoded, cotangent, parent, assignment, attn_in, attn_out, ffn_in, ffn_out, shifts, gains, ffn_bias
):
    shape = Shape(lax.axis_size("leaf"), lax.axis_size("path"))
    leafs, paths = shape.leafs, shape.paths
    devices = leafs * paths
    scale = HEAD ** (-0.5)
    tokens, encoded, cotangent = tokens[0], encoded[0], cotangent[0]
    rows, width = tokens.shape
    enc_rows = encoded.shape[0]
    hidden_width = ffn_in.shape[1]
    tree_rows, tree_enc = rows * paths, enc_rows * paths
    piece = shifts.shape[1]
    n_shift, n_gain, n_bias = shifts.shape[0], gains.shape[0], ffn_bias.shape[0]
    n_vec = n_shift + n_gain
    ffn_in, ffn_out = ffn_in[None], ffn_out[None]

    def sds(shape_, dtype=BF16):
        return jax.ShapeDtypeStruct(shape_, dtype)

    small = jnp.concatenate([shifts.reshape(-1), gains.reshape(-1), ffn_bias])
    small_rows = -(-small.shape[0] // 4096) * 16
    small = jnp.pad(small, (0, small_rows * 256 - small.shape[0])).reshape(1, small_rows, 256)
    blocks = parent.shape[1]
    ids = jnp.arange(blocks, dtype=jnp.int32)
    lanes = jnp.arange(128, dtype=jnp.int32)
    links = jnp.concatenate(
        [
            (parent[0][:, None] == lanes[None, :]) & (ids[:, None] != lanes[None, :]),
            assignment[0][:, None] == lanes[None, :],
        ]
    ).astype(F32)

    three = 3
    all_tok, g_small, w_qkv, bias = kernel_call(
        functools.partial(opening_kernel, shape, blocks.bit_length()),
        "opening",
        0,
        [tokens, small, attn_in, links],
        [ANY, ANY, ANY, VMEM],
        [
            sds((paths, rows, width)),
            sds((1, leafs, paths) + small.shape[1:]),
            sds((three, leafs, paths) + attn_in.shape[1:]),
            sds((rows, tree_rows)),
        ],
        [ANY, ANY, ANY, VMEM],
        mail_scratch()
        + [pltpu.VMEM(links.shape, F32), pltpu.VMEM((128, 128), F32), pltpu.VMEM((128, 128), F32)],
    )
    flat = g_small.reshape(devices, -1)
    vec = flat[:, : n_vec * piece].reshape(devices, n_vec, piece).transpose(1, 0, 2)
    vec = jnp.pad(vec.reshape(n_vec, width).astype(F32), ((0, -n_vec % 8), (0, 0)))
    b1 = flat[:, n_vec * piece : n_vec * piece + n_bias].reshape(1, hidden_width).astype(F32)
    w_qkv = w_qkv.reshape(three, width, width)

    rest_in = attn_in.shape[0] - three
    q, k, v, attended, self_mass, all_enc, w_in, w_out, z_1 = kernel_call(
        functools.partial(self_kernel, shape),
        "self_attention",
        1,
        [all_tok, w_qkv, vec, bias, encoded, attn_in, attn_out, ffn_in],
        [VMEM] * 4 + [ANY] * 4,
        [
            sds((rows, width)),
            sds((tree_rows, width)),
            sds((tree_rows, width)),
            sds((rows, width)),
            sds((rows, width), F32),
            sds((paths, enc_rows, width)),
            sds((rest_in, leafs, paths) + attn_in.shape[1:]),
            sds((attn_out.shape[0], leafs, paths) + attn_out.shape[1:]),
            sds((1, paths) + ffn_in.shape[1:]),
        ],
        [VMEM] * 5 + [ANY] * 4,
        mail_scratch(),
        late=(3,),
        early=(0, 1, 2),
    )
    w_in = w_in.reshape(rest_in, width, width)
    w_out = w_out.reshape(attn_out.shape[0], width, width)

    hat1, inv1, first_low, cq, ck, cv, crossed, cross_mass, w1, w2, my_cot = kernel_call(
        functools.partial(cross_kernel, shape, n_shift),
        "cross_attention",
        2,
        [attended, all_tok, all_enc, w_in, w_out, vec, z_1, ffn_out, cotangent],
        [VMEM, ANY] + [VMEM] * 4 + [ANY] * 3,
        [
            sds((rows, width), F32),
            sds((rows, 128), F32),
            sds((rows, width)),
            sds((rows, width)),
            sds((tree_enc, width)),
            sds((tree_enc, width)),
            sds((rows, width)),
            sds((rows, width), F32),
            sds((1, leafs, paths) + ffn_in.shape[1:]),
            sds((1, leafs, paths) + ffn_out.shape[1:]),
            sds((rows, width)),
        ],
        [VMEM] * 8 + [ANY] * 3,
        [pltpu.VMEM((rows, width), BF16)] + mail_scratch(),
        late=(0, 4),
        early=(0, 1, 2, 3, 4, 5),
    )
    w1 = w1.reshape(width, hidden_width)
    w2 = w2.reshape(hidden_width, width)
    vm = lambda s, dtype=BF16: pltpu.VMEM(s, dtype)
    output, g_w1, g_w2, g_wo1, g_crossed, g_pre2, sums, g_b1 = kernel_call(
        functools.partial(ffn_kernel, n_shift),
        "feed_forward",
        None,
        [hat1, crossed, w_out, w1, w2, vec, b1, my_cot],
        [VMEM] * 8,
        [
            sds((rows, width)),
            sds((width, hidden_width)),
            sds((hidden_width, width)),
            sds((width, width)),
            sds((rows, width)),
            sds((rows, width), F32),
            sds(vec.shape, F32),
            sds((1, hidden_width), F32),
        ],
        [VMEM] * 8,
        [
            vm((rows, width), F32),
            vm((rows, 128), F32),
            vm((rows, width)),
            vm((rows, width), F32),
            vm((rows, hidden_width), F32),
            vm((rows, hidden_width)),
            vm((rows, width), F32),
            vm((rows, width)),
            vm((rows, width), F32),
            vm((rows, width)),
        ],
        late=(3, 4, 7),
        early=(0, 1, 2),
    )

    def spread(g):
        return g.reshape(
            g.shape[0], shape.A, shape.B, 2, paths, g.shape[1] // devices, g.shape[2]
        )

    r1, r2 = ffn_in.shape[1:], ffn_out.shape[1:]
    g_rest, g_wo0, g_enc, g_att, g_pre1, sums, s_1, o_w2, output = kernel_call(
        functools.partial(cross_back_kernel, shape, n_shift),
        "cross_back",
        3,
        [
            cq, ck, cv, g_crossed, crossed, cross_mass, first_low, hat1, inv1, all_enc, w_in, w_out, attended,
            g_pre2, vec, sums, spread(g_w1[None]), spread(g_w2[None]), output,
        ],
        [VMEM] * 16 + [ANY] * 3,
        [
            sds((rest_in, width, width)),
            sds((width, width)),
            sds((paths, enc_rows, width)),
            sds((rows, width)),
            sds((rows, width), F32),
            sds(vec.shape, F32),
            sds((1, paths) + r1),
            sds((1,) + r2, F32),
            sds((rows, width)),
        ],
        [VMEM] * 8 + [ANY],
        [vm((rows, width)), vm((tree_enc, width)), vm((tree_enc, width)), vm((rows, width))]
        + [pltpu.VMEM((tree_enc, PAIR), F32)] * 2
        + mail_scratch()
        + fold_scratch(shape, 1, *r2, BF16)
        + fold_scratch(shape, 1, *r1, BF16)
        + line_scratch(shape, 1, *r2, BF16),
        late=(6, 7, 8, 9, 10, 11, 12, 13),
        early=(0, 2, 3, 4),
    )
    ri = attn_in.shape[1:]
    g_q, g_k, g_v, g_qkv, o_w1, o_in, o_o0, o_o1, o_enc, sums = kernel_call(
        functools.partial(self_back_kernel, shape),
        "self_back",
        4,
        [
            q, k, v, bias, g_att, attended, self_mass, s_1, sums, all_tok, spread(g_rest),
            spread(g_wo0[None]), spread(g_wo1[None]), g_enc,
        ],
        [VMEM] * 10 + [ANY] * 3 + [VMEM],
        [
            sds((rows, width)),
            sds((tree_rows, width)),
            sds((tree_rows, width)),
            sds((three, width, width)),
            sds((1,) + r1, F32),
            sds((rest_in,) + ri, F32),
            sds((1,) + ri, F32),
            sds((1,) + ri, F32),
            sds((enc_rows, width), F32),
            sds(vec.shape, F32),
        ],
        [VMEM] * 10,
        [pltpu.VMEM((tree_rows, PAIR), F32)] * 2
        + mail_scratch()
        + line_scratch(shape, 1, *r1, BF16)
        + fold_scratch(shape, rest_in, *ri, BF16)
        + fold_scratch(shape, 1, *ri, BF16)
        + fold_scratch(shape, 1, *ri, BF16)
        + line_scratch(shape, rest_in, *ri, BF16)
        + line_scratch(shape, 1, *ri, BF16)
        + line_scratch(shape, 1, *ri, BF16)
        + pair_sum_scratch(shape, enc_rows, width),
        late=(9,),
        early=(0, 1, 2),
    )
    g_vec = sums[:n_vec]
    g_small = jnp.concatenate(
        [
            g_vec.reshape(n_vec, devices, piece).transpose(1, 0, 2).reshape(devices, -1),
            g_b1.reshape(devices, n_bias),
        ],
        axis=1,
    )
    small_count = g_small.shape[1]
    g_small_rows = -(-small_count // 2048) * 8
    g_small = jnp.pad(g_small, ((0, 0), (0, g_small_rows * 256 - small_count)))
    p_small = g_small.reshape(1, shape.A, shape.B, 2, paths, g_small_rows, 256)
    o_qkv, o_small, o_tok = kernel_call(
        functools.partial(closing_kernel, shape),
        "closing",
        5,
        [spread(g_qkv), p_small, g_q, g_k, g_v, w_qkv, g_pre1],
        [ANY, ANY] + [VMEM] * 5,
        [
            sds((three,) + ri, F32),
            sds((1, g_small_rows, 256), F32),
            sds((rows, width), F32),
        ],
        [VMEM] * 3,
        [vm((paths, rows, width))]
        + mail_scratch()
        + fold_scratch(shape, three, *ri, BF16)
        + fold_scratch(shape, 1, g_small_rows, 256, F32)
        + line_scratch(shape, three, *ri, BF16)
        + line_scratch(shape, 1, g_small_rows, 256, F32)
        + pair_sum_scratch(shape, rows, width),
    )
    o_small = o_small.reshape(-1)
    o_vec = o_small[: n_vec * piece].reshape(n_vec, piece)
    return (
        output[None],
        o_tok[None],
        o_enc[None],
        jnp.concatenate([o_qkv, o_in]),
        jnp.concatenate([o_o0, o_o1]),
        o_w1[0],
        o_w2[0],
        o_vec[:n_shift],
        o_vec[n_shift:],
        o_small[n_vec * piece : n_vec * piece + n_bias],
    )


def solution(mesh):
    both = ("leaf", "path")
    rows = P("leaf", "path", None)
    weights = (P(None, both, None), P(None, both, None), P(both, None), P(both, None), P(None, both), P(None, both), P(both))
    return jax.shard_map(
        body,
        mesh=mesh,
        in_specs=(rows, rows, rows, P("leaf", None), P("leaf", None)) + weights,
        out_specs=(rows, rows, rows) + weights,
        check_vma=False,
    )
```

```python
import functools

import jax
import jax.numpy as jnp
from jax import lax
from jax.experimental import pallas as pl
from jax.experimental.pallas import tpu as pltpu
from jax.sharding import PartitionSpec as P

HEAD = 64
BLK = 128
PAIR = 2 * HEAD
MESH = pl.DeviceIdType.MESH
F32 = jnp.float32
BF16 = jnp.bfloat16
VMEM_OF = {"opening": 8}
ANY = pl.BlockSpec(memory_space=pl.ANY)
VMEM = pl.BlockSpec(memory_space=pltpu.VMEM)


class Shape:
    def __init__(self, leafs, paths):
        self.leafs, self.paths, self.half = leafs, paths, paths // 2
        outer = leafs // 2
        self.A = 2 if outer % 2 == 0 else 1
        self.B = outer // self.A


class Place:
    def __init__(self, shape):
        self.shape = shape
        self.leafs, self.paths, self.half = shape.leafs, shape.paths, shape.half
        self.A, self.B = shape.A, shape.B
        leaf = lax.axis_index("leaf")
        self.leaf, self.p = leaf, lax.axis_index("path")
        self.c = leaf % 2
        self.a = (leaf // 2) // self.B
        self.b = (leaf // 2) % self.B
        n = self.paths
        self.tree = jnp.where(self.p >= self.half, 1, 0)
        self.primary = self.c == self.tree
        self.pm = jnp.where(self.tree == 0, self.p, n - 1 - self.p)
        self.inward = jnp.where(self.tree == 0, 1, -1)
        self.own_rank = jnp.where(self.c == 0, self.p, n - 1 - self.p)
        self.block = jnp.where(self.primary, self.p, n - 1 - self.p)

    def leaf_at(self, a, b, c):
        return (a * self.B + b) * 2 + c

    def at_core(self):
        return (self.leaf_at(self.a, self.b, 1 - self.c), self.p)

    def at_a(self, a):
        return (self.leaf_at(a, self.b, self.c), self.p)

    def at_b(self, b):
        return (self.leaf_at(self.a, b, self.c), self.p)

    def at_p(self, p):
        return (self.leaf, clamp(p, self.paths))

    def at_mirror(self):
        return (self.leaf_at(self.a, self.b, 1 - self.c), self.paths - 1 - self.p)

    def shard_of_rank(self, rank):
        return jnp.where(self.tree == 0, rank, self.paths - 1 - rank)

    def line_p(self):
        return (self.paths, self.p, self.at_p)

    def line_a(self):
        return (self.A, self.a, self.at_a)

    def line_b(self):
        return (self.B, self.b, self.at_b)


def clamp(index, size):
    return jnp.clip(index, 0, size - 1)


def guarded(when, action):
    if when is None:
        action()
    else:

        @pl.when(when)
        def _():
            action()


def run(actions):
    for action in actions:
        action()


def greet(place, column, mirror):
    barrier = pltpu.get_barrier_semaphore()
    peers = 1

    def signal(to):
        pl.semaphore_signal(barrier, inc=1, device_id=to, device_id_type=MESH)

    signal(place.at_core())
    if column:
        for k in range(1, place.paths):
            for core in range(2):
                there = (place.p + k) % place.paths
                signal((place.leaf_at(place.a, place.b, core), there))
        peers = peers + 2 * (place.paths - 1)
    for size, pos, to in (place.line_a(), place.line_b()):
        if size == 1:
            continue
        if size == 2:
            signal(to(1 - pos))
            peers = peers + 1
            continue
        for step in (-1, 1):
            there = pos + step
            inside = (there >= 0) & (there < size)

            @pl.when(inside)
            def _():
                signal(to(clamp(there, size)))

            peers = peers + jnp.where(inside, 1, 0)
    if mirror and not column:

        @pl.when(jnp.logical_not(place.primary))
        def _():
            signal(place.at_mirror())

        peers = peers + jnp.where(place.primary, 0, 1)
    pl.semaphore_wait(barrier, peers)


class Mail:
    def __init__(self, send_sems, recv_sems, own_sems):
        self.send_sems, self.recv_sems, self.own_sems = send_sems, recv_sems, own_sems
        self.sends = self.recvs = self.owns = 0
        self.sent = []

    def new_recv(self, count=1):
        self.recvs += count
        return self.recvs - count

    def send(self, when, src, dst, to, recv):
        k = self.sends
        self.sends += 1
        copy = pltpu.make_async_remote_copy(
            src_ref=src,
            dst_ref=dst,
            send_sem=self.send_sems.at[k],
            recv_sem=self.recv_sems.at[recv],
            device_id=to,
            device_id_type=MESH,
        )
        self.sent.append((when, copy))
        return functools.partial(guarded, when, copy.start)

    def hear(self, when, landing, to, recv):
        copy = pltpu.make_async_remote_copy(
            src_ref=landing,
            dst_ref=landing,
            send_sem=self.send_sems.at[0],
            recv_sem=self.recv_sems.at[recv],
            device_id=to,
            device_id_type=MESH,
        )
        return functools.partial(guarded, when, copy.wait_recv)

    def post(self, when, src, dst, to, hear_when, landing):
        k = self.new_recv()
        return self.send(when, src, dst, to, k), self.hear(hear_when, landing, to, k)

    def local(self, when, src, dst):
        k = self.owns
        self.owns += 1
        copy = pltpu.make_async_copy(src, dst, self.own_sems.at[k])
        return functools.partial(guarded, when, copy.start), functools.partial(guarded, when, copy.wait)

    def finish(self):
        for when, copy in self.sent:
            guarded(when, copy.wait_send)


def mail_scratch(count=160, own=24):
    return [
        pltpu.SemaphoreType.DMA((count,)),
        pltpu.SemaphoreType.DMA((count,)),
        pltpu.SemaphoreType.DMA((own,)),
    ]


def flood(mail, line, views, first=None):
    size, pos, to = line
    steps = []
    if size == 1:
        return steps
    first = first if first is not None else views(pos)
    if size == 2:
        jobs = [
            mail.post(None, s, d, to(1 - pos), None, w)
            for s, d, w in zip(first, views(pos), views(1 - pos))
        ]
        return [([j[0] for j in jobs], [j[1] for j in jobs])]
    for step in range(1, size):
        starts, waits = [], []
        for sign in (1, -1):
            item = pos - sign * (step - 1)
            there = pos + sign
            when = (there >= 0) & (there < size) & (item >= 0) & (item < size)
            heard = pos - sign * step
            hear_when = (heard >= 0) & (heard < size)
            item_c = clamp(item, size)
            sources = first if step == 1 else views(item_c)
            for s, d, w in zip(sources, views(item_c), views(clamp(heard, size))):
                start, wait = mail.post(when, s, d, to(clamp(there, size)), hear_when, w)
                starts.append(start)
                waits.append(wait)
        steps.append((starts, waits))
    return steps


def chain(steps, first_starts=()):
    stages, pending = [], []
    for k, (starts, waits) in enumerate(steps):
        stages.append(functools.partial(run, pending + (list(first_starts) if k == 0 else []) + starts))
        pending = waits
    stages.append(functools.partial(run, pending))
    return stages


def half_columns(ref, leaf, h):
    width = ref.shape[-1] // 2
    return ref.at[:, leaf, :, :, pl.ds(h * width, width)]


def block_stages(mail, place, shards, block_views):
    n = place.paths
    own = [mail.local(None, s, d) for s, d in zip(shards, block_views(place.p))]
    starts, waits = [], []
    lands = [mail.new_recv(n) for _ in shards]
    relay = n == 4
    for k in (1, 3, 2) if relay else range(1, n):
        there = (place.p + k) % n
        near = None
        if relay and k != 2:
            near = (there - place.p != 3) & (place.p - there != 3)
        for s, d, w, land in zip(shards, block_views(place.p), block_views(there), lands):
            starts.append(mail.send(near, s, d, place.at_p(there), land + place.p))
            waits.append((there, mail.hear(None, w, place.at_p(there), land + there)))
    starts += [o[0] for o in own]
    ends = [o[1] for o in own]
    if not relay:
        return [functools.partial(run, starts), functools.partial(run, [w[1] for w in waits] + ends)]
    middle = (place.p == 1) | (place.p == 2)
    passed = jnp.where(place.p == 1, 3, 0)
    to = place.at_p(jnp.where(place.p == 1, 0, 3))
    passes = []
    for item, land in zip(block_views(passed), lands):
        passes.append(mail.hear(middle, item, to, land + passed))
        passes.append(mail.send(middle, item, item, to, land + passed))
    for there, wait in waits:
        ends.append(functools.partial(guarded, jnp.logical_not(middle & (there == passed)), wait))
    return [functools.partial(run, starts), functools.partial(run, passes), functools.partial(run, ends)]


def path_half(ref, h):
    n = ref.shape[1] // 2
    return ref.at[:, pl.ds(h * n, n)]


def spread_stages(mail, place, wholes, blocks=None):
    if (place.A, place.B) != (2, 2):
        return spread_lines(mail, place, wholes, blocks)
    a, b, c = place.a, place.b, place.c
    at = lambda w, a, b, c: w.at[:, place.leaf_at(a, b, c)]
    to_a, to_b, to_core = place.at_a(1 - a), place.at_b(1 - b), place.at_core()
    own = []
    sources = [at(w, a, b, c) for w in wholes]
    if blocks is not None:
        own = [mail.local(None, x, s) for x, s in zip(blocks, sources)]
        sources = list(blocks)
    urgent, calm, relay, near, far = [], [], [], [], []
    for w, s in zip(wholes, sources):
        mine, from_a, from_b = at(w, a, b, c), at(w, 1 - a, b, c), at(w, a, 1 - b, c)
        from_ab = at(w, 1 - a, 1 - b, c)

        def post(src, dst, to, landing, h):
            return mail.post(
                None, path_half(src, h), path_half(dst, h), to, None, path_half(landing, h)
            )

        urgent += [post(s, mine, to_b, from_b, 0), post(s, mine, to_a, from_a, 1)]
        calm += [post(s, mine, to_b, from_b, 1), post(s, mine, to_a, from_a, 0)]
        relay += [post(from_b, from_b, to_a, from_ab, 0), post(from_a, from_a, to_b, from_ab, 1)]
        near.append(mail.post(None, s, mine, to_core, None, at(w, a, b, 1 - c)))
        for x, y, l in ((1 - a, b, near), (a, 1 - b, near), (1 - a, 1 - b, far)):
            l.append(mail.post(None, at(w, x, y, c), at(w, x, y, c), to_core, None, at(w, x, y, 1 - c)))
    start = lambda jobs: run([j[0] for j in jobs])
    wait = lambda jobs: run([j[1] for j in jobs])
    first = near[::3]
    second = [j for k, j in enumerate(near) if k % 3]

    def opening():
        start(urgent)
        start(calm)
        start(first)
        run([o[0] for o in own])

    def passing():
        wait(urgent)
        start(relay)

    def sharing():
        wait(calm)
        run([o[1] for o in own])
        start(second)

    def ending():
        wait(relay)
        start(far)

    return [opening, passing, sharing, ending, lambda: wait(near + far)]


def spread_lines(mail, place, wholes, blocks=None):
    A, B, c = place.A, place.B, place.c

    def of_b(h, across_a):
        ays = range(A) if across_a else [place.a]
        return lambda i: [half_columns(w, place.leaf_at(a, i, c), h) for a in ays for w in wholes]

    def of_a(h, across_b):
        bees = range(B) if across_b else [place.b]
        return lambda i: [half_columns(w, place.leaf_at(i, b, c), h) for b in bees for w in wholes]

    own = []
    firsts = [None, None]
    sources = [w.at[:, place.leaf] for w in wholes]
    if blocks is not None:
        own = [mail.local(None, x, w.at[:, place.leaf]) for x, w in zip(blocks, wholes)]
        firsts = [
            [x.at[:, :, :, pl.ds(h * (x.shape[-1] // 2), x.shape[-1] // 2)] for x in blocks]
            for h in range(2)
        ]
        sources = list(blocks)
    line_a, line_b = place.line_a(), place.line_b()
    phases = [
        (flood(mail, line_b, of_b(0, False), firsts[0]), flood(mail, line_a, of_a(1, False), firsts[1])),
        (flood(mail, line_a, of_a(0, True)), flood(mail, line_b, of_b(1, True))),
    ]
    core = [
        mail.post(
            None,
            s,
            w.at[:, place.leaf],
            place.at_core(),
            None,
            w.at[:, place.leaf_at(place.a, place.b, 1 - c)],
        )
        for s, w in zip(sources, wholes)
    ]
    rest = []
    for offset in range(1, A * B):
        spot = (place.a * B + place.b + offset) % (A * B)
        for w in wholes:
            mine, other = w.at[:, spot * 2 + c], w.at[:, spot * 2 + 1 - c]
            rest.append(mail.post(None, mine, mine, place.at_core(), None, other))
    steps = []
    opening = [o[0] for o in own] + [j[0] for j in core]
    for n_phase, phase in enumerate(phases):
        before = [o[1] for o in own] if n_phase == 1 else []
        for s in range(max(len(f) for f in phase)):
            starts, waits = list(before), []
            before = []
            for f in phase:
                if s < len(f):
                    starts += f[s][0]
                    waits += f[s][1]
            steps.append((starts + opening, waits))
            opening = []
    steps.append((opening + [j[0] for j in rest], [j[1] for j in core + rest]))
    return chain(steps)


def pair_gather_stages(mail, place, shard, whole, pieces=1):
    n, h = place.paths, place.half
    rows = shard.shape[0] // (2 * pieces)
    part = lambda ref, u, s: ref.at[pl.ds(pl.multiple_of((u * pieces + s) * rows, rows), rows)]
    half = lambda ref, u: ref.at[pl.ds(pl.multiple_of(u * pieces * rows, rows), pieces * rows)]
    lands = [mail.new_recv(n) for _ in range(pieces)]
    core_lands = mail.new_recv(n)
    own = mail.local(place.primary, shard, whole.at[place.p])
    first = jnp.where(place.c == 0, 0, h)
    edge = jnp.where(place.c == 0, h - 1, h)
    starts = []
    for s in range(pieces):
        for u in range(2):
            for q in range(h):
                q = first + q
                to = (place.leaf_at(place.a, place.b, u), q)
                near = place.primary & jnp.logical_not((q == place.p) & (place.c == u))
                away = near | (jnp.logical_not(place.primary) & (q == edge))
                starts.append(
                    mail.send(
                        away, part(shard, u, s), part(whole.at[place.p], u, s), to, lands[s] + place.p
                    )
                )
    k = mail.new_recv()
    mate = whole.at[place.p]
    starts.append(
        mail.send(place.primary, half(shard, place.c), half(mate, place.c), place.at_core(), k)
    )
    starts.append(own[0])
    stages = [functools.partial(run, starts)]
    outward = place.at_p(place.p - place.inward)
    for s in range(pieces):
        for r in list(range(h, n)) + list(range(h)):
            j = place.shard_of_rank(r)
            item = part(whole.at[j], place.c, s)
            got = jnp.logical_not(place.primary & (place.p == j))
            actions = [mail.hear(got, item, place.at_core(), lands[s] + j)]
            if r >= h and h > 1:
                actions.append(mail.send(place.pm > 0, item, item, outward, lands[s] + j))
            if s == pieces - 1:
                whole_half = half(whole.at[j], place.c)
                actions.append(
                    mail.send(
                        jnp.logical_not(place.p == j),
                        whole_half,
                        whole_half,
                        place.at_core(),
                        core_lands + j,
                    )
                )
            stages.append(functools.partial(run, actions))
    rest = [own[1]]
    rest.append(
        mail.hear(jnp.logical_not(place.primary), half(mate, 1 - place.c), place.at_core(), k)
    )
    for r in range(n):
        j = place.shard_of_rank(r)
        rest.append(
            mail.hear(
                jnp.logical_not(place.p == j),
                half(whole.at[j], 1 - place.c),
                place.at_core(),
                core_lands + j,
            )
        )
    stages.append(functools.partial(run, rest))
    return stages


def mirror_stages(mail, place, own, mine):
    local = mail.local(place.primary, own, mine)
    other = jnp.logical_not(place.primary)
    start, wait = mail.post(other, own, mine, place.at_mirror(), other, mine)
    return [lambda: run([local[0], start]), lambda: run([local[1], wait])]


def add_rows(dst, src):
    lead = dst.shape[:-2]
    total = 1
    for extent in lead:
        total *= extent

    def body(i, _):
        index = []
        rest = i
        for extent in reversed(lead):
            index.insert(0, rest % extent)
            rest = rest // extent
        index = tuple(index)
        dst[index] = dst[index] + src[index]
        return 0

    if total == 1:
        body(0, 0)
    else:
        lax.fori_loop(0, total, body, 0)


def add_tall(dst, src):
    rows = dst.shape[0]
    step = 64 if rows % 64 == 0 else rows

    def body(r, _):
        at = pl.ds(pl.multiple_of(r * step, step), step)
        dst[at] = dst[at] + src[at]
        return 0

    lax.fori_loop(0, rows // step, body, 0)


def shift_sum(mail, line, mine, slots_up, slots_down, add):
    size, pos, to = line
    if size == 1:
        return []
    if size == 2:
        jobs = [
            mail.post(None, s, slot, to(1 - pos), None, slot)
            for s, slot in zip(mine(1 - pos), slots_up[0])
        ]

        def end():
            for job, dst, slot in zip(jobs, mine(pos), slots_up[0]):
                job[1]()
                add(dst, slot)

        return [lambda: run([j[0] for j in jobs]), end]
    stages = []
    for k in range(size - 1):
        early, actions = [], []
        for sign, slots in ((1, slots_up), (-1, slots_down)):
            dest = size - 1 - k if sign == 1 else k
            when = (pos < dest) if sign == 1 else (pos > dest)
            hear_when = (
                ((pos > 0) & (pos <= dest)) if sign == 1 else ((pos < size - 1) & (pos >= dest))
            )
            there = clamp(pos + sign, size)
            jobs = [
                mail.post(when, s, slot, to(there), None, slot)
                for s, slot in zip(mine(dest), slots[k])
            ]

            def take(jobs=jobs, dst_refs=mine(dest), slot_refs=slots[k]):
                for job, dst, slot in zip(jobs, dst_refs, slot_refs):
                    job[1]()
                    add(dst, slot)

            end = (pos == 0) if sign == 1 else (pos == size - 1)
            starts = functools.partial(run, [job[0] for job in jobs])
            early.append(functools.partial(guarded, end, starts))
            actions.append(functools.partial(guarded, hear_when, take))
            actions.append(functools.partial(guarded, jnp.logical_not(end), starts))
        stages.append(functools.partial(run, early + actions))
    return stages


def fold_scratch(shape, k, R, C, dtype):
    if (shape.A, shape.B) != (2, 2):
        return fold_lines_scratch(shape, k, R, C, dtype)
    block = (k, 2, 2, shape.paths, R, C)
    halves = (2, k, shape.paths // 2, R, C)
    return [pltpu.VMEM(block, dtype)] * 2 + [pltpu.VMEM(halves, dtype)] * 3 + [pltpu.VMEM((1, R, C), dtype)]


def fold_lines_scratch(shape, k, R, C, dtype):
    A, B, paths = shape.A, shape.B, shape.paths
    nb, na = max(B - 1, 1) * (2 if B > 2 else 1), max(A - 1, 1)
    return [
        pltpu.VMEM((k, A, B, paths, R, C), dtype),
        pltpu.VMEM((k, A, B, paths, R, C), dtype),
        pltpu.VMEM((nb, k, A, paths, R, C // 2), dtype),
        pltpu.VMEM((na, k, paths, R, C // 2), dtype),
        pltpu.VMEM((na, k, B, paths, R, C // 2), dtype),
        pltpu.VMEM((nb, k, paths, R, C // 2), dtype),
    ]


N_FOLD = 6


def up_down(ref, size):
    if size <= 2:
        return [[ref.at[0]]], None
    return (
        [[ref.at[k]] for k in range(size - 1)],
        [[ref.at[size - 1 + k]] for k in range(size - 1)],
    )


def fold_stages(mail, place, partial, scratch):
    if (place.A, place.B) != (2, 2):
        return fold_lines(mail, place, partial, scratch)
    a, b, c = place.a, place.b, place.c
    acc, got, far, direct, relayed = scratch[:5]
    own = mail.local(None, partial.at[:, :, :, c], acc)
    core = mail.post(None, partial.at[:, :, :, 1 - c], got, place.at_core(), None, got)
    to_a, to_b = place.at_a(1 - a), place.at_b(1 - b)
    of_a, of_b, of_ab = acc.at[:, 1 - a, b], acc.at[:, a, 1 - b], acc.at[:, 1 - a, 1 - b]
    mine = acc.at[:, a, b]

    def post(src, h, slot, to):
        return mail.post(None, path_half(src, h), slot, to, None, slot)

    urgent = [post(of_ab, 0, far.at[0], to_b), post(of_ab, 1, far.at[1], to_a)]
    calm = [post(of_b, 0, direct.at[0], to_b), post(of_a, 1, direct.at[1], to_a)]
    late = [post(of_a, 0, relayed.at[0], to_a), post(of_b, 1, relayed.at[1], to_b)]

    def join():
        own[1]()
        core[1]()
        add_rows(of_ab, got.at[:, 1 - a, 1 - b])
        run([j[0] for j in urgent])
        add_rows(of_b, got.at[:, a, 1 - b])
        calm[0][0]()
        add_rows(of_a, got.at[:, 1 - a, b])
        calm[1][0]()
        add_rows(mine, got.at[:, a, b])

    def passing():
        urgent[0][1]()
        add_rows(path_half(of_a, 0), far.at[0])
        late[0][0]()
        urgent[1][1]()
        add_rows(path_half(of_b, 1), far.at[1])
        late[1][0]()

    def taking():
        for h in range(2):
            calm[h][1]()
            add_rows(path_half(mine, h), direct.at[h])

    def ending():
        for h in range(2):
            late[h][1]()
            add_rows(path_half(mine, h), relayed.at[h])

    return [lambda: run([own[0], core[0]]), join, passing, taking, ending], mine


def fold_lines(mail, place, partial, scratch):
    c = place.c
    acc, got, sb0, sa0, sa1, sb1 = scratch
    own = mail.local(None, partial.at[:, :, :, c], acc)
    core = mail.post(None, partial.at[:, :, :, 1 - c], got, place.at_core(), None, got)
    width = acc.shape[-1] // 2
    left, right = pl.ds(0, width), pl.ds(width, width)

    def join():
        own[1]()
        core[1]()
        add_rows(acc, got)

    line_a, line_b = place.line_a(), place.line_b()
    h0_b = shift_sum(
        mail, line_b, lambda d: [acc.at[:, :, d, :, :, left]], *up_down(sb0, place.B), add_rows
    )
    h1_a = shift_sum(
        mail, line_a, lambda d: [acc.at[:, d, :, :, :, right]], *up_down(sa1, place.A), add_rows
    )
    h0_a = shift_sum(
        mail, line_a, lambda d: [acc.at[:, d, place.b, :, :, left]], *up_down(sa0, place.A), add_rows
    )
    h1_b = shift_sum(
        mail, line_b, lambda d: [acc.at[:, place.a, d, :, :, right]], *up_down(sb1, place.B), add_rows
    )

    def beside(one, two):
        return [
            functools.partial(run, [s[k] for s in (one, two) if k < len(s)])
            for k in range(max(len(one), len(two)))
        ]

    def joined(first, second):
        if not first or not second:
            return first + second
        return first[:-1] + [functools.partial(run, [first[-1], second[0]])] + second[1:]

    stages = joined(
        [lambda: run([own[0], core[0]]), join], beside(h0_b, h1_a)
    )
    stages = joined(stages, beside(h0_a, h1_b))
    return stages, acc.at[:, place.a, place.b]


def line_scratch(shape, k, R, C, dtype):
    return [pltpu.VMEM((max(shape.paths - 1, 1), k, R, C), dtype)]


def line_stages(mail, place, sums, slots, out):
    n = place.paths
    jobs = []
    for k in range(1, n):
        there = (place.p + k) % n
        slot = slots.at[k - 1]
        jobs.append(mail.post(None, sums.at[:, there], slot, place.at_p(there), None, slot))

    def end():
        run([j[1] for j in jobs])
        for j in range(out.shape[0]):
            total = sums[j, place.p].astype(F32)
            for k in range(n - 1):
                total = total + slots[k, j].astype(F32)
            out[j] = total.astype(out.dtype)

    return [lambda: run([j[0] for j in jobs]), end]


def pair_sum_scratch(shape, R, C):
    return [
        pltpu.VMEM((shape.paths, R // 2, C), BF16),
        pltpu.VMEM((shape.paths, R // 2, C), BF16),
        pltpu.VMEM((shape.half, R, C), BF16),
    ]


def pair_sum_stages(mail, place, part, scratch, out):
    n, h = place.paths, place.half
    core_slot, in_slot, landing = scratch
    rows = part.shape[1] // 2
    half = lambda ref, u: ref.at[pl.ds(pl.multiple_of(u * rows, rows), rows)]
    lands = [mail.new_recv(2) for _ in range(h)]
    inner = place.at_p(place.p + place.inward)
    sends, sums, passes = [], [], []
    for r in range(n - 1, -1, -1):
        j = place.shard_of_rank(r)
        item = part.at[j]
        mine = half(item, place.c)
        send, hear = mail.post(
            None, half(item, 1 - place.c), core_slot.at[r], place.at_core(), None, core_slot.at[r]
        )
        owner = (place.leaf_at(place.a, place.b, place.tree), j)
        leave = []
        if r >= h:
            k = mail.new_recv()
            slot = in_slot.at[r]
            in_send = mail.send(place.pm < h - 1, mine, slot, inner, k)
            in_hear = mail.hear(None, slot, place.at_core(), k)
            go = mail.send(
                place.pm == h - 1, mine, half(landing.at[h - 1], place.c), owner, lands[h - 1] + place.c
            )

            def inward(in_send=in_send, in_hear=in_hear, mine=mine, slot=slot, go=go):
                if h > 1:

                    @pl.when(place.pm > 0)
                    def _():
                        in_hear()
                        add_tall(mine, slot)

                    in_send()
                go()

            passes.append(inward)
        else:
            away = jnp.logical_not(place.primary & (place.p == j))
            for q in range(h):
                leave.append(
                    mail.send(
                        away & (place.pm == q),
                        mine,
                        half(landing.at[q], place.c),
                        owner,
                        lands[q] + place.c,
                    )
                )

        def settle(hear=hear, mine=mine, slot=core_slot.at[r], leave=leave):
            hear()
            add_tall(mine, slot)
            run(leave)

        sends.append(send)
        sums.append(settle)
    stages = [[sends[0]]]
    for k in range(1, n):
        stages.append([sends[k], sums[k - 1]])
    stages.append([sums[n - 1]])
    for k, step in enumerate(passes):
        stages[k + 1].append(step)

    def end():
        for q in range(h):
            for u in range(2):
                self_made = place.primary & (place.own_rank == q) & (place.c == u)
                comes = jnp.logical_not(self_made) & (place.primary | (q == h - 1))
                mail.hear(comes, half(landing.at[q], u), place.at_core(), lands[q] + u)()

        step = 64 if rows % 64 == 0 else rows
        for u in range(2):

            def body(i, _, u=u):
                at = pl.ds(pl.multiple_of(u * rows + i * step, step), step)

                @pl.when(place.primary)
                def _():
                    for q in range(h):
                        self_made = (place.own_rank == q) & (place.c == u)
                        term = jnp.where(self_made, part[place.p, at], landing[q, at]).astype(F32)
                        total = term if q == 0 else total + term
                    out[at] = total

                @pl.when(jnp.logical_not(place.primary))
                def _():
                    out[at] = landing[h - 1, at].astype(F32)

                return 0

            lax.fori_loop(0, rows // step, body, 0)

    return [functools.partial(run, x) for x in stages] + [end]


def at_units(hooks, stages, units):
    for stage, unit in zip(stages, units, strict=True):
        hooks.setdefault(unit, []).append(stage)


def hooked(count, unit, hooks):
    def body(i, _):
        for at, stages in hooks.items():
            if at < count:

                @pl.when(i == at)
                def _():
                    run(stages)

        unit(i)
        return 0

    lax.fori_loop(0, count, body, 0)
    for at in sorted(hooks):
        if at >= count:
            run(hooks[at])


def kernel_call(kernel, name, collective_id, ins, in_specs, outs, out_specs, scratch, late=(), early=()):
    n_in, n_out = len(ins), len(outs)
    in_specs, out_specs = list(in_specs), list(out_specs)
    for i in late:
        in_specs[i] = ANY
    for i in early:
        out_specs[i] = ANY
    held = [pltpu.VMEM(ins[i].shape, ins[i].dtype) for i in late]
    held += [pltpu.VMEM(outs[i].shape, outs[i].dtype) for i in early]
    moving = [pltpu.SemaphoreType.DMA((len(held),))] if held else []

    def whole(*refs):
        refs, extra = list(refs[: len(refs) - len(held) - 1]), refs[len(refs) - len(held) - 1 :]
        buffers, sems = extra[:-1], extra[-1]
        loads, stores = [], {}
        for k, i in enumerate(late):
            loads.append(pltpu.make_async_copy(refs[i], buffers[k], sems.at[k]))
            refs[i] = buffers[k]
        for k, i in enumerate(early):
            k = len(late) + k
            stores[i] = pltpu.make_async_copy(buffers[k], refs[n_in + i], sems.at[k])
            refs[n_in + i] = buffers[k]
        for load in loads:
            load.start()

        def arrive():
            for load in loads:
                load.wait()

        def leave(*which):
            for i in which:
                stores[i].start()

        kernel(arrive, leave, *refs)
        for store in stores.values():
            store.wait()

    limit = VMEM_OF.get(name, 62) * 1024 * 1024
    if collective_id is None:
        params = pltpu.CompilerParams(vmem_limit_bytes=limit)
    else:
        params = pltpu.CompilerParams(
            collective_id=collective_id, has_side_effects=True, vmem_limit_bytes=limit
        )
    return pl.pallas_call(
        whole if held else kernel,
        out_shape=outs,
        in_specs=in_specs,
        out_specs=out_specs,
        scratch_shapes=list(scratch) + held + moving,
        compiler_params=params,
        name=name,
    )(*ins)


def dot(x, y, contract):
    return lax.dot_general(x, y, (contract, ((), ())), preferred_element_type=F32)


def mm(x, w):
    return dot(x, w, ((1,), (0,)))


def mm_t(x, w):
    return dot(x, w, ((1,), (1,)))


def t_mm(x, y):
    return dot(x, y, ((0,), (0,)))


def open_kernel(shape, column, mirror, sems):
    place = Place(shape)
    greet(place, column, mirror)
    return place, Mail(*sems)


def opening_kernel(shape, turns, tok, small, attn_in, links, all_tok, g_small, g_qkv, bias, *scratch):
    sems, (links_got, reach, spot) = scratch[:3], scratch[3:]
    place, mail = open_kernel(shape, True, False, sems)
    three = g_qkv.shape[0]
    to_core = mail.post(None, links, links_got, place.at_core(), None, links_got)
    to_core[0]()
    shards = [small, attn_in.at[pl.ds(0, three)]]
    wholes = [g_small, g_qkv]
    weights = block_stages(
        mail, place, shards, lambda i: [w.at[:, place.leaf, i] for w in wholes]
    )
    spread = spread_stages(mail, place, wholes)
    tokens = pair_gather_stages(mail, place, tok, all_tok)
    weights[0]()
    tokens[0]()
    to_core[1]()

    count = links.shape[0] // 2
    mine = jnp.where(place.primary, links[...], links_got[...])
    reach[...] = jnp.zeros_like(reach)
    spot[...] = jnp.zeros_like(spot)
    reach[pl.ds(0, count)] = mine[:count]
    spot[pl.ds(0, count)] = mine[count:]
    for _ in range(turns):
        r = reach[...]
        reach[...] = jnp.minimum(r + mm(r.astype(BF16), r.astype(BF16)), 1.0)
    placed = spot[...].astype(BF16)
    linked = mm_t(mm(placed, reach[...].astype(BF16)).astype(BF16), placed).astype(BF16)
    rows, keys = bias.shape
    step = min(128, rows)

    def fill(i, _):
        first = i * step
        at = pl.ds(pl.multiple_of(first, step), step)
        q_slot = (place.block * rows + first + lax.broadcasted_iota(jnp.int32, (step, 128), 0)) // BLK
        pick_q = (q_slot == lax.broadcasted_iota(jnp.int32, (step, 128), 1)).astype(F32)
        own = mm(pick_q.astype(BF16), linked).astype(BF16)
        k_slot = lax.broadcasted_iota(jnp.int32, (128, keys), 1) // BLK
        pick_k = (k_slot == lax.broadcasted_iota(jnp.int32, (128, keys), 0)).astype(F32)
        seen = mm(own, pick_k.astype(BF16))
        q_at = place.block * rows + first + lax.broadcasted_iota(jnp.int32, (step, keys), 0)
        k_at = lax.broadcasted_iota(jnp.int32, (step, keys), 1)
        inside = (q_at // BLK == k_at // BLK) & (k_at <= q_at)
        bias[at] = jnp.where((seen > 0.5) | inside, 0.0, -1e30).astype(bias.dtype)
        return 0

    run(weights[1:] + spread[:1])
    run(tokens[1:-3])
    spread[1]()
    lax.fori_loop(0, rows // step, fill, 0)
    run(tokens[-3:-1])
    run(spread[2:])
    tokens[-1]()
    mail.finish()


def attend_unit(q_ref, k_ref, v_ref, bias_ref, o_ref, lse_ref, row, step, pair):
    at = pl.ds(pl.multiple_of(row, step), step)
    cols = pl.ds(pl.multiple_of(pair * PAIR, PAIR), PAIR)
    lane = lax.broadcasted_iota(jnp.int32, (1, PAIR), 1)
    q = q_ref[at, cols]
    k = k_ref[:, cols]
    v = v_ref[:, cols]
    out = jnp.zeros((step, PAIR), F32)
    lse = jnp.zeros((step, PAIR), F32)
    for h in range(2):
        own = (lane >= HEAD) if h else (lane < HEAD)
        s = mm_t(jnp.where(own, q, jnp.zeros_like(q)), k)
        if bias_ref is not None:
            s = s + bias_ref[at].astype(F32)
        peak = jnp.max(s, axis=1, keepdims=True)
        e = jnp.exp(s - peak)
        mass = jnp.sum(e, axis=1, keepdims=True)
        o = mm(e.astype(BF16), v)
        out = jnp.where(own, o / mass, out)
        lse = jnp.where(own, peak + jnp.log(mass), lse)
    o_ref[at, cols] = out.astype(BF16)
    lse_ref[at, cols] = lse


def attend_back_unit(q_ref, k_ref, v_ref, bias_ref, do_ref, o_ref, lse_ref, dq_ref, dk_acc, dv_acc, row, step, pair):
    at = pl.ds(pl.multiple_of(row, step), step)
    cols = pl.ds(pl.multiple_of(pair * PAIR, PAIR), PAIR)
    lane = lax.broadcasted_iota(jnp.int32, (1, PAIR), 1)
    k = k_ref[:, cols]
    v = v_ref[:, cols]
    q = q_ref[at, cols]
    do = do_ref[at, cols]
    both = do.astype(F32) * o_ref[at, cols].astype(F32)
    lse_pair = lse_ref[at, cols]
    dq = jnp.zeros((step, PAIR), F32)
    for h in range(2):
        own = (lane >= HEAD) if h else (lane < HEAD)
        q_h = jnp.where(own, q, jnp.zeros_like(q))
        do_h = jnp.where(own, do, jnp.zeros_like(do))
        delta = jnp.sum(jnp.where(own, both, 0.0), axis=1, keepdims=True)
        lse = lse_pair[:, h * HEAD : h * HEAD + 1]
        s = mm_t(q_h, k)
        if bias_ref is not None:
            s = s + bias_ref[at].astype(F32)
        e = jnp.exp(s - lse)
        dp = mm_t(do_h, v)
        ds = (e * (dp - delta)).astype(BF16)
        dq = jnp.where(own, mm(ds, k), dq)
        dk_acc[...] += t_mm(ds, q_h)
        dv_acc[...] += t_mm(e.astype(BF16), do_h)
    dq_ref[at, cols] = dq.astype(BF16) * BF16(HEAD**-0.5)


def attend_units(rows, width):
    step = min(256, rows)
    return rows // step, step, width // PAIR


def self_kernel(
    shape, arrive, leave, all_tok, w_qkv, vec, bias, enc, attn_in, attn_out, ffn_in,
    q, k, v, att, lse, all_enc, g_in, g_out, z_1, *sems,
):
    place, mail = open_kernel(shape, True, False, sems)
    n, rows, width = all_tok.shape
    three = g_in.shape[0]
    e = pair_gather_stages(mail, place, enc, all_enc)
    shards = [attn_in.at[pl.ds(attn_in.shape[0] - three, three)], attn_out]
    wholes = [g_in, g_out]
    w = block_stages(mail, place, shards, lambda i: [g.at[:, place.leaf, i] for g in wholes])
    zw = len(w)
    w += spread_stages(mail, place, wholes)
    f = block_stages(mail, place, [ffn_in], lambda i: [z_1.at[:, i]])
    w[0]()
    scale = HEAD**-0.5
    q[...] = ((mm(all_tok[place.block], w_qkv[0]) + vec[pl.ds(0, 1)]) * scale).astype(BF16)

    def project(i):
        x = all_tok[i]
        at = pl.ds(pl.multiple_of(i * rows, rows), rows)
        k[at] = mm(x, w_qkv[1]).astype(BF16)
        v[at] = (mm(x, w_qkv[2]) + vec[pl.ds(1, 1)]).astype(BF16)

    blocks, step, pairs = attend_units(rows, width)
    units = blocks * pairs
    t = lambda x: n + (x * units) // 12
    hooks, last = {}, n + units
    at_units(hooks, w[1 : zw - 1], [t(2)] * (zw - 2))
    at_units(hooks, f[:1] + w[zw - 1 : zw + 1], [t(2), t(3), t(3)])
    at_units(hooks, f[1:-1] + e[:1] + f[-1:], [t(7)] * (len(f) - 2) + [t(7), t(10)])
    tail = w[zw + 1 : -1] + e[1:-1] + w[-1:] + e[-1:]
    at_units(hooks, tail, [last] * len(tail))
    early = {at: stages for at, stages in hooks.items() if at < n}
    late = {at - n: stages for at, stages in hooks.items() if at >= n}
    hooked(n, project, early)
    leave(0, 1, 2)
    arrive()

    def unit(i):
        attend_unit(q, k, v, bias, att, lse, (i % blocks) * step, step, i // blocks)

    hooked(blocks * pairs, unit, late)
    mail.finish()


ROOT_HALF = 0.7071067811865476
NORM = 0.3989422804014327


def normed(v):
    centre = v - jnp.mean(v, axis=1, keepdims=True)
    inverse = lax.rsqrt(jnp.mean(centre * centre, axis=1, keepdims=True) + 1e-05)
    return centre * inverse, inverse


def normed_back(g, gain, hat, inverse):
    gx = g * gain
    mean_g = jnp.mean(gx, axis=1, keepdims=True)
    mean_gh = jnp.mean(gx * hat, axis=1, keepdims=True)
    return inverse * (gx - mean_g - hat * mean_gh)


def by_rows(rows, action):
    step = min(128, rows)

    def one(i, _):
        action(pl.ds(pl.multiple_of(i * step, step), step))
        return 0

    lax.fori_loop(0, rows // step, one, 0)


def row_sum(x):
    return jnp.sum(x, axis=0, keepdims=True)


def cross_kernel(
    shape, shifts, arrive, leave, att, all_tok, all_enc, w_in, w_out, vec, z_1, ffn_out, cot,
    hat1, inv1, first_low, cq, ck, cv, crossed, lse, g_1, g_2, my_cot, toks, *sems,
):
    place, mail = open_kernel(shape, True, True, sems)
    rows, width = cq.shape
    n, enc_rows, _ = all_enc.shape
    f = spread_stages(mail, place, [g_1], [z_1])
    w = block_stages(mail, place, [ffn_out], lambda i: [g_2.at[:, place.leaf, i]])
    zw = len(w)
    w += spread_stages(mail, place, [g_2])
    c = mirror_stages(mail, place, cot, my_cot)
    mine = mail.local(None, all_tok.at[place.block], toks)
    mine[0]()
    w[0]()
    f[0]()

    def project(i):
        x = all_enc[i]
        at = pl.ds(pl.multiple_of(i * enc_rows, enc_rows), enc_rows)
        ck[at] = mm(x, w_in[1]).astype(BF16)
        cv[at] = (mm(x, w_in[2]) + vec[pl.ds(4, 1)]).astype(BF16)

    hooked(n, project, {})
    leave(4, 5)
    arrive()
    mine[1]()
    scale = HEAD**-0.5

    def first(at):
        v = toks[at].astype(F32) + mm(att[at], w_out[0]) + vec[pl.ds(2, 1)]
        hat, inverse = normed(v)
        hat1[at] = hat
        inv1[at] = jnp.broadcast_to(inverse, (hat.shape[0], 128))
        low = (hat * vec[pl.ds(shifts, 1)] + vec[pl.ds(7, 1)]).astype(BF16)
        first_low[at] = low
        cq[at] = ((mm(low, w_in[0]) + vec[pl.ds(3, 1)]) * scale).astype(BF16)

    by_rows(rows, first)
    leave(0, 1, 2, 3)
    blocks, step, pairs = attend_units(rows, width)
    total = blocks * pairs
    t = lambda x: (x * total) // 12
    late = {}
    at_units(late, f[1:], [t(4), t(6)] + [t(10)] * (len(f) - 4) + [total])
    at_units(late, w[1 : zw - 1] + c[:1], [t(1)] * (zw - 2) + [t(3)])
    at_units(late, w[zw - 1 : zw + 1], [t(7)] * 2)
    at_units(late, w[zw + 1 :] + c[1:], [total] * (len(w) - zw))

    def unit(i):
        attend_unit(cq, ck, cv, None, crossed, lse, (i % blocks) * step, step, i // blocks)

    hooked(total, unit, late)
    mail.finish()


def ffn_kernel(
    shifts, arrive, leave, hat1, crossed, w_out, w1, w2, vec, b1, cot,
    out, gw1, gw2, gwo, g_crossed, g_pre2, sums, gb1,
    hat2, inv2, low2, acc, slope, hidden, g_pre3, g_ffn, acc2, g_cb,
):
    rows, width = crossed.shape
    wide = hidden.shape[1]
    piece = 512
    gain = lambda i: vec[pl.ds(shifts + i, 1)]
    shift = lambda i: vec[pl.ds(i, 1)]
    sums[...] = jnp.zeros_like(sums)

    def second(at):
        v = hat1[at] * gain(0) + shift(7) + mm(crossed[at], w_out[1]) + shift(5)
        hat, inverse = normed(v)
        hat2[at] = hat
        inv2[at] = jnp.broadcast_to(inverse, (hat.shape[0], 128))
        low2[at] = (hat * gain(1) + shift(8)).astype(BF16)

    by_rows(rows, second)
    arrive()
    acc[...] = jnp.zeros_like(acc)

    def up(j, _):
        cols = pl.ds(pl.multiple_of(j * piece, piece), piece)
        u = mm(low2[...], w1[:, cols]) + b1[:, cols]
        phi = 0.5 * (1.0 + lax.erf(u * ROOT_HALF))
        slope[:, cols] = phi + u * jnp.exp(-0.5 * u * u) * NORM
        h = (u * phi).astype(BF16)
        hidden[:, cols] = h
        acc[...] += mm(h, w2[cols])
        return 0

    lax.fori_loop(0, wide // piece, up, 0)

    def third(at):
        v = hat2[at] * gain(1) + shift(8) + acc[at] + shift(6)
        hat, inverse = normed(v)
        out[at] = (hat * gain(2) + shift(9)).astype(BF16)
        g = cot[at].astype(F32)
        sums[pl.ds(shifts + 2, 1)] += row_sum(g * hat)
        sums[pl.ds(9, 1)] += row_sum(g)
        back = normed_back(g, gain(2), hat, inverse)
        g_pre3[at] = back
        low = back.astype(BF16)
        g_ffn[at] = low
        sums[pl.ds(6, 1)] += row_sum(low.astype(F32))

    by_rows(rows, third)
    leave(0)
    acc2[...] = jnp.zeros_like(acc2)

    def down(j, _):
        cols = pl.ds(pl.multiple_of(j * piece, piece), piece)
        g = (mm_t(g_ffn[...], w2[cols]) * slope[:, cols]).astype(BF16)
        gb1[:, cols] = row_sum(g.astype(F32))
        gw2[cols] = t_mm(hidden[:, cols], g_ffn[...]).astype(BF16)
        gw1[:, cols] = t_mm(low2[...], g).astype(BF16)
        acc2[...] += mm_t(g, w1[:, cols])
        return 0

    lax.fori_loop(0, wide // piece, down, 0)
    leave(1, 2)

    def back_two(at):
        g = g_pre3[at] + acc2[at]
        hat = hat2[at]
        sums[pl.ds(shifts + 1, 1)] += row_sum(g * hat)
        sums[pl.ds(8, 1)] += row_sum(g)
        back = normed_back(g, gain(1), hat, inv2[at, :1])
        g_pre2[at] = back
        low = back.astype(BF16)
        g_cb[at] = low
        sums[pl.ds(5, 1)] += row_sum(low.astype(F32))
        g_crossed[at] = mm_t(low, w_out[1]).astype(BF16)

    by_rows(rows, back_two)
    gwo[...] = t_mm(crossed[...], g_cb[...]).astype(BF16)


def cross_back_kernel(
    shape, shifts, arrive, leave, cq, ck, cv, do, o, lse, first_low, hat1, inv1, all_enc, w_in, w_out, att, g_pre2, vec, sums_in, p_1, p_2, out_rows,
    g_in, g_wo, g_enc, g_att, g_pre1, sums, s_1, o_2, my_out, dq, dk, dv, g_br, dk_acc, dv_acc, *scratch,
):
    sems, scratch = scratch[:3], scratch[3:]
    place, mail = open_kernel(shape, True, True, sems)
    rows, width = cq.shape
    f_2, sum_2 = fold_stages(mail, place, p_2, scratch[:N_FOLD])
    f_1, sum_1 = fold_stages(mail, place, p_1, scratch[N_FOLD : 2 * N_FOLD])
    l_2 = line_stages(mail, place, sum_2, scratch[2 * N_FOLD], o_2)
    c = mirror_stages(mail, place, out_rows, my_out)
    f_2[0]()
    c[0]()
    blocks, step, pairs = attend_units(rows, width)
    total = blocks * pairs
    t = lambda x: (x * total) // 12
    hooks = {}
    more = len(f_1) - 5
    at_units(hooks, f_2[1:], [t(2), t(8), t(9), total] + [total] * more)
    at_units(hooks, l_2, [total, total + 6])
    at_units(hooks, f_1, [t(3), t(9), total + 3, total + 4, total + 6] + [total + 6] * more)
    at_units(hooks, c[1:], [total + 6])

    def unit(i):
        first = i % blocks == 0

        @pl.when(first)
        def _():
            dk_acc[...] = jnp.zeros_like(dk_acc)
            dv_acc[...] = jnp.zeros_like(dv_acc)

        pair = i // blocks
        attend_back_unit(cq, ck, cv, None, do, o, lse, dq, dk_acc, dv_acc, (i % blocks) * step, step, pair)

        @pl.when(i % blocks == blocks - 1)
        def _():
            cols = pl.ds(pl.multiple_of(pair * PAIR, PAIR), PAIR)
            dk[:, cols] = dk_acc[...].astype(BF16)
            dv[:, cols] = dv_acc[...].astype(BF16)

    late = {at: hooks.pop(at) for at in list(hooks) if at >= total}
    hooked(total, unit, hooks)
    n, enc_rows, _ = all_enc.shape
    arrive()
    flat = all_enc.reshape(n * enc_rows, width)

    def query_grads():
        sums[...] = sums_in[...]
        sums[pl.ds(3, 1)] = row_sum(dq[...].astype(F32))
        sums[pl.ds(4, 1)] = row_sum(dv[...].astype(F32))
        g_in[0] = t_mm(first_low[...], dq[...]).astype(BF16)

    def key_grads():
        g_in[1] = t_mm(flat[...], dk[...]).astype(BF16)

    def value_grads():
        g_in[2] = t_mm(flat[...], dv[...]).astype(BF16)

    def encoder(i, _):
        at = pl.ds(pl.multiple_of(i * enc_rows, enc_rows), enc_rows)
        g_enc[i] = (mm_t(dk[at], w_in[1]) + mm_t(dv[at], w_in[2])).astype(BF16)
        return 0

    def back_one(at):
        g = g_pre2[at] + mm_t(dq[at], w_in[0])
        hat = hat1[at]
        sums[pl.ds(shifts, 1)] += row_sum(g * hat)
        sums[pl.ds(7, 1)] += row_sum(g)
        back = normed_back(g, vec[pl.ds(shifts, 1)], hat, inv1[at, :1])
        g_pre1[at] = back
        low = back.astype(BF16)
        g_br[at] = low
        sums[pl.ds(2, 1)] += row_sum(low.astype(F32))
        g_att[at] = mm_t(low, w_out[0]).astype(BF16)

    def out_grads():
        leave(0, 2, 3, 4)
        g_wo[...] = t_mm(att[...], g_br[...]).astype(BF16)

    steps = [
        query_grads,
        key_grads,
        value_grads,
        lambda: lax.fori_loop(0, n, encoder, 0),
        lambda: by_rows(rows, back_one),
        out_grads,
    ]
    for at, step_of in enumerate(steps):
        run(late.get(total + at, []))
        step_of()
    run(late[total + len(steps)])
    s_1[...] = sum_1[...]
    mail.finish()


def self_back_kernel(
    shape, arrive, leave, q, k, v, bias, do, o, lse, z_1, sums_in, all_tok, p_in, p_o0, p_o1, p_enc,
    dq, dk, dv, g_qkv, o_1, o_in, o_o0, o_o1, o_enc, sums, dk_acc, dv_acc, *scratch,
):
    sems, scratch = scratch[:3], scratch[3:]
    place, mail = open_kernel(shape, True, False, sems)
    rows, width = q.shape
    l_1 = line_stages(mail, place, z_1, scratch[0], o_1)
    rest = scratch[1:]
    f_in, sum_in = fold_stages(mail, place, p_in, rest[:N_FOLD])
    f_o0, sum_o0 = fold_stages(mail, place, p_o0, rest[N_FOLD : 2 * N_FOLD])
    f_o1, sum_o1 = fold_stages(mail, place, p_o1, rest[2 * N_FOLD : 3 * N_FOLD])
    rest = rest[3 * N_FOLD :]
    l_in = line_stages(mail, place, sum_in, rest[0], o_in)
    l_o0 = line_stages(mail, place, sum_o0, rest[1], o_o0)
    l_o1 = line_stages(mail, place, sum_o1, rest[2], o_o1)
    e = pair_sum_stages(mail, place, p_enc, rest[3:], o_enc)
    f_w = [functools.partial(run, three) for three in zip(f_in, f_o0, f_o1)]
    l_w = [functools.partial(run, three) for three in zip(l_in, l_o0, l_o1)]
    f_w[0]()
    l_1[0]()
    blocks, step, pairs = attend_units(rows, width)
    total = blocks * pairs
    t = lambda x: (x * total) // 12
    hooks = {}
    more = len(f_w) - 5
    at_units(hooks, f_w[1:], [t(2), t(6), t(7), t(10)] + [t(10)] * more)
    at_units(hooks, e[:-1], [t(2), t(3), t(4)] + [t(5)] * (len(e) - 4))
    at_units(hooks, l_1[1:] + l_w[:1], [t(6), t(10)])
    at_units(hooks, e[-1:] + l_w[1:], [total] * 2)

    def unit(i):
        @pl.when(i % blocks == 0)
        def _():
            dk_acc[...] = jnp.zeros_like(dk_acc)
            dv_acc[...] = jnp.zeros_like(dv_acc)

        pair = i // blocks
        attend_back_unit(q, k, v, bias, do, o, lse, dq, dk_acc, dv_acc, (i % blocks) * step, step, pair)

        @pl.when(i % blocks == blocks - 1)
        def _():
            cols = pl.ds(pl.multiple_of(pair * PAIR, PAIR), PAIR)
            dk[:, cols] = dk_acc[...].astype(BF16)
            dv[:, cols] = dv_acc[...].astype(BF16)

    last = hooks.pop(total)
    hooked(total, unit, hooks)
    sums[...] = sums_in[...]
    sums[pl.ds(0, 1)] = row_sum(dq[...].astype(F32))
    sums[pl.ds(1, 1)] = row_sum(dv[...].astype(F32))
    leave(0, 1, 2)
    arrive()
    flat = all_tok.reshape(k.shape[0], width)
    g_qkv[0] = t_mm(all_tok[place.block], dq[...]).astype(BF16)
    g_qkv[1] = t_mm(flat[...], dk[...]).astype(BF16)
    g_qkv[2] = t_mm(flat[...], dv[...]).astype(BF16)
    run(last)
    mail.finish()


def closing_kernel(shape, arrive, leave, p_qkv, p_small, dq, dk, dv, w_qkv, g_pre1, o_qkv, o_small, o_tok, p_tok, *scratch):
    sems, scratch = scratch[:3], scratch[3:]
    place, mail = open_kernel(shape, True, False, sems)
    f_q, sum_q = fold_stages(mail, place, p_qkv, scratch[:N_FOLD])
    f_s, sum_s = fold_stages(mail, place, p_small, scratch[N_FOLD : 2 * N_FOLD])
    rest = scratch[2 * N_FOLD :]
    l_q = line_stages(mail, place, sum_q, rest[0], o_qkv)
    l_s = line_stages(mail, place, sum_s, rest[1], o_small)
    t = pair_sum_stages(mail, place, p_tok, rest[2:], o_tok)
    a = [functools.partial(run, two) for two in zip(f_q, f_s)]
    b = [functools.partial(run, two) for two in zip(l_q, l_s)]
    n, rows, width = p_tok.shape
    step = min(128, rows)

    def terms(r):
        j = place.shard_of_rank(r)

        def some(i, _):
            at = pl.ds(pl.multiple_of(i * step, step), step)
            far = pl.ds(pl.multiple_of(j * rows + i * step, step), step)
            total = mm_t(dk[far], w_qkv[1]) + mm_t(dv[far], w_qkv[2])
            p_tok[j, at] = total.astype(BF16)

            @pl.when(j == place.block)
            def _():
                own = g_pre1[at] + mm_t(dq[at], w_qkv[0])
                p_tok[j, at] = (total + own).astype(BF16)

            return 0

        lax.fori_loop(0, rows // step, some, 0)

    a[0]()
    arrive()
    terms(n - 1)
    t[0]()
    for k in range(1, n):
        terms(n - 1 - k)
        t[k]()
        if k < len(a):
            a[k]()
    run(a[n:])
    run(b[:1])
    run(t[n:-1])
    t[-1]()
    run(b[1:])
    mail.finish()


def body(
    tokens, encoded, cotangent, parent, assignment, attn_in, attn_out, ffn_in, ffn_out, shifts, gains, ffn_bias
):
    shape = Shape(lax.axis_size("leaf"), lax.axis_size("path"))
    leafs, paths = shape.leafs, shape.paths
    devices = leafs * paths
    scale = HEAD ** (-0.5)
    tokens, encoded, cotangent = tokens[0], encoded[0], cotangent[0]
    rows, width = tokens.shape
    enc_rows = encoded.shape[0]
    hidden_width = ffn_in.shape[1]
    tree_rows, tree_enc = rows * paths, enc_rows * paths
    piece = shifts.shape[1]
    n_shift, n_gain, n_bias = shifts.shape[0], gains.shape[0], ffn_bias.shape[0]
    n_vec = n_shift + n_gain
    ffn_in, ffn_out = ffn_in[None], ffn_out[None]

    def sds(shape_, dtype=BF16):
        return jax.ShapeDtypeStruct(shape_, dtype)

    small = jnp.concatenate([shifts.reshape(-1), gains.reshape(-1), ffn_bias])
    small_rows = -(-small.shape[0] // 4096) * 16
    small = jnp.pad(small, (0, small_rows * 256 - small.shape[0])).reshape(1, small_rows, 256)
    blocks = parent.shape[1]
    ids = jnp.arange(blocks, dtype=jnp.int32)
    lanes = jnp.arange(128, dtype=jnp.int32)
    links = jnp.concatenate(
        [
            (parent[0][:, None] == lanes[None, :]) & (ids[:, None] != lanes[None, :]),
            assignment[0][:, None] == lanes[None, :],
        ]
    ).astype(F32)

    three = 3
    all_tok, g_small, w_qkv, bias = kernel_call(
        functools.partial(opening_kernel, shape, blocks.bit_length()),
        "opening",
        0,
        [tokens, small, attn_in, links],
        [ANY, ANY, ANY, VMEM],
        [
            sds((paths, rows, width)),
            sds((1, leafs, paths) + small.shape[1:]),
            sds((three, leafs, paths) + attn_in.shape[1:]),
            sds((rows, tree_rows)),
        ],
        [ANY, ANY, ANY, VMEM],
        mail_scratch()
        + [pltpu.VMEM(links.shape, F32), pltpu.VMEM((128, 128), F32), pltpu.VMEM((128, 128), F32)],
    )
    flat = g_small.reshape(devices, -1)
    vec = flat[:, : n_vec * piece].reshape(devices, n_vec, piece).transpose(1, 0, 2)
    vec = jnp.pad(vec.reshape(n_vec, width).astype(F32), ((0, -n_vec % 8), (0, 0)))
    b1 = flat[:, n_vec * piece : n_vec * piece + n_bias].reshape(1, hidden_width).astype(F32)
    w_qkv = w_qkv.reshape(three, width, width)

    rest_in = attn_in.shape[0] - three
    q, k, v, attended, self_mass, all_enc, w_in, w_out, z_1 = kernel_call(
        functools.partial(self_kernel, shape),
        "self_attention",
        1,
        [all_tok, w_qkv, vec, bias, encoded, attn_in, attn_out, ffn_in],
        [VMEM] * 4 + [ANY] * 4,
        [
            sds((rows, width)),
            sds((tree_rows, width)),
            sds((tree_rows, width)),
            sds((rows, width)),
            sds((rows, width), F32),
            sds((paths, enc_rows, width)),
            sds((rest_in, leafs, paths) + attn_in.shape[1:]),
            sds((attn_out.shape[0], leafs, paths) + attn_out.shape[1:]),
            sds((1, paths) + ffn_in.shape[1:]),
        ],
        [VMEM] * 5 + [ANY] * 4,
        mail_scratch(),
        late=(3,),
        early=(0, 1, 2),
    )
    w_in = w_in.reshape(rest_in, width, width)
    w_out = w_out.reshape(attn_out.shape[0], width, width)

    hat1, inv1, first_low, cq, ck, cv, crossed, cross_mass, w1, w2, my_cot = kernel_call(
        functools.partial(cross_kernel, shape, n_shift),
        "cross_attention",
        2,
        [attended, all_tok, all_enc, w_in, w_out, vec, z_1, ffn_out, cotangent],
        [VMEM, ANY] + [VMEM] * 4 + [ANY] * 3,
        [
            sds((rows, width), F32),
            sds((rows, 128), F32),
            sds((rows, width)),
            sds((rows, width)),
            sds((tree_enc, width)),
            sds((tree_enc, width)),
            sds((rows, width)),
            sds((rows, width), F32),
            sds((1, leafs, paths) + ffn_in.shape[1:]),
            sds((1, leafs, paths) + ffn_out.shape[1:]),
            sds((rows, width)),
        ],
        [VMEM] * 8 + [ANY] * 3,
        [pltpu.VMEM((rows, width), BF16)] + mail_scratch(),
        late=(0, 4),
        early=(0, 1, 2, 3, 4, 5),
    )
    w1 = w1.reshape(width, hidden_width)
    w2 = w2.reshape(hidden_width, width)
    vm = lambda s, dtype=BF16: pltpu.VMEM(s, dtype)
    output, g_w1, g_w2, g_wo1, g_crossed, g_pre2, sums, g_b1 = kernel_call(
        functools.partial(ffn_kernel, n_shift),
        "feed_forward",
        None,
        [hat1, crossed, w_out, w1, w2, vec, b1, my_cot],
        [VMEM] * 8,
        [
            sds((rows, width)),
            sds((width, hidden_width)),
            sds((hidden_width, width)),
            sds((width, width)),
            sds((rows, width)),
            sds((rows, width), F32),
            sds(vec.shape, F32),
            sds((1, hidden_width), F32),
        ],
        [VMEM] * 8,
        [
            vm((rows, width), F32),
            vm((rows, 128), F32),
            vm((rows, width)),
            vm((rows, width), F32),
            vm((rows, hidden_width), F32),
            vm((rows, hidden_width)),
            vm((rows, width), F32),
            vm((rows, width)),
            vm((rows, width), F32),
            vm((rows, width)),
        ],
        late=(3, 4, 7),
        early=(0, 1, 2),
    )

    def spread(g):
        return g.reshape(
            g.shape[0], shape.A, shape.B, 2, paths, g.shape[1] // devices, g.shape[2]
        )

    r1, r2 = ffn_in.shape[1:], ffn_out.shape[1:]
    g_rest, g_wo0, g_enc, g_att, g_pre1, sums, s_1, o_w2, output = kernel_call(
        functools.partial(cross_back_kernel, shape, n_shift),
        "cross_back",
        3,
        [
            cq, ck, cv, g_crossed, crossed, cross_mass, first_low, hat1, inv1, all_enc, w_in, w_out, attended,
            g_pre2, vec, sums, spread(g_w1[None]), spread(g_w2[None]), output,
        ],
        [VMEM] * 16 + [ANY] * 3,
        [
            sds((rest_in, width, width)),
            sds((width, width)),
            sds((paths, enc_rows, width)),
            sds((rows, width)),
            sds((rows, width), F32),
            sds(vec.shape, F32),
            sds((1, paths) + r1),
            sds((1,) + r2, F32),
            sds((rows, width)),
        ],
        [VMEM] * 8 + [ANY],
        [vm((rows, width)), vm((tree_enc, width)), vm((tree_enc, width)), vm((rows, width))]
        + [pltpu.VMEM((tree_enc, PAIR), F32)] * 2
        + mail_scratch()
        + fold_scratch(shape, 1, *r2, BF16)
        + fold_scratch(shape, 1, *r1, BF16)
        + line_scratch(shape, 1, *r2, BF16),
        late=(6, 7, 8, 9, 10, 11, 12, 13),
        early=(0, 2, 3, 4),
    )
    ri = attn_in.shape[1:]
    g_q, g_k, g_v, g_qkv, o_w1, o_in, o_o0, o_o1, o_enc, sums = kernel_call(
        functools.partial(self_back_kernel, shape),
        "self_back",
        4,
        [
            q, k, v, bias, g_att, attended, self_mass, s_1, sums, all_tok, spread(g_rest),
            spread(g_wo0[None]), spread(g_wo1[None]), g_enc,
        ],
        [VMEM] * 10 + [ANY] * 3 + [VMEM],
        [
            sds((rows, width)),
            sds((tree_rows, width)),
            sds((tree_rows, width)),
            sds((three, width, width)),
            sds((1,) + r1, F32),
            sds((rest_in,) + ri, F32),
            sds((1,) + ri, F32),
            sds((1,) + ri, F32),
            sds((enc_rows, width), F32),
            sds(vec.shape, F32),
        ],
        [VMEM] * 10,
        [pltpu.VMEM((tree_rows, PAIR), F32)] * 2
        + mail_scratch()
        + line_scratch(shape, 1, *r1, BF16)
        + fold_scratch(shape, rest_in, *ri, BF16)
        + fold_scratch(shape, 1, *ri, BF16)
        + fold_scratch(shape, 1, *ri, BF16)
        + line_scratch(shape, rest_in, *ri, BF16)
        + line_scratch(shape, 1, *ri, BF16)
        + line_scratch(shape, 1, *ri, BF16)
        + pair_sum_scratch(shape, enc_rows, width),
        late=(9,),
        early=(0, 1, 2),
    )
    g_vec = sums[:n_vec]
    g_small = jnp.concatenate(
        [
            g_vec.reshape(n_vec, devices, piece).transpose(1, 0, 2).reshape(devices, -1),
            g_b1.reshape(devices, n_bias),
        ],
        axis=1,
    )
    small_count = g_small.shape[1]
    g_small_rows = -(-small_count // 2048) * 8
    g_small = jnp.pad(g_small, ((0, 0), (0, g_small_rows * 256 - small_count)))
    p_small = g_small.reshape(1, shape.A, shape.B, 2, paths, g_small_rows, 256)
    o_qkv, o_small, o_tok = kernel_call(
        functools.partial(closing_kernel, shape),
        "closing",
        5,
        [spread(g_qkv), p_small, g_q, g_k, g_v, w_qkv, g_pre1],
        [ANY, ANY] + [VMEM] * 5,
        [
            sds((three,) + ri, F32),
            sds((1, g_small_rows, 256), F32),
            sds((rows, width), F32),
        ],
        [VMEM] * 3,
        [vm((paths, rows, width))]
        + mail_scratch()
        + fold_scratch(shape, three, *ri, BF16)
        + fold_scratch(shape, 1, g_small_rows, 256, F32)
        + line_scratch(shape, three, *ri, BF16)
        + line_scratch(shape, 1, g_small_rows, 256, F32)
        + pair_sum_scratch(shape, rows, width),
        late=(2, 3, 4, 5, 6),
    )
    o_small = o_small.reshape(-1)
    o_vec = o_small[: n_vec * piece].reshape(n_vec, piece)
    return (
        output[None],
        o_tok[None],
        o_enc[None],
        jnp.concatenate([o_qkv, o_in]),
        jnp.concatenate([o_o0, o_o1]),
        o_w1[0],
        o_w2[0],
        o_vec[:n_shift],
        o_vec[n_shift:],
        o_small[n_vec * piece : n_vec * piece + n_bias],
    )


def solution(mesh):
    both = ("leaf", "path")
    rows = P("leaf", "path", None)
    weights = (P(None, both, None), P(None, both, None), P(both, None), P(both, None), P(None, both), P(None, both), P(both))
    return jax.shard_map(
        body,
        mesh=mesh,
        in_specs=(rows, rows, rows, P("leaf", None), P("leaf", None)) + weights,
        out_specs=(rows, rows, rows) + weights,
        check_vma=False,
    )
```
